32 devices in a mesh: dp: 8 (over z, x), space: 4 (over y, core).
Axes of the slice: x: 2, y: 2, z: 4, core: 2. Of those that a mesh axis runs over, the one named last changes fastest.
Arguments:
- volume_in: bfloat16 [8, 4, 16, 64, 128], P('dp', 'space'), may hold values from -6 to 6
- hidden_act: bfloat16 [8, 4, 32, 64, 128], P('dp', 'space'), may hold values from -6 to 6
- out_cot: bfloat16 [8, 4, 32, 64, 128], P('dp', 'space'), may hold values from -6 to 6
- kernel_one: bfloat16 [3, 3, 3, 16, 32], replicated, may hold values from -0.3125 to 0.3125
- kernel_two: bfloat16 [3, 3, 3, 32, 32], replicated, may hold values from -0.21875 to 0.21875
- grad_bucket: float32 [32, 524288], P(('dp', 'space')), may hold values from -1 to 1
Outputs:
- grad_input: bfloat16 [8, 4, 16, 64, 128], P('dp', 'space')
- grad_kernel_one: float32 [3, 3, 3, 16, 32], replicated
- grad_kernel_two: float32 [3, 3, 3, 32, 32], replicated
- bucket_sum: float32 [524288], replicated
The draws below stay inside these ranges and needn't reach their ends.
All inputs are finite; a program needn't handle non-finite values.
Results may differ from the reference program's by a relative error of at most 0.013.
Values may be sent and summed in bfloat16 or wider, within the bound.
No kernel may reach another device: no remote copies, remote signals or barrier semaphores. Data moves between devices by JAX's collectives and lax.ppermute only.
A program may use at most 128 MiB of HBM per device.

```python
import math
import jax
import jax.numpy as jnp
from jax import lax

C0 = 16
C1 = 32
C2 = 32
NX = 64
NY = 128
BUCKET = 524288
SAMPLES = 8
NZ = 4
DEVICES = 32


def block_scale(own_key, dims, cuts, least, top_value):
    gain, own = 1.0, jax.random.fold_in(own_key, 6)
    for dim, parts in cuts:
        draws = jnp.exp(jax.random.uniform(jax.random.fold_in(own, dim), (parts,), jnp.float32, least / len(cuts), top_value / len(cuts)))
        gain = gain * jnp.repeat(draws, dims[dim] // parts).reshape([-1 if axis == dim else 1 for axis in range(len(dims))])
    return gain


def normal_values(own_key, extent, spread, reach, shards=(), dtype=jnp.bfloat16):
    result = jax.random.normal(own_key, extent, jnp.float32) * spread
    if len(shards) > 0:
        result = block_scale(own_key, extent, shards, -0.22, 0.18) * result
    return jnp.clip(result, min=-reach, max=reach).astype(dtype)


def setup_inputs(seed: int = 0) -> dict:
    key_of = jax.random.split(jax.random.key(seed), 7)
    volume_in = normal_values(key_of[0], (SAMPLES, NZ, C0, NX, NY), 1.0, 6.0, ((0, 8), (1, 4)))
    hidden_act = normal_values(key_of[1], (SAMPLES, NZ, C1, NX, NY), 1.0, 6.0, ((0, 8), (1, 4)))
    out_cot = normal_values(key_of[2], (SAMPLES, NZ, C2, NX, NY), 1.0, 6.0, ((0, 8), (1, 4)))
    kernel_one = normal_values(key_of[3], (3, 3, 3, C0, C1), (27 * C0) ** -0.5, 0.3125)
    kernel_two = normal_values(key_of[4], (3, 3, 3, C1, C2), (27 * C1) ** -0.5, 0.21875)
    grad_bucket = normal_values(key_of[5], (DEVICES, BUCKET), 0.0625, 1.0, ((0, 32),), jnp.float32)
    return dict(volume_in=volume_in, hidden_act=hidden_act, out_cot=out_cot, kernel_one=kernel_one, kernel_two=kernel_two, grad_bucket=grad_bucket)


def convolve(field, kernel):
    numbers = lax.ConvDimensionNumbers(lhs_spec=(0, 2, 1, 3, 4), rhs_spec=(4, 3, 0, 1, 2), out_spec=(0, 2, 1, 3, 4))
    return lax.conv_general_dilated(field.astype(jnp.float32), kernel.astype(jnp.float32), (1, 1, 1), ((1, 1), (1, 1), (1, 1)), dimension_numbers=numbers, precision=lax.Precision.HIGHEST)

def flipped(kernel):
    return jnp.swapaxes(kernel[::-1, ::-1, ::-1], 3, 4)

def kernel_terms(field, cotan):
    padded = jnp.pad(field.astype(jnp.float32), ((0, 0), (1, 1), (0, 0), (1, 1), (1, 1)))
    depth_cells, width_x, width_y = (cotan.shape[1], cotan.shape[3], cotan.shape[4])
    cot_wide = cotan.astype(jnp.float32)
    planes = []
    for along_z in range(3):
        for along_x in range(3):
            for along_y in range(3):
                window = padded[:, along_z:along_z + depth_cells, :, along_x:along_x + width_x, along_y:along_y + width_y]
                planes.append(jnp.einsum('nzcxy,nzdxy->cd', window, cot_wide, precision=lax.Precision.HIGHEST))
    return jnp.stack(planes).reshape((3, 3, 3) + planes[0].shape)

def reference(volume_in, hidden_act, out_cot, kernel_one, kernel_two, grad_bucket):

    def single(sample):
        volume, act, cotan = sample
        volume, act, cotan = (volume[None], act[None], cotan[None])
        act_grad = convolve(cotan, flipped(kernel_two))
        slope = jnp.where(act > 0, 1.0, 0.2).astype(jnp.float32)
        pre_grad = (act_grad * slope).astype(jnp.bfloat16)
        grad_in = convolve(pre_grad, flipped(kernel_one)).astype(jnp.bfloat16)
        return (grad_in[0], kernel_terms(volume, pre_grad), kernel_terms(act, cotan))
    grad_input, terms_one, terms_two = lax.map(single, (volume_in, hidden_act, out_cot))
    scale = 1.0 / math.sqrt(SAMPLES * NZ * NX * NY)
    grad_kernel_one = lax.optimization_barrier(jnp.sum(terms_one, axis=0)) * scale
    grad_kernel_two = lax.optimization_barrier(jnp.sum(terms_two, axis=0)) * scale
    bucket_sum = lax.optimization_barrier(jnp.sum(grad_bucket, axis=0))
    return (grad_input, grad_kernel_one, grad_kernel_two, bucket_sum)
```

```python
import math

import jax
import jax.numpy as jnp
from jax import lax
from jax.sharding import PartitionSpec as P

EVERY = ("dp", "space")


def extended(value, sides, width):
    for axis, dim in sides:
        count, length = (lax.axis_size(axis), value.shape[dim])
        up = [(i, (i + 1) % count) for i in range(count - 1)]
        down = [(j, i) for i, j in up]
        last = lax.slice_in_dim(value, length - width, length, axis=dim)
        leading = lax.slice_in_dim(value, 0, width, axis=dim)
        before = lax.ppermute(last, axis, up)
        after = lax.ppermute(leading, axis, down)
        value = jnp.concatenate([before, value, after], axis=dim)
    return value


def convolve_planar(field, kernel):
    numbers = lax.ConvDimensionNumbers(
        lhs_spec=(0, 2, 1, 3, 4), rhs_spec=(4, 3, 0, 1, 2), out_spec=(0, 2, 1, 3, 4)
    )
    return lax.conv_general_dilated(
        field,
        kernel,
        (1, 1, 1),
        ((0, 0), (1, 1), (1, 1)),
        dimension_numbers=numbers,
        preferred_element_type=jnp.float32,
    )


def flipped(kernel):
    return jnp.swapaxes(kernel[::-1, ::-1, ::-1], 3, 4)


def kernel_terms(field, haloed_cotan):
    padded = jnp.pad(field, ((0, 0), (0, 0), (0, 0), (1, 1), (1, 1)))
    depth_cells, width_x, width_y = (field.shape[1], field.shape[3], field.shape[4])
    planes = []
    for along_z in range(3):
        cotan = haloed_cotan[:, 2 - along_z : 2 - along_z + depth_cells]
        for along_x in range(3):
            for along_y in range(3):
                window = padded[:, :, :, along_x : along_x + width_x, along_y : along_y + width_y]
                planes.append(
                    jnp.einsum("nzcxy,nzdxy->cd", window, cotan, preferred_element_type=jnp.float32)
                )
    return jnp.stack(planes).reshape((3, 3, 3) + planes[0].shape)


def summed_share(value):
    count = lax.axis_size(EVERY)
    parts = value.astype(jnp.bfloat16).reshape(count, -1)
    parts = lax.all_to_all(parts, EVERY, 0, 0)
    return jnp.sum(parts.astype(jnp.float32), axis=0)


def per_device(volume_in, hidden_act, out_cot, kernel_one, kernel_two, grad_bucket):
    bucket_share = summed_share(grad_bucket[0]).astype(jnp.bfloat16)
    bucket_sum = lax.all_gather(bucket_share, EVERY, tiled=True).astype(jnp.float32)
    haloed_cot = extended(out_cot, (("space", 1),), 1)
    act_grad = convolve_planar(haloed_cot, flipped(kernel_two))
    slope = jnp.where(hidden_act > 0, 1.0, 0.2).astype(jnp.float32)
    pre_grad = (act_grad * slope).astype(jnp.bfloat16)
    haloed_pre = extended(pre_grad, (("space", 1),), 1)
    grad_input = convolve_planar(haloed_pre, flipped(kernel_one)).astype(jnp.bfloat16)
    local_two = kernel_terms(hidden_act, haloed_cot)
    local_one = kernel_terms(volume_in, haloed_pre)
    count = (
        volume_in.shape[0]
        * lax.axis_size("dp")
        * volume_in.shape[1]
        * lax.axis_size("space")
        * volume_in.shape[3]
        * volume_in.shape[4]
    )
    scale = 1.0 / math.sqrt(count)
    flat = jnp.concatenate([local_one.reshape(-1), local_two.reshape(-1)]) * scale
    pad = -flat.shape[0] % lax.axis_size(EVERY)
    flat = jnp.pad(flat, (0, pad))
    total = lax.all_gather(summed_share(flat), EVERY, tiled=True)
    total_one = total[: local_one.size].reshape(local_one.shape)
    total_two = total[local_one.size : local_one.size + local_two.size].reshape(local_two.shape)
    return (grad_input, total_one, total_two, bucket_sum)


def solution(mesh):
    in_specs = (
        P("dp", "space", None, None, None),
        P("dp", "space", None, None, None),
        P("dp", "space", None, None, None),
        P(),
        P(),
        P(("dp", "space"), None),
    )
    out_specs = (P("dp", "space", None, None, None), P(), P(), P())
    return jax.shard_map(
        per_device, mesh=mesh, in_specs=in_specs, out_specs=out_specs, check_vma=False
    )
```

```python
import math

import jax
import jax.numpy as jnp
from jax import lax
from jax.experimental import pallas as pl
from jax.experimental.pallas import tpu as pltpu
from jax.sharding import Mesh, PartitionSpec as P

SPACE = ("slab", "core")
EVERY = ("dp", "slab", "core")
GROUP = 4
LANES = 128
BF16 = jnp.bfloat16
F32 = jnp.float32


def ceil_to(value, step):
    return -(-value // step) * step


def slid(value, step):
    lane = lax.broadcasted_iota(jnp.int32, value.shape, 1)
    width = value.shape[1]
    keep = lane >= step if step > 0 else lane < width + step
    return jnp.where(keep, pltpu.roll(value, step % width, 1), 0.0)


def beside(window, rows, step, count):
    return jnp.concatenate([window[g * step : g * step + rows] for g in range(count)], axis=1)


def turned(src, flat, dst, offset, pitch, lead):
    chans, length, _ = src.shape

    def stage(c, carry):
        flat[pl.ds(pl.multiple_of(c * length, length), length), :] = src[c].astype(F32)
        return carry

    lax.fori_loop(0, chans, stage, 0, unroll=4)

    def gather(x, carry):
        rows = flat[pl.ds(x, chans, stride=length), :]
        at = pl.multiple_of((x + lead) * pitch + offset, 16)
        dst[pl.ds(at, chans), :] = rows.astype(BF16)
        return carry

    lax.fori_loop(0, length, gather, 0, unroll=4)


def compute_kernel(
    cot_m, cot_0, cot_p, act, vol_m, vol_0, vol_p, w_two, w_one,
    terms, own, up, down,
    flat, cots, acts, vols, pres, acc_two, acc_one,
):
    c1, length, _ = act.shape
    c0 = vol_0.shape[0]
    c2 = cot_0.shape[0]
    wide_two, wide_one = 3 * c2, 3 * c0

    for buffer, rows in ((cots, wide_two), (vols, wide_one), (pres, c1)):
        zeros = jnp.zeros((rows, LANES), BF16)
        buffer[0:rows, :] = zeros
        buffer[(length + 1) * rows : (length + 2) * rows, :] = zeros
    for place, src in enumerate((cot_m, cot_0, cot_p)):
        turned(src, flat, cots, place * c2, wide_two, 1)
    for place, src in enumerate((vol_m, vol_0, vol_p)):
        turned(src, flat, vols, place * c0, wide_one, 1)
    turned(act, flat, acts, 0, c1, 0)
    acc_two[...] = jnp.zeros_like(acc_two)
    acc_one[...] = jnp.zeros_like(acc_one)

    def first(step, carry):
        x = step * GROUP
        window = cots[pl.ds(pl.multiple_of(x * wide_two, 16), (GROUP + 2) * wide_two), :]
        right = beside(window, 3 * wide_two, wide_two, GROUP)
        sums = jnp.dot(w_two[...], right, preferred_element_type=F32)
        field = acts[pl.ds(pl.multiple_of(x * c1, 16), GROUP * c1), :].astype(F32)
        columns = []
        for g in range(GROUP):
            part = sums[:, g * LANES : (g + 1) * LANES]
            grad = slid(part[0:c1], 1) + part[c1 : 2 * c1] + slid(part[2 * c1 : 3 * c1], -1)
            value = field[g * c1 : (g + 1) * c1]
            pre = (grad * jnp.where(value > 0, 1.0, 0.2)).astype(BF16)
            pres[pl.ds(pl.multiple_of((x + g + 1) * c1, 16), c1), :] = pre
            columns.append(
                jnp.concatenate([slid(value, 1), value, slid(value, -1)], axis=0).astype(BF16)
            )
        left = jnp.concatenate(columns, axis=1)
        acc_two[...] += lax.dot_general(
            right, left, (((1,), (1,)), ((), ())), preferred_element_type=F32
        )
        return carry

    lax.fori_loop(0, length // GROUP, first, 0)

    def second(step, carry):
        x = step * GROUP
        window = pres[pl.ds(pl.multiple_of(x * c1, 16), (GROUP + 2) * c1), :]
        sums = jnp.dot(w_one[...], beside(window, 3 * c1, c1, GROUP), preferred_element_type=F32)
        columns = []
        for g in range(GROUP):
            part = sums[:, g * LANES : (g + 1) * LANES]
            at = pl.ds(pl.multiple_of((x + g) * c0, 16), c0)
            for i, out in ((0, up), (1, own), (2, down)):
                b = 3 * i * c0
                grad = (
                    slid(part[b : b + c0], 1)
                    + part[b + c0 : b + 2 * c0]
                    + slid(part[b + 2 * c0 : b + 3 * c0], -1)
                )
                out[at, :] = grad.astype(out.dtype)
            value = window[(g + 1) * c1 : (g + 2) * c1].astype(F32)
            columns.append(
                jnp.concatenate([slid(value, -1), value, slid(value, 1)], axis=0).astype(BF16)
            )
        left = jnp.concatenate(columns, axis=1)
        volume = vols[pl.ds(pl.multiple_of(x * wide_one, 16), (GROUP + 2) * wide_one), :]
        right = beside(volume, 3 * wide_one, wide_one, GROUP)
        acc_one[...] += lax.dot_general(
            right, left, (((1,), (1,)), ((), ())), preferred_element_type=F32
        )
        return carry

    lax.fori_loop(0, length // GROUP, second, 0)

    terms[...] = jnp.zeros_like(terms)
    two = acc_two[...].T
    rows, width = two.shape
    blocks = -(-width // LANES)
    for block in range(blocks):
        part = two[:, block * LANES : min(width, (block + 1) * LANES)]
        terms[block * rows : (block + 1) * rows, 0 : part.shape[1]] = part.astype(terms.dtype)
    one = acc_one[...]
    terms[blocks * rows : blocks * rows + one.shape[0], 0 : one.shape[1]] = one.astype(terms.dtype)


def vmem_call(body, out_shape, scratch=(), cost=None, limit=48 * 2**20):
    spec = pl.BlockSpec(memory_space=pltpu.VMEM)
    return pl.pallas_call(
        body,
        out_shape=out_shape,
        out_specs=jax.tree.map(lambda _: spec, out_shape),
        scratch_shapes=list(scratch),
        compiler_params=pltpu.CompilerParams(vmem_limit_bytes=limit),
        cost_estimate=cost,
    )


def compute(cots, act, vols, kernel_two, kernel_one, rows):
    c1, length, width = act.shape
    c0, c2 = (vols[0].shape[0], cots[0].shape[0])
    w_two = kernel_two[::-1, ::-1, ::-1].transpose(2, 3, 1, 0, 4).reshape(3 * c1, 9 * c2)
    w_one = kernel_one[::-1, ::-1, ::-1].transpose(0, 2, 3, 1, 4).reshape(9 * c0, 3 * c1)
    plane = (length * c0, width)
    flops = 2 * 27 * length * width * c1 * 2 * (c0 + c2)
    return vmem_call(
        compute_kernel,
        (
            jax.ShapeDtypeStruct((rows, LANES), BF16),
            jax.ShapeDtypeStruct(plane, F32),
            jax.ShapeDtypeStruct(plane, BF16),
            jax.ShapeDtypeStruct(plane, BF16),
        ),
        (
            pltpu.VMEM((max(c0, c1, c2) * length, width), F32),
            pltpu.VMEM(((length + 2) * 3 * c2, width), BF16),
            pltpu.VMEM((length * c1, width), BF16),
            pltpu.VMEM(((length + 2) * 3 * c0, width), BF16),
            pltpu.VMEM(((length + 2) * c1, width), BF16),
            pltpu.VMEM((9 * c2, 3 * c1), F32),
            pltpu.VMEM((9 * c0, 3 * c1), F32),
        ),
        pl.CostEstimate(flops=flops, bytes_accessed=5 * 2**20, transcendentals=0),
    )(*cots, act, *vols, w_two, w_one)


def merge_kernel(own, from_below, from_above, out, flat):
    chans, length, _ = out.shape

    def add(step, carry):
        at = pl.ds(pl.multiple_of(step * 64, 64), 64)
        flat[at, :] = own[at, :] + from_below[at, :].astype(F32) + from_above[at, :].astype(F32)
        return carry

    lax.fori_loop(0, own.shape[0] // 64, add, 0, unroll=4)

    def gather(c, carry):
        out[c] = flat[pl.ds(c, length, stride=chans), :].astype(out.dtype)
        return carry

    lax.fori_loop(0, chans, gather, 0, unroll=4)


def merge(own, from_below, from_above, shape):
    return vmem_call(
        merge_kernel,
        jax.ShapeDtypeStruct(shape, BF16),
        (pltpu.VMEM(own.shape, F32),),
        pl.CostEstimate(flops=2 * own.size, bytes_accessed=8 * own.size, transcendentals=0),
    )(own, from_below, from_above)


def share_kernel(scale, bucket, terms, out):
    total = jnp.sum(bucket[...].astype(F32), axis=0).astype(BF16)
    grads = (jnp.sum(terms[...].astype(F32), axis=0) * scale).astype(BF16)
    height = total.shape[0]

    def write(n, carry):
        out[n, 0:height, :] = total
        out[n, height : height + grads.shape[0], :] = grads
        return carry

    lax.fori_loop(0, out.shape[0], write, 0)


def share(bucket, terms, scale, copies):
    rows = bucket.shape[1] + terms.shape[1]
    return vmem_call(
        lambda *refs: share_kernel(scale, *refs),
        jax.ShapeDtypeStruct((copies, rows, LANES), BF16),
        (),
        pl.CostEstimate(flops=bucket.size, bytes_accessed=3 * bucket.size, transcendentals=0),
    )(bucket, terms)


def finish_kernel(sizes, core, mine, other, bucket, out_one, out_two, raw):
    c0, c1, c2 = sizes
    copies, rows, _ = mine.shape
    height = bucket.shape[0] // (2 * copies)
    extra = rows - height
    me = core[0]

    def place(q, carry):
        for source, which in ((mine, me), (other, 1 - me)):
            chunk = 2 * q + which
            bucket[pl.ds(pl.multiple_of(chunk * height, 8), height), :] = source[q, 0:height, :].astype(F32)
            raw[pl.ds(pl.multiple_of(chunk * extra, 8), extra), :] = source[q, height:rows, :].astype(F32)
        return carry

    lax.fori_loop(0, copies, place, 0)
    block = 3 * c1
    first = -(-9 * c2 // LANES) * block
    for i in range(3):
        for j in range(3):
            column = ((2 - j) * 3 + 2 - i) * c2
            whole, lane = (column // LANES, column % LANES)
            out_two[(3 * i + j) * block : (3 * i + j + 1) * block, :] = raw[
                whole * block : (whole + 1) * block, lane : lane + c2
            ]
            row = first + (3 * j + i) * c0
            for k in range(3):
                to = (9 * i + 3 * j + k) * c0
                out_one[to : to + c0, :] = raw[row : row + c0, k * c1 : (k + 1) * c1]


def finish(core, mine, other, length, sizes):
    c0, c1, c2 = sizes
    copies, rows, _ = mine.shape
    extra = rows - length // LANES // (2 * copies)
    spec = pl.BlockSpec(memory_space=pltpu.VMEM)
    return pl.pallas_call(
        lambda *refs: finish_kernel(sizes, *refs),
        out_shape=(
            jax.ShapeDtypeStruct((length // LANES, LANES), F32),
            jax.ShapeDtypeStruct((27 * c0, c1), F32),
            jax.ShapeDtypeStruct((27 * c1, c2), F32),
        ),
        in_specs=[pl.BlockSpec(memory_space=pltpu.SMEM), spec, spec],
        out_specs=(spec, spec, spec),
        scratch_shapes=[pltpu.VMEM((2 * copies * extra, LANES), F32)],
        compiler_params=pltpu.CompilerParams(vmem_limit_bytes=48 * 2**20),
    )(core, mine, other)


def halos(value):
    count = lax.axis_size(SPACE)
    up = [(i, i + 1) for i in range(count - 1)]
    down = [(j, i) for i, j in up]
    return (lax.ppermute(value, SPACE, up), lax.ppermute(value, SPACE, down))


def per_device(volume_in, hidden_act, out_cot, kernel_one, kernel_two, grad_bucket):
    c0, c1, c2 = (volume_in.shape[2], hidden_act.shape[2], out_cot.shape[2])
    devices, copies = (lax.axis_size(EVERY), lax.axis_size(("dp", "slab")))
    cot, vol = (out_cot[0, 0], volume_in[0, 0])
    cot_m, cot_p = halos(cot)
    vol_m, vol_p = halos(vol)
    length = grad_bucket.shape[1]
    parts = grad_bucket.reshape(devices, length // devices // LANES, LANES).astype(BF16)
    parts = lax.all_to_all(parts, EVERY, 0, 0)

    used = -(-9 * c2 // LANES) * 3 * c1 + 9 * c0
    rows = ceil_to(used, 16 * devices)
    terms, own, up, down = compute(
        (cot_m, cot, cot_p), hidden_act[0, 0], (vol_m, vol, vol_p), kernel_two, kernel_one, rows
    )
    terms = lax.all_to_all(terms.reshape(devices, rows // devices, LANES), EVERY, 0, 0)
    count = lax.axis_size(SPACE)
    upward = [(i, i + 1) for i in range(count - 1)]
    from_below = lax.ppermute(up, SPACE, upward)
    from_above = lax.ppermute(down, SPACE, [(j, i) for i, j in upward])
    grad_input = merge(own, from_below, from_above, vol.shape)

    cells = volume_in.shape[3] * volume_in.shape[4] * devices
    shares = share(parts, terms, 1.0 / math.sqrt(cells), copies)
    mine = lax.all_to_all(shares, ("dp", "slab"), 0, 0)
    other = lax.ppermute(mine, "core", [(0, 1), (1, 0)])
    core = lax.axis_index("core").astype(jnp.int32).reshape(1)
    bucket_sum, total_one, total_two = finish(core, mine, other, length, (c0, c1, c2))
    return (
        grad_input[None, None],
        total_one.reshape(3, 3, 3, c0, c1),
        total_two.reshape(3, 3, 3, c1, c2),
        bucket_sum.reshape(length),
    )


def solution(mesh):
    dp, space = (mesh.shape["dp"], mesh.shape["space"])
    split = Mesh(mesh.devices.reshape(dp, space // 2, 2), EVERY)
    volume = P("dp", SPACE, None, None, None)
    in_specs = (volume, volume, volume, P(), P(), P(EVERY, None))
    out_specs = (volume, P(), P(), P())
    return jax.shard_map(
        per_device, mesh=split, in_specs=in_specs, out_specs=out_specs, check_vma=False
    )
```

```python
import math

import jax
import jax.numpy as jnp
from jax import lax
from jax.experimental import pallas as pl
from jax.experimental.pallas import tpu as pltpu
from jax.sharding import Mesh, PartitionSpec as P

SPACE = ("slab", "core")
EVERY = ("dp", "slab", "core")
GROUP = 4
LANES = 128
BF16 = jnp.bfloat16
F32 = jnp.float32


def ceil_to(value, step):
    return -(-value // step) * step


def slid(value, step):
    lane = lax.broadcasted_iota(jnp.int32, value.shape, 1)
    width = value.shape[1]
    keep = lane >= step if step > 0 else lane < width + step
    return jnp.where(keep, pltpu.roll(value, step % width, 1), 0.0)


def beside(window, rows, step, count):
    return jnp.concatenate([window[g * step : g * step + rows] for g in range(count)], axis=1)


def turned(src, flat, dst, offset, pitch, lead):
    chans, length, _ = src.shape

    def stage(c, carry):
        flat[pl.ds(pl.multiple_of(c * length, length), length), :] = src[c].astype(F32)
        return carry

    lax.fori_loop(0, chans, stage, 0, unroll=4)

    def gather(x, carry):
        rows = flat[pl.ds(x, chans, stride=length), :]
        at = pl.multiple_of((x + lead) * pitch + offset, 16)
        dst[pl.ds(at, chans), :] = rows.astype(BF16)
        return carry

    lax.fori_loop(0, length, gather, 0, unroll=4)


def pack_kernel(cot, vol, out, flat):
    c2, length, width = cot.shape
    pitch = c2 + vol.shape[0]
    zeros = jnp.zeros((pitch, width), BF16)
    out[0:pitch, :] = zeros
    out[(length + 1) * pitch : (length + 2) * pitch, :] = zeros
    turned(cot, flat, out, 0, pitch, 1)
    turned(vol, flat, out, c2, pitch, 1)


def pack(cot, vol):
    c2, length, width = cot.shape
    pitch = c2 + vol.shape[0]
    return vmem_call(
        pack_kernel,
        jax.ShapeDtypeStruct(((length + 2) * pitch, width), BF16),
        (pltpu.VMEM((max(c2, vol.shape[0]) * length, width), F32),),
        pl.CostEstimate(flops=0, bytes_accessed=4 * cot.size, transcendentals=0),
    )(cot, vol)


def slide_kernel(act, out, flat, rows):
    c1, length, _ = act.shape
    turned(act, flat, rows, 0, c1, 0)

    def slide(x, carry):
        value = rows[pl.ds(pl.multiple_of(x * c1, 16), c1), :].astype(F32)
        stack = jnp.concatenate([slid(value, 1), value, slid(value, -1)], axis=0)
        out[pl.ds(pl.multiple_of(x * 3 * c1, 16), 3 * c1), :] = stack.astype(BF16)
        return carry

    lax.fori_loop(0, length, slide, 0, unroll=4)


def slide(act):
    c1, length, width = act.shape
    return vmem_call(
        slide_kernel,
        jax.ShapeDtypeStruct((length * 3 * c1, width), BF16),
        (
            pltpu.VMEM((c1 * length, width), F32),
            pltpu.VMEM((c1 * length, width), BF16),
        ),
        pl.CostEstimate(flops=0, bytes_accessed=8 * act.size, transcendentals=0),
    )(act)


def cast_kernel(src, out):
    out[...] = src[...].reshape(out.shape).astype(out.dtype)


def cast(value, devices):
    rows = value.shape[0] // devices
    steps = 4
    return pl.pallas_call(
        cast_kernel,
        grid=(steps,),
        out_shape=jax.ShapeDtypeStruct((devices, rows, LANES), BF16),
        in_specs=[pl.BlockSpec((value.shape[0] // steps, LANES), lambda n: (n, 0))],
        out_specs=pl.BlockSpec((devices // steps, rows, LANES), lambda n: (n, 0, 0)),
        cost_estimate=pl.CostEstimate(flops=0, bytes_accessed=6 * value.size, transcendentals=0),
    )(value)


def compute_kernel(
    pack_m, pack_0, pack_p, acts, w_two, w_one,
    terms, own, up, down,
    pres, acc_two, acc_one,
):
    length = acts.shape[0] // w_two.shape[0]
    c1 = w_two.shape[0] // 3
    c2 = w_two.shape[1] // 9
    c0 = w_one.shape[0] // 9
    pitch = c0 + c2
    packs = (pack_m, pack_0, pack_p)

    pres[0:c1, :] = jnp.zeros((c1, LANES), BF16)
    pres[(length + 1) * c1 : (length + 2) * c1, :] = jnp.zeros((c1, LANES), BF16)
    acc_two[...] = jnp.zeros_like(acc_two)
    acc_one[...] = jnp.zeros_like(acc_one)

    def windows(x, offset, count):
        rows = [
            [p[pl.ds(pl.multiple_of((x + n) * pitch + offset, 16), count), :] for p in packs]
            for n in range(GROUP + 2)
        ]
        return jnp.concatenate(
            [jnp.concatenate(sum(rows[g : g + 3], []), axis=0) for g in range(GROUP)], axis=1
        )

    def first(step, carry):
        x = step * GROUP
        right = windows(x, 0, c2)
        sums = jnp.dot(w_two[...], right, preferred_element_type=F32)
        columns = []
        for g in range(GROUP):
            part = sums[:, g * LANES : (g + 1) * LANES]
            grad = slid(part[0:c1], 1) + part[c1 : 2 * c1] + slid(part[2 * c1 : 3 * c1], -1)
            stack = acts[pl.ds(pl.multiple_of((x + g) * 3 * c1, 16), 3 * c1), :]
            value = stack[c1 : 2 * c1].astype(F32)
            pre = (grad * jnp.where(value > 0, 1.0, 0.2)).astype(BF16)
            pres[pl.ds(pl.multiple_of((x + g + 1) * c1, 16), c1), :] = pre
            columns.append(stack)
        left = jnp.concatenate(columns, axis=1)
        acc_two[...] += lax.dot_general(
            right, left, (((1,), (1,)), ((), ())), preferred_element_type=F32
        )
        return carry

    lax.fori_loop(0, length // GROUP, first, 0)

    def second(step, carry):
        x = step * GROUP
        window = pres[pl.ds(pl.multiple_of(x * c1, 16), (GROUP + 2) * c1), :]
        sums = jnp.dot(w_one[...], beside(window, 3 * c1, c1, GROUP), preferred_element_type=F32)
        columns = []
        for g in range(GROUP):
            part = sums[:, g * LANES : (g + 1) * LANES]
            at = pl.ds(pl.multiple_of((x + g) * c0, 16), c0)
            for i, out in ((0, up), (1, own), (2, down)):
                b = 3 * i * c0
                grad = (
                    slid(part[b : b + c0], 1)
                    + part[b + c0 : b + 2 * c0]
                    + slid(part[b + 2 * c0 : b + 3 * c0], -1)
                )
                out[at, :] = grad.astype(out.dtype)
            value = window[(g + 1) * c1 : (g + 2) * c1].astype(F32)
            columns.append(
                jnp.concatenate([slid(value, -1), value, slid(value, 1)], axis=0).astype(BF16)
            )
        left = jnp.concatenate(columns, axis=1)
        acc_one[...] += lax.dot_general(
            windows(x, c2, c0), left, (((1,), (1,)), ((), ())), preferred_element_type=F32
        )
        return carry

    lax.fori_loop(0, length // GROUP, second, 0)

    terms[...] = jnp.zeros_like(terms)
    two = acc_two[...].T
    rows, width = two.shape
    blocks = -(-width // LANES)
    for block in range(blocks):
        part = two[:, block * LANES : min(width, (block + 1) * LANES)]
        terms[block * rows : (block + 1) * rows, 0 : part.shape[1]] = part.astype(terms.dtype)
    one = acc_one[...]
    terms[blocks * rows : blocks * rows + one.shape[0], 0 : one.shape[1]] = one.astype(terms.dtype)


def vmem_call(body, out_shape, scratch=(), cost=None, limit=24 * 2**20):
    spec = pl.BlockSpec(memory_space=pltpu.VMEM)
    return pl.pallas_call(
        body,
        out_shape=out_shape,
        out_specs=jax.tree.map(lambda _: spec, out_shape),
        scratch_shapes=list(scratch),
        compiler_params=pltpu.CompilerParams(vmem_limit_bytes=limit),
        cost_estimate=cost,
    )


def compute(packs, acts, kernel_two, kernel_one, rows):
    c0, c1 = kernel_one.shape[3:]
    c2 = kernel_two.shape[4]
    w_two = kernel_two[::-1, ::-1, ::-1].transpose(2, 3, 1, 0, 4).reshape(3 * c1, 9 * c2)
    w_one = kernel_one[::-1, ::-1, ::-1].transpose(0, 2, 3, 1, 4).reshape(9 * c0, 3 * c1)
    length, width = (acts.shape[0] // (3 * c1), acts.shape[1])
    plane = (length * c0, width)
    return vmem_call(
        compute_kernel,
        (
            jax.ShapeDtypeStruct((rows, LANES), BF16),
            jax.ShapeDtypeStruct(plane, F32),
            jax.ShapeDtypeStruct(plane, BF16),
            jax.ShapeDtypeStruct(plane, BF16),
        ),
        (
            pltpu.VMEM(((length + 2) * c1, width), BF16),
            pltpu.VMEM((9 * c2, 3 * c1), F32),
            pltpu.VMEM((9 * c0, 3 * c1), F32),
        ),
        pl.CostEstimate(flops=10**10, bytes_accessed=40 * 2**20, transcendentals=0),
    )(*packs, acts, w_two, w_one)


def merge_kernel(own, from_below, from_above, out, flat):
    chans, length, _ = out.shape

    def add(step, carry):
        at = pl.ds(pl.multiple_of(step * 64, 64), 64)
        flat[at, :] = own[at, :] + from_below[at, :].astype(F32) + from_above[at, :].astype(F32)
        return carry

    lax.fori_loop(0, own.shape[0] // 64, add, 0, unroll=4)

    def gather(c, carry):
        out[c] = flat[pl.ds(c, length, stride=chans), :].astype(out.dtype)
        return carry

    lax.fori_loop(0, chans, gather, 0, unroll=4)


def merge(own, from_below, from_above, shape):
    return vmem_call(
        merge_kernel,
        jax.ShapeDtypeStruct(shape, BF16),
        (pltpu.VMEM(own.shape, F32),),
        pl.CostEstimate(flops=2 * own.size, bytes_accessed=8 * own.size, transcendentals=0),
    )(own, from_below, from_above)


def share_kernel(scale, bucket, terms, out):
    total = jnp.sum(bucket[...].astype(F32), axis=0).astype(BF16)
    grads = (jnp.sum(terms[...].astype(F32), axis=0) * scale).astype(BF16)
    height = total.shape[0]

    def write(n, carry):
        out[n, 0:height, :] = total
        out[n, height : height + grads.shape[0], :] = grads
        return carry

    lax.fori_loop(0, out.shape[0], write, 0)


def share(bucket, terms, scale, copies):
    rows = bucket.shape[1] + terms.shape[1]
    return vmem_call(
        lambda *refs: share_kernel(scale, *refs),
        jax.ShapeDtypeStruct((copies, rows, LANES), BF16),
        (),
        pl.CostEstimate(flops=bucket.size, bytes_accessed=3 * bucket.size, transcendentals=0),
    )(bucket, terms)


def finish_kernel(sizes, core, mine, other, bucket, out_one, out_two, raw):
    c0, c1, c2 = sizes
    copies, rows, _ = mine.shape
    height = bucket.shape[0] // (2 * copies)
    extra = rows - height
    me = core[0]

    def place(q, carry):
        for source, which in ((mine, me), (other, 1 - me)):
            chunk = 2 * q + which
            bucket[pl.ds(pl.multiple_of(chunk * height, 8), height), :] = source[q, 0:height, :].astype(F32)
            raw[pl.ds(pl.multiple_of(chunk * extra, 8), extra), :] = source[q, height:rows, :].astype(F32)
        return carry

    lax.fori_loop(0, copies, place, 0)
    block = 3 * c1
    first = -(-9 * c2 // LANES) * block
    for i in range(3):
        for j in range(3):
            column = ((2 - j) * 3 + 2 - i) * c2
            whole, lane = (column // LANES, column % LANES)
            out_two[(3 * i + j) * block : (3 * i + j + 1) * block, :] = raw[
                whole * block : (whole + 1) * block, lane : lane + c2
            ]
            row = first + (3 * j + i) * c0
            for k in range(3):
                to = (9 * i + 3 * j + k) * c0
                out_one[to : to + c0, :] = raw[row : row + c0, k * c1 : (k + 1) * c1]


def finish(core, mine, other, length, sizes):
    c0, c1, c2 = sizes
    copies, rows, _ = mine.shape
    extra = rows - length // LANES // (2 * copies)
    spec = pl.BlockSpec(memory_space=pltpu.VMEM)
    return pl.pallas_call(
        lambda *refs: finish_kernel(sizes, *refs),
        out_shape=(
            jax.ShapeDtypeStruct((length // LANES, LANES), F32),
            jax.ShapeDtypeStruct((27 * c0, c1), F32),
            jax.ShapeDtypeStruct((27 * c1, c2), F32),
        ),
        in_specs=[pl.BlockSpec(memory_space=pltpu.SMEM), spec, spec],
        out_specs=(spec, spec, spec),
        scratch_shapes=[pltpu.VMEM((2 * copies * extra, LANES), F32)],
        compiler_params=pltpu.CompilerParams(vmem_limit_bytes=24 * 2**20),
    )(core, mine, other)


def halos(value):
    count = lax.axis_size(SPACE)
    up = [(i, i + 1) for i in range(count - 1)]
    down = [(j, i) for i, j in up]
    return (lax.ppermute(value, SPACE, up), lax.ppermute(value, SPACE, down))


def per_device(volume_in, hidden_act, out_cot, kernel_one, kernel_two, grad_bucket):
    c0, c1, c2 = (volume_in.shape[2], hidden_act.shape[2], out_cot.shape[2])
    devices, copies = (lax.axis_size(EVERY), lax.axis_size(("dp", "slab")))
    length = grad_bucket.shape[1]
    packed = pack(out_cot[0, 0], volume_in[0, 0])
    below, above = halos(packed)
    parts = cast(grad_bucket.reshape(length // LANES, LANES), devices)
    act, parts = lax.optimization_barrier((hidden_act[0, 0], parts))
    parts = lax.all_to_all(parts, EVERY, 0, 0)

    used = -(-9 * c2 // LANES) * 3 * c1 + 9 * c0
    rows = ceil_to(used, 16 * devices)
    terms, own, up, down = compute(
        (below, packed, above), slide(act), kernel_two, kernel_one, rows
    )
    terms, parts = lax.optimization_barrier((terms, parts))
    terms = lax.all_to_all(terms.reshape(devices, rows // devices, LANES), EVERY, 0, 0)
    count = lax.axis_size(SPACE)
    upward = [(i, i + 1) for i in range(count - 1)]
    from_below = lax.ppermute(up, SPACE, upward)
    from_above = lax.ppermute(down, SPACE, [(j, i) for i, j in upward])
    grad_input = merge(own, from_below, from_above, volume_in.shape[2:])

    cells = volume_in.shape[3] * volume_in.shape[4] * devices
    shares = share(parts, terms, 1.0 / math.sqrt(cells), copies)
    grad_input, shares = lax.optimization_barrier((grad_input, shares))
    mine = lax.all_to_all(shares, ("dp", "slab"), 0, 0)
    other = lax.ppermute(mine, "core", [(0, 1), (1, 0)])
    core = lax.axis_index("core").astype(jnp.int32).reshape(1)
    bucket_sum, total_one, total_two = finish(core, mine, other, length, (c0, c1, c2))
    return (
        grad_input[None, None],
        total_one.reshape(3, 3, 3, c0, c1),
        total_two.reshape(3, 3, 3, c1, c2),
        bucket_sum.reshape(length),
    )


def solution(mesh):
    dp, space = (mesh.shape["dp"], mesh.shape["space"])
    split = Mesh(mesh.devices.reshape(dp, space // 2, 2), EVERY)
    volume = P("dp", SPACE, None, None, None)
    in_specs = (volume, volume, volume, P(), P(), P(EVERY, None))
    out_specs = (volume, P(), P(), P())
    return jax.shard_map(
        per_device, mesh=split, in_specs=in_specs, out_specs=out_specs, check_vma=False
    )
```

```python
import math

import jax
import jax.numpy as jnp
from jax import lax
from jax.experimental import pallas as pl
from jax.experimental.pallas import tpu as pltpu
from jax.sharding import Mesh, PartitionSpec as P

SPACE = ("slab", "core")
EVERY = ("dp", "slab", "core")
GROUP = 8
LANES = 128
BF16 = jnp.bfloat16
F32 = jnp.float32


def ceil_to(value, step):
    return -(-value // step) * step


def slid(value, step):
    lane = lax.broadcasted_iota(jnp.int32, value.shape, 1)
    width = value.shape[1]
    keep = lane >= step if step > 0 else lane < width + step
    return jnp.where(keep, pltpu.roll(value, step % width, 1), 0.0)


def beside(window, rows, step, count):
    return jnp.concatenate([window[g * step : g * step + rows] for g in range(count)], axis=1)


def turned(src, flat, dst, offset, pitch, lead):
    chans, length, _ = src.shape

    def stage(c, carry):
        flat[pl.ds(pl.multiple_of(c * length, length), length), :] = src[c].astype(F32)
        return carry

    lax.fori_loop(0, chans, stage, 0, unroll=4)

    def gather(x, carry):
        rows = flat[pl.ds(x, chans, stride=length), :]
        at = pl.multiple_of((x + lead) * pitch + offset, 16)
        dst[pl.ds(at, chans), :] = rows.astype(BF16)
        return carry

    lax.fori_loop(0, length, gather, 0, unroll=4)


def pack_kernel(cot, vol, out, flat):
    c2, length, width = cot.shape
    pitch = c2 + vol.shape[0]
    zeros = jnp.zeros((pitch, width), BF16)
    out[0:pitch, :] = zeros
    out[(length + 1) * pitch : (length + 2) * pitch, :] = zeros
    turned(cot, flat, out, 0, pitch, 1)
    turned(vol, flat, out, c2, pitch, 1)


def pack(cot, vol):
    c2, length, width = cot.shape
    pitch = c2 + vol.shape[0]
    return vmem_call(
        pack_kernel,
        jax.ShapeDtypeStruct(((length + 2) * pitch, width), BF16),
        (pltpu.VMEM((max(c2, vol.shape[0]) * length, width), F32),),
        pl.CostEstimate(flops=0, bytes_accessed=4 * cot.size, transcendentals=0),
    )(cot, vol)


def slide_kernel(act, two, one, out, w_two, w_one, flat, rows):
    c1, length, _ = act.shape
    turned(act, flat, rows, 0, c1, 0)

    def slide(x, carry):
        value = rows[pl.ds(pl.multiple_of(x * c1, 16), c1), :].astype(F32)
        stack = jnp.concatenate([slid(value, 1), value, slid(value, -1)], axis=0)
        out[pl.ds(pl.multiple_of(x * 3 * c1, 16), 3 * c1), :] = stack.astype(BF16)
        return carry

    lax.fori_loop(0, length, slide, 0, unroll=4)

    offsets = [(j, i) for j in range(3) for i in range(3)]
    w_two[...] = jnp.concatenate(
        [
            jnp.concatenate([two[2 - i, 2 - j, 2 - k].astype(F32) for k in range(3)], axis=0)
            for j, i in offsets
        ],
        axis=1,
    ).astype(BF16)
    w_one[...] = jnp.concatenate(
        [
            jnp.concatenate([one[2 - i, 2 - j, k].astype(F32) for i in range(3)], axis=0)
            for j, k in offsets
        ],
        axis=1,
    ).astype(BF16)


def slide(act, kernel_two, kernel_one):
    c1, length, width = act.shape
    c0, c2 = (kernel_one.shape[3], kernel_two.shape[4])
    return vmem_call(
        slide_kernel,
        (
            jax.ShapeDtypeStruct((length * 3 * c1, width), BF16),
            jax.ShapeDtypeStruct((3 * c1, 9 * c2), BF16),
            jax.ShapeDtypeStruct((3 * c0, 9 * c1), BF16),
        ),
        (
            pltpu.VMEM((c1 * length, width), F32),
            pltpu.VMEM((c1 * length, width), BF16),
        ),
        pl.CostEstimate(flops=0, bytes_accessed=8 * act.size, transcendentals=0),
    )(act, kernel_two, kernel_one)


def cast_kernel(core, src, out):
    out[...] = src[...].astype(out.dtype)


def half_call(body, core, steps, height, which, value, others, cost):
    block = (height // steps, LANES)
    plain = pl.BlockSpec(block, lambda n, core: (n, 0))
    chosen = pl.BlockSpec(block, lambda n, core: (which(core[0]) * steps + n, 0))
    return pl.pallas_call(
        body,
        grid_spec=pltpu.PrefetchScalarGridSpec(
            num_scalar_prefetch=1,
            grid=(steps,),
            in_specs=[chosen] + [plain] * len(others),
            out_specs=plain,
        ),
        out_shape=jax.ShapeDtypeStruct((height, LANES), BF16),
        cost_estimate=pl.CostEstimate(flops=0, bytes_accessed=cost, transcendentals=0),
    )(core, value, *others)


def add_kernel(core, src, other, out):
    out[...] = (src[...] + other[...].astype(F32)).astype(out.dtype)


def swapped_half(core, value):
    height = value.shape[0] // 2
    steps = 2
    send = half_call(cast_kernel, core, steps, height, lambda c: 1 - c, value, [], 6 * value.size // 2)
    other = lax.ppermute(send, "core", [(0, 1), (1, 0)])
    return half_call(add_kernel, core, steps, height, lambda c: c, value, [other], 4 * value.size)


def compute_kernel(
    pack_m, pack_0, pack_p, acts, w_two, w_one,
    terms, own, up, down,
    pres, acc_two, acc_one,
):
    length = acts.shape[0] // w_two.shape[0]
    c1 = w_two.shape[0] // 3
    c2 = w_two.shape[1] // 9
    c0 = w_one.shape[0] // 3
    pitch = c0 + c2
    packs = (pack_m, pack_0, pack_p)

    stacked = 3 * c1
    pres[0:stacked, :] = jnp.zeros((stacked, LANES), BF16)
    pres[(length + 1) * stacked : (length + 2) * stacked, :] = jnp.zeros((stacked, LANES), BF16)
    acc_two[...] = jnp.zeros_like(acc_two)
    acc_one[...] = jnp.zeros_like(acc_one)

    def windows(x, offset, count):
        rows = [
            [p[pl.ds(pl.multiple_of((x + n) * pitch + offset, 16), count), :] for p in packs]
            for n in range(GROUP + 2)
        ]
        return jnp.concatenate(
            [jnp.concatenate(sum(rows[g : g + 3], []), axis=0) for g in range(GROUP)], axis=1
        )

    def first(step, carry):
        x = step * GROUP
        right = windows(x, 0, c2)
        sums = jnp.dot(w_two[...], right, preferred_element_type=F32)
        columns = []
        for g in range(GROUP):
            part = sums[:, g * LANES : (g + 1) * LANES]
            grad = slid(part[0:c1], 1) + part[c1 : 2 * c1] + slid(part[2 * c1 : 3 * c1], -1)
            stack = acts[pl.ds(pl.multiple_of((x + g) * stacked, 16), stacked), :]
            value = stack[c1 : 2 * c1].astype(F32)
            pre = (grad * jnp.where(value > 0, 1.0, 0.2)).astype(BF16).astype(F32)
            moved = jnp.concatenate([slid(pre, -1), pre, slid(pre, 1)], axis=0).astype(BF16)
            pres[pl.ds(pl.multiple_of((x + g + 1) * stacked, 16), stacked), :] = moved
            columns.append(stack)
        left = jnp.concatenate(columns, axis=1)
        acc_two[...] += lax.dot_general(
            right, left, (((1,), (1,)), ((), ())), preferred_element_type=F32
        )
        return carry

    lax.fori_loop(0, length // GROUP, first, 0, unroll=2)

    def second(step, carry):
        x = step * GROUP
        window = pres[pl.ds(pl.multiple_of(x * stacked, 16), (GROUP + 2) * stacked), :]
        moved = beside(window, 3 * stacked, stacked, GROUP)
        sums = jnp.dot(w_one[...], moved, preferred_element_type=F32)
        for g in range(GROUP):
            part = sums[:, g * LANES : (g + 1) * LANES]
            at = pl.ds(pl.multiple_of((x + g) * c0, 16), c0)
            for i, out in ((0, up), (1, own), (2, down)):
                out[at, :] = part[i * c0 : (i + 1) * c0].astype(out.dtype)
        acc_one[...] += lax.dot_general(
            windows(x, c2, c0),
            moved[stacked : 2 * stacked],
            (((1,), (1,)), ((), ())),
            preferred_element_type=F32,
        )
        return carry

    lax.fori_loop(0, length // GROUP, second, 0, unroll=2)

    terms[...] = jnp.zeros_like(terms)
    two = acc_two[...].T
    rows, width = two.shape
    blocks = -(-width // LANES)
    for block in range(blocks):
        part = two[:, block * LANES : min(width, (block + 1) * LANES)]
        terms[block * rows : (block + 1) * rows, 0 : part.shape[1]] = part.astype(terms.dtype)
    one = acc_one[...]
    terms[blocks * rows : blocks * rows + one.shape[0], 0 : one.shape[1]] = one.astype(terms.dtype)


def vmem_call(body, out_shape, scratch=(), cost=None, limit=24 * 2**20):
    spec = pl.BlockSpec(memory_space=pltpu.VMEM)
    return pl.pallas_call(
        body,
        out_shape=out_shape,
        out_specs=jax.tree.map(lambda _: spec, out_shape),
        scratch_shapes=list(scratch),
        compiler_params=pltpu.CompilerParams(vmem_limit_bytes=limit),
        cost_estimate=cost,
    )


def compute(packs, acts, w_two, w_one, rows):
    c0, c1, c2 = (w_one.shape[0] // 3, w_two.shape[0] // 3, w_two.shape[1] // 9)
    length, width = (acts.shape[0] // (3 * c1), acts.shape[1])
    plane = (length * c0, width)
    return vmem_call(
        compute_kernel,
        (
            jax.ShapeDtypeStruct((rows, LANES), BF16),
            jax.ShapeDtypeStruct(plane, F32),
            jax.ShapeDtypeStruct(plane, BF16),
            jax.ShapeDtypeStruct(plane, BF16),
        ),
        (
            pltpu.VMEM(((length + 2) * 3 * c1, width), BF16),
            pltpu.VMEM((9 * c2, 3 * c1), F32),
            pltpu.VMEM((9 * c0, 3 * c1), F32),
        ),
        pl.CostEstimate(flops=10**10, bytes_accessed=40 * 2**20, transcendentals=0),
    )(*packs, acts, w_two, w_one)


def merge_kernel(own, from_below, from_above, out, flat):
    chans, length, _ = out.shape

    def add(step, carry):
        at = pl.ds(pl.multiple_of(step * 64, 64), 64)
        flat[at, :] = own[at, :] + from_below[at, :].astype(F32) + from_above[at, :].astype(F32)
        return carry

    lax.fori_loop(0, own.shape[0] // 64, add, 0, unroll=4)

    def gather(c, carry):
        out[c] = flat[pl.ds(c, length, stride=chans), :].astype(out.dtype)
        return carry

    lax.fori_loop(0, chans, gather, 0, unroll=4)


def merge(own, from_below, from_above, shape):
    return vmem_call(
        merge_kernel,
        jax.ShapeDtypeStruct(shape, BF16),
        (pltpu.VMEM(own.shape, F32),),
        pl.CostEstimate(flops=2 * own.size, bytes_accessed=8 * own.size, transcendentals=0),
    )(own, from_below, from_above)


def share_kernel(scale, bucket, terms, out):
    total = jnp.sum(bucket[...].astype(F32), axis=0).astype(BF16)
    grads = (jnp.sum(terms[...].astype(F32), axis=0) * scale).astype(BF16)
    height = total.shape[0]

    def write(n, carry):
        out[n, 0:height, :] = total
        out[n, height : height + grads.shape[0], :] = grads
        return carry

    lax.fori_loop(0, out.shape[0], write, 0)


def share(bucket, terms, scale, copies):
    rows = bucket.shape[1] + terms.shape[1]
    return vmem_call(
        lambda *refs: share_kernel(scale, *refs),
        jax.ShapeDtypeStruct((copies, rows, LANES), BF16),
        (),
        pl.CostEstimate(flops=bucket.size, bytes_accessed=3 * bucket.size, transcendentals=0),
    )(bucket, terms)


def finish_kernel(sizes, core, mine, other, bucket, out_one, out_two, raw):
    c0, c1, c2 = sizes
    copies, rows, _ = mine.shape
    height = bucket.shape[0] // (2 * copies)
    extra = rows - height
    me = core[0]

    def place(q, carry):
        for source, which in ((mine, me), (other, 1 - me)):
            at = pl.multiple_of((which * copies + q) * height, 8)
            bucket[pl.ds(at, height), :] = source[q, 0:height, :].astype(F32)
            at = pl.multiple_of((2 * q + which) * extra, 8)
            raw[pl.ds(at, extra), :] = source[q, height:rows, :].astype(F32)
        return carry

    lax.fori_loop(0, copies, place, 0)
    block = 3 * c1
    first = -(-9 * c2 // LANES) * block
    for i in range(3):
        for j in range(3):
            column = ((2 - j) * 3 + 2 - i) * c2
            whole, lane = (column // LANES, column % LANES)
            out_two[(3 * i + j) * block : (3 * i + j + 1) * block, :] = raw[
                whole * block : (whole + 1) * block, lane : lane + c2
            ]
            row = first + (3 * j + i) * c0
            for k in range(3):
                to = (9 * i + 3 * j + k) * c0
                out_one[to : to + c0, :] = raw[row : row + c0, k * c1 : (k + 1) * c1]


def finish(core, mine, other, length, sizes):
    c0, c1, c2 = sizes
    copies, rows, _ = mine.shape
    extra = rows - length // LANES // (2 * copies)
    spec = pl.BlockSpec(memory_space=pltpu.VMEM)
    return pl.pallas_call(
        lambda *refs: finish_kernel(sizes, *refs),
        out_shape=(
            jax.ShapeDtypeStruct((length // LANES, LANES), F32),
            jax.ShapeDtypeStruct((27 * c0, c1), F32),
            jax.ShapeDtypeStruct((27 * c1, c2), F32),
        ),
        in_specs=[pl.BlockSpec(memory_space=pltpu.SMEM), spec, spec],
        out_specs=(spec, spec, spec),
        scratch_shapes=[pltpu.VMEM((2 * copies * extra, LANES), F32)],
        compiler_params=pltpu.CompilerParams(vmem_limit_bytes=24 * 2**20),
    )(core, mine, other)


def halos(value):
    count = lax.axis_size(SPACE)
    up = [(i, i + 1) for i in range(count - 1)]
    down = [(j, i) for i, j in up]
    return (lax.ppermute(value, SPACE, up), lax.ppermute(value, SPACE, down))


def per_device(volume_in, hidden_act, out_cot, kernel_one, kernel_two, grad_bucket):
    c0, c1, c2 = (volume_in.shape[2], hidden_act.shape[2], out_cot.shape[2])
    devices, copies = (lax.axis_size(EVERY), lax.axis_size(("dp", "slab")))
    length = grad_bucket.shape[1]
    core = lax.axis_index("core").astype(jnp.int32).reshape(1)
    packed = pack(out_cot[0, 0], volume_in[0, 0])
    below, above = halos(packed)
    half = swapped_half(core, grad_bucket.reshape(length // LANES, LANES))
    acts, w_two, w_one = slide(hidden_act[0, 0], kernel_two, kernel_one)
    acts, half = lax.optimization_barrier((acts, half))
    parts = lax.all_to_all(half.reshape(copies, -1, LANES), ("dp", "slab"), 0, 0)

    used = -(-9 * c2 // LANES) * 3 * c1 + 9 * c0
    rows = ceil_to(used, 16 * devices)
    terms, own, up, down = compute((below, packed, above), acts, w_two, w_one, rows)
    terms, parts = lax.optimization_barrier((terms, parts))
    terms = lax.all_to_all(terms.reshape(devices, rows // devices, LANES), EVERY, 0, 0)
    count = lax.axis_size(SPACE)
    upward = [(i, i + 1) for i in range(count - 1)]
    from_below = lax.ppermute(up, SPACE, upward)
    from_above = lax.ppermute(down, SPACE, [(j, i) for i, j in upward])
    grad_input = merge(own, from_below, from_above, volume_in.shape[2:])

    cells = volume_in.shape[3] * volume_in.shape[4] * devices
    shares = share(parts, terms, 1.0 / math.sqrt(cells), copies)
    grad_input, shares = lax.optimization_barrier((grad_input, shares))
    mine = lax.all_to_all(shares, ("dp", "slab"), 0, 0)
    other = lax.ppermute(mine, "core", [(0, 1), (1, 0)])
    bucket_sum, total_one, total_two = finish(core, mine, other, length, (c0, c1, c2))
    return (
        grad_input[None, None],
        total_one.reshape(3, 3, 3, c0, c1),
        total_two.reshape(3, 3, 3, c1, c2),
        bucket_sum.reshape(length),
    )


def solution(mesh):
    dp, space = (mesh.shape["dp"], mesh.shape["space"])
    split = Mesh(mesh.devices.reshape(dp, space // 2, 2), EVERY)
    volume = P("dp", SPACE, None, None, None)
    in_specs = (volume, volume, volume, P(), P(), P(EVERY, None))
    out_specs = (volume, P(), P(), P())
    return jax.shard_map(
        per_device, mesh=split, in_specs=in_specs, out_specs=out_specs, check_vma=False
    )
```

```python
import math

import jax
import jax.numpy as jnp
from jax import lax
from jax.experimental import pallas as pl
from jax.experimental.pallas import tpu as pltpu
from jax.sharding import Mesh, PartitionSpec as P

SPACE = ("slab", "core")
EVERY = ("dp", "slab", "core")
GROUP = 8
LANES = 128
BF16 = jnp.bfloat16
F32 = jnp.float32


def ceil_to(value, step):
    return -(-value // step) * step


def slid(value, step):
    lane = lax.broadcasted_iota(jnp.int32, value.shape, 1)
    width = value.shape[1]
    keep = lane >= step if step > 0 else lane < width + step
    return jnp.where(keep, pltpu.roll(value, step % width, 1), 0.0)


def beside(window, rows, step, count):
    return jnp.concatenate([window[g * step : g * step + rows] for g in range(count)], axis=1)


def turned(src, flat, dst, offset, pitch, lead):
    chans, length, _ = src.shape

    def stage(c, carry):
        flat[pl.ds(pl.multiple_of(c * length, length), length), :] = src[c].astype(F32)
        return carry

    lax.fori_loop(0, chans, stage, 0, unroll=4)

    def gather(x, carry):
        rows = flat[pl.ds(x, chans, stride=length), :]
        at = pl.multiple_of((x + lead) * pitch + offset, 16)
        dst[pl.ds(at, chans), :] = rows.astype(BF16)
        return carry

    lax.fori_loop(0, length, gather, 0, unroll=4)


def pack_kernel(cot, vol, out, fetched, flat, sems):
    step = vol.shape[0]
    length, width = vol.shape[1:]
    pitch = cot.shape[0] + step
    pieces = [cot.at[pl.ds(n, step)] for n in range(0, cot.shape[0], step)] + [vol]
    copies = [
        pltpu.make_async_copy(piece, fetched.at[n], sems.at[n]) for n, piece in enumerate(pieces)
    ]
    for copy in copies:
        copy.start()
    zeros = jnp.zeros((pitch, width), BF16)
    out[0:pitch, :] = zeros
    out[(length + 1) * pitch : (length + 2) * pitch, :] = zeros
    for n, copy in enumerate(copies):
        copy.wait()
        turned(fetched.at[n], flat, out, n * step, pitch, 1)


def pack(cot, vol):
    c2, length, width = cot.shape
    pitch = c2 + vol.shape[0]
    pieces = pitch // vol.shape[0]
    source = pl.BlockSpec(memory_space=pltpu.HBM)
    return pl.pallas_call(
        pack_kernel,
        out_shape=jax.ShapeDtypeStruct(((length + 2) * pitch, width), BF16),
        in_specs=[source, source],
        out_specs=pl.BlockSpec(memory_space=pltpu.VMEM),
        scratch_shapes=[
            pltpu.VMEM((pieces,) + vol.shape, BF16),
            pltpu.VMEM((vol.shape[0] * length, width), F32),
            pltpu.SemaphoreType.DMA((pieces,)),
        ],
        compiler_params=pltpu.CompilerParams(vmem_limit_bytes=24 * 2**20),
        cost_estimate=pl.CostEstimate(flops=0, bytes_accessed=4 * cot.size, transcendentals=0),
    )(cot, vol)


def slide_kernel(act, two, one, out, w_two, w_one, flat, rows):
    c1, length, _ = act.shape
    turned(act, flat, rows, 0, c1, 0)

    def slide(x, carry):
        value = rows[pl.ds(pl.multiple_of(x * c1, 16), c1), :].astype(F32)
        stack = jnp.concatenate([slid(value, 1), value, slid(value, -1)], axis=0)
        out[pl.ds(pl.multiple_of(x * 3 * c1, 16), 3 * c1), :] = stack.astype(BF16)
        return carry

    lax.fori_loop(0, length, slide, 0, unroll=4)

    offsets = [(j, i) for j in range(3) for i in range(3)]
    w_two[...] = jnp.concatenate(
        [
            jnp.concatenate([two[2 - i, 2 - j, 2 - k].astype(F32) for k in range(3)], axis=0)
            for j, i in offsets
        ],
        axis=1,
    ).astype(BF16)
    w_one[...] = jnp.concatenate(
        [
            jnp.concatenate([one[2 - i, 2 - j, k].astype(F32) for i in range(3)], axis=0)
            for j, k in offsets
        ],
        axis=1,
    ).astype(BF16)


def slide(act, kernel_two, kernel_one):
    c1, length, width = act.shape
    c0, c2 = (kernel_one.shape[3], kernel_two.shape[4])
    return vmem_call(
        slide_kernel,
        (
            jax.ShapeDtypeStruct((length * 3 * c1, width), BF16),
            jax.ShapeDtypeStruct((3 * c1, 9 * c2), BF16),
            jax.ShapeDtypeStruct((3 * c0, 9 * c1), BF16),
        ),
        (
            pltpu.VMEM((c1 * length, width), F32),
            pltpu.VMEM((c1 * length, width), BF16),
        ),
        pl.CostEstimate(flops=0, bytes_accessed=8 * act.size, transcendentals=0),
    )(act, kernel_two, kernel_one)


def cast_kernel(core, src, out):
    out[...] = src[...].astype(out.dtype)


def half_call(body, core, steps, height, which, value, others, cost):
    block = (height // steps, LANES)
    plain = pl.BlockSpec(block, lambda n, core: (n, 0))
    chosen = pl.BlockSpec(block, lambda n, core: (which(core[0]) * steps + n, 0))
    return pl.pallas_call(
        body,
        grid_spec=pltpu.PrefetchScalarGridSpec(
            num_scalar_prefetch=1,
            grid=(steps,),
            in_specs=[chosen] + [plain] * len(others),
            out_specs=plain,
        ),
        out_shape=jax.ShapeDtypeStruct((height, LANES), BF16),
        cost_estimate=pl.CostEstimate(flops=0, bytes_accessed=cost, transcendentals=0),
    )(core, value, *others)


def add_kernel(core, src, other, out):
    out[...] = (src[...] + other[...].astype(F32)).astype(out.dtype)


def swapped_half(core, value):
    height = value.shape[0] // 2
    steps = 2
    send = half_call(cast_kernel, core, steps, height, lambda c: 1 - c, value, [], 6 * value.size // 2)
    other = lax.ppermute(send, "core", [(0, 1), (1, 0)])
    return half_call(add_kernel, core, steps, height, lambda c: c, value, [other], 4 * value.size)


def compute_kernel(
    pack_m, pack_0, pack_p, acts, w_two, w_one,
    terms, own, up, down,
    pres, acc_two, acc_one,
):
    length = acts.shape[0] // w_two.shape[0]
    c1 = w_two.shape[0] // 3
    c2 = w_two.shape[1] // 9
    c0 = w_one.shape[0] // 3
    pitch = c0 + c2
    packs = (pack_m, pack_0, pack_p)

    stacked = 3 * c1
    pres[0:stacked, :] = jnp.zeros((stacked, LANES), BF16)
    pres[(length + 1) * stacked : (length + 2) * stacked, :] = jnp.zeros((stacked, LANES), BF16)
    acc_two[...] = jnp.zeros_like(acc_two)
    acc_one[...] = jnp.zeros_like(acc_one)

    def windows(x, offset, count):
        rows = [
            [p[pl.ds(pl.multiple_of((x + n) * pitch + offset, 16), count), :] for p in packs]
            for n in range(GROUP + 2)
        ]
        return jnp.concatenate(
            [jnp.concatenate(sum(rows[g : g + 3], []), axis=0) for g in range(GROUP)], axis=1
        )

    def first(step, carry):
        x = step * GROUP
        right = windows(x, 0, c2)
        sums = jnp.dot(w_two[...], right, preferred_element_type=F32)
        columns = []
        for g in range(GROUP):
            part = sums[:, g * LANES : (g + 1) * LANES]
            grad = slid(part[0:c1], 1) + part[c1 : 2 * c1] + slid(part[2 * c1 : 3 * c1], -1)
            stack = acts[pl.ds(pl.multiple_of((x + g) * stacked, 16), stacked), :]
            value = stack[c1 : 2 * c1].astype(F32)
            pre = (grad * jnp.where(value > 0, 1.0, 0.2)).astype(BF16).astype(F32)
            moved = jnp.concatenate([slid(pre, -1), pre, slid(pre, 1)], axis=0).astype(BF16)
            pres[pl.ds(pl.multiple_of((x + g + 1) * stacked, 16), stacked), :] = moved
            columns.append(stack)
        left = jnp.concatenate(columns, axis=1)
        acc_two[...] += lax.dot_general(
            right, left, (((1,), (1,)), ((), ())), preferred_element_type=F32
        )
        return carry

    lax.fori_loop(0, length // GROUP, first, 0, unroll=2)

    def second(step, carry):
        x = step * GROUP
        window = pres[pl.ds(pl.multiple_of(x * stacked, 16), (GROUP + 2) * stacked), :]
        moved = beside(window, 3 * stacked, stacked, GROUP)
        sums = jnp.dot(w_one[...], moved, preferred_element_type=F32)
        for g in range(GROUP):
            part = sums[:, g * LANES : (g + 1) * LANES]
            at = pl.ds(pl.multiple_of((x + g) * c0, 16), c0)
            for i, out in ((0, up), (1, own), (2, down)):
                out[at, :] = part[i * c0 : (i + 1) * c0].astype(out.dtype)
        acc_one[...] += lax.dot_general(
            windows(x, c2, c0),
            moved[stacked : 2 * stacked],
            (((1,), (1,)), ((), ())),
            preferred_element_type=F32,
        )
        return carry

    lax.fori_loop(0, length // GROUP, second, 0, unroll=2)

    terms[...] = jnp.zeros_like(terms)
    two = acc_two[...].T
    rows, width = two.shape
    blocks = -(-width // LANES)
    for block in range(blocks):
        part = two[:, block * LANES : min(width, (block + 1) * LANES)]
        terms[block * rows : (block + 1) * rows, 0 : part.shape[1]] = part.astype(terms.dtype)
    one = acc_one[...]
    terms[blocks * rows : blocks * rows + one.shape[0], 0 : one.shape[1]] = one.astype(terms.dtype)


def vmem_call(body, out_shape, scratch=(), cost=None, limit=24 * 2**20):
    spec = pl.BlockSpec(memory_space=pltpu.VMEM)
    return pl.pallas_call(
        body,
        out_shape=out_shape,
        out_specs=jax.tree.map(lambda _: spec, out_shape),
        scratch_shapes=list(scratch),
        compiler_params=pltpu.CompilerParams(vmem_limit_bytes=limit),
        cost_estimate=cost,
    )


def compute(packs, acts, w_two, w_one, rows):
    c0, c1, c2 = (w_one.shape[0] // 3, w_two.shape[0] // 3, w_two.shape[1] // 9)
    length, width = (acts.shape[0] // (3 * c1), acts.shape[1])
    plane = (length * c0, width)
    return vmem_call(
        compute_kernel,
        (
            jax.ShapeDtypeStruct((rows, LANES), BF16),
            jax.ShapeDtypeStruct(plane, F32),
            jax.ShapeDtypeStruct(plane, BF16),
            jax.ShapeDtypeStruct(plane, BF16),
        ),
        (
            pltpu.VMEM(((length + 2) * 3 * c1, width), BF16),
            pltpu.VMEM((9 * c2, 3 * c1), F32),
            pltpu.VMEM((9 * c0, 3 * c1), F32),
        ),
        pl.CostEstimate(flops=10**10, bytes_accessed=40 * 2**20, transcendentals=0),
    )(*packs, acts, w_two, w_one)


def merge_kernel(own, from_below, from_above, out, flat):
    chans, length, _ = out.shape

    def add(step, carry):
        at = pl.ds(pl.multiple_of(step * 64, 64), 64)
        flat[at, :] = own[at, :] + from_below[at, :].astype(F32) + from_above[at, :].astype(F32)
        return carry

    lax.fori_loop(0, own.shape[0] // 64, add, 0, unroll=4)

    def gather(c, carry):
        out[c] = flat[pl.ds(c, length, stride=chans), :].astype(out.dtype)
        return carry

    lax.fori_loop(0, chans, gather, 0, unroll=4)


def merge(own, from_below, from_above, shape):
    return vmem_call(
        merge_kernel,
        jax.ShapeDtypeStruct(shape, BF16),
        (pltpu.VMEM(own.shape, F32),),
        pl.CostEstimate(flops=2 * own.size, bytes_accessed=8 * own.size, transcendentals=0),
    )(own, from_below, from_above)


def share_kernel(scale, parts, out):
    total = (jnp.sum(parts[...].astype(F32), axis=0) * scale).astype(BF16)

    def write(n, carry):
        out[n] = total
        return carry

    lax.fori_loop(0, out.shape[0], write, 0)


def share(parts, scale):
    return vmem_call(
        lambda *refs: share_kernel(scale, *refs),
        jax.ShapeDtypeStruct(parts.shape, BF16),
        (),
        pl.CostEstimate(flops=parts.size, bytes_accessed=4 * parts.size, transcendentals=0),
    )(parts)


def gathered(parts, axes, scale=1.0):
    return lax.all_to_all(share(parts, scale), axes, 0, 0)


def finish_kernel(sizes, core, mine, other, raw_parts, bucket, out_one, out_two, raw):
    c0, c1, c2 = sizes
    half = mine.shape[0]
    me = core[0]
    bucket[pl.ds(pl.multiple_of(me * half, 8), half), :] = mine[...].astype(F32)
    bucket[pl.ds(pl.multiple_of((1 - me) * half, 8), half), :] = other[...].astype(F32)
    raw[...] = raw_parts[...].astype(F32)
    block = 3 * c1
    first = -(-9 * c2 // LANES) * block
    for i in range(3):
        for j in range(3):
            column = ((2 - j) * 3 + 2 - i) * c2
            whole, lane = (column // LANES, column % LANES)
            out_two[(3 * i + j) * block : (3 * i + j + 1) * block, :] = raw[
                whole * block : (whole + 1) * block, lane : lane + c2
            ]
            row = first + (3 * j + i) * c0
            for k in range(3):
                to = (9 * i + 3 * j + k) * c0
                out_one[to : to + c0, :] = raw[row : row + c0, k * c1 : (k + 1) * c1]


def finish(core, mine, other, raw, sizes):
    c0, c1, c2 = sizes
    spec = pl.BlockSpec(memory_space=pltpu.VMEM)
    return pl.pallas_call(
        lambda *refs: finish_kernel(sizes, *refs),
        out_shape=(
            jax.ShapeDtypeStruct((2 * mine.shape[0], LANES), F32),
            jax.ShapeDtypeStruct((27 * c0, c1), F32),
            jax.ShapeDtypeStruct((27 * c1, c2), F32),
        ),
        in_specs=[pl.BlockSpec(memory_space=pltpu.SMEM), spec, spec, spec],
        out_specs=(spec, spec, spec),
        scratch_shapes=[pltpu.VMEM(raw.shape, F32)],
        compiler_params=pltpu.CompilerParams(vmem_limit_bytes=24 * 2**20),
    )(core, mine, other, raw)


def halos(value):
    count = lax.axis_size(SPACE)
    up = [(i, i + 1) for i in range(count - 1)]
    down = [(j, i) for i, j in up]
    return (lax.ppermute(value, SPACE, up), lax.ppermute(value, SPACE, down))


def per_device(volume_in, hidden_act, out_cot, kernel_one, kernel_two, grad_bucket):
    c0, c1, c2 = (volume_in.shape[2], hidden_act.shape[2], out_cot.shape[2])
    devices, copies = (lax.axis_size(EVERY), lax.axis_size(("dp", "slab")))
    length = grad_bucket.shape[1]
    core = lax.axis_index("core").astype(jnp.int32).reshape(1)
    packed = pack(out_cot[0, 0], volume_in[0, 0])
    below, above = halos(packed)
    half = swapped_half(core, grad_bucket.reshape(length // LANES, LANES))
    act, half = lax.optimization_barrier((hidden_act[0, 0], half))
    parts = lax.all_to_all(half.reshape(copies, -1, LANES), ("dp", "slab"), 0, 0)
    mine = gathered(parts, ("dp", "slab")).reshape(-1, LANES)

    used = -(-9 * c2 // LANES) * 3 * c1 + 9 * c0
    rows = ceil_to(used, 16 * devices)
    acts, w_two, w_one = slide(act, kernel_two, kernel_one)
    terms, own, up, down = compute((below, packed, above), acts, w_two, w_one, rows)
    terms = lax.all_to_all(terms.reshape(devices, rows // devices, LANES), EVERY, 0, 0)
    cells = volume_in.shape[3] * volume_in.shape[4] * devices
    raw = gathered(terms, EVERY, 1.0 / math.sqrt(cells)).reshape(-1, LANES)

    count = lax.axis_size(SPACE)
    upward = [(i, i + 1) for i in range(count - 1)]
    from_below = lax.ppermute(up, SPACE, upward)
    from_above = lax.ppermute(down, SPACE, [(j, i) for i, j in upward])
    grad_input = merge(own, from_below, from_above, volume_in.shape[2:])

    mine, grad_input = lax.optimization_barrier((mine, grad_input))
    other = lax.ppermute(mine, "core", [(0, 1), (1, 0)])
    bucket_sum, total_one, total_two = finish(core, mine, other, raw, (c0, c1, c2))
    return (
        grad_input[None, None],
        total_one.reshape(3, 3, 3, c0, c1),
        total_two.reshape(3, 3, 3, c1, c2),
        bucket_sum.reshape(length),
    )


def solution(mesh):
    dp, space = (mesh.shape["dp"], mesh.shape["space"])
    split = Mesh(mesh.devices.reshape(dp, space // 2, 2), EVERY)
    volume = P("dp", SPACE, None, None, None)
    in_specs = (volume, volume, volume, P(), P(), P(EVERY, None))
    out_specs = (volume, P(), P(), P())
    return jax.shard_map(
        per_device, mesh=split, in_specs=in_specs, out_specs=out_specs, check_vma=False
    )
```

```python
import math

import jax
import jax.numpy as jnp
from jax import lax
from jax.experimental import pallas as pl
from jax.experimental.pallas import tpu as pltpu
from jax.sharding import Mesh, PartitionSpec as P

SPACE = ("slab", "core")
EVERY = ("dp", "slab", "core")
GROUP = 8
LANES = 128
BF16 = jnp.bfloat16
F32 = jnp.float32


def ceil_to(value, step):
    return -(-value // step) * step


def slid(value, step):
    lane = lax.broadcasted_iota(jnp.int32, value.shape, 1)
    width = value.shape[1]
    keep = lane >= step if step > 0 else lane < width + step
    return jnp.where(keep, pltpu.roll(value, step % width, 1), 0.0)


def beside(window, rows, step, count):
    return jnp.concatenate([window[g * step : g * step + rows] for g in range(count)], axis=1)


def turned(src, flat, dst, offset, pitch, lead):
    chans, length, _ = src.shape

    def stage(c, carry):
        flat[pl.ds(pl.multiple_of(c * length, length), length), :] = src[c].astype(F32)
        return carry

    lax.fori_loop(0, chans, stage, 0, unroll=4)

    def gather(x, carry):
        rows = flat[pl.ds(x, chans, stride=length), :]
        at = pl.multiple_of((x + lead) * pitch + offset, 16)
        dst[pl.ds(at, chans), :] = rows.astype(BF16)
        return carry

    lax.fori_loop(0, length, gather, 0, unroll=4)


def pack_kernel(cot, vol, out, fetched, flat, sems):
    step = vol.shape[0]
    length, width = vol.shape[1:]
    pitch = cot.shape[0] + step
    pieces = [cot.at[pl.ds(n, step)] for n in range(0, cot.shape[0], step)] + [vol]
    copies = [
        pltpu.make_async_copy(piece, fetched.at[n], sems.at[n]) for n, piece in enumerate(pieces)
    ]
    for copy in copies:
        copy.start()
    zeros = jnp.zeros((pitch, width), BF16)
    out[0:pitch, :] = zeros
    out[(length + 1) * pitch : (length + 2) * pitch, :] = zeros
    for n, copy in enumerate(copies):
        copy.wait()
        turned(fetched.at[n], flat, out, n * step, pitch, 1)


def pack(cot, vol):
    c2, length, width = cot.shape
    pitch = c2 + vol.shape[0]
    pieces = pitch // vol.shape[0]
    source = pl.BlockSpec(memory_space=pltpu.HBM)
    return pl.pallas_call(
        pack_kernel,
        out_shape=jax.ShapeDtypeStruct(((length + 2) * pitch, width), BF16),
        in_specs=[source, source],
        out_specs=pl.BlockSpec(memory_space=pltpu.VMEM),
        scratch_shapes=[
            pltpu.VMEM((pieces,) + vol.shape, BF16),
            pltpu.VMEM((vol.shape[0] * length, width), F32),
            pltpu.SemaphoreType.DMA((pieces,)),
        ],
        cost_estimate=pl.CostEstimate(flops=0, bytes_accessed=4 * cot.size, transcendentals=0),
    )(cot, vol)


def fetched_chunks(src, start, buffer, sems):
    count = sems.shape[0]
    step = buffer.shape[0] // count
    copies = []
    for n in range(count):
        at = pl.ds(pl.multiple_of(start + n * step, 8), step)
        copies.append(
            pltpu.make_async_copy(src.at[at], buffer.at[pl.ds(n * step, step)], sems.at[n])
        )
        copies[-1].start()
    return [(pl.ds(n * step, step), copy) for n, copy in enumerate(copies)]


def cast_kernel(core, src, out, buffer, sems):
    for rows, copy in fetched_chunks(src, (1 - core[0]) * out.shape[0], buffer, sems):
        copy.wait()
        out[rows, :] = buffer[rows, :].astype(out.dtype)


def add_kernel(core, src, other, out, buffer, more, sems, more_sems):
    chunks = fetched_chunks(src, core[0] * out.shape[0], buffer, sems)
    for (rows, copy), (_, second) in zip(chunks, fetched_chunks(other, 0, more, more_sems)):
        copy.wait()
        second.wait()
        out[rows, :] = (buffer[rows, :] + more[rows, :].astype(F32)).astype(out.dtype)


def half_call(body, core, value, others, chunks=8):
    half = (value.shape[0] // 2, LANES)
    source = pl.BlockSpec(memory_space=pltpu.HBM)
    return pl.pallas_call(
        body,
        out_shape=jax.ShapeDtypeStruct(half, BF16),
        in_specs=[pl.BlockSpec(memory_space=pltpu.SMEM)] + [source] * (1 + len(others)),
        out_specs=pl.BlockSpec(memory_space=pltpu.VMEM),
        scratch_shapes=[pltpu.VMEM(half, F32)]
        + [pltpu.VMEM(half, BF16) for _ in others]
        + [pltpu.SemaphoreType.DMA((chunks,)) for _ in range(1 + len(others))],
        cost_estimate=pl.CostEstimate(flops=0, bytes_accessed=6 * value.size, transcendentals=0),
    )(core, value, *others)


def compute_kernel(
    pack_m, pack_0, pack_p, act, two, one,
    terms, own, up, down,
    flat, acts, pres, w_two, w_one, acc_two, acc_one,
):
    c1, length, _ = act.shape
    c2, c0 = (two.shape[4], one.shape[3])
    pitch = c0 + c2
    packs = (pack_m, pack_0, pack_p)

    turned(act, flat, acts, 0, c1, 0)
    offsets = [(m, n) for m in range(3) for n in range(3)]
    w_two[...] = jnp.concatenate(
        [
            jnp.concatenate([two[2 - i, 2 - j, 2 - k].astype(F32) for k in range(3)], axis=0)
            for j, i in offsets
        ],
        axis=1,
    ).astype(BF16)
    w_one[...] = jnp.concatenate(
        [
            jnp.concatenate([one[2 - i, 2 - j, k].astype(F32) for i in range(3)], axis=0)
            for j, k in offsets
        ],
        axis=1,
    ).astype(BF16)
    stacked = 3 * c1
    pres[0:stacked, :] = jnp.zeros((stacked, LANES), BF16)
    pres[(length + 1) * stacked : (length + 2) * stacked, :] = jnp.zeros((stacked, LANES), BF16)
    acc_two[...] = jnp.zeros_like(acc_two)
    acc_one[...] = jnp.zeros_like(acc_one)

    def windows(x, offset, count):
        rows = [
            [p[pl.ds(pl.multiple_of((x + n) * pitch + offset, 16), count), :] for p in packs]
            for n in range(GROUP + 2)
        ]
        return jnp.concatenate(
            [jnp.concatenate(sum(rows[g : g + 3], []), axis=0) for g in range(GROUP)], axis=1
        )

    def first(step, carry):
        x = step * GROUP
        right = windows(x, 0, c2)
        sums = jnp.dot(w_two[...], right, preferred_element_type=F32)
        columns = []
        for g in range(GROUP):
            part = sums[:, g * LANES : (g + 1) * LANES]
            grad = slid(part[0:c1], 1) + part[c1 : 2 * c1] + slid(part[2 * c1 : 3 * c1], -1)
            value = acts[pl.ds(pl.multiple_of((x + g) * c1, 16), c1), :].astype(F32)
            pre = (grad * jnp.where(value > 0, 1.0, 0.2)).astype(BF16).astype(F32)
            moved = jnp.concatenate([slid(pre, -1), pre, slid(pre, 1)], axis=0).astype(BF16)
            pres[pl.ds(pl.multiple_of((x + g + 1) * stacked, 16), stacked), :] = moved
            stack = jnp.concatenate([slid(value, 1), value, slid(value, -1)], axis=0)
            columns.append(stack.astype(BF16))
        left = jnp.concatenate(columns, axis=1)
        acc_two[...] += lax.dot_general(
            right, left, (((1,), (1,)), ((), ())), preferred_element_type=F32
        )
        return carry

    lax.fori_loop(0, length // GROUP, first, 0, unroll=2)

    def second(step, carry):
        x = step * GROUP
        window = pres[pl.ds(pl.multiple_of(x * stacked, 16), (GROUP + 2) * stacked), :]
        moved = beside(window, 3 * stacked, stacked, GROUP)
        sums = jnp.dot(w_one[...], moved, preferred_element_type=F32)
        for g in range(GROUP):
            part = sums[:, g * LANES : (g + 1) * LANES]
            at = pl.ds(pl.multiple_of((x + g) * c0, 16), c0)
            for i, out in ((0, up), (1, own), (2, down)):
                out[at, :] = part[i * c0 : (i + 1) * c0].astype(out.dtype)
        acc_one[...] += lax.dot_general(
            windows(x, c2, c0),
            moved[stacked : 2 * stacked],
            (((1,), (1,)), ((), ())),
            preferred_element_type=F32,
        )
        return carry

    lax.fori_loop(0, length // GROUP, second, 0, unroll=2)

    terms[...] = jnp.zeros_like(terms)
    two = acc_two[...].T
    rows, width = two.shape
    blocks = -(-width // LANES)
    for block in range(blocks):
        part = two[:, block * LANES : min(width, (block + 1) * LANES)]
        terms[block * rows : (block + 1) * rows, 0 : part.shape[1]] = part.astype(terms.dtype)
    one = acc_one[...]
    terms[blocks * rows : blocks * rows + one.shape[0], 0 : one.shape[1]] = one.astype(terms.dtype)


def vmem_call(body, out_shape, scratch=(), cost=None, limit=24 * 2**20):
    spec = pl.BlockSpec(memory_space=pltpu.VMEM)
    return pl.pallas_call(
        body,
        out_shape=out_shape,
        out_specs=jax.tree.map(lambda _: spec, out_shape),
        scratch_shapes=list(scratch),
        compiler_params=pltpu.CompilerParams(vmem_limit_bytes=limit),
        cost_estimate=cost,
    )


def compute(packs, act, kernel_two, kernel_one, rows):
    c1, length, width = act.shape
    c0, c2 = (kernel_one.shape[3], kernel_two.shape[4])
    plane = (length * c0, width)
    return vmem_call(
        compute_kernel,
        (
            jax.ShapeDtypeStruct((rows, LANES), BF16),
            jax.ShapeDtypeStruct(plane, F32),
            jax.ShapeDtypeStruct(plane, BF16),
            jax.ShapeDtypeStruct(plane, BF16),
        ),
        (
            pltpu.VMEM((c1 * length, width), F32),
            pltpu.VMEM((c1 * length, width), BF16),
            pltpu.VMEM(((length + 2) * 3 * c1, width), BF16),
            pltpu.VMEM((3 * c1, 9 * c2), BF16),
            pltpu.VMEM((3 * c0, 9 * c1), BF16),
            pltpu.VMEM((9 * c2, 3 * c1), F32),
            pltpu.VMEM((9 * c0, 3 * c1), F32),
        ),
        pl.CostEstimate(flops=10**10, bytes_accessed=40 * 2**20, transcendentals=0),
    )(*packs, act, kernel_two, kernel_one)


def merge_kernel(own, from_below, from_above, out, flat):
    chans, length, _ = out.shape

    def add(step, carry):
        at = pl.ds(pl.multiple_of(step * 64, 64), 64)
        flat[at, :] = own[at, :] + from_below[at, :].astype(F32) + from_above[at, :].astype(F32)
        return carry

    lax.fori_loop(0, own.shape[0] // 64, add, 0, unroll=4)

    def gather(c, carry):
        out[c] = flat[pl.ds(c, length, stride=chans), :].astype(out.dtype)
        return carry

    lax.fori_loop(0, chans, gather, 0, unroll=4)


def merge(own, from_below, from_above, shape):
    return vmem_call(
        merge_kernel,
        jax.ShapeDtypeStruct(shape, BF16),
        (pltpu.VMEM(own.shape, F32),),
        pl.CostEstimate(flops=2 * own.size, bytes_accessed=8 * own.size, transcendentals=0),
    )(own, from_below, from_above)


def share_kernel(scale, bucket, terms, out):
    total = jnp.sum(bucket[...].astype(F32), axis=0).astype(BF16)
    grads = (jnp.sum(terms[...].astype(F32), axis=0) * scale).astype(BF16)
    height = total.shape[0]

    def write(n, carry):
        out[n, 0:height, :] = total
        out[n, height : height + grads.shape[0], :] = grads
        return carry

    lax.fori_loop(0, out.shape[0], write, 0)


def share(bucket, terms, scale, copies):
    rows = bucket.shape[1] + terms.shape[1]
    return vmem_call(
        lambda *refs: share_kernel(scale, *refs),
        jax.ShapeDtypeStruct((copies, rows, LANES), BF16),
        (),
        pl.CostEstimate(flops=bucket.size, bytes_accessed=3 * bucket.size, transcendentals=0),
    )(bucket, terms)


def place(source, height, which, bucket, buffer, sems):
    copies, count = (source.shape[0], sems.shape[0])
    size = copies * height
    step = copies // count
    sent = []
    for n in range(count):
        for q in range(n * step, (n + 1) * step):
            buffer[q * height : (q + 1) * height, :] = source[q, 0:height, :].astype(F32)
        rows = pl.ds(n * step * height, step * height)
        at = pl.ds(pl.multiple_of(which * size + n * step * height, 8), step * height)
        sent.append(pltpu.make_async_copy(buffer.at[rows], bucket.at[at], sems.at[n]))
        sent[-1].start()
    return sent


def start_kernel(height, core, mine, bucket, buffer, sems):
    for copy in place(mine, height, core[0], bucket, buffer, sems):
        copy.wait()


def finish_kernel(sizes, height, core, mine, other, partial, bucket, out_one, out_two, raw, buffer, sems):
    c0, c1, c2 = sizes
    copies, rows, _ = mine.shape
    extra = rows - height
    me = core[0]
    sent = place(other, height, 1 - me, bucket, buffer, sems)

    def unpack(q, carry):
        for source, which in ((mine, me), (other, 1 - me)):
            at = pl.multiple_of((2 * q + which) * extra, 8)
            raw[pl.ds(at, extra), :] = source[q, height:rows, :].astype(F32)
        return carry

    lax.fori_loop(0, copies, unpack, 0)
    block = 3 * c1
    first = -(-9 * c2 // LANES) * block
    for i in range(3):
        for j in range(3):
            column = ((2 - j) * 3 + 2 - i) * c2
            whole, lane = (column // LANES, column % LANES)
            out_two[(3 * i + j) * block : (3 * i + j + 1) * block, :] = raw[
                whole * block : (whole + 1) * block, lane : lane + c2
            ]
            row = first + (3 * j + i) * c0
            for k in range(3):
                to = (9 * i + 3 * j + k) * c0
                out_one[to : to + c0, :] = raw[row : row + c0, k * c1 : (k + 1) * c1]
    for copy in sent:
        copy.wait()


def finish(core, mine, other, length, sizes):
    c0, c1, c2 = sizes
    copies, rows, _ = mine.shape
    height = length // LANES // (2 * copies)
    spec = pl.BlockSpec(memory_space=pltpu.VMEM)
    scalar, remote = (pl.BlockSpec(memory_space=pltpu.SMEM), pl.BlockSpec(memory_space=pltpu.HBM))
    whole = jax.ShapeDtypeStruct((length // LANES, LANES), F32)
    chunks = 4
    scratch = [
        pltpu.VMEM((copies * height, LANES), F32),
        pltpu.SemaphoreType.DMA((chunks,)),
    ]
    params = pltpu.CompilerParams(vmem_limit_bytes=24 * 2**20)
    partial = pl.pallas_call(
        lambda *refs: start_kernel(height, *refs),
        out_shape=whole,
        in_specs=[scalar, spec],
        out_specs=remote,
        scratch_shapes=scratch,
        compiler_params=params,
    )(core, mine)
    return pl.pallas_call(
        lambda *refs: finish_kernel(sizes, height, *refs),
        out_shape=(
            whole,
            jax.ShapeDtypeStruct((27 * c0, c1), F32),
            jax.ShapeDtypeStruct((27 * c1, c2), F32),
        ),
        in_specs=[scalar, spec, spec, remote],
        out_specs=(remote, spec, spec),
        scratch_shapes=[pltpu.VMEM((2 * copies * (rows - height), LANES), F32)] + scratch,
        input_output_aliases={3: 0},
        compiler_params=params,
    )(core, mine, other, partial)


def halos(value):
    count = lax.axis_size(SPACE)
    up = [(i, i + 1) for i in range(count - 1)]
    down = [(j, i) for i, j in up]
    return (lax.ppermute(value, SPACE, up), lax.ppermute(value, SPACE, down))


def per_device(volume_in, hidden_act, out_cot, kernel_one, kernel_two, grad_bucket):
    c0, c1, c2 = (volume_in.shape[2], hidden_act.shape[2], out_cot.shape[2])
    devices, copies = (lax.axis_size(EVERY), lax.axis_size(("dp", "slab")))
    length = grad_bucket.shape[1]
    core = lax.axis_index("core").astype(jnp.int32).reshape(1)
    swap = [(0, 1), (1, 0)]
    bucket = grad_bucket.reshape(length // LANES, LANES)
    send = half_call(cast_kernel, core, bucket, [])
    cot, vol, send = lax.optimization_barrier((out_cot[0, 0], volume_in[0, 0], send))
    packed = pack(cot, vol)
    other, packed = lax.optimization_barrier((lax.ppermute(send, "core", swap), packed))
    below, above = halos(packed)
    half = half_call(add_kernel, core, bucket, [other])
    act, half = lax.optimization_barrier((hidden_act[0, 0], half))
    parts = lax.all_to_all(half.reshape(copies, -1, LANES), ("dp", "slab"), 0, 0)

    used = -(-9 * c2 // LANES) * 3 * c1 + 9 * c0
    rows = ceil_to(used, 16 * devices)
    terms, own, up, down = compute((below, packed, above), act, kernel_two, kernel_one, rows)
    terms, parts = lax.optimization_barrier((terms, parts))
    terms = lax.all_to_all(terms.reshape(devices, rows // devices, LANES), EVERY, 0, 0)
    cells = volume_in.shape[3] * volume_in.shape[4] * devices
    shares = share(parts, terms, 1.0 / math.sqrt(cells), copies)

    up, down, shares = lax.optimization_barrier((up, down, shares))
    mine = lax.all_to_all(shares, ("dp", "slab"), 0, 0)
    count = lax.axis_size(SPACE)
    upward = [(i, i + 1) for i in range(count - 1)]
    from_below = lax.ppermute(up, SPACE, upward)
    from_above = lax.ppermute(down, SPACE, [(j, i) for i, j in upward])
    grad_input = merge(own, from_below, from_above, volume_in.shape[2:])
    mine, grad_input = lax.optimization_barrier((mine, grad_input))
    other = lax.ppermute(mine, "core", swap)
    bucket_sum, total_one, total_two = finish(core, mine, other, length, (c0, c1, c2))
    return (
        grad_input[None, None],
        total_one.reshape(3, 3, 3, c0, c1),
        total_two.reshape(3, 3, 3, c1, c2),
        bucket_sum.reshape(length),
    )


def solution(mesh):
    dp, space = (mesh.shape["dp"], mesh.shape["space"])
    split = Mesh(mesh.devices.reshape(dp, space // 2, 2), EVERY)
    volume = P("dp", SPACE, None, None, None)
    in_specs = (volume, volume, volume, P(), P(), P(EVERY, None))
    out_specs = (volume, P(), P(), P())
    return jax.shard_map(
        per_device, mesh=split, in_specs=in_specs, out_specs=out_specs, check_vma=False
    )
```

```python
import math

import jax
import jax.numpy as jnp
from jax import lax
from jax.experimental import pallas as pl
from jax.experimental.pallas import tpu as pltpu
from jax.sharding import Mesh, PartitionSpec as P

SPACE = ("y", "core")
EVERY = ("z", "x", "y", "core")
GROUP = 8
LANES = 128
BF16 = jnp.bfloat16
F32 = jnp.float32


def ceil_to(value, step):
    return -(-value // step) * step


def slid(value, step):
    lane = lax.broadcasted_iota(jnp.int32, value.shape, 1)
    width = value.shape[1]
    keep = lane >= step if step > 0 else lane < width + step
    return jnp.where(keep, pltpu.roll(value, step % width, 1), 0.0)


def beside(window, rows, step, count):
    return jnp.concatenate([window[g * step : g * step + rows] for g in range(count)], axis=1)


def turned(src, flat, dst, offset, pitch, lead):
    chans, length, _ = src.shape

    def stage(c, carry):
        flat[pl.ds(pl.multiple_of(c * length, length), length), :] = src[c].astype(F32)
        return carry

    lax.fori_loop(0, chans, stage, 0, unroll=4)

    def gather(x, carry):
        rows = flat[pl.ds(x, chans, stride=length), :]
        at = pl.multiple_of((x + lead) * pitch + offset, 16)
        dst[pl.ds(at, chans), :] = rows.astype(BF16)
        return carry

    lax.fori_loop(0, length, gather, 0, unroll=4)


def pack_kernel(cot, vol, out, fetched, flat, sems):
    step = vol.shape[0]
    length, width = vol.shape[1:]
    pitch = cot.shape[0] + step
    pieces = [cot.at[pl.ds(n, step)] for n in range(0, cot.shape[0], step)] + [vol]
    copies = [
        pltpu.make_async_copy(piece, fetched.at[n], sems.at[n]) for n, piece in enumerate(pieces)
    ]
    for copy in copies:
        copy.start()
    zeros = jnp.zeros((pitch, width), BF16)
    out[0:pitch, :] = zeros
    out[(length + 1) * pitch : (length + 2) * pitch, :] = zeros
    for n, copy in enumerate(copies):
        copy.wait()
        turned(fetched.at[n], flat, out, n * step, pitch, 1)


def pack(cot, vol):
    c2, length, width = cot.shape
    pitch = c2 + vol.shape[0]
    pieces = pitch // vol.shape[0]
    source = pl.BlockSpec(memory_space=pltpu.HBM)
    return pl.pallas_call(
        pack_kernel,
        out_shape=jax.ShapeDtypeStruct(((length + 2) * pitch, width), BF16),
        in_specs=[source, source],
        out_specs=pl.BlockSpec(memory_space=pltpu.VMEM),
        scratch_shapes=[
            pltpu.VMEM((pieces,) + vol.shape, BF16),
            pltpu.VMEM((vol.shape[0] * length, width), F32),
            pltpu.SemaphoreType.DMA((pieces,)),
        ],
        compiler_params=pltpu.CompilerParams(vmem_limit_bytes=24 * 2**20),
        cost_estimate=pl.CostEstimate(flops=0, bytes_accessed=4 * cot.size, transcendentals=0),
    )(cot, vol)


def fetched_chunks(src, start, buffer, sems):
    count = sems.shape[0]
    step = buffer.shape[0] // count
    copies = []
    for n in range(count):
        at = pl.ds(pl.multiple_of(start + n * step, 8), step)
        copies.append(
            pltpu.make_async_copy(src.at[at], buffer.at[pl.ds(n * step, step)], sems.at[n])
        )
        copies[-1].start()
    return [(pl.ds(n * step, step), copy) for n, copy in enumerate(copies)]


def cast_kernel(src, out, buffer, sems):
    start = (1 - lax.axis_index("core")) * out.shape[0]
    for rows, copy in fetched_chunks(src, start, buffer, sems):
        copy.wait()
        out[rows, :] = buffer[rows, :].astype(out.dtype)


def cast(value, chunks=8):
    half = (value.shape[0] // 2, LANES)
    return pl.pallas_call(
        cast_kernel,
        out_shape=jax.ShapeDtypeStruct(half, BF16),
        in_specs=[pl.BlockSpec(memory_space=pltpu.HBM)],
        out_specs=pl.BlockSpec(memory_space=pltpu.VMEM),
        scratch_shapes=[pltpu.VMEM(half, F32), pltpu.SemaphoreType.DMA((chunks,))],
        cost_estimate=pl.CostEstimate(flops=0, bytes_accessed=6 * value.size, transcendentals=0),
    )(value)


def add_kernel(src, other, out):
    rows = out.shape[0]
    step = rows // 8
    start = lax.axis_index("core") * rows

    def add(n, carry):
        at = pl.ds(pl.multiple_of(n * step, 16), step)
        own = src[pl.ds(pl.multiple_of(start + n * step, 16), step), :]
        out[at, :] = (own + other[at, :].astype(F32)).astype(out.dtype)
        return carry

    lax.fori_loop(0, 8, add, 0)


def add(value, other):
    return vmem_call(
        add_kernel,
        jax.ShapeDtypeStruct(other.shape, BF16),
        (),
        pl.CostEstimate(flops=0, bytes_accessed=4 * value.size, transcendentals=0),
    )(value, other)


def bit(axis, distance):
    return lax.rem(lax.axis_index(axis) // distance, 2)


def split_to(total, mine, send, keep):
    half = total.shape[0] // 2
    keep[...] = total[pl.ds(pl.multiple_of(mine * half, 16), half), :]
    send[...] = total[pl.ds(pl.multiple_of((1 - mine) * half, 16), half), :].astype(send.dtype)


def halve_kernel(axis, distance, keep, other, send_out, keep_out, total):
    total[...] = keep[...] + other[...].astype(F32)
    split_to(total, bit(axis, distance), send_out, keep_out)


def halve(keep, other, axis, distance):
    half = (keep.shape[0] // 2, LANES)
    return vmem_call(
        lambda *refs: halve_kernel(axis, distance, *refs),
        (jax.ShapeDtypeStruct(half, BF16), jax.ShapeDtypeStruct(half, F32)),
        (pltpu.VMEM(keep.shape, F32),),
        pl.CostEstimate(flops=0, bytes_accessed=8 * keep.size, transcendentals=0),
    )(keep, other)


def exchanged(value, axis, distance):
    return lax.ppermute(value, axis, [(i, i ^ distance) for i in range(lax.axis_size(axis))])


def compute_kernel(
    pack_m, pack_0, pack_p, act, two, one,
    send, keep, own, up, down,
    terms, flat, acts, pres, w_two, w_one, acc_two, acc_one,
):
    c1, length, _ = act.shape
    c2, c0 = (two.shape[4], one.shape[3])
    pitch = c0 + c2
    packs = (pack_m, pack_0, pack_p)

    turned(act, flat, acts, 0, c1, 0)
    offsets = [(m, n) for m in range(3) for n in range(3)]
    w_two[...] = jnp.concatenate(
        [
            jnp.concatenate([two[2 - i, 2 - j, 2 - k].astype(F32) for k in range(3)], axis=0)
            for j, i in offsets
        ],
        axis=1,
    ).astype(BF16)
    w_one[...] = jnp.concatenate(
        [
            jnp.concatenate([one[2 - i, 2 - j, k].astype(F32) for i in range(3)], axis=0)
            for j, k in offsets
        ],
        axis=1,
    ).astype(BF16)
    stacked = 3 * c1
    pres[0:stacked, :] = jnp.zeros((stacked, LANES), BF16)
    pres[(length + 1) * stacked : (length + 2) * stacked, :] = jnp.zeros((stacked, LANES), BF16)
    acc_two[...] = jnp.zeros_like(acc_two)
    acc_one[...] = jnp.zeros_like(acc_one)

    def windows(x, offset, count):
        rows = [
            [p[pl.ds(pl.multiple_of((x + n) * pitch + offset, 16), count), :] for p in packs]
            for n in range(GROUP + 2)
        ]
        return jnp.concatenate(
            [jnp.concatenate(sum(rows[g : g + 3], []), axis=0) for g in range(GROUP)], axis=1
        )

    def first(step, carry):
        x = step * GROUP
        right = windows(x, 0, c2)
        sums = jnp.dot(w_two[...], right, preferred_element_type=F32)
        columns = []
        for g in range(GROUP):
            part = sums[:, g * LANES : (g + 1) * LANES]
            grad = slid(part[0:c1], 1) + part[c1 : 2 * c1] + slid(part[2 * c1 : 3 * c1], -1)
            value = acts[pl.ds(pl.multiple_of((x + g) * c1, 16), c1), :].astype(F32)
            pre = (grad * jnp.where(value > 0, 1.0, 0.2)).astype(BF16).astype(F32)
            moved = jnp.concatenate([slid(pre, -1), pre, slid(pre, 1)], axis=0).astype(BF16)
            pres[pl.ds(pl.multiple_of((x + g + 1) * stacked, 16), stacked), :] = moved
            stack = jnp.concatenate([slid(value, 1), value, slid(value, -1)], axis=0)
            columns.append(stack.astype(BF16))
        left = jnp.concatenate(columns, axis=1)
        acc_two[...] += lax.dot_general(
            right, left, (((1,), (1,)), ((), ())), preferred_element_type=F32
        )
        return carry

    lax.fori_loop(0, length // GROUP, first, 0, unroll=2)

    def second(step, carry):
        x = step * GROUP
        window = pres[pl.ds(pl.multiple_of(x * stacked, 16), (GROUP + 2) * stacked), :]
        moved = beside(window, 3 * stacked, stacked, GROUP)
        sums = jnp.dot(w_one[...], moved, preferred_element_type=F32)
        for g in range(GROUP):
            part = sums[:, g * LANES : (g + 1) * LANES]
            at = pl.ds(pl.multiple_of((x + g) * c0, 16), c0)
            for i, out in ((0, up), (1, own), (2, down)):
                out[at, :] = part[i * c0 : (i + 1) * c0].astype(out.dtype)
        acc_one[...] += lax.dot_general(
            windows(x, c2, c0),
            moved[stacked : 2 * stacked],
            (((1,), (1,)), ((), ())),
            preferred_element_type=F32,
        )
        return carry

    lax.fori_loop(0, length // GROUP, second, 0, unroll=2)

    terms[...] = jnp.zeros_like(terms)
    two = acc_two[...].T
    rows, width = two.shape
    blocks = -(-width // LANES)
    for block in range(blocks):
        part = two[:, block * LANES : min(width, (block + 1) * LANES)]
        terms[block * rows : (block + 1) * rows, 0 : part.shape[1]] = part
    one = acc_one[...]
    terms[blocks * rows : blocks * rows + one.shape[0], 0 : one.shape[1]] = one
    split_to(terms, bit("core", 1), send, keep)


def vmem_call(body, out_shape, scratch=(), cost=None, limit=24 * 2**20):
    spec = pl.BlockSpec(memory_space=pltpu.VMEM)
    return pl.pallas_call(
        body,
        out_shape=out_shape,
        out_specs=jax.tree.map(lambda _: spec, out_shape),
        scratch_shapes=list(scratch),
        compiler_params=pltpu.CompilerParams(vmem_limit_bytes=limit),
        cost_estimate=cost,
    )


def compute(packs, act, kernel_two, kernel_one, rows):
    c1, length, width = act.shape
    c0, c2 = (kernel_one.shape[3], kernel_two.shape[4])
    plane = (length * c0, width)
    return vmem_call(
        compute_kernel,
        (
            jax.ShapeDtypeStruct((rows // 2, LANES), BF16),
            jax.ShapeDtypeStruct((rows // 2, LANES), F32),
            jax.ShapeDtypeStruct(plane, F32),
            jax.ShapeDtypeStruct(plane, BF16),
            jax.ShapeDtypeStruct(plane, BF16),
        ),
        (
            pltpu.VMEM((rows, LANES), F32),
            pltpu.VMEM((c1 * length, width), F32),
            pltpu.VMEM((c1 * length, width), BF16),
            pltpu.VMEM(((length + 2) * 3 * c1, width), BF16),
            pltpu.VMEM((3 * c1, 9 * c2), BF16),
            pltpu.VMEM((3 * c0, 9 * c1), BF16),
            pltpu.VMEM((9 * c2, 3 * c1), F32),
            pltpu.VMEM((9 * c0, 3 * c1), F32),
        ),
        pl.CostEstimate(flops=10**10, bytes_accessed=40 * 2**20, transcendentals=0),
    )(*packs, act, kernel_two, kernel_one)


def merge_kernel(own, from_below, from_above, out, flat):
    chans, length, _ = out.shape

    def add(step, carry):
        at = pl.ds(pl.multiple_of(step * 64, 64), 64)
        flat[at, :] = own[at, :] + from_below[at, :].astype(F32) + from_above[at, :].astype(F32)
        return carry

    lax.fori_loop(0, own.shape[0] // 64, add, 0, unroll=4)

    def gather(c, carry):
        out[c] = flat[pl.ds(c, length, stride=chans), :].astype(out.dtype)
        return carry

    lax.fori_loop(0, chans, gather, 0, unroll=4)


def merge(own, from_below, from_above, shape):
    return vmem_call(
        merge_kernel,
        jax.ShapeDtypeStruct(shape, BF16),
        (pltpu.VMEM(own.shape, F32),),
        pl.CostEstimate(flops=2 * own.size, bytes_accessed=8 * own.size, transcendentals=0),
    )(own, from_below, from_above)


def share_kernel(parts, keep, other, out):
    total = jnp.sum(parts[...].astype(F32), axis=0).astype(BF16)
    grads = (keep[...] + other[...].astype(F32)).astype(BF16)
    height = total.shape[0]

    def write(n, carry):
        out[n, 0:height, :] = total
        out[n, height : height + grads.shape[0], :] = grads
        return carry

    lax.fori_loop(0, out.shape[0], write, 0)


def share(parts, keep, other, copies):
    rows = parts.shape[1] + keep.shape[0]
    return vmem_call(
        share_kernel,
        jax.ShapeDtypeStruct((copies, rows, LANES), BF16),
        (),
        pl.CostEstimate(flops=parts.size, bytes_accessed=3 * parts.size, transcendentals=0),
    )(parts, keep, other)


def column_kernel(scale, height, column, out):
    along, rows, _ = column.shape
    grads = jnp.sum(column[:, height:rows, :].astype(F32), axis=0) * scale
    grads = grads.astype(BF16)

    def write(n, carry):
        for m in range(along):
            out[n, m * height : (m + 1) * height, :] = column[m, 0:height, :]
        out[n, along * height : along * height + rows - height, :] = grads
        return carry

    lax.fori_loop(0, out.shape[0], write, 0)


def column_share(column, height, scale, copies):
    along, rows, _ = column.shape
    return vmem_call(
        lambda *refs: column_kernel(scale, height, *refs),
        jax.ShapeDtypeStruct((copies, along * height + rows - height, LANES), BF16),
        (),
        pl.CostEstimate(flops=0, bytes_accessed=4 * column.size, transcendentals=0),
    )(column)


def place(source, height, along, which, bucket, buffer, sems):
    count = source.shape[0]
    sent = []
    for z in range(along):
        for n in range(count):
            rows = slice((z * count + n) * height, (z * count + n + 1) * height)
            buffer[rows, :] = source[n, z * height : (z + 1) * height, :].astype(F32)
        rows = pl.ds(z * count * height, count * height)
        at = pl.ds(pl.multiple_of((which * along + z) * count * height, 8), count * height)
        sent.append(pltpu.make_async_copy(buffer.at[rows], bucket.at[at], sems.at[z]))
        sent[-1].start()
    return sent


def start_kernel(height, along, mine, bucket, buffer, sems):
    for copy in place(mine, height, along, lax.axis_index("core"), bucket, buffer, sems):
        copy.wait()


def finish_kernel(sizes, height, along, across, mine, other, partial, bucket, out_one, out_two, raw, buffer, sems):
    c0, c1, c2 = sizes
    count, rows, _ = mine.shape
    extra = rows - along * height
    me = lax.axis_index("core")
    sent = place(other, height, along, 1 - me, bucket, buffer, sems)

    nx, ny = across
    for x in range(nx):
        for y in range(ny):
            for source, which in ((mine, me), (other, 1 - me)):
                at = pl.multiple_of((which * count + y * nx + x) * extra, 8)
                raw[pl.ds(at, extra), :] = source[x * ny + y, along * height : rows, :].astype(F32)
    block = 3 * c1
    first = -(-9 * c2 // LANES) * block
    for i in range(3):
        for j in range(3):
            column = ((2 - j) * 3 + 2 - i) * c2
            whole, lane = (column // LANES, column % LANES)
            out_two[(3 * i + j) * block : (3 * i + j + 1) * block, :] = raw[
                whole * block : (whole + 1) * block, lane : lane + c2
            ]
            row = first + (3 * j + i) * c0
            for k in range(3):
                to = (9 * i + 3 * j + k) * c0
                out_one[to : to + c0, :] = raw[row : row + c0, k * c1 : (k + 1) * c1]
    for copy in sent:
        copy.wait()


def finish(mine, other, length, along, across, sizes):
    c0, c1, c2 = sizes
    count, rows, _ = mine.shape
    height = length // LANES // (2 * along * count)
    spec, remote = (pl.BlockSpec(memory_space=pltpu.VMEM), pl.BlockSpec(memory_space=pltpu.HBM))
    whole = jax.ShapeDtypeStruct((length // LANES, LANES), F32)
    scratch = [
        pltpu.VMEM((along * count * height, LANES), F32),
        pltpu.SemaphoreType.DMA((along,)),
    ]
    params = pltpu.CompilerParams(vmem_limit_bytes=24 * 2**20)
    partial = pl.pallas_call(
        lambda *refs: start_kernel(height, along, *refs),
        out_shape=whole,
        in_specs=[spec],
        out_specs=remote,
        scratch_shapes=scratch,
        compiler_params=params,
    )(mine)
    return pl.pallas_call(
        lambda *refs: finish_kernel(sizes, height, along, across, *refs),
        out_shape=(
            whole,
            jax.ShapeDtypeStruct((27 * c0, c1), F32),
            jax.ShapeDtypeStruct((27 * c1, c2), F32),
        ),
        in_specs=[spec, spec, remote],
        out_specs=(remote, spec, spec),
        scratch_shapes=[pltpu.VMEM((2 * count * (rows - along * height), LANES), F32)] + scratch,
        input_output_aliases={2: 0},
        compiler_params=params,
    )(mine, other, partial)


def halos(value):
    count = lax.axis_size(SPACE)
    up = [(i, i + 1) for i in range(count - 1)]
    down = [(j, i) for i, j in up]
    return (lax.ppermute(value, SPACE, up), lax.ppermute(value, SPACE, down))


def per_device(volume_in, hidden_act, out_cot, kernel_one, kernel_two, grad_bucket):
    c0, c1, c2 = (volume_in.shape[2], hidden_act.shape[2], out_cot.shape[2])
    devices, planar = (lax.axis_size(EVERY), lax.axis_size(("x", "y")))
    along, across = (lax.axis_size("z"), (lax.axis_size("x"), lax.axis_size("y")))
    length = grad_bucket.shape[1]
    bucket = grad_bucket.reshape(length // LANES, LANES)
    send = cast(bucket)
    cot, vol, send = lax.optimization_barrier((out_cot[0, 0], volume_in[0, 0], send))
    packed = pack(cot, vol)
    other, packed = lax.optimization_barrier((exchanged(send, "core", 1), packed))
    below, above = halos(packed)
    half = add(bucket, other)
    act, half = lax.optimization_barrier((hidden_act[0, 0], half))
    parts = lax.all_to_all(half.reshape(along * planar, -1, LANES), ("z", "x", "y"), 0, 0)

    used = -(-9 * c2 // LANES) * 3 * c1 + 9 * c0
    rows = ceil_to(used, 16 * 2 * planar)
    send, keep, own, up, down = compute((below, packed, above), act, kernel_two, kernel_one, rows)
    other = exchanged(send, "core", 1)
    for axis in ("y", "x"):
        distance = lax.axis_size(axis) // 2
        while distance >= 1:
            send, keep = halve(keep, other, axis, distance)
            other = exchanged(send, axis, distance)
            distance //= 2
    shares = share(parts, keep, other, along)

    up, down, shares = lax.optimization_barrier((up, down, shares))
    column = lax.all_to_all(shares, "z", 0, 0)
    cells = volume_in.shape[3] * volume_in.shape[4] * devices
    shares = column_share(column, parts.shape[1], 1.0 / math.sqrt(cells), planar)
    mine = lax.all_to_all(shares, ("x", "y"), 0, 0)
    count = lax.axis_size(SPACE)
    upward = [(i, i + 1) for i in range(count - 1)]
    from_below = lax.ppermute(up, SPACE, upward)
    from_above = lax.ppermute(down, SPACE, [(j, i) for i, j in upward])
    grad_input = merge(own, from_below, from_above, volume_in.shape[2:])
    mine, grad_input = lax.optimization_barrier((mine, grad_input))
    other = exchanged(mine, "core", 1)
    bucket_sum, total_one, total_two = finish(mine, other, length, along, across, (c0, c1, c2))
    return (
        grad_input[None, None],
        total_one.reshape(3, 3, 3, c0, c1),
        total_two.reshape(3, 3, 3, c1, c2),
        bucket_sum.reshape(length),
    )


def solution(mesh):
    dp, space = (mesh.shape["dp"], mesh.shape["space"])
    split = Mesh(mesh.devices.reshape(dp // 2, 2, space // 2, 2), EVERY)
    volume = P(("z", "x"), SPACE, None, None, None)
    in_specs = (volume, volume, volume, P(), P(), P(EVERY, None))
    out_specs = (volume, P(), P(), P())
    return jax.shard_map(
        per_device, mesh=split, in_specs=in_specs, out_specs=out_specs, check_vma=False
    )
```

```python
import math

import jax
import jax.numpy as jnp
from jax import lax
from jax.experimental import pallas as pl
from jax.experimental.pallas import tpu as pltpu
from jax.sharding import Mesh, PartitionSpec as P

SPACE = ("slab", "core")
SAME = ("dp", "slab")
EVERY = ("dp", "slab", "core")
GROUP = 8
LANES = 128
BF16 = jnp.bfloat16
F32 = jnp.float32


def ceil_to(value, step):
    return -(-value // step) * step


def slid(value, step):
    lane = lax.broadcasted_iota(jnp.int32, value.shape, 1)
    width = value.shape[1]
    keep = lane >= step if step > 0 else lane < width + step
    return jnp.where(keep, pltpu.roll(value, step % width, 1), 0.0)


def beside(window, rows, step, count):
    return jnp.concatenate([window[g * step : g * step + rows] for g in range(count)], axis=1)


def turned(src, flat, dst, offset, pitch, lead):
    chans, length, _ = src.shape

    def stage(c, carry):
        flat[pl.ds(pl.multiple_of(c * length, length), length), :] = src[c].astype(F32)
        return carry

    lax.fori_loop(0, chans, stage, 0, unroll=4)

    def gather(x, carry):
        rows = flat[pl.ds(x, chans, stride=length), :]
        at = pl.multiple_of((x + lead) * pitch + offset, 16)
        dst[pl.ds(at, chans), :] = rows.astype(BF16)
        return carry

    lax.fori_loop(0, length, gather, 0, unroll=4)


def pack_kernel(cot, vol, out, fetched, flat, sems):
    step = vol.shape[0]
    length, width = vol.shape[1:]
    pitch = cot.shape[0] + step
    pieces = [cot.at[pl.ds(n, step)] for n in range(0, cot.shape[0], step)] + [vol]
    copies = [
        pltpu.make_async_copy(piece, fetched.at[n], sems.at[n]) for n, piece in enumerate(pieces)
    ]
    for copy in copies:
        copy.start()
    zeros = jnp.zeros((pitch, width), BF16)
    out[0:pitch, :] = zeros
    out[(length + 1) * pitch : (length + 2) * pitch, :] = zeros
    for n, copy in enumerate(copies):
        copy.wait()
        turned(fetched.at[n], flat, out, n * step, pitch, 1)


def pack(cot, vol):
    c2, length, width = cot.shape
    pitch = c2 + vol.shape[0]
    pieces = pitch // vol.shape[0]
    source = pl.BlockSpec(memory_space=pltpu.HBM)
    return pl.pallas_call(
        pack_kernel,
        out_shape=jax.ShapeDtypeStruct(((length + 2) * pitch, width), BF16),
        in_specs=[source, source],
        out_specs=pl.BlockSpec(memory_space=pltpu.VMEM),
        scratch_shapes=[
            pltpu.VMEM((pieces,) + vol.shape, BF16),
            pltpu.VMEM((vol.shape[0] * length, width), F32),
            pltpu.SemaphoreType.DMA((pieces,)),
        ],
        compiler_params=pltpu.CompilerParams(vmem_limit_bytes=24 * 2**20),
        cost_estimate=pl.CostEstimate(flops=0, bytes_accessed=4 * cot.size, transcendentals=0),
    )(cot, vol)


def fetched_chunks(src, start, buffer, sems):
    count = sems.shape[0]
    step = buffer.shape[0] // count
    copies = []
    for n in range(count):
        at = pl.ds(pl.multiple_of(start + n * step, 8), step)
        copies.append(
            pltpu.make_async_copy(src.at[at], buffer.at[pl.ds(n * step, step)], sems.at[n])
        )
        copies[-1].start()
    return [(pl.ds(n * step, step), copy) for n, copy in enumerate(copies)]


def cast_kernel(src, out, buffer, sems):
    start = (1 - lax.axis_index("core")) * out.shape[0]
    for rows, copy in fetched_chunks(src, start, buffer, sems):
        copy.wait()
        out[rows, :] = buffer[rows, :].astype(out.dtype)


def cast(value, chunks=8):
    half = (value.shape[0] // 2, LANES)
    return pl.pallas_call(
        cast_kernel,
        out_shape=jax.ShapeDtypeStruct(half, BF16),
        in_specs=[pl.BlockSpec(memory_space=pltpu.HBM)],
        out_specs=pl.BlockSpec(memory_space=pltpu.VMEM),
        scratch_shapes=[pltpu.VMEM(half, F32), pltpu.SemaphoreType.DMA((chunks,))],
        cost_estimate=pl.CostEstimate(flops=0, bytes_accessed=6 * value.size, transcendentals=0),
    )(value)


def add_kernel(src, other, out):
    rows = out.shape[0]
    step = rows // 8
    start = lax.axis_index("core") * rows

    def add(n, carry):
        at = pl.ds(pl.multiple_of(n * step, 16), step)
        own = src[pl.ds(pl.multiple_of(start + n * step, 16), step), :]
        out[at, :] = (own + other[at, :].astype(F32)).astype(out.dtype)
        return carry

    lax.fori_loop(0, 8, add, 0)


def add(value, other):
    return vmem_call(
        add_kernel,
        jax.ShapeDtypeStruct(other.shape, BF16),
        (),
        pl.CostEstimate(flops=0, bytes_accessed=4 * value.size, transcendentals=0),
    )(value, other)


def split_to(total, mine, send, keep):
    half = total.shape[0] // 2
    keep[...] = total[pl.ds(pl.multiple_of(mine * half, 16), half), :]
    send[...] = total[pl.ds(pl.multiple_of((1 - mine) * half, 16), half), :].astype(send.dtype)


def pair_kernel(keep, other, out):
    out[...] = (keep[...] + other[...].astype(F32)).astype(out.dtype)


def pair_sum(keep, other):
    return vmem_call(
        pair_kernel,
        jax.ShapeDtypeStruct(other.shape, BF16),
        (),
        pl.CostEstimate(flops=0, bytes_accessed=8 * keep.size, transcendentals=0),
    )(keep, other)


def swapped(value):
    return lax.ppermute(value, "core", [(0, 1), (1, 0)])


def compute_kernel(
    pack_m, pack_0, pack_p, act, two, one,
    send, keep, own, up, down,
    terms, flat, acts, pres, w_two, w_one, acc_two, acc_one,
):
    c1, length, _ = act.shape
    c2, c0 = (two.shape[4], one.shape[3])
    pitch = c0 + c2
    packs = (pack_m, pack_0, pack_p)

    turned(act, flat, acts, 0, c1, 0)
    offsets = [(m, n) for m in range(3) for n in range(3)]
    w_two[...] = jnp.concatenate(
        [
            jnp.concatenate([two[2 - i, 2 - j, 2 - k].astype(F32) for k in range(3)], axis=0)
            for j, i in offsets
        ],
        axis=1,
    ).astype(BF16)
    w_one[...] = jnp.concatenate(
        [
            jnp.concatenate([one[2 - i, 2 - j, k].astype(F32) for i in range(3)], axis=0)
            for j, k in offsets
        ],
        axis=1,
    ).astype(BF16)
    stacked = 3 * c1
    pres[0:stacked, :] = jnp.zeros((stacked, LANES), BF16)
    pres[(length + 1) * stacked : (length + 2) * stacked, :] = jnp.zeros((stacked, LANES), BF16)
    acc_two[...] = jnp.zeros_like(acc_two)
    acc_one[...] = jnp.zeros_like(acc_one)

    def windows(x, offset, count):
        rows = [
            [p[pl.ds(pl.multiple_of((x + n) * pitch + offset, 16), count), :] for p in packs]
            for n in range(GROUP + 2)
        ]
        return jnp.concatenate(
            [jnp.concatenate(sum(rows[g : g + 3], []), axis=0) for g in range(GROUP)], axis=1
        )

    def first(step, carry):
        x = step * GROUP
        right = windows(x, 0, c2)
        sums = jnp.dot(w_two[...], right, preferred_element_type=F32)
        columns = []
        for g in range(GROUP):
            part = sums[:, g * LANES : (g + 1) * LANES]
            grad = slid(part[0:c1], 1) + part[c1 : 2 * c1] + slid(part[2 * c1 : 3 * c1], -1)
            value = acts[pl.ds(pl.multiple_of((x + g) * c1, 16), c1), :].astype(F32)
            pre = (grad * jnp.where(value > 0, 1.0, 0.2)).astype(BF16).astype(F32)
            moved = jnp.concatenate([slid(pre, -1), pre, slid(pre, 1)], axis=0).astype(BF16)
            pres[pl.ds(pl.multiple_of((x + g + 1) * stacked, 16), stacked), :] = moved
            stack = jnp.concatenate([slid(value, 1), value, slid(value, -1)], axis=0)
            columns.append(stack.astype(BF16))
        left = jnp.concatenate(columns, axis=1)
        acc_two[...] += lax.dot_general(
            right, left, (((1,), (1,)), ((), ())), preferred_element_type=F32
        )
        return carry

    lax.fori_loop(0, length // GROUP, first, 0, unroll=2)

    def second(step, carry):
        x = step * GROUP
        window = pres[pl.ds(pl.multiple_of(x * stacked, 16), (GROUP + 2) * stacked), :]
        moved = beside(window, 3 * stacked, stacked, GROUP)
        sums = jnp.dot(w_one[...], moved, preferred_element_type=F32)
        for g in range(GROUP):
            part = sums[:, g * LANES : (g + 1) * LANES]
            at = pl.ds(pl.multiple_of((x + g) * c0, 16), c0)
            for i, out in ((0, up), (1, own), (2, down)):
                out[at, :] = part[i * c0 : (i + 1) * c0].astype(out.dtype)
        acc_one[...] += lax.dot_general(
            windows(x, c2, c0),
            moved[stacked : 2 * stacked],
            (((1,), (1,)), ((), ())),
            preferred_element_type=F32,
        )
        return carry

    lax.fori_loop(0, length // GROUP, second, 0, unroll=2)

    terms[...] = jnp.zeros_like(terms)
    two = acc_two[...].T
    rows, width = two.shape
    blocks = -(-width // LANES)
    for block in range(blocks):
        part = two[:, block * LANES : min(width, (block + 1) * LANES)]
        terms[block * rows : (block + 1) * rows, 0 : part.shape[1]] = part
    one = acc_one[...]
    terms[blocks * rows : blocks * rows + one.shape[0], 0 : one.shape[1]] = one
    split_to(terms, lax.axis_index("core"), send, keep)


def vmem_call(body, out_shape, scratch=(), cost=None, limit=24 * 2**20):
    spec = pl.BlockSpec(memory_space=pltpu.VMEM)
    return pl.pallas_call(
        body,
        out_shape=out_shape,
        out_specs=jax.tree.map(lambda _: spec, out_shape),
        scratch_shapes=list(scratch),
        compiler_params=pltpu.CompilerParams(vmem_limit_bytes=limit),
        cost_estimate=cost,
    )


def compute(packs, act, kernel_two, kernel_one, rows):
    c1, length, width = act.shape
    c0, c2 = (kernel_one.shape[3], kernel_two.shape[4])
    plane = (length * c0, width)
    return vmem_call(
        compute_kernel,
        (
            jax.ShapeDtypeStruct((rows // 2, LANES), BF16),
            jax.ShapeDtypeStruct((rows // 2, LANES), F32),
            jax.ShapeDtypeStruct(plane, F32),
            jax.ShapeDtypeStruct(plane, BF16),
            jax.ShapeDtypeStruct(plane, BF16),
        ),
        (
            pltpu.VMEM((rows, LANES), F32),
            pltpu.VMEM((c1 * length, width), F32),
            pltpu.VMEM((c1 * length, width), BF16),
            pltpu.VMEM(((length + 2) * 3 * c1, width), BF16),
            pltpu.VMEM((3 * c1, 9 * c2), BF16),
            pltpu.VMEM((3 * c0, 9 * c1), BF16),
            pltpu.VMEM((9 * c2, 3 * c1), F32),
            pltpu.VMEM((9 * c0, 3 * c1), F32),
        ),
        pl.CostEstimate(flops=10**10, bytes_accessed=40 * 2**20, transcendentals=0),
    )(*packs, act, kernel_two, kernel_one)


def merge_kernel(own, from_below, from_above, out, flat):
    chans, length, _ = out.shape

    def add(step, carry):
        at = pl.ds(pl.multiple_of(step * 64, 64), 64)
        flat[at, :] = own[at, :] + from_below[at, :].astype(F32) + from_above[at, :].astype(F32)
        return carry

    lax.fori_loop(0, own.shape[0] // 64, add, 0, unroll=4)

    def gather(c, carry):
        out[c] = flat[pl.ds(c, length, stride=chans), :].astype(out.dtype)
        return carry

    lax.fori_loop(0, chans, gather, 0, unroll=4)


def merge(own, from_below, from_above, shape):
    return vmem_call(
        merge_kernel,
        jax.ShapeDtypeStruct(shape, BF16),
        (pltpu.VMEM(own.shape, F32),),
        pl.CostEstimate(flops=2 * own.size, bytes_accessed=8 * own.size, transcendentals=0),
    )(own, from_below, from_above)


def share_kernel(scale, bucket, terms, out):
    total = jnp.sum(bucket[...].astype(F32), axis=0).astype(BF16)
    grads = (jnp.sum(terms[...].astype(F32), axis=0) * scale).astype(BF16)
    height = total.shape[0]

    def write(n, carry):
        out[n, 0:height, :] = total
        out[n, height : height + grads.shape[0], :] = grads
        return carry

    lax.fori_loop(0, out.shape[0], write, 0)


def share(bucket, terms, scale, copies):
    rows = bucket.shape[1] + terms.shape[1]
    return vmem_call(
        lambda *refs: share_kernel(scale, *refs),
        jax.ShapeDtypeStruct((copies, rows, LANES), BF16),
        (),
        pl.CostEstimate(flops=bucket.size, bytes_accessed=3 * bucket.size, transcendentals=0),
    )(bucket, terms)


def place(source, height, which, bucket, buffer, sems):
    copies, count = (source.shape[0], sems.shape[0])
    size = copies * height
    step = copies // count
    sent = []
    for n in range(count):
        for q in range(n * step, (n + 1) * step):
            buffer[q * height : (q + 1) * height, :] = source[q, 0:height, :].astype(F32)
        rows = pl.ds(n * step * height, step * height)
        at = pl.ds(pl.multiple_of(which * size + n * step * height, 8), step * height)
        sent.append(pltpu.make_async_copy(buffer.at[rows], bucket.at[at], sems.at[n]))
        sent[-1].start()
    return sent


def start_kernel(height, mine, bucket, buffer, sems):
    for copy in place(mine, height, lax.axis_index("core"), bucket, buffer, sems):
        copy.wait()


def finish_kernel(sizes, height, mine, other, partial, bucket, out_one, out_two, raw, buffer, sems):
    c0, c1, c2 = sizes
    copies, rows, _ = mine.shape
    extra = rows - height
    me = lax.axis_index("core")
    sent = place(other, height, 1 - me, bucket, buffer, sems)

    def unpack(q, carry):
        for source, which in ((mine, me), (other, 1 - me)):
            at = pl.multiple_of((which * copies + q) * extra, 8)
            raw[pl.ds(at, extra), :] = source[q, height:rows, :].astype(F32)
        return carry

    lax.fori_loop(0, copies, unpack, 0)
    block = 3 * c1
    first = -(-9 * c2 // LANES) * block
    for i in range(3):
        for j in range(3):
            column = ((2 - j) * 3 + 2 - i) * c2
            whole, lane = (column // LANES, column % LANES)
            out_two[(3 * i + j) * block : (3 * i + j + 1) * block, :] = raw[
                whole * block : (whole + 1) * block, lane : lane + c2
            ]
            row = first + (3 * j + i) * c0
            for k in range(3):
                to = (9 * i + 3 * j + k) * c0
                out_one[to : to + c0, :] = raw[row : row + c0, k * c1 : (k + 1) * c1]
    for copy in sent:
        copy.wait()


def finish(mine, other, length, sizes):
    c0, c1, c2 = sizes
    copies, rows, _ = mine.shape
    height = length // LANES // (2 * copies)
    spec = pl.BlockSpec(memory_space=pltpu.VMEM)
    remote = pl.BlockSpec(memory_space=pltpu.HBM)
    whole = jax.ShapeDtypeStruct((length // LANES, LANES), F32)
    chunks = 4
    scratch = [
        pltpu.VMEM((copies * height, LANES), F32),
        pltpu.SemaphoreType.DMA((chunks,)),
    ]
    params = pltpu.CompilerParams(vmem_limit_bytes=24 * 2**20)
    partial = pl.pallas_call(
        lambda *refs: start_kernel(height, *refs),
        out_shape=whole,
        in_specs=[spec],
        out_specs=remote,
        scratch_shapes=scratch,
        compiler_params=params,
    )(mine)
    return pl.pallas_call(
        lambda *refs: finish_kernel(sizes, height, *refs),
        out_shape=(
            whole,
            jax.ShapeDtypeStruct((27 * c0, c1), F32),
            jax.ShapeDtypeStruct((27 * c1, c2), F32),
        ),
        in_specs=[spec, spec, remote],
        out_specs=(remote, spec, spec),
        scratch_shapes=[pltpu.VMEM((2 * copies * (rows - height), LANES), F32)] + scratch,
        input_output_aliases={2: 0},
        compiler_params=params,
    )(mine, other, partial)


def halos(value):
    count = lax.axis_size(SPACE)
    up = [(i, i + 1) for i in range(count - 1)]
    down = [(j, i) for i, j in up]
    return (lax.ppermute(value, SPACE, up), lax.ppermute(value, SPACE, down))


def per_device(volume_in, hidden_act, out_cot, kernel_one, kernel_two, grad_bucket):
    c0, c1, c2 = (volume_in.shape[2], hidden_act.shape[2], out_cot.shape[2])
    devices, copies = (lax.axis_size(EVERY), lax.axis_size(SAME))
    length = grad_bucket.shape[1]
    bucket = grad_bucket.reshape(length // LANES, LANES)
    send = cast(bucket)
    cot, vol, send = lax.optimization_barrier((out_cot[0, 0], volume_in[0, 0], send))
    packed = pack(cot, vol)
    other, packed = lax.optimization_barrier((swapped(send), packed))
    below, above = halos(packed)
    half = add(bucket, other)
    act, half = lax.optimization_barrier((hidden_act[0, 0], half))
    parts = lax.all_to_all(half.reshape(copies, -1, LANES), SAME, 0, 0)

    used = -(-9 * c2 // LANES) * 3 * c1 + 9 * c0
    rows = ceil_to(used, 16 * devices)
    send, keep, own, up, down = compute((below, packed, above), act, kernel_two, kernel_one, rows)
    terms = pair_sum(keep, swapped(send))
    terms, parts = lax.optimization_barrier((terms, parts))
    terms = lax.all_to_all(terms.reshape(copies, -1, LANES), SAME, 0, 0)
    cells = volume_in.shape[3] * volume_in.shape[4] * devices
    shares = share(parts, terms, 1.0 / math.sqrt(cells), copies)

    up, down, shares = lax.optimization_barrier((up, down, shares))
    mine = lax.all_to_all(shares, SAME, 0, 0)
    count = lax.axis_size(SPACE)
    upward = [(i, i + 1) for i in range(count - 1)]
    from_below = lax.ppermute(up, SPACE, upward)
    from_above = lax.ppermute(down, SPACE, [(j, i) for i, j in upward])
    grad_input = merge(own, from_below, from_above, volume_in.shape[2:])
    mine, grad_input = lax.optimization_barrier((mine, grad_input))
    bucket_sum, total_one, total_two = finish(mine, swapped(mine), length, (c0, c1, c2))
    return (
        grad_input[None, None],
        total_one.reshape(3, 3, 3, c0, c1),
        total_two.reshape(3, 3, 3, c1, c2),
        bucket_sum.reshape(length),
    )


def solution(mesh):
    dp, space = (mesh.shape["dp"], mesh.shape["space"])
    split = Mesh(mesh.devices.reshape(dp, space // 2, 2), EVERY)
    volume = P("dp", SPACE, None, None, None)
    in_specs = (volume, volume, volume, P(), P(), P(EVERY, None))
    out_specs = (volume, P(), P(), P())
    return jax.shard_map(
        per_device, mesh=split, in_specs=in_specs, out_specs=out_specs, check_vma=False
    )
```

```python
import math

import jax
import jax.numpy as jnp
from jax import lax
from jax.experimental import pallas as pl
from jax.experimental.pallas import tpu as pltpu
from jax.sharding import Mesh, PartitionSpec as P

SPACE = ("slab", "core")
SAME = ("dp", "slab")
EVERY = ("dp", "slab", "core")
GROUP = 8
LANES = 128
BF16 = jnp.bfloat16
F32 = jnp.float32


def ceil_to(value, step):
    return -(-value // step) * step


def slid(value, step):
    lane = lax.broadcasted_iota(jnp.int32, value.shape, 1)
    width = value.shape[1]
    keep = lane >= step if step > 0 else lane < width + step
    return jnp.where(keep, pltpu.roll(value, step % width, 1), 0.0)


def beside(window, rows, step, count):
    return jnp.concatenate([window[g * step : g * step + rows] for g in range(count)], axis=1)


def turned(src, flat, dst, offset, pitch, lead):
    chans, length, _ = src.shape

    def stage(c, carry):
        flat[pl.ds(pl.multiple_of(c * length, length), length), :] = src[c].astype(F32)
        return carry

    lax.fori_loop(0, chans, stage, 0, unroll=4)

    def gather(x, carry):
        rows = flat[pl.ds(x, chans, stride=length), :]
        at = pl.multiple_of((x + lead) * pitch + offset, 16)
        dst[pl.ds(at, chans), :] = rows.astype(BF16)
        return carry

    lax.fori_loop(0, length, gather, 0, unroll=4)


def pack_kernel(cot, vol, out, fetched, flat, sems):
    step = vol.shape[0]
    length, width = vol.shape[1:]
    pitch = cot.shape[0] + step
    pieces = [cot.at[pl.ds(n, step)] for n in range(0, cot.shape[0], step)] + [vol]
    copies = [
        pltpu.make_async_copy(piece, fetched.at[n], sems.at[n]) for n, piece in enumerate(pieces)
    ]
    for copy in copies:
        copy.start()
    zeros = jnp.zeros((pitch, width), BF16)
    out[0:pitch, :] = zeros
    out[(length + 1) * pitch : (length + 2) * pitch, :] = zeros
    for n, copy in enumerate(copies):
        copy.wait()
        turned(fetched.at[n], flat, out, n * step, pitch, 1)


def pack(cot, vol):
    c2, length, width = cot.shape
    pitch = c2 + vol.shape[0]
    pieces = pitch // vol.shape[0]
    source = pl.BlockSpec(memory_space=pltpu.HBM)
    return pl.pallas_call(
        pack_kernel,
        out_shape=jax.ShapeDtypeStruct(((length + 2) * pitch, width), BF16),
        in_specs=[source, source],
        out_specs=pl.BlockSpec(memory_space=pltpu.VMEM),
        scratch_shapes=[
            pltpu.VMEM((pieces,) + vol.shape, BF16),
            pltpu.VMEM((vol.shape[0] * length, width), F32),
            pltpu.SemaphoreType.DMA((pieces,)),
        ],
        cost_estimate=pl.CostEstimate(flops=0, bytes_accessed=4 * cot.size, transcendentals=0),
    )(cot, vol)


def fetched_chunks(src, start, buffer, sems):
    count = sems.shape[0]
    step = buffer.shape[0] // count
    copies = []
    for n in range(count):
        at = pl.ds(pl.multiple_of(start + n * step, 8), step)
        copies.append(
            pltpu.make_async_copy(src.at[at], buffer.at[pl.ds(n * step, step)], sems.at[n])
        )
        copies[-1].start()
    return [(pl.ds(n * step, step), copy) for n, copy in enumerate(copies)]


def cast_kernel(src, out, buffer, sems):
    start = (1 - lax.axis_index("core")) * out.shape[0]
    for rows, copy in fetched_chunks(src, start, buffer, sems):
        copy.wait()
        out[rows, :] = buffer[rows, :].astype(out.dtype)


def cast(value, chunks=8):
    half = (value.shape[0] // 2, LANES)
    return pl.pallas_call(
        cast_kernel,
        out_shape=jax.ShapeDtypeStruct(half, BF16),
        in_specs=[pl.BlockSpec(memory_space=pltpu.HBM)],
        out_specs=pl.BlockSpec(memory_space=pltpu.VMEM),
        scratch_shapes=[pltpu.VMEM(half, F32), pltpu.SemaphoreType.DMA((chunks,))],
        cost_estimate=pl.CostEstimate(flops=0, bytes_accessed=6 * value.size, transcendentals=0),
    )(value)


def fetch_kernel(src, out, sems):
    for _, copy in fetched_chunks(src, lax.axis_index("core") * out.shape[0], out, sems):
        copy.wait()


def fetch(value, chunks=4):
    half = (value.shape[0] // 2, LANES)
    return pl.pallas_call(
        fetch_kernel,
        out_shape=jax.ShapeDtypeStruct(half, F32),
        in_specs=[pl.BlockSpec(memory_space=pltpu.HBM)],
        out_specs=pl.BlockSpec(memory_space=pltpu.VMEM),
        scratch_shapes=[pltpu.SemaphoreType.DMA((chunks,))],
        compiler_params=pltpu.CompilerParams(vmem_limit_bytes=61 * 2**20),
        cost_estimate=pl.CostEstimate(flops=0, bytes_accessed=4 * value.size, transcendentals=0),
    )(value)


def add_kernel(own, other, out):
    out[...] = (own[...] + other[...].astype(F32)).astype(out.dtype)


def add(own, other):
    return vmem_call(
        add_kernel,
        jax.ShapeDtypeStruct(other.shape, BF16),
        (),
        pl.CostEstimate(flops=0, bytes_accessed=8 * own.size, transcendentals=0),
    )(own, other)


def split_to(total, mine, send, keep):
    half = total.shape[0] // 2
    keep[...] = total[pl.ds(pl.multiple_of(mine * half, 16), half), :]
    send[...] = total[pl.ds(pl.multiple_of((1 - mine) * half, 16), half), :].astype(send.dtype)


def swapped(value):
    return lax.ppermute(value, "core", [(0, 1), (1, 0)])


def compute_kernel(
    pack_m, pack_0, pack_p, act, two, one,
    send, keep, own, up, down,
    terms, flat, acts, pres, w_two, w_one, acc_two, acc_one,
):
    c1, length, _ = act.shape
    c2, c0 = (two.shape[4], one.shape[3])
    pitch = c0 + c2
    packs = (pack_m, pack_0, pack_p)

    turned(act, flat, acts, 0, c1, 0)
    offsets = [(m, n) for m in range(3) for n in range(3)]
    w_two[...] = jnp.concatenate(
        [
            jnp.concatenate([two[2 - i, 2 - j, 2 - k].astype(F32) for k in range(3)], axis=0)
            for j, i in offsets
        ],
        axis=1,
    ).astype(BF16)
    w_one[...] = jnp.concatenate(
        [
            jnp.concatenate([one[2 - i, 2 - j, k].astype(F32) for i in range(3)], axis=0)
            for j, k in offsets
        ],
        axis=1,
    ).astype(BF16)
    stacked = 3 * c1
    pres[0:stacked, :] = jnp.zeros((stacked, LANES), BF16)
    pres[(length + 1) * stacked : (length + 2) * stacked, :] = jnp.zeros((stacked, LANES), BF16)
    acc_two[...] = jnp.zeros_like(acc_two)
    acc_one[...] = jnp.zeros_like(acc_one)

    def windows(x, offset, count):
        rows = [
            [p[pl.ds(pl.multiple_of((x + n) * pitch + offset, 16), count), :] for p in packs]
            for n in range(GROUP + 2)
        ]
        return jnp.concatenate(
            [jnp.concatenate(sum(rows[g : g + 3], []), axis=0) for g in range(GROUP)], axis=1
        )

    def first(step, carry):
        x = step * GROUP
        right = windows(x, 0, c2)
        sums = jnp.dot(w_two[...], right, preferred_element_type=F32)
        columns = []
        for g in range(GROUP):
            part = sums[:, g * LANES : (g + 1) * LANES]
            grad = slid(part[0:c1], 1) + part[c1 : 2 * c1] + slid(part[2 * c1 : 3 * c1], -1)
            value = acts[pl.ds(pl.multiple_of((x + g) * c1, 16), c1), :].astype(F32)
            pre = (grad * jnp.where(value > 0, 1.0, 0.2)).astype(BF16).astype(F32)
            moved = jnp.concatenate([slid(pre, -1), pre, slid(pre, 1)], axis=0).astype(BF16)
            pres[pl.ds(pl.multiple_of((x + g + 1) * stacked, 16), stacked), :] = moved
            stack = jnp.concatenate([slid(value, 1), value, slid(value, -1)], axis=0)
            columns.append(stack.astype(BF16))
        left = jnp.concatenate(columns, axis=1)
        acc_two[...] += lax.dot_general(
            right, left, (((1,), (1,)), ((), ())), preferred_element_type=F32
        )
        return carry

    lax.fori_loop(0, length // GROUP, first, 0, unroll=2)

    def second(step, carry):
        x = step * GROUP
        window = pres[pl.ds(pl.multiple_of(x * stacked, 16), (GROUP + 2) * stacked), :]
        moved = beside(window, 3 * stacked, stacked, GROUP)
        sums = jnp.dot(w_one[...], moved, preferred_element_type=F32)
        for g in range(GROUP):
            part = sums[:, g * LANES : (g + 1) * LANES]
            at = pl.ds(pl.multiple_of((x + g) * c0, 16), c0)
            for i, out in ((0, up), (1, own), (2, down)):
                out[at, :] = part[i * c0 : (i + 1) * c0].astype(out.dtype)
        acc_one[...] += lax.dot_general(
            windows(x, c2, c0),
            moved[stacked : 2 * stacked],
            (((1,), (1,)), ((), ())),
            preferred_element_type=F32,
        )
        return carry

    lax.fori_loop(0, length // GROUP, second, 0, unroll=2)

    terms[...] = jnp.zeros_like(terms)
    two = acc_two[...].T
    rows, width = two.shape
    blocks = -(-width // LANES)
    for block in range(blocks):
        part = two[:, block * LANES : min(width, (block + 1) * LANES)]
        terms[block * rows : (block + 1) * rows, 0 : part.shape[1]] = part
    one = acc_one[...]
    terms[blocks * rows : blocks * rows + one.shape[0], 0 : one.shape[1]] = one
    split_to(terms, lax.axis_index("core"), send, keep)


def vmem_call(body, out_shape, scratch=(), cost=None, limit=24 * 2**20):
    spec = pl.BlockSpec(memory_space=pltpu.VMEM)
    return pl.pallas_call(
        body,
        out_shape=out_shape,
        out_specs=jax.tree.map(lambda _: spec, out_shape),
        scratch_shapes=list(scratch),
        compiler_params=pltpu.CompilerParams(vmem_limit_bytes=limit),
        cost_estimate=cost,
    )


def compute(packs, act, kernel_two, kernel_one, rows):
    c1, length, width = act.shape
    c0, c2 = (kernel_one.shape[3], kernel_two.shape[4])
    plane = (length * c0, width)
    return vmem_call(
        compute_kernel,
        (
            jax.ShapeDtypeStruct((rows // 2, LANES), BF16),
            jax.ShapeDtypeStruct((rows // 2, LANES), F32),
            jax.ShapeDtypeStruct(plane, F32),
            jax.ShapeDtypeStruct(plane, BF16),
            jax.ShapeDtypeStruct(plane, BF16),
        ),
        (
            pltpu.VMEM((rows, LANES), F32),
            pltpu.VMEM((c1 * length, width), F32),
            pltpu.VMEM((c1 * length, width), BF16),
            pltpu.VMEM(((length + 2) * 3 * c1, width), BF16),
            pltpu.VMEM((3 * c1, 9 * c2), BF16),
            pltpu.VMEM((3 * c0, 9 * c1), BF16),
            pltpu.VMEM((9 * c2, 3 * c1), F32),
            pltpu.VMEM((9 * c0, 3 * c1), F32),
        ),
        pl.CostEstimate(flops=10**10, bytes_accessed=40 * 2**20, transcendentals=0),
    )(*packs, act, kernel_two, kernel_one)


def merge_kernel(own, from_below, from_above, out, flat):
    chans, length, _ = out.shape

    def add(step, carry):
        at = pl.ds(pl.multiple_of(step * 64, 64), 64)
        flat[at, :] = own[at, :] + from_below[at, :].astype(F32) + from_above[at, :].astype(F32)
        return carry

    lax.fori_loop(0, own.shape[0] // 64, add, 0, unroll=4)

    def gather(c, carry):
        out[c] = flat[pl.ds(c, length, stride=chans), :].astype(out.dtype)
        return carry

    lax.fori_loop(0, chans, gather, 0, unroll=4)


def merge(own, from_below, from_above, shape):
    return vmem_call(
        merge_kernel,
        jax.ShapeDtypeStruct(shape, BF16),
        (pltpu.VMEM(own.shape, F32),),
        pl.CostEstimate(flops=2 * own.size, bytes_accessed=8 * own.size, transcendentals=0),
    )(own, from_below, from_above)


def share_kernel(scale, bucket, terms, out):
    total = jnp.sum(bucket[...].astype(F32), axis=0).astype(BF16)
    grads = (jnp.sum(terms[...].astype(F32), axis=0) * scale).astype(BF16)
    height = total.shape[0]

    def write(n, carry):
        out[n, 0:height, :] = total
        out[n, height : height + grads.shape[0], :] = grads
        return carry

    lax.fori_loop(0, out.shape[0], write, 0)


def share(bucket, terms, scale, copies):
    rows = bucket.shape[1] + terms.shape[1]
    return vmem_call(
        lambda *refs: share_kernel(scale, *refs),
        jax.ShapeDtypeStruct((copies, rows, LANES), BF16),
        (),
        pl.CostEstimate(flops=bucket.size, bytes_accessed=3 * bucket.size, transcendentals=0),
    )(bucket, terms)


def place(source, height, which, bucket, buffer, sems):
    copies, count = (source.shape[0], sems.shape[0])
    size = copies * height
    step = copies // count
    sent = []
    for n in range(count):
        for q in range(n * step, (n + 1) * step):
            buffer[q * height : (q + 1) * height, :] = source[q, 0:height, :].astype(F32)
        rows = pl.ds(n * step * height, step * height)
        at = pl.ds(pl.multiple_of(which * size + n * step * height, 8), step * height)
        sent.append(pltpu.make_async_copy(buffer.at[rows], bucket.at[at], sems.at[n]))
        sent[-1].start()
    return sent


def start_kernel(height, mine, bucket, buffer, sems):
    for copy in place(mine, height, lax.axis_index("core"), bucket, buffer, sems):
        copy.wait()


def finish_kernel(
    sizes, height, mine, other, partial,
    bucket, out_one, out_two,
    raw, one, two, out_sems, buffer, sems,
):
    c0, c1, c2 = sizes
    copies, rows, _ = mine.shape
    extra = rows - height
    me = lax.axis_index("core")
    sent = place(other, height, 1 - me, bucket, buffer, sems)

    def unpack(q, carry):
        for source, which in ((mine, me), (other, 1 - me)):
            at = pl.multiple_of((which * copies + q) * extra, 8)
            raw[pl.ds(at, extra), :] = source[q, height:rows, :].astype(F32)
        return carry

    lax.fori_loop(0, copies, unpack, 0, unroll=4)
    block = 3 * c1
    first = -(-9 * c2 // LANES) * block
    for i in range(3):
        for j in range(3):
            column = ((2 - j) * 3 + 2 - i) * c2
            whole, lane = (column // LANES, column % LANES)
            two[(3 * i + j) * block : (3 * i + j + 1) * block, :] = raw[
                whole * block : (whole + 1) * block, lane : lane + c2
            ]
        at = pl.ds(3 * i * block, 3 * block)
        sent.append(pltpu.make_async_copy(two.at[at], out_two.at[at], out_sems.at[i]))
        sent[-1].start()
    for i in range(3):
        for j in range(3):
            row = first + (3 * j + i) * c0
            for k in range(3):
                to = (9 * i + 3 * j + k) * c0
                one[to : to + c0, :] = raw[row : row + c0, k * c1 : (k + 1) * c1]
        at = pl.ds(9 * i * c0, 9 * c0)
        sent.append(pltpu.make_async_copy(one.at[at], out_one.at[at], out_sems.at[3 + i]))
        sent[-1].start()
    for copy in sent:
        copy.wait()


def finish(mine, other, length, sizes):
    c0, c1, c2 = sizes
    copies, rows, _ = mine.shape
    height = length // LANES // (2 * copies)
    spec = pl.BlockSpec(memory_space=pltpu.VMEM)
    remote = pl.BlockSpec(memory_space=pltpu.HBM)
    whole = jax.ShapeDtypeStruct((length // LANES, LANES), F32)
    chunks = 4
    scratch = [
        pltpu.VMEM((copies * height, LANES), F32),
        pltpu.SemaphoreType.DMA((chunks,)),
    ]
    params = pltpu.CompilerParams(vmem_limit_bytes=24 * 2**20)
    partial = pl.pallas_call(
        lambda *refs: start_kernel(height, *refs),
        out_shape=whole,
        in_specs=[spec],
        out_specs=remote,
        scratch_shapes=scratch,
        compiler_params=params,
    )(mine)
    return pl.pallas_call(
        lambda *refs: finish_kernel(sizes, height, *refs),
        out_shape=(
            whole,
            jax.ShapeDtypeStruct((27 * c0, c1), F32),
            jax.ShapeDtypeStruct((27 * c1, c2), F32),
        ),
        in_specs=[spec, spec, remote],
        out_specs=(remote, remote, remote),
        scratch_shapes=[
            pltpu.VMEM((2 * copies * (rows - height), LANES), F32),
            pltpu.VMEM((27 * c0, c1), F32),
            pltpu.VMEM((27 * c1, c2), F32),
            pltpu.SemaphoreType.DMA((6,)),
        ]
        + scratch,
        input_output_aliases={2: 0},
        compiler_params=params,
    )(mine, other, partial)


def halos(value):
    count = lax.axis_size(SPACE)
    up = [(i, i + 1) for i in range(count - 1)]
    down = [(j, i) for i, j in up]
    return (lax.ppermute(value, SPACE, up), lax.ppermute(value, SPACE, down))


def per_device(volume_in, hidden_act, out_cot, kernel_one, kernel_two, grad_bucket):
    c0, c1, c2 = (volume_in.shape[2], hidden_act.shape[2], out_cot.shape[2])
    devices, copies = (lax.axis_size(EVERY), lax.axis_size(SAME))
    length = grad_bucket.shape[1]
    bucket = grad_bucket.reshape(length // LANES, LANES)
    packed = pack(out_cot[0, 0], volume_in[0, 0])
    packed, bucket = lax.optimization_barrier((packed, bucket))
    below, above = halos(packed)
    send, bucket = lax.optimization_barrier((cast(bucket), bucket))
    half = add(fetch(bucket), swapped(send))
    act, half = lax.optimization_barrier((hidden_act[0, 0], half))
    parts = lax.all_to_all(half.reshape(copies, -1, LANES), SAME, 0, 0)

    used = -(-9 * c2 // LANES) * 3 * c1 + 9 * c0
    rows = ceil_to(used, 16 * devices)
    send, keep, own, up, down = compute((below, packed, above), act, kernel_two, kernel_one, rows)
    terms = add(keep, swapped(send))
    terms, parts = lax.optimization_barrier((terms, parts))
    terms = lax.all_to_all(terms.reshape(copies, -1, LANES), SAME, 0, 0)
    cells = volume_in.shape[3] * volume_in.shape[4] * devices
    shares = share(parts, terms, 1.0 / math.sqrt(cells), copies)

    up, down, shares = lax.optimization_barrier((up, down, shares))
    mine = lax.all_to_all(shares, SAME, 0, 0)
    count = lax.axis_size(SPACE)
    upward = [(i, i + 1) for i in range(count - 1)]
    from_below = lax.ppermute(up, SPACE, upward)
    from_above = lax.ppermute(down, SPACE, [(j, i) for i, j in upward])
    grad_input = merge(own, from_below, from_above, volume_in.shape[2:])
    mine, grad_input = lax.optimization_barrier((mine, grad_input))
    bucket_sum, total_one, total_two = finish(mine, swapped(mine), length, (c0, c1, c2))
    return (
        grad_input[None, None],
        total_one.reshape(3, 3, 3, c0, c1),
        total_two.reshape(3, 3, 3, c1, c2),
        bucket_sum.reshape(length),
    )


def solution(mesh):
    dp, space = (mesh.shape["dp"], mesh.shape["space"])
    split = Mesh(mesh.devices.reshape(dp, space // 2, 2), EVERY)
    volume = P("dp", SPACE, None, None, None)
    in_specs = (volume, volume, volume, P(), P(), P(EVERY, None))
    out_specs = (volume, P(), P(), P())
    return jax.shard_map(
        per_device, mesh=split, in_specs=in_specs, out_specs=out_specs, check_vma=False
    )
```

```python
import math

import jax
import jax.numpy as jnp
from jax import lax
from jax.experimental import pallas as pl
from jax.experimental.pallas import tpu as pltpu
from jax.sharding import Mesh, PartitionSpec as P

SPACE = ("slab", "core")
SAME = ("dp", "slab")
EVERY = ("dp", "slab", "core")
GROUP = 8
LANES = 128
BF16 = jnp.bfloat16
F32 = jnp.float32


def ceil_to(value, step):
    return -(-value // step) * step


def slid(value, step):
    lane = lax.broadcasted_iota(jnp.int32, value.shape, 1)
    width = value.shape[1]
    keep = lane >= step if step > 0 else lane < width + step
    return jnp.where(keep, pltpu.roll(value, step % width, 1), 0.0)


def beside(window, rows, step, count):
    return jnp.concatenate([window[g * step : g * step + rows] for g in range(count)], axis=1)


def turned(src, flat, dst, offset, pitch, lead):
    chans, length, _ = src.shape

    def stage(c, carry):
        flat[pl.ds(pl.multiple_of(c * length, length), length), :] = src[c].astype(F32)
        return carry

    lax.fori_loop(0, chans, stage, 0, unroll=4)

    def gather(x, carry):
        rows = flat[pl.ds(x, chans, stride=length), :]
        at = pl.multiple_of((x + lead) * pitch + offset, 16)
        dst[pl.ds(at, chans), :] = rows.astype(BF16)
        return carry

    lax.fori_loop(0, length, gather, 0, unroll=4)


def pack_kernel(cot, vol, out, flat):
    c2, length, width = cot.shape
    pitch = c2 + vol.shape[0]
    zeros = jnp.zeros((pitch, width), BF16)
    out[0:pitch, :] = zeros
    out[(length + 1) * pitch : (length + 2) * pitch, :] = zeros
    turned(cot, flat, out, 0, pitch, 1)
    turned(vol, flat, out, c2, pitch, 1)


def pack(cot, vol):
    c2, length, width = cot.shape
    pitch = c2 + vol.shape[0]
    return vmem_call(
        pack_kernel,
        jax.ShapeDtypeStruct(((length + 2) * pitch, width), BF16),
        (pltpu.VMEM((max(c2, vol.shape[0]) * length, width), F32),),
        pl.CostEstimate(flops=0, bytes_accessed=32 * cot.size, transcendentals=0),
    )(cot, vol)


def in_steps(body, rows, count=8):
    step = rows // count

    def one(n, carry):
        body(n * step, step)
        return carry

    lax.fori_loop(0, count, one, 0)


def cast_kernel(src, out):
    rows = out.shape[0]
    start = (1 - lax.axis_index("core")) * rows

    def cast(at, step):
        value = src[pl.ds(pl.multiple_of(start + at, 16), step), :]
        out[pl.ds(pl.multiple_of(at, 16), step), :] = value.astype(out.dtype)

    in_steps(cast, rows)


def cast(value):
    return vmem_call(
        cast_kernel,
        jax.ShapeDtypeStruct((value.shape[0] // 2, LANES), BF16),
        (),
        pl.CostEstimate(flops=0, bytes_accessed=4 * value.size, transcendentals=0),
    )(value)


def add_kernel(src, other, out):
    rows = out.shape[0]
    start = lax.axis_index("core") * rows if src.shape[0] > rows else 0

    def add(at, step):
        value = src[pl.ds(pl.multiple_of(start + at, 16), step), :]
        at = pl.ds(pl.multiple_of(at, 16), step)
        out[at, :] = (value + other[at, :].astype(F32)).astype(out.dtype)

    in_steps(add, rows)


def add(value, other):
    return vmem_call(
        add_kernel,
        jax.ShapeDtypeStruct(other.shape, BF16),
        (),
        pl.CostEstimate(flops=0, bytes_accessed=4 * value.size, transcendentals=0),
    )(value, other)


def split_to(total, mine, send, keep):
    half = total.shape[0] // 2
    keep[...] = total[pl.ds(pl.multiple_of(mine * half, 16), half), :]
    send[...] = total[pl.ds(pl.multiple_of((1 - mine) * half, 16), half), :].astype(send.dtype)


def swapped(value):
    return lax.ppermute(value, "core", [(0, 1), (1, 0)])


def compute_kernel(
    pack_m, pack_0, pack_p, act, two, one,
    send, keep, own, up, down,
    terms, flat, acts, pres, w_two, w_one, acc_two, acc_one,
):
    c1, length, _ = act.shape
    c2, c0 = (two.shape[4], one.shape[3])
    pitch = c0 + c2
    packs = (pack_m, pack_0, pack_p)

    turned(act, flat, acts, 0, c1, 0)
    offsets = [(m, n) for m in range(3) for n in range(3)]
    w_two[...] = jnp.concatenate(
        [
            jnp.concatenate([two[2 - i, 2 - j, 2 - k].astype(F32) for k in range(3)], axis=0)
            for j, i in offsets
        ],
        axis=1,
    ).astype(BF16)
    w_one[...] = jnp.concatenate(
        [
            jnp.concatenate([one[2 - i, 2 - j, k].astype(F32) for i in range(3)], axis=0)
            for j, k in offsets
        ],
        axis=1,
    ).astype(BF16)
    stacked = 3 * c1
    pres[0:stacked, :] = jnp.zeros((stacked, LANES), BF16)
    pres[(length + 1) * stacked : (length + 2) * stacked, :] = jnp.zeros((stacked, LANES), BF16)
    acc_two[...] = jnp.zeros_like(acc_two)
    acc_one[...] = jnp.zeros_like(acc_one)

    def windows(x, offset, count):
        rows = [
            [p[pl.ds(pl.multiple_of((x + n) * pitch + offset, 16), count), :] for p in packs]
            for n in range(GROUP + 2)
        ]
        return jnp.concatenate(
            [jnp.concatenate(sum(rows[g : g + 3], []), axis=0) for g in range(GROUP)], axis=1
        )

    def first(step, carry):
        x = step * GROUP
        right = windows(x, 0, c2)
        sums = jnp.dot(w_two[...], right, preferred_element_type=F32)
        columns = []
        for g in range(GROUP):
            part = sums[:, g * LANES : (g + 1) * LANES]
            grad = slid(part[0:c1], 1) + part[c1 : 2 * c1] + slid(part[2 * c1 : 3 * c1], -1)
            value = acts[pl.ds(pl.multiple_of((x + g) * c1, 16), c1), :].astype(F32)
            pre = (grad * jnp.where(value > 0, 1.0, 0.2)).astype(BF16).astype(F32)
            moved = jnp.concatenate([slid(pre, -1), pre, slid(pre, 1)], axis=0).astype(BF16)
            pres[pl.ds(pl.multiple_of((x + g + 1) * stacked, 16), stacked), :] = moved
            stack = jnp.concatenate([slid(value, 1), value, slid(value, -1)], axis=0)
            columns.append(stack.astype(BF16))
        left = jnp.concatenate(columns, axis=1)
        acc_two[...] += lax.dot_general(
            right, left, (((1,), (1,)), ((), ())), preferred_element_type=F32
        )
        return carry

    lax.fori_loop(0, length // GROUP, first, 0, unroll=2)

    def second(step, carry):
        x = step * GROUP
        window = pres[pl.ds(pl.multiple_of(x * stacked, 16), (GROUP + 2) * stacked), :]
        moved = beside(window, 3 * stacked, stacked, GROUP)
        sums = jnp.dot(w_one[...], moved, preferred_element_type=F32)
        for g in range(GROUP):
            part = sums[:, g * LANES : (g + 1) * LANES]
            at = pl.ds(pl.multiple_of((x + g) * c0, 16), c0)
            for i, out in ((0, up), (1, own), (2, down)):
                out[at, :] = part[i * c0 : (i + 1) * c0].astype(out.dtype)
        acc_one[...] += lax.dot_general(
            windows(x, c2, c0),
            moved[stacked : 2 * stacked],
            (((1,), (1,)), ((), ())),
            preferred_element_type=F32,
        )
        return carry

    lax.fori_loop(0, length // GROUP, second, 0, unroll=2)

    terms[...] = jnp.zeros_like(terms)
    two = acc_two[...].T
    rows, width = two.shape
    blocks = -(-width // LANES)
    for block in range(blocks):
        part = two[:, block * LANES : min(width, (block + 1) * LANES)]
        terms[block * rows : (block + 1) * rows, 0 : part.shape[1]] = part
    one = acc_one[...]
    terms[blocks * rows : blocks * rows + one.shape[0], 0 : one.shape[1]] = one
    split_to(terms, lax.axis_index("core"), send, keep)


def vmem_call(body, out_shape, scratch=(), cost=None, limit=24 * 2**20):
    spec = pl.BlockSpec(memory_space=pltpu.VMEM)
    return pl.pallas_call(
        body,
        out_shape=out_shape,
        out_specs=jax.tree.map(lambda _: spec, out_shape),
        scratch_shapes=list(scratch),
        compiler_params=pltpu.CompilerParams(vmem_limit_bytes=limit),
        cost_estimate=cost,
    )


def compute(packs, act, kernel_two, kernel_one, rows):
    c1, length, width = act.shape
    c0, c2 = (kernel_one.shape[3], kernel_two.shape[4])
    plane = (length * c0, width)
    return vmem_call(
        compute_kernel,
        (
            jax.ShapeDtypeStruct((rows // 2, LANES), BF16),
            jax.ShapeDtypeStruct((rows // 2, LANES), F32),
            jax.ShapeDtypeStruct(plane, F32),
            jax.ShapeDtypeStruct(plane, BF16),
            jax.ShapeDtypeStruct(plane, BF16),
        ),
        (
            pltpu.VMEM((rows, LANES), F32),
            pltpu.VMEM((c1 * length, width), F32),
            pltpu.VMEM((c1 * length, width), BF16),
            pltpu.VMEM(((length + 2) * 3 * c1, width), BF16),
            pltpu.VMEM((3 * c1, 9 * c2), BF16),
            pltpu.VMEM((3 * c0, 9 * c1), BF16),
            pltpu.VMEM((9 * c2, 3 * c1), F32),
            pltpu.VMEM((9 * c0, 3 * c1), F32),
        ),
        pl.CostEstimate(flops=10**10, bytes_accessed=40 * 2**20, transcendentals=0),
    )(*packs, act, kernel_two, kernel_one)


def merge_kernel(own, from_below, from_above, out, flat):
    chans, length, _ = out.shape

    def add(step, carry):
        at = pl.ds(pl.multiple_of(step * 64, 64), 64)
        flat[at, :] = own[at, :] + from_below[at, :].astype(F32) + from_above[at, :].astype(F32)
        return carry

    lax.fori_loop(0, own.shape[0] // 64, add, 0, unroll=4)

    def gather(c, carry):
        out[c] = flat[pl.ds(c, length, stride=chans), :].astype(out.dtype)
        return carry

    lax.fori_loop(0, chans, gather, 0, unroll=4)


def merge(own, from_below, from_above, shape):
    return vmem_call(
        merge_kernel,
        jax.ShapeDtypeStruct(shape, BF16),
        (pltpu.VMEM(own.shape, F32),),
        pl.CostEstimate(flops=2 * own.size, bytes_accessed=8 * own.size, transcendentals=0),
    )(own, from_below, from_above)


def share_kernel(scale, bucket, terms, out):
    total = jnp.sum(bucket[...].astype(F32), axis=0).astype(BF16)
    grads = (jnp.sum(terms[...].astype(F32), axis=0) * scale).astype(BF16)
    height = total.shape[0]

    def write(n, carry):
        out[n, 0:height, :] = total
        out[n, height : height + grads.shape[0], :] = grads
        return carry

    lax.fori_loop(0, out.shape[0], write, 0)


def share(bucket, terms, scale, copies):
    rows = bucket.shape[1] + terms.shape[1]
    return vmem_call(
        lambda *refs: share_kernel(scale, *refs),
        jax.ShapeDtypeStruct((copies, rows, LANES), BF16),
        (),
        pl.CostEstimate(flops=bucket.size, bytes_accessed=3 * bucket.size, transcendentals=0),
    )(bucket, terms)


def place(source, height, which, bucket, buffer, sems):
    copies, count = (source.shape[0], sems.shape[0])
    size = copies * height
    step = copies // count
    sent = []
    for n in range(count):
        for q in range(n * step, (n + 1) * step):
            buffer[q * height : (q + 1) * height, :] = source[q, 0:height, :].astype(F32)
        rows = pl.ds(n * step * height, step * height)
        at = pl.ds(pl.multiple_of(which * size + n * step * height, 8), step * height)
        sent.append(pltpu.make_async_copy(buffer.at[rows], bucket.at[at], sems.at[n]))
        sent[-1].start()
    return sent


def start_kernel(height, mine, bucket, buffer, sems):
    for copy in place(mine, height, lax.axis_index("core"), bucket, buffer, sems):
        copy.wait()


def finish_kernel(
    sizes, height, mine, other, partial,
    bucket, out_one, out_two,
    raw, one, two, out_sems, buffer, sems,
):
    c0, c1, c2 = sizes
    copies, rows, _ = mine.shape
    extra = rows - height
    me = lax.axis_index("core")
    sent = place(other, height, 1 - me, bucket, buffer, sems)

    def unpack(q, carry):
        for source, which in ((mine, me), (other, 1 - me)):
            at = pl.multiple_of((which * copies + q) * extra, 8)
            raw[pl.ds(at, extra), :] = source[q, height:rows, :].astype(F32)
        return carry

    lax.fori_loop(0, copies, unpack, 0, unroll=4)
    block = 3 * c1
    first = -(-9 * c2 // LANES) * block
    for i in range(3):
        for j in range(3):
            column = ((2 - j) * 3 + 2 - i) * c2
            whole, lane = (column // LANES, column % LANES)
            two[(3 * i + j) * block : (3 * i + j + 1) * block, :] = raw[
                whole * block : (whole + 1) * block, lane : lane + c2
            ]
        at = pl.ds(3 * i * block, 3 * block)
        sent.append(pltpu.make_async_copy(two.at[at], out_two.at[at], out_sems.at[i]))
        sent[-1].start()
    for i in range(3):
        for j in range(3):
            row = first + (3 * j + i) * c0
            for k in range(3):
                to = (9 * i + 3 * j + k) * c0
                one[to : to + c0, :] = raw[row : row + c0, k * c1 : (k + 1) * c1]
        at = pl.ds(9 * i * c0, 9 * c0)
        sent.append(pltpu.make_async_copy(one.at[at], out_one.at[at], out_sems.at[3 + i]))
        sent[-1].start()
    for copy in sent:
        copy.wait()


def finish(mine, other, length, sizes):
    c0, c1, c2 = sizes
    copies, rows, _ = mine.shape
    height = length // LANES // (2 * copies)
    spec = pl.BlockSpec(memory_space=pltpu.VMEM)
    remote = pl.BlockSpec(memory_space=pltpu.HBM)
    whole = jax.ShapeDtypeStruct((length // LANES, LANES), F32)
    chunks = 4
    scratch = [
        pltpu.VMEM((copies * height, LANES), F32),
        pltpu.SemaphoreType.DMA((chunks,)),
    ]
    params = pltpu.CompilerParams(vmem_limit_bytes=24 * 2**20)
    partial = pl.pallas_call(
        lambda *refs: start_kernel(height, *refs),
        out_shape=whole,
        in_specs=[spec],
        out_specs=remote,
        scratch_shapes=scratch,
        compiler_params=params,
    )(mine)
    return pl.pallas_call(
        lambda *refs: finish_kernel(sizes, height, *refs),
        out_shape=(
            whole,
            jax.ShapeDtypeStruct((27 * c0, c1), F32),
            jax.ShapeDtypeStruct((27 * c1, c2), F32),
        ),
        in_specs=[spec, spec, remote],
        out_specs=(remote, remote, remote),
        scratch_shapes=[
            pltpu.VMEM((2 * copies * (rows - height), LANES), F32),
            pltpu.VMEM((27 * c0, c1), F32),
            pltpu.VMEM((27 * c1, c2), F32),
            pltpu.SemaphoreType.DMA((6,)),
        ]
        + scratch,
        input_output_aliases={2: 0},
        compiler_params=params,
    )(mine, other, partial)


def halos(value):
    count = lax.axis_size(SPACE)
    up = [(i, i + 1) for i in range(count - 1)]
    down = [(j, i) for i, j in up]
    return (lax.ppermute(value, SPACE, up), lax.ppermute(value, SPACE, down))


def per_device(volume_in, hidden_act, out_cot, kernel_one, kernel_two, grad_bucket):
    c0, c1, c2 = (volume_in.shape[2], hidden_act.shape[2], out_cot.shape[2])
    devices, copies = (lax.axis_size(EVERY), lax.axis_size(SAME))
    length = grad_bucket.shape[1]
    bucket = grad_bucket.reshape(length // LANES, LANES)
    packed = pack(out_cot[0, 0], volume_in[0, 0])
    packed, bucket = lax.optimization_barrier((packed, bucket))
    below, above = halos(packed)
    half = add(bucket, swapped(cast(bucket)))
    act, half = lax.optimization_barrier((hidden_act[0, 0], half))
    parts = lax.all_to_all(half.reshape(copies, -1, LANES), SAME, 0, 0)

    used = -(-9 * c2 // LANES) * 3 * c1 + 9 * c0
    rows = ceil_to(used, 16 * devices)
    send, keep, own, up, down = compute((below, packed, above), act, kernel_two, kernel_one, rows)
    terms = add(keep, swapped(send))
    terms, parts = lax.optimization_barrier((terms, parts))
    terms = lax.all_to_all(terms.reshape(copies, -1, LANES), SAME, 0, 0)
    cells = volume_in.shape[3] * volume_in.shape[4] * devices
    shares = share(parts, terms, 1.0 / math.sqrt(cells), copies)

    up, down, shares = lax.optimization_barrier((up, down, shares))
    mine = lax.all_to_all(shares, SAME, 0, 0)
    count = lax.axis_size(SPACE)
    upward = [(i, i + 1) for i in range(count - 1)]
    from_below = lax.ppermute(up, SPACE, upward)
    from_above = lax.ppermute(down, SPACE, [(j, i) for i, j in upward])
    grad_input = merge(own, from_below, from_above, volume_in.shape[2:])
    mine, grad_input = lax.optimization_barrier((mine, grad_input))
    bucket_sum, total_one, total_two = finish(mine, swapped(mine), length, (c0, c1, c2))
    return (
        grad_input[None, None],
        total_one.reshape(3, 3, 3, c0, c1),
        total_two.reshape(3, 3, 3, c1, c2),
        bucket_sum.reshape(length),
    )


def solution(mesh):
    dp, space = (mesh.shape["dp"], mesh.shape["space"])
    split = Mesh(mesh.devices.reshape(dp, space // 2, 2), EVERY)
    volume = P("dp", SPACE, None, None, None)
    in_specs = (volume, volume, volume, P(), P(), P(EVERY, None))
    out_specs = (volume, P(), P(), P())
    return jax.shard_map(
        per_device, mesh=split, in_specs=in_specs, out_specs=out_specs, check_vma=False
    )
```

```python
import math

import jax
import jax.numpy as jnp
from jax import lax
from jax.experimental import pallas as pl
from jax.experimental.pallas import tpu as pltpu
from jax.sharding import Mesh, PartitionSpec as P

SPACE = ("slab", "core")
SAME = ("dp", "slab")
EVERY = ("dp", "slab", "core")
GROUP = 8
LANES = 128
BF16 = jnp.bfloat16
F32 = jnp.float32


def ceil_to(value, step):
    return -(-value // step) * step


def slid(value, step):
    lane = lax.broadcasted_iota(jnp.int32, value.shape, 1)
    width = value.shape[1]
    keep = lane >= step if step > 0 else lane < width + step
    return jnp.where(keep, pltpu.roll(value, step % width, 1), 0.0)


def beside(window, rows, step, count):
    return jnp.concatenate([window[g * step : g * step + rows] for g in range(count)], axis=1)


def turned(src, flat, dst, offset, pitch, lead):
    chans, length, _ = src.shape

    def stage(c, carry):
        flat[pl.ds(pl.multiple_of(c * length, length), length), :] = src[c].astype(F32)
        return carry

    lax.fori_loop(0, chans, stage, 0, unroll=4)

    def gather(x, carry):
        rows = flat[pl.ds(x, chans, stride=length), :]
        at = pl.multiple_of((x + lead) * pitch + offset, 16)
        dst[pl.ds(at, chans), :] = rows.astype(BF16)
        return carry

    lax.fori_loop(0, length, gather, 0, unroll=4)


def pack_kernel(cot, vol, out, flat):
    c2, length, width = cot.shape
    pitch = c2 + vol.shape[0]
    zeros = jnp.zeros((pitch, width), BF16)
    out[0:pitch, :] = zeros
    out[(length + 1) * pitch : (length + 2) * pitch, :] = zeros
    turned(cot, flat, out, 0, pitch, 1)
    turned(vol, flat, out, c2, pitch, 1)


def pack(cot, vol):
    c2, length, width = cot.shape
    pitch = c2 + vol.shape[0]
    return vmem_call(
        pack_kernel,
        jax.ShapeDtypeStruct(((length + 2) * pitch, width), BF16),
        (pltpu.VMEM((max(c2, vol.shape[0]) * length, width), F32),),
        pl.CostEstimate(flops=0, bytes_accessed=32 * cot.size, transcendentals=0),
    )(cot, vol)


def in_steps(body, rows, count=8):
    step = rows // count

    def one(n, carry):
        body(n * step, step)
        return carry

    lax.fori_loop(0, count, one, 0)


def cast_kernel(src, after, out):
    rows = out.shape[0]
    start = (1 - lax.axis_index("core")) * rows

    def cast(at, step):
        value = src[pl.ds(pl.multiple_of(start + at, 16), step), :]
        out[pl.ds(pl.multiple_of(at, 16), step), :] = value.astype(out.dtype)

    in_steps(cast, rows)


def cast(value, after):
    spec = pl.BlockSpec(memory_space=pltpu.VMEM)
    return pl.pallas_call(
        cast_kernel,
        out_shape=jax.ShapeDtypeStruct((value.shape[0] // 2, LANES), BF16),
        in_specs=[spec, pl.BlockSpec(memory_space=pl.ANY)],
        out_specs=spec,
        compiler_params=pltpu.CompilerParams(vmem_limit_bytes=24 * 2**20),
        cost_estimate=pl.CostEstimate(flops=0, bytes_accessed=4 * value.size, transcendentals=0),
    )(value, after)


def add_kernel(src, other, out):
    rows = out.shape[0]
    start = lax.axis_index("core") * rows if src.shape[0] > rows else 0

    def add(at, step):
        value = src[pl.ds(pl.multiple_of(start + at, 16), step), :]
        at = pl.ds(pl.multiple_of(at, 16), step)
        out[at, :] = (value + other[at, :].astype(F32)).astype(out.dtype)

    in_steps(add, rows)


def add(value, other):
    return vmem_call(
        add_kernel,
        jax.ShapeDtypeStruct(other.shape, BF16),
        (),
        pl.CostEstimate(flops=0, bytes_accessed=4 * value.size, transcendentals=0),
    )(value, other)


def split_to(total, mine, send, keep):
    half = total.shape[0] // 2
    keep[...] = total[pl.ds(pl.multiple_of(mine * half, 16), half), :]
    send[...] = total[pl.ds(pl.multiple_of((1 - mine) * half, 16), half), :].astype(send.dtype)


def swapped(value):
    return lax.ppermute(value, "core", [(0, 1), (1, 0)])


def compute_kernel(
    pack_m, pack_0, pack_p, act, two, one,
    send, keep, own, up, down,
    terms, flat, acts, pres, w_two, w_one, acc_two, acc_one,
):
    c1, length, _ = act.shape
    c2, c0 = (two.shape[4], one.shape[3])
    pitch = c0 + c2
    packs = (pack_m, pack_0, pack_p)

    turned(act, flat, acts, 0, c1, 0)
    offsets = [(m, n) for m in range(3) for n in range(3)]
    w_two[...] = jnp.concatenate(
        [
            jnp.concatenate([two[2 - i, 2 - j, 2 - k].astype(F32) for k in range(3)], axis=0)
            for j, i in offsets
        ],
        axis=1,
    ).astype(BF16)
    w_one[...] = jnp.concatenate(
        [
            jnp.concatenate([one[2 - i, 2 - j, k].astype(F32) for i in range(3)], axis=0)
            for j, k in offsets
        ],
        axis=1,
    ).astype(BF16)
    stacked = 3 * c1
    pres[0:stacked, :] = jnp.zeros((stacked, LANES), BF16)
    pres[(length + 1) * stacked : (length + 2) * stacked, :] = jnp.zeros((stacked, LANES), BF16)
    acc_two[...] = jnp.zeros_like(acc_two)
    acc_one[...] = jnp.zeros_like(acc_one)

    def windows(x, offset, count):
        rows = [
            [p[pl.ds(pl.multiple_of((x + n) * pitch + offset, 16), count), :] for p in packs]
            for n in range(GROUP + 2)
        ]
        return jnp.concatenate(
            [jnp.concatenate(sum(rows[g : g + 3], []), axis=0) for g in range(GROUP)], axis=1
        )

    def first(step, carry):
        x = step * GROUP
        right = windows(x, 0, c2)
        sums = jnp.dot(w_two[...], right, preferred_element_type=F32)
        columns = []
        for g in range(GROUP):
            part = sums[:, g * LANES : (g + 1) * LANES]
            grad = slid(part[0:c1], 1) + part[c1 : 2 * c1] + slid(part[2 * c1 : 3 * c1], -1)
            value = acts[pl.ds(pl.multiple_of((x + g) * c1, 16), c1), :].astype(F32)
            pre = (grad * jnp.where(value > 0, 1.0, 0.2)).astype(BF16).astype(F32)
            moved = jnp.concatenate([slid(pre, -1), pre, slid(pre, 1)], axis=0).astype(BF16)
            pres[pl.ds(pl.multiple_of((x + g + 1) * stacked, 16), stacked), :] = moved
            stack = jnp.concatenate([slid(value, 1), value, slid(value, -1)], axis=0)
            columns.append(stack.astype(BF16))
        left = jnp.concatenate(columns, axis=1)
        acc_two[...] += lax.dot_general(
            right, left, (((1,), (1,)), ((), ())), preferred_element_type=F32
        )
        return carry

    lax.fori_loop(0, length // GROUP, first, 0, unroll=2)

    def second(step, carry):
        x = step * GROUP
        window = pres[pl.ds(pl.multiple_of(x * stacked, 16), (GROUP + 2) * stacked), :]
        moved = beside(window, 3 * stacked, stacked, GROUP)
        sums = jnp.dot(w_one[...], moved, preferred_element_type=F32)
        for g in range(GROUP):
            part = sums[:, g * LANES : (g + 1) * LANES]
            at = pl.ds(pl.multiple_of((x + g) * c0, 16), c0)
            for i, out in ((0, up), (1, own), (2, down)):
                out[at, :] = part[i * c0 : (i + 1) * c0].astype(out.dtype)
        acc_one[...] += lax.dot_general(
            windows(x, c2, c0),
            moved[stacked : 2 * stacked],
            (((1,), (1,)), ((), ())),
            preferred_element_type=F32,
        )
        return carry

    lax.fori_loop(0, length // GROUP, second, 0, unroll=2)

    terms[...] = jnp.zeros_like(terms)
    two = acc_two[...].T
    rows, width = two.shape
    blocks = -(-width // LANES)
    for block in range(blocks):
        part = two[:, block * LANES : min(width, (block + 1) * LANES)]
        terms[block * rows : (block + 1) * rows, 0 : part.shape[1]] = part
    one = acc_one[...]
    terms[blocks * rows : blocks * rows + one.shape[0], 0 : one.shape[1]] = one
    split_to(terms, lax.axis_index("core"), send, keep)


def vmem_call(body, out_shape, scratch=(), cost=None, limit=24 * 2**20):
    spec = pl.BlockSpec(memory_space=pltpu.VMEM)
    return pl.pallas_call(
        body,
        out_shape=out_shape,
        out_specs=jax.tree.map(lambda _: spec, out_shape),
        scratch_shapes=list(scratch),
        compiler_params=pltpu.CompilerParams(vmem_limit_bytes=limit),
        cost_estimate=cost,
    )


def compute(packs, act, kernel_two, kernel_one, rows):
    c1, length, width = act.shape
    c0, c2 = (kernel_one.shape[3], kernel_two.shape[4])
    plane = (length * c0, width)
    return vmem_call(
        compute_kernel,
        (
            jax.ShapeDtypeStruct((rows // 2, LANES), BF16),
            jax.ShapeDtypeStruct((rows // 2, LANES), F32),
            jax.ShapeDtypeStruct(plane, F32),
            jax.ShapeDtypeStruct(plane, BF16),
            jax.ShapeDtypeStruct(plane, BF16),
        ),
        (
            pltpu.VMEM((rows, LANES), F32),
            pltpu.VMEM((c1 * length, width), F32),
            pltpu.VMEM((c1 * length, width), BF16),
            pltpu.VMEM(((length + 2) * 3 * c1, width), BF16),
            pltpu.VMEM((3 * c1, 9 * c2), BF16),
            pltpu.VMEM((3 * c0, 9 * c1), BF16),
            pltpu.VMEM((9 * c2, 3 * c1), F32),
            pltpu.VMEM((9 * c0, 3 * c1), F32),
        ),
        pl.CostEstimate(flops=10**10, bytes_accessed=40 * 2**20, transcendentals=0),
    )(*packs, act, kernel_two, kernel_one)


def merge_kernel(own, from_below, from_above, out, flat):
    chans, length, _ = out.shape

    def add(step, carry):
        at = pl.ds(pl.multiple_of(step * 64, 64), 64)
        flat[at, :] = own[at, :] + from_below[at, :].astype(F32) + from_above[at, :].astype(F32)
        return carry

    lax.fori_loop(0, own.shape[0] // 64, add, 0, unroll=4)

    def gather(c, carry):
        out[c] = flat[pl.ds(c, length, stride=chans), :].astype(out.dtype)
        return carry

    lax.fori_loop(0, chans, gather, 0, unroll=4)


def merge(own, from_below, from_above, shape):
    return vmem_call(
        merge_kernel,
        jax.ShapeDtypeStruct(shape, BF16),
        (pltpu.VMEM(own.shape, F32),),
        pl.CostEstimate(flops=2 * own.size, bytes_accessed=8 * own.size, transcendentals=0),
    )(own, from_below, from_above)


def share_kernel(scale, bucket, terms, out):
    total = jnp.sum(bucket[...].astype(F32), axis=0).astype(BF16)
    grads = (jnp.sum(terms[...].astype(F32), axis=0) * scale).astype(BF16)
    height = total.shape[0]

    def write(n, carry):
        out[n, 0:height, :] = total
        out[n, height : height + grads.shape[0], :] = grads
        return carry

    lax.fori_loop(0, out.shape[0], write, 0)


def share(bucket, terms, scale, copies):
    rows = bucket.shape[1] + terms.shape[1]
    return vmem_call(
        lambda *refs: share_kernel(scale, *refs),
        jax.ShapeDtypeStruct((copies, rows, LANES), BF16),
        (),
        pl.CostEstimate(flops=bucket.size, bytes_accessed=3 * bucket.size, transcendentals=0),
    )(bucket, terms)


def place(source, height, which, bucket, buffer, sems):
    copies, count = (source.shape[0], sems.shape[0])
    size = copies * height
    step = copies // count
    sent = []
    for n in range(count):
        for q in range(n * step, (n + 1) * step):
            buffer[q * height : (q + 1) * height, :] = source[q, 0:height, :].astype(F32)
        rows = pl.ds(n * step * height, step * height)
        at = pl.ds(pl.multiple_of(which * size + n * step * height, 8), step * height)
        sent.append(pltpu.make_async_copy(buffer.at[rows], bucket.at[at], sems.at[n]))
        sent[-1].start()
    return sent


def start_kernel(height, mine, bucket, buffer, sems):
    for copy in place(mine, height, lax.axis_index("core"), bucket, buffer, sems):
        copy.wait()


def finish_kernel(
    sizes, height, mine, other, partial,
    bucket, out_one, out_two,
    raw, one, two, out_sems, buffer, sems,
):
    c0, c1, c2 = sizes
    copies, rows, _ = mine.shape
    extra = rows - height
    me = lax.axis_index("core")
    sent = place(other, height, 1 - me, bucket, buffer, sems)

    def unpack(q, carry):
        for source, which in ((mine, me), (other, 1 - me)):
            at = pl.multiple_of((which * copies + q) * extra, 8)
            raw[pl.ds(at, extra), :] = source[q, height:rows, :].astype(F32)
        return carry

    lax.fori_loop(0, copies, unpack, 0, unroll=4)
    block = 3 * c1
    first = -(-9 * c2 // LANES) * block
    for i in range(3):
        for j in range(3):
            column = ((2 - j) * 3 + 2 - i) * c2
            whole, lane = (column // LANES, column % LANES)
            two[(3 * i + j) * block : (3 * i + j + 1) * block, :] = raw[
                whole * block : (whole + 1) * block, lane : lane + c2
            ]
        at = pl.ds(3 * i * block, 3 * block)
        sent.append(pltpu.make_async_copy(two.at[at], out_two.at[at], out_sems.at[i]))
        sent[-1].start()
    for i in range(3):
        for j in range(3):
            row = first + (3 * j + i) * c0
            for k in range(3):
                to = (9 * i + 3 * j + k) * c0
                one[to : to + c0, :] = raw[row : row + c0, k * c1 : (k + 1) * c1]
        at = pl.ds(9 * i * c0, 9 * c0)
        sent.append(pltpu.make_async_copy(one.at[at], out_one.at[at], out_sems.at[3 + i]))
        sent[-1].start()
    for copy in sent:
        copy.wait()


def finish(mine, other, length, sizes):
    c0, c1, c2 = sizes
    copies, rows, _ = mine.shape
    height = length // LANES // (2 * copies)
    spec = pl.BlockSpec(memory_space=pltpu.VMEM)
    remote = pl.BlockSpec(memory_space=pltpu.HBM)
    whole = jax.ShapeDtypeStruct((length // LANES, LANES), F32)
    chunks = 4
    scratch = [
        pltpu.VMEM((copies * height, LANES), F32),
        pltpu.SemaphoreType.DMA((chunks,)),
    ]
    params = pltpu.CompilerParams(vmem_limit_bytes=24 * 2**20)
    partial = pl.pallas_call(
        lambda *refs: start_kernel(height, *refs),
        out_shape=whole,
        in_specs=[spec],
        out_specs=remote,
        scratch_shapes=scratch,
        compiler_params=params,
    )(mine)
    return pl.pallas_call(
        lambda *refs: finish_kernel(sizes, height, *refs),
        out_shape=(
            whole,
            jax.ShapeDtypeStruct((27 * c0, c1), F32),
            jax.ShapeDtypeStruct((27 * c1, c2), F32),
        ),
        in_specs=[spec, spec, remote],
        out_specs=(remote, remote, remote),
        scratch_shapes=[
            pltpu.VMEM((2 * copies * (rows - height), LANES), F32),
            pltpu.VMEM((27 * c0, c1), F32),
            pltpu.VMEM((27 * c1, c2), F32),
            pltpu.SemaphoreType.DMA((6,)),
        ]
        + scratch,
        input_output_aliases={2: 0},
        compiler_params=params,
    )(mine, other, partial)


def halos(value):
    count = lax.axis_size(SPACE)
    up = [(i, i + 1) for i in range(count - 1)]
    down = [(j, i) for i, j in up]
    return (lax.ppermute(value, SPACE, up), lax.ppermute(value, SPACE, down))


def per_device(volume_in, hidden_act, out_cot, kernel_one, kernel_two, grad_bucket):
    c0, c1, c2 = (volume_in.shape[2], hidden_act.shape[2], out_cot.shape[2])
    devices, copies = (lax.axis_size(EVERY), lax.axis_size(SAME))
    length = grad_bucket.shape[1]
    bucket = grad_bucket.reshape(length // LANES, LANES)
    packed = pack(out_cot[0, 0], volume_in[0, 0])
    packed, send = lax.optimization_barrier((packed, cast(bucket, packed)))
    below, above = halos(packed)
    half = add(bucket, swapped(send))
    act, half = lax.optimization_barrier((hidden_act[0, 0], half))
    parts = lax.all_to_all(half.reshape(copies, -1, LANES), SAME, 0, 0)

    used = -(-9 * c2 // LANES) * 3 * c1 + 9 * c0
    rows = ceil_to(used, 16 * devices)
    send, keep, own, up, down = compute((below, packed, above), act, kernel_two, kernel_one, rows)
    terms = add(keep, swapped(send))
    terms, parts = lax.optimization_barrier((terms, parts))
    terms = lax.all_to_all(terms.reshape(copies, -1, LANES), SAME, 0, 0)
    cells = volume_in.shape[3] * volume_in.shape[4] * devices
    shares = share(parts, terms, 1.0 / math.sqrt(cells), copies)

    up, down, shares = lax.optimization_barrier((up, down, shares))
    mine = lax.all_to_all(shares, SAME, 0, 0)
    count = lax.axis_size(SPACE)
    upward = [(i, i + 1) for i in range(count - 1)]
    from_below = lax.ppermute(up, SPACE, upward)
    from_above = lax.ppermute(down, SPACE, [(j, i) for i, j in upward])
    grad_input = merge(own, from_below, from_above, volume_in.shape[2:])
    mine, grad_input = lax.optimization_barrier((mine, grad_input))
    bucket_sum, total_one, total_two = finish(mine, swapped(mine), length, (c0, c1, c2))
    return (
        grad_input[None, None],
        total_one.reshape(3, 3, 3, c0, c1),
        total_two.reshape(3, 3, 3, c1, c2),
        bucket_sum.reshape(length),
    )


def solution(mesh):
    dp, space = (mesh.shape["dp"], mesh.shape["space"])
    split = Mesh(mesh.devices.reshape(dp, space // 2, 2), EVERY)
    volume = P("dp", SPACE, None, None, None)
    in_specs = (volume, volume, volume, P(), P(), P(EVERY, None))
    out_specs = (volume, P(), P(), P())
    return jax.shard_map(
        per_device, mesh=split, in_specs=in_specs, out_specs=out_specs, check_vma=False
    )
```

```python
import math

import jax
import jax.numpy as jnp
from jax import lax
from jax.experimental import pallas as pl
from jax.experimental.pallas import tpu as pltpu
from jax.sharding import Mesh, PartitionSpec as P

SPACE = ("y", "core")
COLUMN = ("z", "y")
SAME = ("x", "z", "y")
EVERY = ("z", "x", "y", "core")
GROUP = 8
LANES = 128
BF16 = jnp.bfloat16
F32 = jnp.float32


def ceil_to(value, step):
    return -(-value // step) * step


def slid(value, step):
    lane = lax.broadcasted_iota(jnp.int32, value.shape, 1)
    width = value.shape[1]
    keep = lane >= step if step > 0 else lane < width + step
    return jnp.where(keep, pltpu.roll(value, step % width, 1), 0.0)


def beside(window, rows, step, count):
    return jnp.concatenate([window[g * step : g * step + rows] for g in range(count)], axis=1)


def turned(src, flat, dst, offset, pitch, lead):
    chans, length, _ = src.shape

    def stage(c, carry):
        flat[pl.ds(pl.multiple_of(c * length, length), length), :] = src[c].astype(F32)
        return carry

    lax.fori_loop(0, chans, stage, 0, unroll=4)

    def gather(x, carry):
        rows = flat[pl.ds(x, chans, stride=length), :]
        at = pl.multiple_of((x + lead) * pitch + offset, 16)
        dst[pl.ds(at, chans), :] = rows.astype(BF16)
        return carry

    lax.fori_loop(0, length, gather, 0, unroll=4)


def pack_kernel(cot, vol, out, flat):
    c2, length, width = cot.shape
    pitch = c2 + vol.shape[0]
    zeros = jnp.zeros((pitch, width), BF16)
    out[0:pitch, :] = zeros
    out[(length + 1) * pitch : (length + 2) * pitch, :] = zeros
    turned(cot, flat, out, 0, pitch, 1)
    turned(vol, flat, out, c2, pitch, 1)


def pack(cot, vol):
    c2, length, width = cot.shape
    pitch = c2 + vol.shape[0]
    return vmem_call(
        pack_kernel,
        jax.ShapeDtypeStruct(((length + 2) * pitch, width), BF16),
        (pltpu.VMEM((max(c2, vol.shape[0]) * length, width), F32),),
        pl.CostEstimate(flops=0, bytes_accessed=32 * cot.size, transcendentals=0),
    )(cot, vol)


def in_steps(body, rows, count=8):
    step = rows // count

    def one(n, carry):
        body(n * step, step)
        return carry

    lax.fori_loop(0, count, one, 0)


def cast_kernel(src, after, out):
    rows = out.shape[0]
    start = (1 - lax.axis_index("core")) * rows

    def cast(at, step):
        value = src[pl.ds(pl.multiple_of(start + at, 16), step), :]
        out[pl.ds(pl.multiple_of(at, 16), step), :] = value.astype(out.dtype)

    in_steps(cast, rows)


def cast(value, after):
    spec = pl.BlockSpec(memory_space=pltpu.VMEM)
    return pl.pallas_call(
        cast_kernel,
        out_shape=jax.ShapeDtypeStruct((value.shape[0] // 2, LANES), BF16),
        in_specs=[spec, pl.BlockSpec(memory_space=pl.ANY)],
        out_specs=spec,
        compiler_params=pltpu.CompilerParams(vmem_limit_bytes=24 * 2**20),
        cost_estimate=pl.CostEstimate(flops=0, bytes_accessed=4 * value.size, transcendentals=0),
    )(value, after)


def add_kernel(src, other, send, keep):
    half, rows = (other.shape[0], send.shape[0])
    start = lax.axis_index("core") * half
    mine = lax.axis_index("x") * rows
    theirs = rows - mine

    def total(at, step):
        value = src[pl.ds(pl.multiple_of(start + at, 16), step), :]
        return value + other[pl.ds(pl.multiple_of(at, 16), step), :].astype(F32)

    def add(at, step):
        to = pl.ds(pl.multiple_of(at, 16), step)
        send[to, :] = total(theirs + at, step).astype(send.dtype)
        keep[to, :] = total(mine + at, step)

    in_steps(add, rows)


def add(value, other):
    rows = other.shape[0] // 2
    return vmem_call(
        add_kernel,
        (jax.ShapeDtypeStruct((rows, LANES), BF16), jax.ShapeDtypeStruct((rows, LANES), F32)),
        (),
        pl.CostEstimate(flops=0, bytes_accessed=4 * value.size, transcendentals=0),
    )(value, other)


def combine_kernel(keep, other, terms, more, out):
    height, extra = (keep.shape[0] // out.shape[0], terms.shape[0] // out.shape[0])
    for n in range(out.shape[0]):
        at = slice(n * height, (n + 1) * height)
        out[n, 0:height, :] = (keep[at, :] + other[at, :].astype(F32)).astype(out.dtype)
        at = slice(n * extra, (n + 1) * extra)
        out[n, height : height + extra, :] = (terms[at, :] + more[at, :].astype(F32)).astype(out.dtype)


def combine(keep, other, terms, more, parts):
    rows = (keep.shape[0] + terms.shape[0]) // parts
    return vmem_call(
        combine_kernel,
        jax.ShapeDtypeStruct((parts, rows, LANES), BF16),
        (),
        pl.CostEstimate(flops=0, bytes_accessed=8 * keep.size, transcendentals=0),
    )(keep, other, terms, more)


def split_to(total, mine, send, keep):
    half = total.shape[0] // 2
    keep[...] = total[pl.ds(pl.multiple_of(mine * half, 16), half), :]
    send[...] = total[pl.ds(pl.multiple_of((1 - mine) * half, 16), half), :].astype(send.dtype)


def swapped(value, axis="core"):
    return lax.ppermute(value, axis, [(0, 1), (1, 0)])


def compute_kernel(
    pack_m, pack_0, pack_p, act, two, one,
    send, keep, own, up, down,
    terms, flat, acts, pres, w_two, w_one, acc_two, acc_one,
):
    c1, length, _ = act.shape
    c2, c0 = (two.shape[4], one.shape[3])
    pitch = c0 + c2
    packs = (pack_m, pack_0, pack_p)

    turned(act, flat, acts, 0, c1, 0)
    offsets = [(m, n) for m in range(3) for n in range(3)]
    w_two[...] = jnp.concatenate(
        [
            jnp.concatenate([two[2 - i, 2 - j, 2 - k].astype(F32) for k in range(3)], axis=0)
            for j, i in offsets
        ],
        axis=1,
    ).astype(BF16)
    w_one[...] = jnp.concatenate(
        [
            jnp.concatenate([one[2 - i, 2 - j, k].astype(F32) for i in range(3)], axis=0)
            for j, k in offsets
        ],
        axis=1,
    ).astype(BF16)
    stacked = 3 * c1
    pres[0:stacked, :] = jnp.zeros((stacked, LANES), BF16)
    pres[(length + 1) * stacked : (length + 2) * stacked, :] = jnp.zeros((stacked, LANES), BF16)
    acc_two[...] = jnp.zeros_like(acc_two)
    acc_one[...] = jnp.zeros_like(acc_one)

    def windows(x, offset, count):
        rows = [
            [p[pl.ds(pl.multiple_of((x + n) * pitch + offset, 16), count), :] for p in packs]
            for n in range(GROUP + 2)
        ]
        return jnp.concatenate(
            [jnp.concatenate(sum(rows[g : g + 3], []), axis=0) for g in range(GROUP)], axis=1
        )

    def first(step, carry):
        x = step * GROUP
        right = windows(x, 0, c2)
        sums = jnp.dot(w_two[...], right, preferred_element_type=F32)
        columns = []
        for g in range(GROUP):
            part = sums[:, g * LANES : (g + 1) * LANES]
            grad = slid(part[0:c1], 1) + part[c1 : 2 * c1] + slid(part[2 * c1 : 3 * c1], -1)
            value = acts[pl.ds(pl.multiple_of((x + g) * c1, 16), c1), :].astype(F32)
            pre = (grad * jnp.where(value > 0, 1.0, 0.2)).astype(BF16).astype(F32)
            moved = jnp.concatenate([slid(pre, -1), pre, slid(pre, 1)], axis=0).astype(BF16)
            pres[pl.ds(pl.multiple_of((x + g + 1) * stacked, 16), stacked), :] = moved
            stack = jnp.concatenate([slid(value, 1), value, slid(value, -1)], axis=0)
            columns.append(stack.astype(BF16))
        left = jnp.concatenate(columns, axis=1)
        acc_two[...] += lax.dot_general(
            right, left, (((1,), (1,)), ((), ())), preferred_element_type=F32
        )
        return carry

    lax.fori_loop(0, length // GROUP, first, 0, unroll=2)

    def second(step, carry):
        x = step * GROUP
        window = pres[pl.ds(pl.multiple_of(x * stacked, 16), (GROUP + 2) * stacked), :]
        moved = beside(window, 3 * stacked, stacked, GROUP)
        sums = jnp.dot(w_one[...], moved, preferred_element_type=F32)
        for g in range(GROUP):
            part = sums[:, g * LANES : (g + 1) * LANES]
            at = pl.ds(pl.multiple_of((x + g) * c0, 16), c0)
            for i, out in ((0, up), (1, own), (2, down)):
                out[at, :] = part[i * c0 : (i + 1) * c0].astype(out.dtype)
        acc_one[...] += lax.dot_general(
            windows(x, c2, c0),
            moved[stacked : 2 * stacked],
            (((1,), (1,)), ((), ())),
            preferred_element_type=F32,
        )
        return carry

    lax.fori_loop(0, length // GROUP, second, 0, unroll=2)

    terms[...] = jnp.zeros_like(terms)
    two = acc_two[...].T
    rows, width = two.shape
    blocks = -(-width // LANES)
    for block in range(blocks):
        part = two[:, block * LANES : min(width, (block + 1) * LANES)]
        terms[block * rows : (block + 1) * rows, 0 : part.shape[1]] = part
    one = acc_one[...]
    terms[blocks * rows : blocks * rows + one.shape[0], 0 : one.shape[1]] = one
    split_to(terms, lax.axis_index("core"), send, keep)


def vmem_call(body, out_shape, scratch=(), cost=None, limit=24 * 2**20):
    spec = pl.BlockSpec(memory_space=pltpu.VMEM)
    return pl.pallas_call(
        body,
        out_shape=out_shape,
        out_specs=jax.tree.map(lambda _: spec, out_shape),
        scratch_shapes=list(scratch),
        compiler_params=pltpu.CompilerParams(vmem_limit_bytes=limit),
        cost_estimate=cost,
    )


def compute(packs, act, kernel_two, kernel_one, rows):
    c1, length, width = act.shape
    c0, c2 = (kernel_one.shape[3], kernel_two.shape[4])
    plane = (length * c0, width)
    return vmem_call(
        compute_kernel,
        (
            jax.ShapeDtypeStruct((rows // 2, LANES), BF16),
            jax.ShapeDtypeStruct((rows // 2, LANES), F32),
            jax.ShapeDtypeStruct(plane, F32),
            jax.ShapeDtypeStruct(plane, BF16),
            jax.ShapeDtypeStruct(plane, BF16),
        ),
        (
            pltpu.VMEM((rows, LANES), F32),
            pltpu.VMEM((c1 * length, width), F32),
            pltpu.VMEM((c1 * length, width), BF16),
            pltpu.VMEM(((length + 2) * 3 * c1, width), BF16),
            pltpu.VMEM((3 * c1, 9 * c2), BF16),
            pltpu.VMEM((3 * c0, 9 * c1), BF16),
            pltpu.VMEM((9 * c2, 3 * c1), F32),
            pltpu.VMEM((9 * c0, 3 * c1), F32),
        ),
        pl.CostEstimate(flops=10**10, bytes_accessed=40 * 2**20, transcendentals=0),
    )(*packs, act, kernel_two, kernel_one)


def merge_kernel(own, from_below, from_above, out, flat):
    chans, length, _ = out.shape

    def add(step, carry):
        at = pl.ds(pl.multiple_of(step * 64, 64), 64)
        flat[at, :] = own[at, :] + from_below[at, :].astype(F32) + from_above[at, :].astype(F32)
        return carry

    lax.fori_loop(0, own.shape[0] // 64, add, 0, unroll=4)

    def gather(c, carry):
        out[c] = flat[pl.ds(c, length, stride=chans), :].astype(out.dtype)
        return carry

    lax.fori_loop(0, chans, gather, 0, unroll=4)


def merge(own, from_below, from_above, shape):
    return vmem_call(
        merge_kernel,
        jax.ShapeDtypeStruct(shape, BF16),
        (pltpu.VMEM(own.shape, F32),),
        pl.CostEstimate(flops=2 * own.size, bytes_accessed=8 * own.size, transcendentals=0),
    )(own, from_below, from_above)


def share_kernel(scale, height, parts, out):
    total = jnp.sum(parts[:, 0:height, :].astype(F32), axis=0).astype(BF16)
    rows = parts.shape[1]
    grads = (jnp.sum(parts[:, height:rows, :].astype(F32), axis=0) * scale).astype(BF16)

    def write(n, carry):
        out[n, 0:height, :] = total
        out[n, height:rows, :] = grads
        return carry

    lax.fori_loop(0, out.shape[0], write, 0)


def share(parts, height, scale, copies):
    return vmem_call(
        lambda *refs: share_kernel(scale, height, *refs),
        jax.ShapeDtypeStruct((copies,) + parts.shape[1:], BF16),
        (),
        pl.CostEstimate(flops=parts.size, bytes_accessed=6 * parts.size, transcendentals=0),
    )(parts)


def place(source, height, which, bucket, buffer, sems):
    copies, count = (source.shape[0], sems.shape[0])
    size = copies * height
    step = copies // count
    sent = []
    for n in range(count):
        for q in range(n * step, (n + 1) * step):
            buffer[q * height : (q + 1) * height, :] = source[q, 0:height, :].astype(F32)
        rows = pl.ds(n * step * height, step * height)
        at = pl.ds(pl.multiple_of(which * size + n * step * height, 8), step * height)
        sent.append(pltpu.make_async_copy(buffer.at[rows], bucket.at[at], sems.at[n]))
        sent[-1].start()
    return sent


def start_kernel(height, mine, bucket, buffer, sems):
    for copy in place(mine, height, lax.axis_index("core"), bucket, buffer, sems):
        copy.wait()


def finish_kernel(
    sizes, height, mine, other, partial,
    bucket, out_one, out_two,
    raw, one, two, out_sems, buffer, sems,
):
    c0, c1, c2 = sizes
    copies, rows, _ = mine.shape
    extra = rows - height
    me = lax.axis_index("core")
    sent = place(other, height, 1 - me, bucket, buffer, sems)

    column = copies // 2
    for q in range(column):
        for source, which in ((mine, me), (other, 1 - me)):
            at = pl.multiple_of((which * column + q) * extra, 8)
            near = source[q, height:rows, :].astype(F32)
            raw[pl.ds(at, extra), :] = near + source[column + q, height:rows, :].astype(F32)
    block = 3 * c1
    first = -(-9 * c2 // LANES) * block
    for i in range(3):
        for j in range(3):
            column = ((2 - j) * 3 + 2 - i) * c2
            whole, lane = (column // LANES, column % LANES)
            two[(3 * i + j) * block : (3 * i + j + 1) * block, :] = raw[
                whole * block : (whole + 1) * block, lane : lane + c2
            ]
        at = pl.ds(3 * i * block, 3 * block)
        sent.append(pltpu.make_async_copy(two.at[at], out_two.at[at], out_sems.at[i]))
        sent[-1].start()
    for i in range(3):
        for j in range(3):
            row = first + (3 * j + i) * c0
            for k in range(3):
                to = (9 * i + 3 * j + k) * c0
                one[to : to + c0, :] = raw[row : row + c0, k * c1 : (k + 1) * c1]
        at = pl.ds(9 * i * c0, 9 * c0)
        sent.append(pltpu.make_async_copy(one.at[at], out_one.at[at], out_sems.at[3 + i]))
        sent[-1].start()
    for copy in sent:
        copy.wait()


def finish(mine, other, length, sizes):
    c0, c1, c2 = sizes
    copies, rows, _ = mine.shape
    height = length // LANES // (2 * copies)
    spec = pl.BlockSpec(memory_space=pltpu.VMEM)
    remote = pl.BlockSpec(memory_space=pltpu.HBM)
    whole = jax.ShapeDtypeStruct((length // LANES, LANES), F32)
    chunks = 4
    scratch = [
        pltpu.VMEM((copies * height, LANES), F32),
        pltpu.SemaphoreType.DMA((chunks,)),
    ]
    params = pltpu.CompilerParams(vmem_limit_bytes=24 * 2**20)
    partial = pl.pallas_call(
        lambda *refs: start_kernel(height, *refs),
        out_shape=whole,
        in_specs=[spec],
        out_specs=remote,
        scratch_shapes=scratch,
        compiler_params=params,
    )(mine)
    return pl.pallas_call(
        lambda *refs: finish_kernel(sizes, height, *refs),
        out_shape=(
            whole,
            jax.ShapeDtypeStruct((27 * c0, c1), F32),
            jax.ShapeDtypeStruct((27 * c1, c2), F32),
        ),
        in_specs=[spec, spec, remote],
        out_specs=(remote, remote, remote),
        scratch_shapes=[
            pltpu.VMEM((copies * (rows - height), LANES), F32),
            pltpu.VMEM((27 * c0, c1), F32),
            pltpu.VMEM((27 * c1, c2), F32),
            pltpu.SemaphoreType.DMA((6,)),
        ]
        + scratch,
        input_output_aliases={2: 0},
        compiler_params=params,
    )(mine, other, partial)


def halos(value):
    count = lax.axis_size(SPACE)
    up = [(i, i + 1) for i in range(count - 1)]
    down = [(j, i) for i, j in up]
    return (lax.ppermute(value, SPACE, up), lax.ppermute(value, SPACE, down))


def per_device(volume_in, hidden_act, out_cot, kernel_one, kernel_two, grad_bucket):
    c0, c1, c2 = (volume_in.shape[2], hidden_act.shape[2], out_cot.shape[2])
    devices, copies, column = (lax.axis_size(EVERY), lax.axis_size(SAME), lax.axis_size(COLUMN))
    length = grad_bucket.shape[1]
    bucket = grad_bucket.reshape(length // LANES, LANES)
    packed = pack(out_cot[0, 0], volume_in[0, 0])
    below, above = halos(packed)
    send, near = add(bucket, swapped(cast(bucket, packed)))
    act, send, near = lax.optimization_barrier((hidden_act[0, 0], send, near))
    far = swapped(send, "x")

    used = -(-9 * c2 // LANES) * 3 * c1 + 9 * c0
    rows = ceil_to(used, 16 * 2 * column)
    send, keep, own, up, down = compute((below, packed, above), act, kernel_two, kernel_one, rows)
    parts = combine(near, far, keep, swapped(send), column)
    parts = lax.all_to_all(parts, COLUMN, 0, 0)
    cells = volume_in.shape[3] * volume_in.shape[4] * devices
    height = length // LANES // devices
    shares = share(parts, height, 1.0 / math.sqrt(cells), copies)

    up, down, shares = lax.optimization_barrier((up, down, shares))
    mine = lax.all_to_all(shares, SAME, 0, 0)
    count = lax.axis_size(SPACE)
    upward = [(i, i + 1) for i in range(count - 1)]
    from_below = lax.ppermute(up, SPACE, upward)
    from_above = lax.ppermute(down, SPACE, [(j, i) for i, j in upward])
    grad_input = merge(own, from_below, from_above, volume_in.shape[2:])
    mine, grad_input = lax.optimization_barrier((mine, grad_input))
    bucket_sum, total_one, total_two = finish(mine, swapped(mine), length, (c0, c1, c2))
    return (
        grad_input[None, None],
        total_one.reshape(3, 3, 3, c0, c1),
        total_two.reshape(3, 3, 3, c1, c2),
        bucket_sum.reshape(length),
    )


def solution(mesh):
    dp, space = (mesh.shape["dp"], mesh.shape["space"])
    split = Mesh(mesh.devices.reshape(dp // 2, 2, space // 2, 2), EVERY)
    volume = P(("z", "x"), SPACE, None, None, None)
    in_specs = (volume, volume, volume, P(), P(), P(EVERY, None))
    out_specs = (volume, P(), P(), P())
    return jax.shard_map(
        per_device, mesh=split, in_specs=in_specs, out_specs=out_specs, check_vma=False
    )
```

```python
import math

import jax
import jax.numpy as jnp
from jax import lax
from jax.experimental import pallas as pl
from jax.experimental.pallas import tpu as pltpu
from jax.sharding import Mesh, PartitionSpec as P

SPACE = ("y", "core")
COLUMN = ("z", "y")
SAME = ("x", "z", "y")
EVERY = ("z", "x", "y", "core")
GROUP = 8
LANES = 128
BF16 = jnp.bfloat16
F32 = jnp.float32


def ceil_to(value, step):
    return -(-value // step) * step


def slid(value, step):
    lane = lax.broadcasted_iota(jnp.int32, value.shape, 1)
    width = value.shape[1]
    keep = lane >= step if step > 0 else lane < width + step
    return jnp.where(keep, pltpu.roll(value, step % width, 1), 0.0)


def beside(window, rows, step, count):
    return jnp.concatenate([window[g * step : g * step + rows] for g in range(count)], axis=1)


def turned(src, flat, dst, offset, pitch, lead):
    chans, length, _ = src.shape

    def stage(c, carry):
        flat[pl.ds(pl.multiple_of(c * length, length), length), :] = src[c].astype(F32)
        return carry

    lax.fori_loop(0, chans, stage, 0, unroll=4)

    def gather(x, carry):
        rows = flat[pl.ds(x, chans, stride=length), :]
        at = pl.multiple_of((x + lead) * pitch + offset, 16)
        dst[pl.ds(at, chans), :] = rows.astype(BF16)
        return carry

    lax.fori_loop(0, length, gather, 0, unroll=4)


def pack_kernel(cot, vol, out, flat):
    c2, length, width = cot.shape
    pitch = c2 + vol.shape[0]
    zeros = jnp.zeros((pitch, width), BF16)
    out[0:pitch, :] = zeros
    out[(length + 1) * pitch : (length + 2) * pitch, :] = zeros
    turned(cot, flat, out, 0, pitch, 1)
    turned(vol, flat, out, c2, pitch, 1)


def pack(cot, vol):
    c2, length, width = cot.shape
    pitch = c2 + vol.shape[0]
    return vmem_call(
        pack_kernel,
        jax.ShapeDtypeStruct(((length + 2) * pitch, width), BF16),
        (pltpu.VMEM((max(c2, vol.shape[0]) * length, width), F32),),
        pl.CostEstimate(flops=0, bytes_accessed=32 * cot.size, transcendentals=0),
    )(cot, vol)


def in_steps(body, rows, count=8):
    step = rows // count

    def one(n, carry):
        body(n * step, step)
        return carry

    lax.fori_loop(0, count, one, 0)


def cast_kernel(src, after, out):
    rows = out.shape[0]
    start = (1 - lax.axis_index("core")) * rows

    def cast(at, step):
        value = src[pl.ds(pl.multiple_of(start + at, 16), step), :]
        out[pl.ds(pl.multiple_of(at, 16), step), :] = value.astype(out.dtype)

    in_steps(cast, rows)


def cast(value, after):
    spec = pl.BlockSpec(memory_space=pltpu.VMEM)
    return pl.pallas_call(
        cast_kernel,
        out_shape=jax.ShapeDtypeStruct((value.shape[0] // 2, LANES), BF16),
        in_specs=[spec, pl.BlockSpec(memory_space=pl.ANY)],
        out_specs=spec,
        compiler_params=pltpu.CompilerParams(vmem_limit_bytes=24 * 2**20),
        cost_estimate=pl.CostEstimate(flops=0, bytes_accessed=4 * value.size, transcendentals=0),
    )(value, after)


def add_kernel(src, other, send, keep):
    half, rows = (other.shape[0], send.shape[0])
    start = lax.axis_index("core") * half
    mine = lax.axis_index("x") * rows
    theirs = rows - mine

    def total(at, step):
        value = src[pl.ds(pl.multiple_of(start + at, 16), step), :]
        return value + other[pl.ds(pl.multiple_of(at, 16), step), :].astype(F32)

    def add(at, step):
        to = pl.ds(pl.multiple_of(at, 16), step)
        send[to, :] = total(theirs + at, step).astype(send.dtype)
        keep[to, :] = total(mine + at, step)

    in_steps(add, rows)


def add(value, other):
    rows = other.shape[0] // 2
    return vmem_call(
        add_kernel,
        (jax.ShapeDtypeStruct((rows, LANES), BF16), jax.ShapeDtypeStruct((rows, LANES), F32)),
        (),
        pl.CostEstimate(flops=0, bytes_accessed=4 * value.size, transcendentals=0),
    )(value, other)


def combine_kernel(keep, other, terms, more, out):
    height, extra = (keep.shape[0] // out.shape[0], terms.shape[0] // out.shape[0])
    for n in range(out.shape[0]):
        at = slice(n * height, (n + 1) * height)
        out[n, 0:height, :] = (keep[at, :] + other[at, :].astype(F32)).astype(out.dtype)
        at = slice(n * extra, (n + 1) * extra)
        out[n, height : height + extra, :] = (terms[at, :] + more[at, :].astype(F32)).astype(out.dtype)


def combine(keep, other, terms, more, parts):
    rows = (keep.shape[0] + terms.shape[0]) // parts
    return vmem_call(
        combine_kernel,
        jax.ShapeDtypeStruct((parts, rows, LANES), BF16),
        (),
        pl.CostEstimate(flops=0, bytes_accessed=8 * keep.size, transcendentals=0),
    )(keep, other, terms, more)


def split_to(total, mine, send, keep):
    half = total.shape[0] // 2
    keep[...] = total[pl.ds(pl.multiple_of(mine * half, 16), half), :]
    send[...] = total[pl.ds(pl.multiple_of((1 - mine) * half, 16), half), :].astype(send.dtype)


def swapped(value, axis="core"):
    return lax.ppermute(value, axis, [(0, 1), (1, 0)])


def compute_kernel(
    pack_in, pack_0, pack_out, act, two, one,
    send, keep, own, inner, outer,
    terms, flat, acts, pres, w_two, w_one, acc_two, acc_one,
):
    c1, length, _ = act.shape
    c2, c0 = (two.shape[4], one.shape[3])
    pitch = c0 + c2
    packs = (pack_in, pack_0, pack_out)
    core = lax.axis_index("core")
    ahead = [core * n + (1 - core) * (2 - n) for n in range(3)]
    back = [core * (2 - n) + (1 - core) * n for n in range(3)]

    turned(act, flat, acts, 0, c1, 0)
    offsets = [(m, n) for m in range(3) for n in range(3)]
    w_two[...] = jnp.concatenate(
        [
            jnp.concatenate([two[back[n], 2 - j, 2 - k].astype(F32) for k in range(3)], axis=0)
            for j, n in offsets
        ],
        axis=1,
    ).astype(BF16)
    w_one[...] = jnp.concatenate(
        [
            jnp.concatenate([one[ahead[n], 2 - j, k].astype(F32) for n in range(3)], axis=0)
            for j, k in offsets
        ],
        axis=1,
    ).astype(BF16)
    stacked = 3 * c1
    pres[0:stacked, :] = jnp.zeros((stacked, LANES), BF16)
    pres[(length + 1) * stacked : (length + 2) * stacked, :] = jnp.zeros((stacked, LANES), BF16)
    acc_two[...] = jnp.zeros_like(acc_two)
    acc_one[...] = jnp.zeros_like(acc_one)

    def windows(x, offset, count):
        rows = [
            [p[pl.ds(pl.multiple_of((x + n) * pitch + offset, 16), count), :] for p in packs]
            for n in range(GROUP + 2)
        ]
        return jnp.concatenate(
            [jnp.concatenate(sum(rows[g : g + 3], []), axis=0) for g in range(GROUP)], axis=1
        )

    def first(step, carry):
        x = step * GROUP
        right = windows(x, 0, c2)
        sums = jnp.dot(w_two[...], right, preferred_element_type=F32)
        columns = []
        for g in range(GROUP):
            part = sums[:, g * LANES : (g + 1) * LANES]
            grad = slid(part[0:c1], 1) + part[c1 : 2 * c1] + slid(part[2 * c1 : 3 * c1], -1)
            value = acts[pl.ds(pl.multiple_of((x + g) * c1, 16), c1), :].astype(F32)
            pre = (grad * jnp.where(value > 0, 1.0, 0.2)).astype(BF16).astype(F32)
            moved = jnp.concatenate([slid(pre, -1), pre, slid(pre, 1)], axis=0).astype(BF16)
            pres[pl.ds(pl.multiple_of((x + g + 1) * stacked, 16), stacked), :] = moved
            stack = jnp.concatenate([slid(value, 1), value, slid(value, -1)], axis=0)
            columns.append(stack.astype(BF16))
        left = jnp.concatenate(columns, axis=1)
        acc_two[...] += lax.dot_general(
            right, left, (((1,), (1,)), ((), ())), preferred_element_type=F32
        )
        return carry

    lax.fori_loop(0, length // GROUP, first, 0, unroll=4)

    def second(step, carry):
        x = step * GROUP
        window = pres[pl.ds(pl.multiple_of(x * stacked, 16), (GROUP + 2) * stacked), :]
        moved = beside(window, 3 * stacked, stacked, GROUP)
        sums = jnp.dot(w_one[...], moved, preferred_element_type=F32)
        for g in range(GROUP):
            part = sums[:, g * LANES : (g + 1) * LANES]
            at = pl.ds(pl.multiple_of((x + g) * c0, 16), c0)
            for i, out in ((0, inner), (1, own), (2, outer)):
                out[at, :] = part[i * c0 : (i + 1) * c0].astype(out.dtype)
        acc_one[...] += lax.dot_general(
            windows(x, c2, c0),
            moved[stacked : 2 * stacked],
            (((1,), (1,)), ((), ())),
            preferred_element_type=F32,
        )
        return carry

    lax.fori_loop(0, length // GROUP, second, 0, unroll=4)

    terms[...] = jnp.zeros_like(terms)

    def ordered(acc, count):
        blocks = [pl.multiple_of((3 * j + n) * count, 16) for j in range(3) for n in ahead]
        return jnp.concatenate([acc[pl.ds(at, count), :] for at in blocks], axis=0)

    two = ordered(acc_two, c2).T
    rows, width = two.shape
    blocks = -(-width // LANES)
    for block in range(blocks):
        part = two[:, block * LANES : min(width, (block + 1) * LANES)]
        terms[block * rows : (block + 1) * rows, 0 : part.shape[1]] = part
    one = ordered(acc_one, c0)
    terms[blocks * rows : blocks * rows + one.shape[0], 0 : one.shape[1]] = one
    split_to(terms, lax.axis_index("core"), send, keep)


def vmem_call(body, out_shape, scratch=(), cost=None, limit=24 * 2**20):
    spec = pl.BlockSpec(memory_space=pltpu.VMEM)
    return pl.pallas_call(
        body,
        out_shape=out_shape,
        out_specs=jax.tree.map(lambda _: spec, out_shape),
        scratch_shapes=list(scratch),
        compiler_params=pltpu.CompilerParams(vmem_limit_bytes=limit),
        cost_estimate=cost,
    )


def compute(packs, act, kernel_two, kernel_one, rows):
    c1, length, width = act.shape
    c0, c2 = (kernel_one.shape[3], kernel_two.shape[4])
    plane = (length * c0, width)
    return vmem_call(
        compute_kernel,
        (
            jax.ShapeDtypeStruct((rows // 2, LANES), BF16),
            jax.ShapeDtypeStruct((rows // 2, LANES), F32),
            jax.ShapeDtypeStruct(plane, F32),
            jax.ShapeDtypeStruct(plane, BF16),
            jax.ShapeDtypeStruct(plane, BF16),
        ),
        (
            pltpu.VMEM((rows, LANES), F32),
            pltpu.VMEM((c1 * length, width), F32),
            pltpu.VMEM((c1 * length, width), BF16),
            pltpu.VMEM(((length + 2) * 3 * c1, width), BF16),
            pltpu.VMEM((3 * c1, 9 * c2), BF16),
            pltpu.VMEM((3 * c0, 9 * c1), BF16),
            pltpu.VMEM((9 * c2, 3 * c1), F32),
            pltpu.VMEM((9 * c0, 3 * c1), F32),
        ),
        pl.CostEstimate(flops=10**10, bytes_accessed=40 * 2**20, transcendentals=0),
    )(*packs, act, kernel_two, kernel_one)


def merge_kernel(own, first, second, out, flat):
    chans, length, _ = out.shape

    def add(step, carry):
        at = pl.ds(pl.multiple_of(step * 64, 64), 64)
        flat[at, :] = own[at, :] + first[at, :].astype(F32) + second[at, :].astype(F32)
        return carry

    lax.fori_loop(0, own.shape[0] // 64, add, 0, unroll=4)

    def gather(c, carry):
        out[c] = flat[pl.ds(c, length, stride=chans), :].astype(out.dtype)
        return carry

    lax.fori_loop(0, chans, gather, 0, unroll=4)


def merge(own, first, second, shape):
    return vmem_call(
        merge_kernel,
        jax.ShapeDtypeStruct(shape, BF16),
        (pltpu.VMEM(own.shape, F32),),
        pl.CostEstimate(flops=2 * own.size, bytes_accessed=8 * own.size, transcendentals=0),
    )(own, first, second)


def share_kernel(scale, height, parts, out):
    total = jnp.sum(parts[:, 0:height, :].astype(F32), axis=0).astype(BF16)
    rows = parts.shape[1]
    grads = (jnp.sum(parts[:, height:rows, :].astype(F32), axis=0) * scale).astype(BF16)

    def write(n, carry):
        out[n, 0:height, :] = total
        out[n, height:rows, :] = grads
        return carry

    lax.fori_loop(0, out.shape[0], write, 0)


def share(parts, height, scale, copies):
    return vmem_call(
        lambda *refs: share_kernel(scale, height, *refs),
        jax.ShapeDtypeStruct((copies,) + parts.shape[1:], BF16),
        (),
        pl.CostEstimate(flops=parts.size, bytes_accessed=6 * parts.size, transcendentals=0),
    )(parts)


def place(source, height, which, bucket, buffer, sems):
    copies, count = (source.shape[0], sems.shape[0])
    size = copies * height
    step = copies // count
    sent = []
    for n in range(count):
        for q in range(n * step, (n + 1) * step):
            buffer[q * height : (q + 1) * height, :] = source[q, 0:height, :].astype(F32)
        rows = pl.ds(n * step * height, step * height)
        at = pl.ds(pl.multiple_of(which * size + n * step * height, 8), step * height)
        sent.append(pltpu.make_async_copy(buffer.at[rows], bucket.at[at], sems.at[n]))
        sent[-1].start()
    return sent


def start_kernel(height, mine, bucket, buffer, sems):
    for copy in place(mine, height, lax.axis_index("core"), bucket, buffer, sems):
        copy.wait()


def finish_kernel(
    sizes, height, mine, other, partial,
    bucket, out_one, out_two,
    raw, one, two, out_sems, buffer, sems,
):
    c0, c1, c2 = sizes
    copies, rows, _ = mine.shape
    extra = rows - height
    me = lax.axis_index("core")
    sent = place(other, height, 1 - me, bucket, buffer, sems)

    column = copies // 2
    for q in range(column):
        for source, which in ((mine, me), (other, 1 - me)):
            at = pl.multiple_of((which * column + q) * extra, 8)
            near = source[q, height:rows, :].astype(F32)
            raw[pl.ds(at, extra), :] = near + source[column + q, height:rows, :].astype(F32)
    block = 3 * c1
    first = -(-9 * c2 // LANES) * block
    for i in range(3):
        for j in range(3):
            column = ((2 - j) * 3 + 2 - i) * c2
            whole, lane = (column // LANES, column % LANES)
            two[(3 * i + j) * block : (3 * i + j + 1) * block, :] = raw[
                whole * block : (whole + 1) * block, lane : lane + c2
            ]
        at = pl.ds(3 * i * block, 3 * block)
        sent.append(pltpu.make_async_copy(two.at[at], out_two.at[at], out_sems.at[i]))
        sent[-1].start()
    for i in range(3):
        for j in range(3):
            row = first + (3 * j + i) * c0
            for k in range(3):
                to = (9 * i + 3 * j + k) * c0
                one[to : to + c0, :] = raw[row : row + c0, k * c1 : (k + 1) * c1]
        at = pl.ds(9 * i * c0, 9 * c0)
        sent.append(pltpu.make_async_copy(one.at[at], out_one.at[at], out_sems.at[3 + i]))
        sent[-1].start()
    for copy in sent:
        copy.wait()


def finish(mine, other, length, sizes):
    c0, c1, c2 = sizes
    copies, rows, _ = mine.shape
    height = length // LANES // (2 * copies)
    spec = pl.BlockSpec(memory_space=pltpu.VMEM)
    remote = pl.BlockSpec(memory_space=pltpu.HBM)
    whole = jax.ShapeDtypeStruct((length // LANES, LANES), F32)
    chunks = 4
    scratch = [
        pltpu.VMEM((copies * height, LANES), F32),
        pltpu.SemaphoreType.DMA((chunks,)),
    ]
    params = pltpu.CompilerParams(vmem_limit_bytes=24 * 2**20)
    partial = pl.pallas_call(
        lambda *refs: start_kernel(height, *refs),
        out_shape=whole,
        in_specs=[spec],
        out_specs=remote,
        scratch_shapes=scratch,
        compiler_params=params,
    )(mine)
    return pl.pallas_call(
        lambda *refs: finish_kernel(sizes, height, *refs),
        out_shape=(
            whole,
            jax.ShapeDtypeStruct((27 * c0, c1), F32),
            jax.ShapeDtypeStruct((27 * c1, c2), F32),
        ),
        in_specs=[spec, spec, remote],
        out_specs=(remote, remote, remote),
        scratch_shapes=[
            pltpu.VMEM((copies * (rows - height), LANES), F32),
            pltpu.VMEM((27 * c0, c1), F32),
            pltpu.VMEM((27 * c1, c2), F32),
            pltpu.SemaphoreType.DMA((6,)),
        ]
        + scratch,
        input_output_aliases={2: 0},
        compiler_params=params,
    )(mine, other, partial)


def crossed(value):
    pairs = [(n, n + 1) for n in range(1, lax.axis_size(SPACE) - 1, 2)]
    return lax.ppermute(value, SPACE, pairs + [(m, n) for n, m in pairs])


def per_device(volume_in, hidden_act, out_cot, kernel_one, kernel_two, grad_bucket):
    c0, c1, c2 = (volume_in.shape[2], hidden_act.shape[2], out_cot.shape[2])
    devices, copies, column = (lax.axis_size(EVERY), lax.axis_size(SAME), lax.axis_size(COLUMN))
    length = grad_bucket.shape[1]
    bucket = grad_bucket.reshape(length // LANES, LANES)
    packed = pack(out_cot[0, 0], volume_in[0, 0])
    outer, inner = (crossed(packed), swapped(packed))
    send, near = add(bucket, swapped(cast(bucket, packed)))
    act, send, near = lax.optimization_barrier((hidden_act[0, 0], send, near))
    far = swapped(send, "x")

    used = -(-9 * c2 // LANES) * 3 * c1 + 9 * c0
    rows = ceil_to(used, 16 * 2 * column)
    send, keep, own, inner, outer = compute(
        (inner, packed, outer), act, kernel_two, kernel_one, rows
    )
    parts = combine(near, far, keep, swapped(send), column)
    parts, inner, outer = lax.optimization_barrier((parts, inner, outer))
    parts = lax.all_to_all(parts, COLUMN, 0, 0)
    grad_input = merge(own, swapped(inner), crossed(outer), volume_in.shape[2:])
    parts, grad_input = lax.optimization_barrier((parts, grad_input))
    cells = volume_in.shape[3] * volume_in.shape[4] * devices
    height = length // LANES // devices
    shares = share(parts, height, 1.0 / math.sqrt(cells), copies)

    mine = lax.all_to_all(shares, SAME, 0, 0)
    bucket_sum, total_one, total_two = finish(mine, swapped(mine), length, (c0, c1, c2))
    return (
        grad_input[None, None],
        total_one.reshape(3, 3, 3, c0, c1),
        total_two.reshape(3, 3, 3, c1, c2),
        bucket_sum.reshape(length),
    )


def solution(mesh):
    dp, space = (mesh.shape["dp"], mesh.shape["space"])
    split = Mesh(mesh.devices.reshape(dp // 2, 2, space // 2, 2), EVERY)
    volume = P(("z", "x"), SPACE, None, None, None)
    in_specs = (volume, volume, volume, P(), P(), P(EVERY, None))
    out_specs = (volume, P(), P(), P())
    return jax.shard_map(
        per_device, mesh=split, in_specs=in_specs, out_specs=out_specs, check_vma=False
    )
```

```python
import math

import jax
import jax.numpy as jnp
from jax import lax
from jax.experimental import pallas as pl
from jax.experimental.pallas import tpu as pltpu
from jax.sharding import Mesh, PartitionSpec as P

SPACE = ("y", "core")
COLUMN = ("z", "y")
SAME = ("x", "z", "y")
EVERY = ("z", "x", "y", "core")
GROUP = 8
LANES = 128
BF16 = jnp.bfloat16
F32 = jnp.float32


def ceil_to(value, step):
    return -(-value // step) * step


def slid(value, step):
    lane = lax.broadcasted_iota(jnp.int32, value.shape, 1)
    width = value.shape[1]
    keep = lane >= step if step > 0 else lane < width + step
    return jnp.where(keep, pltpu.roll(value, step % width, 1), 0.0)


def beside(window, rows, step, count):
    return jnp.concatenate([window[g * step : g * step + rows] for g in range(count)], axis=1)


def turned(src, flat, dst, offset, pitch, lead):
    chans, length, _ = src.shape

    def stage(c, carry):
        flat[pl.ds(pl.multiple_of(c * length, length), length), :] = src[c].astype(F32)
        return carry

    lax.fori_loop(0, chans, stage, 0, unroll=4)

    def gather(x, carry):
        rows = flat[pl.ds(x, chans, stride=length), :]
        at = pl.multiple_of((x + lead) * pitch + offset, 16)
        dst[pl.ds(at, chans), :] = rows.astype(BF16)
        return carry

    lax.fori_loop(0, length, gather, 0, unroll=4)


def pack_kernel(field, out, flat):
    chans, length, width = field.shape
    zeros = jnp.zeros((chans, width), BF16)
    out[0:chans, :] = zeros
    out[(length + 1) * chans : (length + 2) * chans, :] = zeros
    turned(field, flat, out, 0, chans, 1)


def pack(field):
    chans, length, width = field.shape
    return vmem_call(
        pack_kernel,
        jax.ShapeDtypeStruct(((length + 2) * chans, width), BF16),
        (pltpu.VMEM((chans * length, width), F32),),
        pl.CostEstimate(flops=0, bytes_accessed=16 * field.size, transcendentals=0),
    )(field)


def in_steps(body, rows, count=8):
    step = rows // count

    def one(n, carry):
        body(n * step, step)
        return carry

    lax.fori_loop(0, count, one, 0)


def cast_kernel(src, after, out):
    rows = out.shape[0]
    start = (1 - lax.axis_index("core")) * rows

    def cast(at, step):
        value = src[pl.ds(pl.multiple_of(start + at, 16), step), :]
        out[pl.ds(pl.multiple_of(at, 16), step), :] = value.astype(out.dtype)

    in_steps(cast, rows)


def cast(value, after):
    spec = pl.BlockSpec(memory_space=pltpu.VMEM)
    return pl.pallas_call(
        cast_kernel,
        out_shape=jax.ShapeDtypeStruct((value.shape[0] // 2, LANES), BF16),
        in_specs=[spec, pl.BlockSpec(memory_space=pl.ANY)],
        out_specs=spec,
        compiler_params=pltpu.CompilerParams(vmem_limit_bytes=24 * 2**20),
        cost_estimate=pl.CostEstimate(flops=0, bytes_accessed=4 * value.size, transcendentals=0),
    )(value, after)


def add_kernel(src, other, send, keep):
    half, rows = (other.shape[0], send.shape[0])
    start = lax.axis_index("core") * half
    mine = lax.axis_index("x") * rows
    theirs = rows - mine

    def total(at, step):
        value = src[pl.ds(pl.multiple_of(start + at, 16), step), :]
        return value + other[pl.ds(pl.multiple_of(at, 16), step), :].astype(F32)

    def add(at, step):
        to = pl.ds(pl.multiple_of(at, 16), step)
        send[to, :] = total(theirs + at, step).astype(send.dtype)
        keep[to, :] = total(mine + at, step)

    in_steps(add, rows)


def add(value, other):
    rows = other.shape[0] // 2
    return vmem_call(
        add_kernel,
        (jax.ShapeDtypeStruct((rows, LANES), BF16), jax.ShapeDtypeStruct((rows, LANES), F32)),
        (),
        pl.CostEstimate(flops=0, bytes_accessed=4 * value.size, transcendentals=0),
    )(value, other)


def combine_kernel(keep, other, terms, more, out):
    height, extra = (keep.shape[0] // out.shape[0], terms.shape[0] // out.shape[0])
    for n in range(out.shape[0]):
        at = slice(n * height, (n + 1) * height)
        out[n, 0:height, :] = (keep[at, :] + other[at, :].astype(F32)).astype(out.dtype)
        at = slice(n * extra, (n + 1) * extra)
        out[n, height : height + extra, :] = (terms[at, :] + more[at, :].astype(F32)).astype(out.dtype)


def combine(keep, other, terms, more, parts):
    rows = (keep.shape[0] + terms.shape[0]) // parts
    return vmem_call(
        combine_kernel,
        jax.ShapeDtypeStruct((parts, rows, LANES), BF16),
        (),
        pl.CostEstimate(flops=0, bytes_accessed=8 * keep.size, transcendentals=0),
    )(keep, other, terms, more)


def split_to(total, mine, send, keep):
    half = total.shape[0] // 2
    keep[...] = total[pl.ds(pl.multiple_of(mine * half, 16), half), :]
    send[...] = total[pl.ds(pl.multiple_of((1 - mine) * half, 16), half), :].astype(send.dtype)


def swapped(value, axis="core"):
    return lax.ppermute(value, axis, [(0, 1), (1, 0)])


def plane_order():
    core = lax.axis_index("core")
    ahead = [core * n + (1 - core) * (2 - n) for n in range(3)]
    back = [core * (2 - n) + (1 - core) * n for n in range(3)]
    return (ahead, back)


def windows(packs, x, count):
    rows = [
        [p[pl.ds(pl.multiple_of((x + n) * count, 16), count), :] for p in packs]
        for n in range(GROUP + 2)
    ]
    return jnp.concatenate(
        [jnp.concatenate(sum(rows[g : g + 3], []), axis=0) for g in range(GROUP)], axis=1
    )


def ordered(acc, count, ahead):
    blocks = [pl.multiple_of((3 * j + n) * count, 16) for j in range(3) for n in ahead]
    return jnp.concatenate([acc[pl.ds(at, count), :] for at in blocks], axis=0)


def across_lanes(first, second):
    return lax.dot_general(
        first, second, (((1,), (1,)), ((), ())), preferred_element_type=F32
    )


def first_kernel(pack_in, pack_0, pack_out, act, two, pres, terms, flat, acts, w_two, acc):
    c1, length, _ = act.shape
    c2 = two.shape[4]
    packs = (pack_in, pack_0, pack_out)
    ahead, back = plane_order()
    turned(act, flat, acts, 0, c1, 0)
    w_two[...] = jnp.concatenate(
        [
            jnp.concatenate([two[back[n], 2 - j, 2 - k].astype(F32) for k in range(3)], axis=0)
            for j in range(3)
            for n in range(3)
        ],
        axis=1,
    ).astype(BF16)
    stacked = 3 * c1
    pres[0:stacked, :] = jnp.zeros((stacked, LANES), BF16)
    pres[(length + 1) * stacked : (length + 2) * stacked, :] = jnp.zeros((stacked, LANES), BF16)
    acc[...] = jnp.zeros_like(acc)

    def body(step, carry):
        x = step * GROUP
        right = windows(packs, x, c2)
        sums = jnp.dot(w_two[...], right, preferred_element_type=F32)
        columns = []
        for g in range(GROUP):
            part = sums[:, g * LANES : (g + 1) * LANES]
            grad = slid(part[0:c1], 1) + part[c1 : 2 * c1] + slid(part[2 * c1 : 3 * c1], -1)
            value = acts[pl.ds(pl.multiple_of((x + g) * c1, 16), c1), :].astype(F32)
            pre = (grad * jnp.where(value > 0, 1.0, 0.2)).astype(BF16).astype(F32)
            moved = jnp.concatenate([slid(pre, -1), pre, slid(pre, 1)], axis=0).astype(BF16)
            pres[pl.ds(pl.multiple_of((x + g + 1) * stacked, 16), stacked), :] = moved
            stack = jnp.concatenate([slid(value, 1), value, slid(value, -1)], axis=0)
            columns.append(stack.astype(BF16))
        acc[...] += across_lanes(right, jnp.concatenate(columns, axis=1))
        return carry

    lax.fori_loop(0, length // GROUP, body, 0, unroll=4)

    terms[...] = jnp.zeros_like(terms)
    total = ordered(acc, c2, ahead).T
    rows, width = total.shape
    for block in range(-(-width // LANES)):
        part = total[:, block * LANES : min(width, (block + 1) * LANES)]
        terms[block * rows : (block + 1) * rows, 0 : part.shape[1]] = part


def second_kernel(
    pack_in, pack_0, pack_out, pres, one, before,
    send, keep, own, inner, outer,
    w_one, acc, terms,
):
    c0, c1 = one.shape[3:]
    packs = (pack_in, pack_0, pack_out)
    ahead, _ = plane_order()
    stacked = 3 * c1
    length = pres.shape[0] // stacked - 2
    w_one[...] = jnp.concatenate(
        [
            jnp.concatenate([one[ahead[n], 2 - j, k].astype(F32) for n in range(3)], axis=0)
            for j in range(3)
            for k in range(3)
        ],
        axis=1,
    ).astype(BF16)
    acc[...] = jnp.zeros_like(acc)

    def body(step, carry):
        x = step * GROUP
        window = pres[pl.ds(pl.multiple_of(x * stacked, 16), (GROUP + 2) * stacked), :]
        moved = beside(window, 3 * stacked, stacked, GROUP)
        sums = jnp.dot(w_one[...], moved, preferred_element_type=F32)
        for g in range(GROUP):
            part = sums[:, g * LANES : (g + 1) * LANES]
            at = pl.ds(pl.multiple_of((x + g) * c0, 16), c0)
            for i, out in ((0, inner), (1, own), (2, outer)):
                out[at, :] = part[i * c0 : (i + 1) * c0].astype(out.dtype)
        acc[...] += across_lanes(windows(packs, x, c0), moved[stacked : 2 * stacked])
        return carry

    lax.fori_loop(0, length // GROUP, body, 0, unroll=4)

    used = before.shape[0]
    terms[0:used, :] = before[...]
    terms[used:, :] = jnp.zeros((terms.shape[0] - used, LANES), F32)
    total = ordered(acc, c0, ahead)
    terms[used : used + total.shape[0], 0 : total.shape[1]] = total
    split_to(terms, lax.axis_index("core"), send, keep)


def vmem_call(body, out_shape, scratch=(), cost=None, limit=24 * 2**20):
    spec = pl.BlockSpec(memory_space=pltpu.VMEM)
    return pl.pallas_call(
        body,
        out_shape=out_shape,
        out_specs=jax.tree.map(lambda _: spec, out_shape),
        scratch_shapes=list(scratch),
        compiler_params=pltpu.CompilerParams(vmem_limit_bytes=limit),
        cost_estimate=cost,
    )


def first_part(packs, act, kernel_two):
    c1, length, width = act.shape
    c2 = kernel_two.shape[4]
    return vmem_call(
        first_kernel,
        (
            jax.ShapeDtypeStruct(((length + 2) * 3 * c1, width), BF16),
            jax.ShapeDtypeStruct((-(-9 * c2 // LANES) * 3 * c1, LANES), F32),
        ),
        (
            pltpu.VMEM((c1 * length, width), F32),
            pltpu.VMEM((c1 * length, width), BF16),
            pltpu.VMEM((3 * c1, 9 * c2), BF16),
            pltpu.VMEM((9 * c2, 3 * c1), F32),
        ),
        pl.CostEstimate(flops=10**9, bytes_accessed=20 * 2**20, transcendentals=0),
    )(*packs, act, kernel_two)


def second_part(packs, pres, kernel_one, terms, rows):
    c0, c1 = kernel_one.shape[3:]
    length, width = (pres.shape[0] // (3 * c1) - 2, pres.shape[1])
    plane = (length * c0, width)
    return vmem_call(
        second_kernel,
        (
            jax.ShapeDtypeStruct((rows // 2, LANES), BF16),
            jax.ShapeDtypeStruct((rows // 2, LANES), F32),
            jax.ShapeDtypeStruct(plane, F32),
            jax.ShapeDtypeStruct(plane, BF16),
            jax.ShapeDtypeStruct(plane, BF16),
        ),
        (
            pltpu.VMEM((3 * c0, 9 * c1), BF16),
            pltpu.VMEM((9 * c0, 3 * c1), F32),
            pltpu.VMEM((rows, LANES), F32),
        ),
        pl.CostEstimate(flops=10**9, bytes_accessed=10 * 2**20, transcendentals=0),
    )(*packs, pres, kernel_one, terms)


def merge_kernel(own, first, second, out, flat):
    chans, length, _ = out.shape

    def add(step, carry):
        at = pl.ds(pl.multiple_of(step * 64, 64), 64)
        flat[at, :] = own[at, :] + first[at, :].astype(F32) + second[at, :].astype(F32)
        return carry

    lax.fori_loop(0, own.shape[0] // 64, add, 0, unroll=4)

    def gather(c, carry):
        out[c] = flat[pl.ds(c, length, stride=chans), :].astype(out.dtype)
        return carry

    lax.fori_loop(0, chans, gather, 0, unroll=4)


def merge(own, first, second, shape):
    return vmem_call(
        merge_kernel,
        jax.ShapeDtypeStruct(shape, BF16),
        (pltpu.VMEM(own.shape, F32),),
        pl.CostEstimate(flops=2 * own.size, bytes_accessed=8 * own.size, transcendentals=0),
    )(own, first, second)


def share_kernel(scale, height, parts, out):
    total = jnp.sum(parts[:, 0:height, :].astype(F32), axis=0).astype(BF16)
    rows = parts.shape[1]
    grads = (jnp.sum(parts[:, height:rows, :].astype(F32), axis=0) * scale).astype(BF16)

    def write(n, carry):
        out[n, 0:height, :] = total
        out[n, height:rows, :] = grads
        return carry

    lax.fori_loop(0, out.shape[0], write, 0)


def share(parts, height, scale, copies):
    return vmem_call(
        lambda *refs: share_kernel(scale, height, *refs),
        jax.ShapeDtypeStruct((copies,) + parts.shape[1:], BF16),
        (),
        pl.CostEstimate(flops=parts.size, bytes_accessed=6 * parts.size, transcendentals=0),
    )(parts)


def place(source, height, which, bucket, buffer, sems):
    copies, count = (source.shape[0], sems.shape[0])
    size = copies * height
    step = copies // count
    sent = []
    for n in range(count):
        for q in range(n * step, (n + 1) * step):
            buffer[q * height : (q + 1) * height, :] = source[q, 0:height, :].astype(F32)
        rows = pl.ds(n * step * height, step * height)
        at = pl.ds(pl.multiple_of(which * size + n * step * height, 8), step * height)
        sent.append(pltpu.make_async_copy(buffer.at[rows], bucket.at[at], sems.at[n]))
        sent[-1].start()
    return sent


def start_kernel(height, mine, bucket, buffer, sems):
    for copy in place(mine, height, lax.axis_index("core"), bucket, buffer, sems):
        copy.wait()


def finish_kernel(
    sizes, height, mine, other, partial,
    bucket, out_one, out_two,
    raw, one, two, out_sems, buffer, sems,
):
    c0, c1, c2 = sizes
    copies, rows, _ = mine.shape
    extra = rows - height
    me = lax.axis_index("core")
    sent = place(other, height, 1 - me, bucket, buffer, sems)

    column = copies // 2
    for q in range(column):
        for source, which in ((mine, me), (other, 1 - me)):
            at = pl.multiple_of((which * column + q) * extra, 8)
            near = source[q, height:rows, :].astype(F32)
            raw[pl.ds(at, extra), :] = near + source[column + q, height:rows, :].astype(F32)
    block = 3 * c1
    first = -(-9 * c2 // LANES) * block
    for i in range(3):
        for j in range(3):
            column = ((2 - j) * 3 + 2 - i) * c2
            whole, lane = (column // LANES, column % LANES)
            two[(3 * i + j) * block : (3 * i + j + 1) * block, :] = raw[
                whole * block : (whole + 1) * block, lane : lane + c2
            ]
        at = pl.ds(3 * i * block, 3 * block)
        sent.append(pltpu.make_async_copy(two.at[at], out_two.at[at], out_sems.at[i]))
        sent[-1].start()
    for i in range(3):
        for j in range(3):
            row = first + (3 * j + i) * c0
            for k in range(3):
                to = (9 * i + 3 * j + k) * c0
                one[to : to + c0, :] = raw[row : row + c0, k * c1 : (k + 1) * c1]
        at = pl.ds(9 * i * c0, 9 * c0)
        sent.append(pltpu.make_async_copy(one.at[at], out_one.at[at], out_sems.at[3 + i]))
        sent[-1].start()
    for copy in sent:
        copy.wait()


def finish(mine, other, length, sizes):
    c0, c1, c2 = sizes
    copies, rows, _ = mine.shape
    height = length // LANES // (2 * copies)
    spec = pl.BlockSpec(memory_space=pltpu.VMEM)
    remote = pl.BlockSpec(memory_space=pltpu.HBM)
    whole = jax.ShapeDtypeStruct((length // LANES, LANES), F32)
    chunks = 4
    scratch = [
        pltpu.VMEM((copies * height, LANES), F32),
        pltpu.SemaphoreType.DMA((chunks,)),
    ]
    params = pltpu.CompilerParams(vmem_limit_bytes=24 * 2**20)
    partial = pl.pallas_call(
        lambda *refs: start_kernel(height, *refs),
        out_shape=whole,
        in_specs=[spec],
        out_specs=remote,
        scratch_shapes=scratch,
        compiler_params=params,
    )(mine)
    return pl.pallas_call(
        lambda *refs: finish_kernel(sizes, height, *refs),
        out_shape=(
            whole,
            jax.ShapeDtypeStruct((27 * c0, c1), F32),
            jax.ShapeDtypeStruct((27 * c1, c2), F32),
        ),
        in_specs=[spec, spec, remote],
        out_specs=(remote, remote, remote),
        scratch_shapes=[
            pltpu.VMEM((copies * (rows - height), LANES), F32),
            pltpu.VMEM((27 * c0, c1), F32),
            pltpu.VMEM((27 * c1, c2), F32),
            pltpu.SemaphoreType.DMA((6,)),
        ]
        + scratch,
        input_output_aliases={2: 0},
        compiler_params=params,
    )(mine, other, partial)


def crossed(value):
    pairs = [(n, n + 1) for n in range(1, lax.axis_size(SPACE) - 1, 2)]
    return lax.ppermute(value, SPACE, pairs + [(m, n) for n, m in pairs])


def per_device(volume_in, hidden_act, out_cot, kernel_one, kernel_two, grad_bucket):
    c0, c1, c2 = (volume_in.shape[2], hidden_act.shape[2], out_cot.shape[2])
    devices, copies, column = (lax.axis_size(EVERY), lax.axis_size(SAME), lax.axis_size(COLUMN))
    length = grad_bucket.shape[1]
    bucket = grad_bucket.reshape(length // LANES, LANES)
    cot = pack(out_cot[0, 0])
    cots = (swapped(cot), cot, crossed(cot))
    vol = pack(volume_in[0, 0])
    vols = (swapped(vol), vol, crossed(vol))
    send, near = add(bucket, swapped(cast(bucket, cot)))
    act, send, near = lax.optimization_barrier((hidden_act[0, 0], send, near))
    far = swapped(send, "x")

    used = -(-9 * c2 // LANES) * 3 * c1 + 9 * c0
    rows = ceil_to(used, 16 * 2 * column)
    pres, terms = first_part(cots, act, kernel_two)
    send, keep, own, inner, outer = second_part(vols, pres, kernel_one, terms, rows)
    parts = combine(near, far, keep, swapped(send), column)
    parts, inner, outer = lax.optimization_barrier((parts, inner, outer))
    parts = lax.all_to_all(parts, COLUMN, 0, 0)
    grad_input = merge(own, swapped(inner), crossed(outer), volume_in.shape[2:])
    parts, grad_input = lax.optimization_barrier((parts, grad_input))
    cells = volume_in.shape[3] * volume_in.shape[4] * devices
    height = length // LANES // devices
    shares = share(parts, height, 1.0 / math.sqrt(cells), copies)

    mine = lax.all_to_all(shares, SAME, 0, 0)
    bucket_sum, total_one, total_two = finish(mine, swapped(mine), length, (c0, c1, c2))
    return (
        grad_input[None, None],
        total_one.reshape(3, 3, 3, c0, c1),
        total_two.reshape(3, 3, 3, c1, c2),
        bucket_sum.reshape(length),
    )


def solution(mesh):
    dp, space = (mesh.shape["dp"], mesh.shape["space"])
    split = Mesh(mesh.devices.reshape(dp // 2, 2, space // 2, 2), EVERY)
    volume = P(("z", "x"), SPACE, None, None, None)
    in_specs = (volume, volume, volume, P(), P(), P(EVERY, None))
    out_specs = (volume, P(), P(), P())
    return jax.shard_map(
        per_device, mesh=split, in_specs=in_specs, out_specs=out_specs, check_vma=False
    )
```

```python
import math

import jax
import jax.numpy as jnp
from jax import lax
from jax.experimental import pallas as pl
from jax.experimental.pallas import tpu as pltpu
from jax.sharding import Mesh, PartitionSpec as P

SPACE = ("y", "core")
SAME = ("x", "z", "y")
EVERY = ("z", "x", "y", "core")
GROUP = 8
LANES = 128
BF16 = jnp.bfloat16
F32 = jnp.float32


def ceil_to(value, step):
    return -(-value // step) * step


def slid(value, step):
    lane = lax.broadcasted_iota(jnp.int32, value.shape, 1)
    width = value.shape[1]
    keep = lane >= step if step > 0 else lane < width + step
    return jnp.where(keep, pltpu.roll(value, step % width, 1), 0.0)


def beside(window, rows, step, count):
    return jnp.concatenate([window[g * step : g * step + rows] for g in range(count)], axis=1)


def turned(src, flat, dst, offset, pitch, lead):
    chans, length, _ = src.shape

    def stage(c, carry):
        flat[pl.ds(pl.multiple_of(c * length, length), length), :] = src[c].astype(F32)
        return carry

    lax.fori_loop(0, chans, stage, 0, unroll=4)

    def gather(x, carry):
        rows = flat[pl.ds(x, chans, stride=length), :]
        at = pl.multiple_of((x + lead) * pitch + offset, 16)
        dst[pl.ds(at, chans), :] = rows.astype(BF16)
        return carry

    lax.fori_loop(0, length, gather, 0, unroll=4)


def pack_kernel(field, out, flat):
    chans, length, width = field.shape
    zeros = jnp.zeros((chans, width), BF16)
    out[0:chans, :] = zeros
    out[(length + 1) * chans : (length + 2) * chans, :] = zeros
    turned(field, flat, out, 0, chans, 1)


def pack(field):
    chans, length, width = field.shape
    return vmem_call(
        pack_kernel,
        jax.ShapeDtypeStruct(((length + 2) * chans, width), BF16),
        (pltpu.VMEM((chans * length, width), F32),),
        pl.CostEstimate(flops=0, bytes_accessed=16 * field.size, transcendentals=0),
    )(field)


def in_steps(body, rows, count=8):
    step = rows // count

    def one(n, carry):
        body(n * step, step)
        return carry

    lax.fori_loop(0, count, one, 0)


def cast_kernel(src, after, out):
    rows = out.shape[0]
    start = (1 - lax.axis_index("core")) * rows

    def cast(at, step):
        value = src[pl.ds(pl.multiple_of(start + at, 16), step), :]
        out[pl.ds(pl.multiple_of(at, 16), step), :] = value.astype(out.dtype)

    in_steps(cast, rows)


def cast(value, after):
    spec = pl.BlockSpec(memory_space=pltpu.VMEM)
    return pl.pallas_call(
        cast_kernel,
        out_shape=jax.ShapeDtypeStruct((value.shape[0] // 2, LANES), BF16),
        in_specs=[spec, pl.BlockSpec(memory_space=pl.ANY)],
        out_specs=spec,
        compiler_params=pltpu.CompilerParams(vmem_limit_bytes=24 * 2**20),
        cost_estimate=pl.CostEstimate(flops=0, bytes_accessed=4 * value.size, transcendentals=0),
    )(value, after)


def add_kernel(src, other, send, keep):
    half, rows = (other.shape[0], send.shape[0])
    start = lax.axis_index("core") * half
    mine = lax.axis_index("x") * rows
    theirs = rows - mine

    def total(at, step):
        value = src[pl.ds(pl.multiple_of(start + at, 16), step), :]
        return value + other[pl.ds(pl.multiple_of(at, 16), step), :].astype(F32)

    def add(at, step):
        to = pl.ds(pl.multiple_of(at, 16), step)
        send[to, :] = total(theirs + at, step).astype(send.dtype)
        keep[to, :] = total(mine + at, step)

    in_steps(add, rows)


def add(value, other):
    rows = other.shape[0] // 2
    return vmem_call(
        add_kernel,
        (jax.ShapeDtypeStruct((rows, LANES), BF16), jax.ShapeDtypeStruct((rows, LANES), F32)),
        (),
        pl.CostEstimate(flops=0, bytes_accessed=4 * value.size, transcendentals=0),
    )(value, other)


def combine_kernel(keep, other, terms, more, out):
    parts, rows, _ = out.shape
    height, extra = (keep.shape[0] // parts, terms.shape[0] // parts)
    padded = rows - extra
    total = keep[...] + other[...].astype(F32)
    grads = terms[...] + more[...].astype(F32)
    for n in range(parts):
        value = total[n * height : (n + 1) * height]
        if padded > height:
            value = jnp.concatenate([value, jnp.zeros((padded - height, LANES), F32)], axis=0)
        out[n, 0:padded, :] = value.astype(out.dtype)
        out[n, padded:rows, :] = grads[n * extra : (n + 1) * extra].astype(out.dtype)


def combine(keep, other, terms, more, parts):
    rows = ceil_to(keep.shape[0] // parts, 16) + terms.shape[0] // parts
    return vmem_call(
        combine_kernel,
        jax.ShapeDtypeStruct((parts, rows, LANES), BF16),
        (),
        pl.CostEstimate(flops=0, bytes_accessed=8 * keep.size, transcendentals=0),
    )(keep, other, terms, more)


def split_to(total, mine, send, keep):
    half = total.shape[0] // 2
    keep[...] = total[pl.ds(pl.multiple_of(mine * half, 16), half), :]
    send[...] = total[pl.ds(pl.multiple_of((1 - mine) * half, 16), half), :].astype(send.dtype)


def swapped(value, axis="core"):
    return lax.ppermute(value, axis, [(0, 1), (1, 0)])


def plane_order():
    core = lax.axis_index("core")
    ahead = [core * n + (1 - core) * (2 - n) for n in range(3)]
    back = [core * (2 - n) + (1 - core) * n for n in range(3)]
    return (ahead, back)


def windows(packs, x, count):
    rows = [
        [p[pl.ds(pl.multiple_of((x + n) * count, 16), count), :] for p in packs]
        for n in range(GROUP + 2)
    ]
    return jnp.concatenate(
        [jnp.concatenate(sum(rows[g : g + 3], []), axis=0) for g in range(GROUP)], axis=1
    )


def ordered(acc, count, ahead):
    blocks = [pl.multiple_of((3 * j + n) * count, 16) for j in range(3) for n in ahead]
    return jnp.concatenate([acc[pl.ds(at, count), :] for at in blocks], axis=0)


def across_lanes(first, second):
    return lax.dot_general(
        first, second, (((1,), (1,)), ((), ())), preferred_element_type=F32
    )


def prepare_kernel(act, two, one, acts, w_two, w_one, flat):
    ahead, back = plane_order()
    turned(act, flat, acts, 0, act.shape[0], 0)
    w_two[...] = jnp.concatenate(
        [
            jnp.concatenate([two[back[n], 2 - j, 2 - k].astype(F32) for k in range(3)], axis=0)
            for j in range(3)
            for n in range(3)
        ],
        axis=1,
    ).astype(BF16)
    w_one[...] = jnp.concatenate(
        [
            jnp.concatenate([one[ahead[n], 2 - j, k].astype(F32) for n in range(3)], axis=0)
            for j in range(3)
            for k in range(3)
        ],
        axis=1,
    ).astype(BF16)


def prepare(act, kernel_two, kernel_one):
    c1, length, width = act.shape
    c0, c2 = (kernel_one.shape[3], kernel_two.shape[4])
    return vmem_call(
        prepare_kernel,
        (
            jax.ShapeDtypeStruct((length * c1, width), BF16),
            jax.ShapeDtypeStruct((3 * c1, 9 * c2), BF16),
            jax.ShapeDtypeStruct((3 * c0, 9 * c1), BF16),
        ),
        (pltpu.VMEM((c1 * length, width), F32),),
        pl.CostEstimate(flops=0, bytes_accessed=16 * act.size, transcendentals=0),
    )(act, kernel_two, kernel_one)


def first_kernel(pack_in, pack_0, pack_out, acts, w_two, pres, terms, acc):
    c1, c2 = (w_two.shape[0] // 3, w_two.shape[1] // 9)
    length = acts.shape[0] // c1
    packs = (pack_in, pack_0, pack_out)
    ahead, _ = plane_order()
    stacked = 3 * c1
    pres[0:stacked, :] = jnp.zeros((stacked, LANES), BF16)
    pres[(length + 1) * stacked : (length + 2) * stacked, :] = jnp.zeros((stacked, LANES), BF16)
    acc[...] = jnp.zeros_like(acc)

    def body(step, carry):
        x = step * GROUP
        right = windows(packs, x, c2)
        sums = jnp.dot(w_two[...], right, preferred_element_type=F32)
        columns = []
        for g in range(GROUP):
            part = sums[:, g * LANES : (g + 1) * LANES]
            grad = slid(part[0:c1], 1) + part[c1 : 2 * c1] + slid(part[2 * c1 : 3 * c1], -1)
            value = acts[pl.ds(pl.multiple_of((x + g) * c1, 16), c1), :].astype(F32)
            pre = (grad * jnp.where(value > 0, 1.0, 0.2)).astype(BF16).astype(F32)
            moved = jnp.concatenate([slid(pre, -1), pre, slid(pre, 1)], axis=0).astype(BF16)
            pres[pl.ds(pl.multiple_of((x + g + 1) * stacked, 16), stacked), :] = moved
            stack = jnp.concatenate([slid(value, 1), value, slid(value, -1)], axis=0)
            columns.append(stack.astype(BF16))
        acc[...] += across_lanes(right, jnp.concatenate(columns, axis=1))
        return carry

    lax.fori_loop(0, length // GROUP, body, 0, unroll=4)

    terms[...] = jnp.zeros_like(terms)
    total = ordered(acc, c2, ahead).T
    rows, width = total.shape
    for block in range(-(-width // LANES)):
        part = total[:, block * LANES : min(width, (block + 1) * LANES)]
        terms[block * rows : (block + 1) * rows, 0 : part.shape[1]] = part


def second_kernel(
    pack_in, pack_0, pack_out, pres, w_one, before,
    send, keep, own, inner, outer,
    acc, terms,
):
    c0, c1 = (w_one.shape[0] // 3, w_one.shape[1] // 9)
    packs = (pack_in, pack_0, pack_out)
    ahead, _ = plane_order()
    stacked = 3 * c1
    length = pres.shape[0] // stacked - 2
    acc[...] = jnp.zeros_like(acc)

    def body(step, carry):
        x = step * GROUP
        window = pres[pl.ds(pl.multiple_of(x * stacked, 16), (GROUP + 2) * stacked), :]
        moved = beside(window, 3 * stacked, stacked, GROUP)
        sums = jnp.dot(w_one[...], moved, preferred_element_type=F32)
        for g in range(GROUP):
            part = sums[:, g * LANES : (g + 1) * LANES]
            at = pl.ds(pl.multiple_of((x + g) * c0, 16), c0)
            for i, out in ((0, inner), (1, own), (2, outer)):
                out[at, :] = part[i * c0 : (i + 1) * c0].astype(out.dtype)
        acc[...] += across_lanes(windows(packs, x, c0), moved[stacked : 2 * stacked])
        return carry

    lax.fori_loop(0, length // GROUP, body, 0, unroll=4)

    used = before.shape[0]
    terms[0:used, :] = before[...]
    terms[used:, :] = jnp.zeros((terms.shape[0] - used, LANES), F32)
    total = ordered(acc, c0, ahead)
    terms[used : used + total.shape[0], 0 : total.shape[1]] = total
    split_to(terms, lax.axis_index("core"), send, keep)


def vmem_call(body, out_shape, scratch=(), cost=None, limit=24 * 2**20):
    spec = pl.BlockSpec(memory_space=pltpu.VMEM)
    return pl.pallas_call(
        body,
        out_shape=out_shape,
        out_specs=jax.tree.map(lambda _: spec, out_shape),
        scratch_shapes=list(scratch),
        compiler_params=pltpu.CompilerParams(vmem_limit_bytes=limit),
        cost_estimate=cost,
    )


def first_part(packs, acts, w_two):
    c1, c2, width = (w_two.shape[0] // 3, w_two.shape[1] // 9, acts.shape[1])
    length = acts.shape[0] // c1
    return vmem_call(
        first_kernel,
        (
            jax.ShapeDtypeStruct(((length + 2) * 3 * c1, width), BF16),
            jax.ShapeDtypeStruct((-(-9 * c2 // LANES) * 3 * c1, LANES), F32),
        ),
        (pltpu.VMEM((9 * c2, 3 * c1), F32),),
        pl.CostEstimate(flops=10**9, bytes_accessed=20 * 2**20, transcendentals=0),
    )(*packs, acts, w_two)


def second_part(packs, pres, w_one, terms, rows):
    c0, c1 = (w_one.shape[0] // 3, w_one.shape[1] // 9)
    length, width = (pres.shape[0] // (3 * c1) - 2, pres.shape[1])
    plane = (length * c0, width)
    return vmem_call(
        second_kernel,
        (
            jax.ShapeDtypeStruct((rows // 2, LANES), BF16),
            jax.ShapeDtypeStruct((rows // 2, LANES), F32),
            jax.ShapeDtypeStruct(plane, F32),
            jax.ShapeDtypeStruct(plane, BF16),
            jax.ShapeDtypeStruct(plane, BF16),
        ),
        (
            pltpu.VMEM((9 * c0, 3 * c1), F32),
            pltpu.VMEM((rows, LANES), F32),
        ),
        pl.CostEstimate(flops=10**9, bytes_accessed=10 * 2**20, transcendentals=0),
    )(*packs, pres, w_one, terms)


def merge_kernel(own, first, second, out, flat):
    chans, length, _ = out.shape

    def add(step, carry):
        at = pl.ds(pl.multiple_of(step * 64, 64), 64)
        flat[at, :] = own[at, :] + first[at, :].astype(F32) + second[at, :].astype(F32)
        return carry

    lax.fori_loop(0, own.shape[0] // 64, add, 0, unroll=4)

    def gather(c, carry):
        out[c] = flat[pl.ds(c, length, stride=chans), :].astype(out.dtype)
        return carry

    lax.fori_loop(0, chans, gather, 0, unroll=4)


def merge(own, first, second, shape):
    return vmem_call(
        merge_kernel,
        jax.ShapeDtypeStruct(shape, BF16),
        (pltpu.VMEM(own.shape, F32),),
        pl.CostEstimate(flops=2 * own.size, bytes_accessed=8 * own.size, transcendentals=0),
    )(own, first, second)


def share_kernel(scale, parts, out):
    copies, rows, _ = parts.shape
    padded = out.shape[1] - rows
    near = jnp.sum(parts[0 : copies // 2, 0:padded, :].astype(F32), axis=0).astype(BF16)
    far = jnp.sum(parts[copies // 2 :, 0:padded, :].astype(F32), axis=0).astype(BF16)
    grads = (jnp.sum(parts[:, padded:rows, :].astype(F32), axis=0) * scale).astype(BF16)

    def write(n, carry):
        out[n, 0:padded, :] = near
        out[n, padded : 2 * padded, :] = far
        out[n, 2 * padded :, :] = grads
        return carry

    lax.fori_loop(0, copies, write, 0)


def share(parts, extra, scale):
    copies, rows, _ = parts.shape
    return vmem_call(
        lambda *refs: share_kernel(scale, *refs),
        jax.ShapeDtypeStruct((copies, 2 * rows - extra, LANES), BF16),
        (),
        pl.CostEstimate(flops=parts.size, bytes_accessed=6 * parts.size, transcendentals=0),
    )(parts)


def place(source, height, padded, which, bucket, buffer, sems):
    copies, count = (source.shape[0], sems.shape[0])
    step = 2 * copies // count
    sent = []
    for n in range(count):
        for m in range(n * step, (n + 1) * step):
            half, q = (m // copies, m % copies)
            value = source[q, half * padded : (half + 1) * padded, :].astype(F32)
            buffer[m * height : (m + 1) * height, :] = value[0:height]
        rows = pl.ds(n * step * height, step * height)
        at = (which * count + n) * step * height
        at = pl.ds(pl.multiple_of(at, 8), step * height)
        sent.append(pltpu.make_async_copy(buffer.at[rows], bucket.at[at], sems.at[n]))
        sent[-1].start()
    return sent


def start_kernel(height, padded, mine, bucket, buffer, sems):
    for copy in place(mine, height, padded, lax.axis_index("core"), bucket, buffer, sems):
        copy.wait()


def finish_kernel(
    sizes, height, padded, mine, other, partial,
    bucket, out_one, out_two,
    raw, one, two, out_sems, buffer, sems,
):
    c0, c1, c2 = sizes
    copies, rows, _ = mine.shape
    extra = rows - 2 * padded
    me = lax.axis_index("core")
    sent = place(other, height, padded, 1 - me, bucket, buffer, sems)

    for q in range(copies):
        for source, which in ((mine, me), (other, 1 - me)):
            at = pl.multiple_of((which * copies + q) * extra, 8)
            raw[pl.ds(at, extra), :] = source[q, 2 * padded : rows, :].astype(F32)
    block = 3 * c1
    first = -(-9 * c2 // LANES) * block
    for i in range(3):
        for j in range(3):
            column = ((2 - j) * 3 + 2 - i) * c2
            whole, lane = (column // LANES, column % LANES)
            two[(3 * i + j) * block : (3 * i + j + 1) * block, :] = raw[
                whole * block : (whole + 1) * block, lane : lane + c2
            ]
        at = pl.ds(3 * i * block, 3 * block)
        sent.append(pltpu.make_async_copy(two.at[at], out_two.at[at], out_sems.at[i]))
        sent[-1].start()
    for i in range(3):
        for j in range(3):
            row = first + (3 * j + i) * c0
            for k in range(3):
                to = (9 * i + 3 * j + k) * c0
                one[to : to + c0, :] = raw[row : row + c0, k * c1 : (k + 1) * c1]
        at = pl.ds(9 * i * c0, 9 * c0)
        sent.append(pltpu.make_async_copy(one.at[at], out_one.at[at], out_sems.at[3 + i]))
        sent[-1].start()
    for copy in sent:
        copy.wait()


def finish(mine, other, length, sizes):
    c0, c1, c2 = sizes
    copies, rows, _ = mine.shape
    height = length // LANES // (4 * copies)
    padded = ceil_to(height, 16)
    spec = pl.BlockSpec(memory_space=pltpu.VMEM)
    remote = pl.BlockSpec(memory_space=pltpu.HBM)
    whole = jax.ShapeDtypeStruct((length // LANES, LANES), F32)
    chunks = 4
    scratch = [
        pltpu.VMEM((2 * copies * height, LANES), F32),
        pltpu.SemaphoreType.DMA((chunks,)),
    ]
    params = pltpu.CompilerParams(vmem_limit_bytes=24 * 2**20)
    partial = pl.pallas_call(
        lambda *refs: start_kernel(height, padded, *refs),
        out_shape=whole,
        in_specs=[spec],
        out_specs=remote,
        scratch_shapes=scratch,
        compiler_params=params,
    )(mine)
    return pl.pallas_call(
        lambda *refs: finish_kernel(sizes, height, padded, *refs),
        out_shape=(
            whole,
            jax.ShapeDtypeStruct((27 * c0, c1), F32),
            jax.ShapeDtypeStruct((27 * c1, c2), F32),
        ),
        in_specs=[spec, spec, remote],
        out_specs=(remote, remote, remote),
        scratch_shapes=[
            pltpu.VMEM((2 * copies * (rows - 2 * padded), LANES), F32),
            pltpu.VMEM((27 * c0, c1), F32),
            pltpu.VMEM((27 * c1, c2), F32),
            pltpu.SemaphoreType.DMA((6,)),
        ]
        + scratch,
        input_output_aliases={2: 0},
        compiler_params=params,
    )(mine, other, partial)


def crossed(value):
    pairs = [(n, n + 1) for n in range(1, lax.axis_size(SPACE) - 1, 2)]
    return lax.ppermute(value, SPACE, pairs + [(m, n) for n, m in pairs])


def per_device(volume_in, hidden_act, out_cot, kernel_one, kernel_two, grad_bucket):
    c0, c1, c2 = (volume_in.shape[2], hidden_act.shape[2], out_cot.shape[2])
    devices, copies = (lax.axis_size(EVERY), lax.axis_size(SAME))
    length = grad_bucket.shape[1]
    bucket = grad_bucket.reshape(length // LANES, LANES)
    cot = pack(out_cot[0, 0])
    cots = (swapped(cot), cot, crossed(cot))
    vol = pack(volume_in[0, 0])
    vols = (swapped(vol), vol, crossed(vol))
    send, near = add(bucket, swapped(cast(bucket, cot)))
    act, send, near = lax.optimization_barrier((hidden_act[0, 0], send, near))
    far = swapped(send, "x")

    used = -(-9 * c2 // LANES) * 3 * c1 + 9 * c0
    rows = ceil_to(used, 16 * devices)
    acts, w_two, w_one = prepare(act, kernel_two, kernel_one)
    pres, terms = first_part(cots, acts, w_two)
    send, keep, own, inner, outer = second_part(vols, pres, w_one, terms, rows)
    parts = combine(near, far, keep, swapped(send), copies)
    parts, inner, outer = lax.optimization_barrier((parts, inner, outer))
    parts = lax.all_to_all(parts, SAME, 0, 0)
    grad_input = merge(own, swapped(inner), crossed(outer), volume_in.shape[2:])
    parts, grad_input = lax.optimization_barrier((parts, grad_input))
    cells = volume_in.shape[3] * volume_in.shape[4] * devices
    shares = share(parts, rows // devices, 1.0 / math.sqrt(cells))

    mine = lax.all_to_all(shares, SAME, 0, 0)
    bucket_sum, total_one, total_two = finish(mine, swapped(mine), length, (c0, c1, c2))
    return (
        grad_input[None, None],
        total_one.reshape(3, 3, 3, c0, c1),
        total_two.reshape(3, 3, 3, c1, c2),
        bucket_sum.reshape(length),
    )


def solution(mesh):
    dp, space = (mesh.shape["dp"], mesh.shape["space"])
    split = Mesh(mesh.devices.reshape(dp // 2, 2, space // 2, 2), EVERY)
    volume = P(("z", "x"), SPACE, None, None, None)
    in_specs = (volume, volume, volume, P(), P(), P(EVERY, None))
    out_specs = (volume, P(), P(), P())
    return jax.shard_map(
        per_device, mesh=split, in_specs=in_specs, out_specs=out_specs, check_vma=False
    )
```

```python
import math

import jax
import jax.numpy as jnp
from jax import lax
from jax.experimental import pallas as pl
from jax.experimental.pallas import tpu as pltpu
from jax.sharding import Mesh, PartitionSpec as P

SPACE = ("y", "core")
SAME = ("x", "z", "y")
EVERY = ("z", "x", "y", "core")
GROUP = 8
LANES = 128
BF16 = jnp.bfloat16
F32 = jnp.float32


def ceil_to(value, step):
    return -(-value // step) * step


def slid(value, step):
    lane = lax.broadcasted_iota(jnp.int32, value.shape, 1)
    width = value.shape[1]
    keep = lane >= step if step > 0 else lane < width + step
    return jnp.where(keep, pltpu.roll(value, step % width, 1), 0.0)


def beside(window, rows, step, count):
    return jnp.concatenate([window[g * step : g * step + rows] for g in range(count)], axis=1)


def turned(src, flat, dst, offset, pitch, lead):
    chans, length, _ = src.shape

    def stage(c, carry):
        flat[pl.ds(pl.multiple_of(c * length, length), length), :] = src[c].astype(F32)
        return carry

    lax.fori_loop(0, chans, stage, 0, unroll=4)

    def gather(x, carry):
        rows = flat[pl.ds(x, chans, stride=length), :]
        at = pl.multiple_of((x + lead) * pitch + offset, 16)
        dst[pl.ds(at, chans), :] = rows.astype(BF16)
        return carry

    lax.fori_loop(0, length, gather, 0, unroll=4)


def pack_kernel(field, out, flat):
    chans, length, width = field.shape
    zeros = jnp.zeros((chans, width), BF16)
    out[0:chans, :] = zeros
    out[(length + 1) * chans : (length + 2) * chans, :] = zeros
    turned(field, flat, out, 0, chans, 1)


def pack(field):
    chans, length, width = field.shape
    return vmem_call(
        pack_kernel,
        jax.ShapeDtypeStruct(((length + 2) * chans, width), BF16),
        (pltpu.VMEM((chans * length, width), F32),),
        pl.CostEstimate(flops=0, bytes_accessed=16 * field.size, transcendentals=0),
    )(field)


def in_steps(body, rows, count=8):
    step = rows // count

    def one(n, carry):
        body(n * step, step)
        return carry

    lax.fori_loop(0, count, one, 0)


def cast_kernel(src, after, out):
    rows = out.shape[0]
    start = (1 - lax.axis_index("core")) * rows

    def cast(at, step):
        value = src[pl.ds(pl.multiple_of(start + at, 16), step), :]
        out[pl.ds(pl.multiple_of(at, 16), step), :] = value.astype(out.dtype)

    in_steps(cast, rows)


def cast(value, after):
    spec = pl.BlockSpec(memory_space=pltpu.VMEM)
    return pl.pallas_call(
        cast_kernel,
        out_shape=jax.ShapeDtypeStruct((value.shape[0] // 2, LANES), BF16),
        in_specs=[spec, pl.BlockSpec(memory_space=pl.ANY)],
        out_specs=spec,
        compiler_params=pltpu.CompilerParams(vmem_limit_bytes=24 * 2**20),
        cost_estimate=pl.CostEstimate(flops=0, bytes_accessed=4 * value.size, transcendentals=0),
    )(value, after)


def add_kernel(src, other, send, keep):
    half, rows = (other.shape[0], send.shape[0])
    start = lax.axis_index("core") * half
    mine = lax.axis_index("x") * rows
    theirs = rows - mine

    def total(at, step):
        value = src[pl.ds(pl.multiple_of(start + at, 16), step), :]
        return value + other[pl.ds(pl.multiple_of(at, 16), step), :].astype(F32)

    def add(at, step):
        to = pl.ds(pl.multiple_of(at, 16), step)
        send[to, :] = total(theirs + at, step).astype(send.dtype)
        keep[to, :] = total(mine + at, step)

    in_steps(add, rows)


def add(value, other):
    rows = other.shape[0] // 2
    return vmem_call(
        add_kernel,
        (jax.ShapeDtypeStruct((rows, LANES), BF16), jax.ShapeDtypeStruct((rows, LANES), F32)),
        (),
        pl.CostEstimate(flops=0, bytes_accessed=4 * value.size, transcendentals=0),
    )(value, other)


def combine_kernel(keep, other, terms, more, out):
    parts, rows, _ = out.shape
    height, extra = (keep.shape[0] // parts, terms.shape[0] // parts)
    padded = rows - extra
    total = keep[...] + other[...].astype(F32)
    grads = terms[...] + more[...].astype(F32)
    for n in range(parts):
        value = total[n * height : (n + 1) * height]
        if padded > height:
            value = jnp.concatenate([value, jnp.zeros((padded - height, LANES), F32)], axis=0)
        out[n, 0:padded, :] = value.astype(out.dtype)
        out[n, padded:rows, :] = grads[n * extra : (n + 1) * extra].astype(out.dtype)


def combine(keep, other, terms, more, parts):
    rows = ceil_to(keep.shape[0] // parts, 16) + terms.shape[0] // parts
    return vmem_call(
        combine_kernel,
        jax.ShapeDtypeStruct((parts, rows, LANES), BF16),
        (),
        pl.CostEstimate(flops=0, bytes_accessed=8 * keep.size, transcendentals=0),
    )(keep, other, terms, more)


def split_to(total, mine, send, keep):
    half = total.shape[0] // 2
    keep[...] = total[pl.ds(pl.multiple_of(mine * half, 16), half), :]
    send[...] = total[pl.ds(pl.multiple_of((1 - mine) * half, 16), half), :].astype(send.dtype)


def swapped(value, axis="core"):
    return lax.ppermute(value, axis, [(0, 1), (1, 0)])


def plane_order():
    core = lax.axis_index("core")
    ahead = [core * n + (1 - core) * (2 - n) for n in range(3)]
    back = [core * (2 - n) + (1 - core) * n for n in range(3)]
    return (ahead, back)


def windows(packs, x, count):
    rows = [
        [p[pl.ds(pl.multiple_of((x + n) * count, 16), count), :] for p in packs]
        for n in range(GROUP + 2)
    ]
    return jnp.concatenate(
        [jnp.concatenate(sum(rows[g : g + 3], []), axis=0) for g in range(GROUP)], axis=1
    )


def ordered(acc, count, ahead):
    blocks = [pl.multiple_of((3 * j + n) * count, 16) for j in range(3) for n in ahead]
    return jnp.concatenate([acc[pl.ds(at, count), :] for at in blocks], axis=0)


def across_lanes(first, second):
    return lax.dot_general(
        first, second, (((1,), (1,)), ((), ())), preferred_element_type=F32
    )


def prepare_kernel(act, two, one, acts, w_two, w_one, flat):
    ahead, back = plane_order()
    turned(act, flat, acts, 0, act.shape[0], 0)
    w_two[...] = jnp.concatenate(
        [
            jnp.concatenate([two[back[n], 2 - j, 2 - k].astype(F32) for k in range(3)], axis=0)
            for j in range(3)
            for n in range(3)
        ],
        axis=1,
    ).astype(BF16)
    w_one[...] = jnp.concatenate(
        [
            jnp.concatenate([one[ahead[n], 2 - j, k].astype(F32) for n in range(3)], axis=0)
            for j in range(3)
            for k in range(3)
        ],
        axis=1,
    ).astype(BF16)


def prepare(act, kernel_two, kernel_one):
    c1, length, width = act.shape
    c0, c2 = (kernel_one.shape[3], kernel_two.shape[4])
    return vmem_call(
        prepare_kernel,
        (
            jax.ShapeDtypeStruct((length * c1, width), BF16),
            jax.ShapeDtypeStruct((3 * c1, 9 * c2), BF16),
            jax.ShapeDtypeStruct((3 * c0, 9 * c1), BF16),
        ),
        (pltpu.VMEM((c1 * length, width), F32),),
        pl.CostEstimate(flops=0, bytes_accessed=16 * act.size, transcendentals=0),
    )(act, kernel_two, kernel_one)


def first_kernel(pack_in, pack_0, pack_out, acts, w_two, pres, terms, acc):
    c1, c2 = (w_two.shape[0] // 3, w_two.shape[1] // 9)
    length = acts.shape[0] // c1
    packs = (pack_in, pack_0, pack_out)
    ahead, _ = plane_order()
    stacked = 3 * c1
    pres[0:stacked, :] = jnp.zeros((stacked, LANES), BF16)
    pres[(length + 1) * stacked : (length + 2) * stacked, :] = jnp.zeros((stacked, LANES), BF16)
    acc[...] = jnp.zeros_like(acc)

    def body(step, carry):
        x = step * GROUP
        right = windows(packs, x, c2)
        sums = jnp.dot(w_two[...], right, preferred_element_type=F32)
        columns = []
        for g in range(GROUP):
            part = sums[:, g * LANES : (g + 1) * LANES]
            grad = slid(part[0:c1], 1) + part[c1 : 2 * c1] + slid(part[2 * c1 : 3 * c1], -1)
            value = acts[pl.ds(pl.multiple_of((x + g) * c1, 16), c1), :].astype(F32)
            pre = (grad * jnp.where(value > 0, 1.0, 0.2)).astype(BF16).astype(F32)
            moved = jnp.concatenate([slid(pre, -1), pre, slid(pre, 1)], axis=0).astype(BF16)
            pres[pl.ds(pl.multiple_of((x + g + 1) * stacked, 16), stacked), :] = moved
            stack = jnp.concatenate([slid(value, 1), value, slid(value, -1)], axis=0)
            columns.append(stack.astype(BF16))
        acc[...] += across_lanes(right, jnp.concatenate(columns, axis=1))
        return carry

    lax.fori_loop(0, length // GROUP, body, 0, unroll=True)

    terms[...] = jnp.zeros_like(terms)
    total = ordered(acc, c2, ahead).T
    rows, width = total.shape
    for block in range(-(-width // LANES)):
        part = total[:, block * LANES : min(width, (block + 1) * LANES)]
        terms[block * rows : (block + 1) * rows, 0 : part.shape[1]] = part


def gradient_kernel(pack_in, pack_0, pack_out, pres, before, send, keep, acc, terms):
    c0, stacked = (acc.shape[0] // 9, acc.shape[1])
    packs = (pack_in, pack_0, pack_out)
    ahead, _ = plane_order()
    length = pres.shape[0] // stacked - 2
    acc[...] = jnp.zeros_like(acc)

    def body(step, carry):
        x = step * GROUP
        rows = [
            pres[pl.ds(pl.multiple_of((x + g + 1) * stacked, 16), stacked), :] for g in range(GROUP)
        ]
        acc[...] += across_lanes(windows(packs, x, c0), jnp.concatenate(rows, axis=1))
        return carry

    lax.fori_loop(0, length // GROUP, body, 0, unroll=True)

    used = before.shape[0]
    terms[0:used, :] = before[...]
    terms[used:, :] = jnp.zeros((terms.shape[0] - used, LANES), F32)
    total = ordered(acc, c0, ahead)
    terms[used : used + total.shape[0], 0 : total.shape[1]] = total
    split_to(terms, lax.axis_index("core"), send, keep)


def input_kernel(pres, w_one, own, inner, outer):
    c0, stacked = (w_one.shape[0] // 3, w_one.shape[1] // 3)
    length = pres.shape[0] // stacked - 2

    def body(step, carry):
        x = step * GROUP
        window = pres[pl.ds(pl.multiple_of(x * stacked, 16), (GROUP + 2) * stacked), :]
        moved = beside(window, 3 * stacked, stacked, GROUP)
        sums = jnp.dot(w_one[...], moved, preferred_element_type=F32)
        for g in range(GROUP):
            part = sums[:, g * LANES : (g + 1) * LANES]
            at = pl.ds(pl.multiple_of((x + g) * c0, 16), c0)
            for i, out in ((0, inner), (1, own), (2, outer)):
                out[at, :] = part[i * c0 : (i + 1) * c0].astype(out.dtype)
        return carry

    lax.fori_loop(0, length // GROUP, body, 0, unroll=True)


def vmem_call(body, out_shape, scratch=(), cost=None, limit=24 * 2**20):
    spec = pl.BlockSpec(memory_space=pltpu.VMEM)
    return pl.pallas_call(
        body,
        out_shape=out_shape,
        out_specs=jax.tree.map(lambda _: spec, out_shape),
        scratch_shapes=list(scratch),
        compiler_params=pltpu.CompilerParams(vmem_limit_bytes=limit),
        cost_estimate=cost,
    )


def first_part(packs, acts, w_two):
    c1, c2, width = (w_two.shape[0] // 3, w_two.shape[1] // 9, acts.shape[1])
    length = acts.shape[0] // c1
    return vmem_call(
        first_kernel,
        (
            jax.ShapeDtypeStruct(((length + 2) * 3 * c1, width), BF16),
            jax.ShapeDtypeStruct((-(-9 * c2 // LANES) * 3 * c1, LANES), F32),
        ),
        (pltpu.VMEM((9 * c2, 3 * c1), F32),),
        pl.CostEstimate(flops=10**9, bytes_accessed=20 * 2**20, transcendentals=0),
    )(*packs, acts, w_two)


def gradient_part(packs, pres, terms, rows, c1):
    width = pres.shape[1]
    c0 = packs[0].shape[0] // (pres.shape[0] // (3 * c1))
    return vmem_call(
        gradient_kernel,
        (
            jax.ShapeDtypeStruct((rows // 2, LANES), BF16),
            jax.ShapeDtypeStruct((rows // 2, LANES), F32),
        ),
        (pltpu.VMEM((9 * c0, 3 * c1), F32), pltpu.VMEM((rows, width), F32)),
        pl.CostEstimate(flops=10**9, bytes_accessed=5 * 2**20, transcendentals=0),
    )(*packs, pres, terms)


def input_part(pres, w_one):
    c0, stacked = (w_one.shape[0] // 3, w_one.shape[1] // 3)
    plane = ((pres.shape[0] // stacked - 2) * c0, pres.shape[1])
    return vmem_call(
        input_kernel,
        (
            jax.ShapeDtypeStruct(plane, F32),
            jax.ShapeDtypeStruct(plane, BF16),
            jax.ShapeDtypeStruct(plane, BF16),
        ),
        (),
        pl.CostEstimate(flops=10**9, bytes_accessed=5 * 2**20, transcendentals=0),
    )(pres, w_one)


def merge_kernel(own, first, second, out, flat):
    chans, length, _ = out.shape

    def add(step, carry):
        at = pl.ds(pl.multiple_of(step * 64, 64), 64)
        flat[at, :] = own[at, :] + first[at, :].astype(F32) + second[at, :].astype(F32)
        return carry

    lax.fori_loop(0, own.shape[0] // 64, add, 0, unroll=4)

    def gather(c, carry):
        out[c] = flat[pl.ds(c, length, stride=chans), :].astype(out.dtype)
        return carry

    lax.fori_loop(0, chans, gather, 0, unroll=4)


def merge(own, first, second, shape):
    return vmem_call(
        merge_kernel,
        jax.ShapeDtypeStruct(shape, BF16),
        (pltpu.VMEM(own.shape, F32),),
        pl.CostEstimate(flops=2 * own.size, bytes_accessed=8 * own.size, transcendentals=0),
    )(own, first, second)


def share_kernel(scale, parts, out):
    copies, rows, _ = parts.shape
    padded = out.shape[1] - rows
    near = jnp.sum(parts[0 : copies // 2, 0:padded, :].astype(F32), axis=0).astype(BF16)
    far = jnp.sum(parts[copies // 2 :, 0:padded, :].astype(F32), axis=0).astype(BF16)
    grads = (jnp.sum(parts[:, padded:rows, :].astype(F32), axis=0) * scale).astype(BF16)

    def write(n, carry):
        out[n, 0:padded, :] = near
        out[n, padded : 2 * padded, :] = far
        out[n, 2 * padded :, :] = grads
        return carry

    lax.fori_loop(0, copies, write, 0)


def share(parts, extra, scale):
    copies, rows, _ = parts.shape
    return vmem_call(
        lambda *refs: share_kernel(scale, *refs),
        jax.ShapeDtypeStruct((copies, 2 * rows - extra, LANES), BF16),
        (),
        pl.CostEstimate(flops=parts.size, bytes_accessed=6 * parts.size, transcendentals=0),
    )(parts)


def place(source, height, padded, which, bucket, buffer, sems):
    copies, count = (source.shape[0], sems.shape[0])
    step = 2 * copies // count
    sent = []
    for n in range(count):
        for m in range(n * step, (n + 1) * step):
            half, q = (m // copies, m % copies)
            value = source[q, half * padded : (half + 1) * padded, :].astype(F32)
            buffer[m * height : (m + 1) * height, :] = value[0:height]
        rows = pl.ds(n * step * height, step * height)
        at = (which * count + n) * step * height
        at = pl.ds(pl.multiple_of(at, 8), step * height)
        sent.append(pltpu.make_async_copy(buffer.at[rows], bucket.at[at], sems.at[n]))
        sent[-1].start()
    return sent


def start_kernel(height, padded, mine, bucket, buffer, sems):
    for copy in place(mine, height, padded, lax.axis_index("core"), bucket, buffer, sems):
        copy.wait()


def finish_kernel(
    sizes, height, padded, mine, other, partial,
    bucket, out_one, out_two,
    raw, one, two, out_sems, buffer, sems,
):
    c0, c1, c2 = sizes
    copies, rows, _ = mine.shape
    extra = rows - 2 * padded
    me = lax.axis_index("core")
    sent = place(other, height, padded, 1 - me, bucket, buffer, sems)

    for q in range(copies):
        for source, which in ((mine, me), (other, 1 - me)):
            at = pl.multiple_of((which * copies + q) * extra, 8)
            raw[pl.ds(at, extra), :] = source[q, 2 * padded : rows, :].astype(F32)
    block = 3 * c1
    first = -(-9 * c2 // LANES) * block
    for i in range(3):
        for j in range(3):
            column = ((2 - j) * 3 + 2 - i) * c2
            whole, lane = (column // LANES, column % LANES)
            two[(3 * i + j) * block : (3 * i + j + 1) * block, :] = raw[
                whole * block : (whole + 1) * block, lane : lane + c2
            ]
        at = pl.ds(3 * i * block, 3 * block)
        sent.append(pltpu.make_async_copy(two.at[at], out_two.at[at], out_sems.at[i]))
        sent[-1].start()
    for i in range(3):
        for j in range(3):
            row = first + (3 * j + i) * c0
            for k in range(3):
                to = (9 * i + 3 * j + k) * c0
                one[to : to + c0, :] = raw[row : row + c0, k * c1 : (k + 1) * c1]
        at = pl.ds(9 * i * c0, 9 * c0)
        sent.append(pltpu.make_async_copy(one.at[at], out_one.at[at], out_sems.at[3 + i]))
        sent[-1].start()
    for copy in sent:
        copy.wait()


def finish(mine, other, length, sizes):
    c0, c1, c2 = sizes
    copies, rows, _ = mine.shape
    height = length // LANES // (4 * copies)
    padded = ceil_to(height, 16)
    spec = pl.BlockSpec(memory_space=pltpu.VMEM)
    remote = pl.BlockSpec(memory_space=pltpu.HBM)
    whole = jax.ShapeDtypeStruct((length // LANES, LANES), F32)
    chunks = 4
    scratch = [
        pltpu.VMEM((2 * copies * height, LANES), F32),
        pltpu.SemaphoreType.DMA((chunks,)),
    ]
    params = pltpu.CompilerParams(vmem_limit_bytes=24 * 2**20)
    partial = pl.pallas_call(
        lambda *refs: start_kernel(height, padded, *refs),
        out_shape=whole,
        in_specs=[spec],
        out_specs=remote,
        scratch_shapes=scratch,
        compiler_params=params,
    )(mine)
    return pl.pallas_call(
        lambda *refs: finish_kernel(sizes, height, padded, *refs),
        out_shape=(
            whole,
            jax.ShapeDtypeStruct((27 * c0, c1), F32),
            jax.ShapeDtypeStruct((27 * c1, c2), F32),
        ),
        in_specs=[spec, spec, remote],
        out_specs=(remote, remote, remote),
        scratch_shapes=[
            pltpu.VMEM((2 * copies * (rows - 2 * padded), LANES), F32),
            pltpu.VMEM((27 * c0, c1), F32),
            pltpu.VMEM((27 * c1, c2), F32),
            pltpu.SemaphoreType.DMA((6,)),
        ]
        + scratch,
        input_output_aliases={2: 0},
        compiler_params=params,
    )(mine, other, partial)


def crossed(value):
    pairs = [(n, n + 1) for n in range(1, lax.axis_size(SPACE) - 1, 2)]
    return lax.ppermute(value, SPACE, pairs + [(m, n) for n, m in pairs])


def per_device(volume_in, hidden_act, out_cot, kernel_one, kernel_two, grad_bucket):
    c0, c1, c2 = (volume_in.shape[2], hidden_act.shape[2], out_cot.shape[2])
    devices, copies = (lax.axis_size(EVERY), lax.axis_size(SAME))
    length = grad_bucket.shape[1]
    bucket = grad_bucket.reshape(length // LANES, LANES)
    cot = pack(out_cot[0, 0])
    cots = (swapped(cot), cot, crossed(cot))
    vol = pack(volume_in[0, 0])
    vols = (swapped(vol), vol, crossed(vol))
    send, near = add(bucket, swapped(cast(bucket, cot)))
    act, send, near = lax.optimization_barrier((hidden_act[0, 0], send, near))
    far = swapped(send, "x")

    used = -(-9 * c2 // LANES) * 3 * c1 + 9 * c0
    rows = ceil_to(used, 16 * devices)
    acts, w_two, w_one = prepare(act, kernel_two, kernel_one)
    pres, terms = first_part(cots, acts, w_two)
    send, keep = gradient_part(vols, pres, terms, rows, c1)
    own, inner, outer = input_part(pres, w_one)
    parts = combine(near, far, keep, swapped(send), copies)
    parts, inner, outer = lax.optimization_barrier((parts, inner, outer))
    parts = lax.all_to_all(parts, SAME, 0, 0)
    parts, inner, outer = lax.optimization_barrier((parts, swapped(inner), crossed(outer)))
    cells = volume_in.shape[3] * volume_in.shape[4] * devices
    shares = share(parts, rows // devices, 1.0 / math.sqrt(cells))

    mine = lax.all_to_all(shares, SAME, 0, 0)
    mine, own = lax.optimization_barrier((mine, own))
    grad_input = merge(own, inner, outer, volume_in.shape[2:])
    bucket_sum, total_one, total_two = finish(mine, swapped(mine), length, (c0, c1, c2))
    return (
        grad_input[None, None],
        total_one.reshape(3, 3, 3, c0, c1),
        total_two.reshape(3, 3, 3, c1, c2),
        bucket_sum.reshape(length),
    )


def solution(mesh):
    dp, space = (mesh.shape["dp"], mesh.shape["space"])
    split = Mesh(mesh.devices.reshape(dp // 2, 2, space // 2, 2), EVERY)
    volume = P(("z", "x"), SPACE, None, None, None)
    in_specs = (volume, volume, volume, P(), P(), P(EVERY, None))
    out_specs = (volume, P(), P(), P())
    return jax.shard_map(
        per_device, mesh=split, in_specs=in_specs, out_specs=out_specs, check_vma=False
    )
```

```python
import math

import jax
import jax.numpy as jnp
from jax import lax
from jax.experimental import pallas as pl
from jax.experimental.pallas import tpu as pltpu
from jax.sharding import Mesh, PartitionSpec as P

SPACE = ("y", "core")
SAME = ("x", "z", "y")
EVERY = ("z", "x", "y", "core")
GROUP = 8
LANES = 128
BF16 = jnp.bfloat16
F32 = jnp.float32


def ceil_to(value, step):
    return -(-value // step) * step


def slid(value, step):
    lane = lax.broadcasted_iota(jnp.int32, value.shape, 1)
    width = value.shape[1]
    keep = lane >= step if step > 0 else lane < width + step
    return jnp.where(keep, pltpu.roll(value, step % width, 1), 0.0)


def beside(window, rows, step, count):
    return jnp.concatenate([window[g * step : g * step + rows] for g in range(count)], axis=1)


def turned(src, flat, dst, offset, pitch, lead):
    chans, length, _ = src.shape

    def stage(c, carry):
        flat[pl.ds(pl.multiple_of(c * length, length), length), :] = src[c].astype(F32)
        return carry

    lax.fori_loop(0, chans, stage, 0, unroll=4)

    def gather(x, carry):
        rows = flat[pl.ds(x, chans, stride=length), :]
        at = pl.multiple_of((x + lead) * pitch + offset, 16)
        dst[pl.ds(at, chans), :] = rows.astype(BF16)
        return carry

    lax.fori_loop(0, length, gather, 0, unroll=4)


def pack_kernel(field, *refs):
    out, flat = refs[-2:]
    chans, length, width = field.shape
    zeros = jnp.zeros((chans, width), BF16)
    out[0:chans, :] = zeros
    out[(length + 1) * chans : (length + 2) * chans, :] = zeros
    turned(field, flat, out, 0, chans, 1)


def pack(field, after, weight):
    chans, length, width = field.shape
    spec = pl.BlockSpec(memory_space=pltpu.VMEM)
    return pl.pallas_call(
        pack_kernel,
        out_shape=jax.ShapeDtypeStruct(((length + 2) * chans, width), BF16),
        in_specs=[spec] + [pl.BlockSpec(memory_space=pl.ANY) for _ in after],
        out_specs=spec,
        scratch_shapes=[pltpu.VMEM((chans * length, width), F32)],
        compiler_params=pltpu.CompilerParams(vmem_limit_bytes=24 * 2**20),
        cost_estimate=pl.CostEstimate(
            flops=0, bytes_accessed=weight * field.size, transcendentals=0
        ),
    )(field, *after)


def in_steps(body, rows, count=8):
    step = rows // count

    def one(n, carry):
        body(n * step, step)
        return carry

    lax.fori_loop(0, count, one, 0)


def add_kernel(own, other, send, keep):
    rows = send.shape[0]
    mine = lax.axis_index("x") * rows
    theirs = rows - mine

    def total(at, step):
        at = pl.ds(pl.multiple_of(at, 16), step)
        return own[at, :] + other[at, :].astype(F32)

    def add(at, step):
        to = pl.ds(pl.multiple_of(at, 16), step)
        send[to, :] = total(theirs + at, step).astype(send.dtype)
        keep[to, :] = total(mine + at, step)

    in_steps(add, rows)


def add(own, other):
    rows = other.shape[0] // 2
    return vmem_call(
        add_kernel,
        (jax.ShapeDtypeStruct((rows, LANES), BF16), jax.ShapeDtypeStruct((rows, LANES), F32)),
        (),
        pl.CostEstimate(flops=0, bytes_accessed=8 * own.size, transcendentals=0),
    )(own, other)


def combine_kernel(keep, other, terms, more, out):
    parts, rows, _ = out.shape
    height, extra = (keep.shape[0] // parts, terms.shape[0] // parts)
    padded = rows - extra
    total = keep[...] + other[...].astype(F32)
    grads = terms[...] + more[...].astype(F32)
    for n in range(parts):
        value = total[n * height : (n + 1) * height]
        if padded > height:
            value = jnp.concatenate([value, jnp.zeros((padded - height, LANES), F32)], axis=0)
        out[n, 0:padded, :] = value.astype(out.dtype)
        out[n, padded:rows, :] = grads[n * extra : (n + 1) * extra].astype(out.dtype)


def combine(keep, other, terms, more, parts):
    rows = ceil_to(keep.shape[0] // parts, 16) + terms.shape[0] // parts
    return vmem_call(
        combine_kernel,
        jax.ShapeDtypeStruct((parts, rows, LANES), BF16),
        (),
        pl.CostEstimate(flops=0, bytes_accessed=8 * keep.size, transcendentals=0),
    )(keep, other, terms, more)


def split_to(total, mine, send, keep):
    half = total.shape[0] // 2
    keep[...] = total[pl.ds(pl.multiple_of(mine * half, 16), half), :]
    send[...] = total[pl.ds(pl.multiple_of((1 - mine) * half, 16), half), :].astype(send.dtype)


def swapped(value, axis="core"):
    return lax.ppermute(value, axis, [(0, 1), (1, 0)])


def plane_order():
    core = lax.axis_index("core")
    ahead = [core * n + (1 - core) * (2 - n) for n in range(3)]
    back = [core * (2 - n) + (1 - core) * n for n in range(3)]
    return (ahead, back)


def windows(packs, x, count):
    rows = [
        [p[pl.ds(pl.multiple_of((x + n) * count, 16), count), :] for p in packs]
        for n in range(GROUP + 2)
    ]
    return jnp.concatenate(
        [jnp.concatenate(sum(rows[g : g + 3], []), axis=0) for g in range(GROUP)], axis=1
    )


def ordered(acc, count, ahead):
    blocks = [pl.multiple_of((3 * j + n) * count, 16) for j in range(3) for n in ahead]
    return jnp.concatenate([acc[pl.ds(at, count), :] for at in blocks], axis=0)


def across_lanes(first, second):
    return lax.dot_general(
        first, second, (((1,), (1,)), ((), ())), preferred_element_type=F32
    )


def prepare_kernel(act, two, one, acts, w_two, w_one, flat):
    ahead, back = plane_order()
    turned(act, flat, acts, 0, act.shape[0], 0)
    w_two[...] = jnp.concatenate(
        [
            jnp.concatenate([two[back[n], 2 - j, 2 - k].astype(F32) for k in range(3)], axis=0)
            for j in range(3)
            for n in range(3)
        ],
        axis=1,
    ).astype(BF16)
    w_one[...] = jnp.concatenate(
        [
            jnp.concatenate([one[ahead[n], 2 - j, k].astype(F32) for n in range(3)], axis=0)
            for j in range(3)
            for k in range(3)
        ],
        axis=1,
    ).astype(BF16)


def prepare(act, kernel_two, kernel_one):
    c1, length, width = act.shape
    c0, c2 = (kernel_one.shape[3], kernel_two.shape[4])
    return vmem_call(
        prepare_kernel,
        (
            jax.ShapeDtypeStruct((length * c1, width), BF16),
            jax.ShapeDtypeStruct((3 * c1, 9 * c2), BF16),
            jax.ShapeDtypeStruct((3 * c0, 9 * c1), BF16),
        ),
        (pltpu.VMEM((c1 * length, width), F32),),
        pl.CostEstimate(flops=0, bytes_accessed=16 * act.size, transcendentals=0),
    )(act, kernel_two, kernel_one)


def first_kernel(pack_in, pack_0, pack_out, acts, w_two, pres, terms, acc):
    c1, c2 = (w_two.shape[0] // 3, w_two.shape[1] // 9)
    length = acts.shape[0] // c1
    packs = (pack_in, pack_0, pack_out)
    ahead, _ = plane_order()
    stacked = 3 * c1
    pres[0:stacked, :] = jnp.zeros((stacked, LANES), BF16)
    pres[(length + 1) * stacked : (length + 2) * stacked, :] = jnp.zeros((stacked, LANES), BF16)
    acc[...] = jnp.zeros_like(acc)

    def body(step, carry):
        x = step * GROUP
        right = windows(packs, x, c2)
        sums = jnp.dot(w_two[...], right, preferred_element_type=F32)
        columns = []
        for g in range(GROUP):
            part = sums[:, g * LANES : (g + 1) * LANES]
            grad = slid(part[0:c1], 1) + part[c1 : 2 * c1] + slid(part[2 * c1 : 3 * c1], -1)
            value = acts[pl.ds(pl.multiple_of((x + g) * c1, 16), c1), :].astype(F32)
            pre = (grad * jnp.where(value > 0, 1.0, 0.2)).astype(BF16).astype(F32)
            moved = jnp.concatenate([slid(pre, -1), pre, slid(pre, 1)], axis=0).astype(BF16)
            pres[pl.ds(pl.multiple_of((x + g + 1) * stacked, 16), stacked), :] = moved
            stack = jnp.concatenate([slid(value, 1), value, slid(value, -1)], axis=0)
            columns.append(stack.astype(BF16))
        acc[...] += across_lanes(right, jnp.concatenate(columns, axis=1))
        return carry

    lax.fori_loop(0, length // GROUP, body, 0, unroll=True)

    terms[...] = jnp.zeros_like(terms)
    total = ordered(acc, c2, ahead).T
    rows, width = total.shape
    for block in range(-(-width // LANES)):
        part = total[:, block * LANES : min(width, (block + 1) * LANES)]
        terms[block * rows : (block + 1) * rows, 0 : part.shape[1]] = part


def gradient_kernel(pack_in, pack_0, pack_out, pres, before, send, keep, acc, terms):
    c0, stacked = (acc.shape[0] // 9, acc.shape[1])
    packs = (pack_in, pack_0, pack_out)
    ahead, _ = plane_order()
    length = pres.shape[0] // stacked - 2
    acc[...] = jnp.zeros_like(acc)

    def body(step, carry):
        x = step * GROUP
        rows = [
            pres[pl.ds(pl.multiple_of((x + g + 1) * stacked, 16), stacked), :] for g in range(GROUP)
        ]
        acc[...] += across_lanes(windows(packs, x, c0), jnp.concatenate(rows, axis=1))
        return carry

    lax.fori_loop(0, length // GROUP, body, 0, unroll=True)

    used = before.shape[0]
    terms[0:used, :] = before[...]
    terms[used:, :] = jnp.zeros((terms.shape[0] - used, LANES), F32)
    total = ordered(acc, c0, ahead)
    terms[used : used + total.shape[0], 0 : total.shape[1]] = total
    split_to(terms, lax.axis_index("core"), send, keep)


def input_kernel(pres, w_one, own, inner, outer):
    c0, stacked = (w_one.shape[0] // 3, w_one.shape[1] // 3)
    length = pres.shape[0] // stacked - 2

    def body(step, carry):
        x = step * GROUP
        window = pres[pl.ds(pl.multiple_of(x * stacked, 16), (GROUP + 2) * stacked), :]
        moved = beside(window, 3 * stacked, stacked, GROUP)
        sums = jnp.dot(w_one[...], moved, preferred_element_type=F32)
        for g in range(GROUP):
            part = sums[:, g * LANES : (g + 1) * LANES]
            at = pl.ds(pl.multiple_of((x + g) * c0, 16), c0)
            for i, out in ((0, inner), (1, own), (2, outer)):
                out[at, :] = part[i * c0 : (i + 1) * c0].astype(out.dtype)
        return carry

    lax.fori_loop(0, length // GROUP, body, 0, unroll=True)


def vmem_call(body, out_shape, scratch=(), cost=None, limit=24 * 2**20):
    spec = pl.BlockSpec(memory_space=pltpu.VMEM)
    return pl.pallas_call(
        body,
        out_shape=out_shape,
        out_specs=jax.tree.map(lambda _: spec, out_shape),
        scratch_shapes=list(scratch),
        compiler_params=pltpu.CompilerParams(vmem_limit_bytes=limit),
        cost_estimate=cost,
    )


def first_part(packs, acts, w_two):
    c1, c2, width = (w_two.shape[0] // 3, w_two.shape[1] // 9, acts.shape[1])
    length = acts.shape[0] // c1
    return vmem_call(
        first_kernel,
        (
            jax.ShapeDtypeStruct(((length + 2) * 3 * c1, width), BF16),
            jax.ShapeDtypeStruct((-(-9 * c2 // LANES) * 3 * c1, LANES), F32),
        ),
        (pltpu.VMEM((9 * c2, 3 * c1), F32),),
        pl.CostEstimate(flops=10**9, bytes_accessed=20 * 2**20, transcendentals=0),
    )(*packs, acts, w_two)


def gradient_part(packs, pres, terms, rows, c1):
    width = pres.shape[1]
    c0 = packs[0].shape[0] // (pres.shape[0] // (3 * c1))
    return vmem_call(
        gradient_kernel,
        (
            jax.ShapeDtypeStruct((rows // 2, LANES), BF16),
            jax.ShapeDtypeStruct((rows // 2, LANES), F32),
        ),
        (pltpu.VMEM((9 * c0, 3 * c1), F32), pltpu.VMEM((rows, width), F32)),
        pl.CostEstimate(flops=10**9, bytes_accessed=5 * 2**20, transcendentals=0),
    )(*packs, pres, terms)


def input_part(pres, w_one):
    c0, stacked = (w_one.shape[0] // 3, w_one.shape[1] // 3)
    plane = ((pres.shape[0] // stacked - 2) * c0, pres.shape[1])
    return vmem_call(
        input_kernel,
        (
            jax.ShapeDtypeStruct(plane, F32),
            jax.ShapeDtypeStruct(plane, BF16),
            jax.ShapeDtypeStruct(plane, BF16),
        ),
        (),
        pl.CostEstimate(flops=10**9, bytes_accessed=5 * 2**20, transcendentals=0),
    )(pres, w_one)


def merge_kernel(own, first, second, out, flat):
    chans, length, _ = out.shape

    def add(step, carry):
        at = pl.ds(pl.multiple_of(step * 64, 64), 64)
        flat[at, :] = own[at, :] + first[at, :].astype(F32) + second[at, :].astype(F32)
        return carry

    lax.fori_loop(0, own.shape[0] // 64, add, 0, unroll=4)

    def gather(c, carry):
        out[c] = flat[pl.ds(c, length, stride=chans), :].astype(out.dtype)
        return carry

    lax.fori_loop(0, chans, gather, 0, unroll=4)


def merge(own, first, second, shape):
    return vmem_call(
        merge_kernel,
        jax.ShapeDtypeStruct(shape, BF16),
        (pltpu.VMEM(own.shape, F32),),
        pl.CostEstimate(flops=2 * own.size, bytes_accessed=8 * own.size, transcendentals=0),
    )(own, first, second)


def share_kernel(scale, parts, out):
    copies, rows, _ = parts.shape
    padded = out.shape[1] - rows
    near = jnp.sum(parts[0 : copies // 2, 0:padded, :].astype(F32), axis=0).astype(BF16)
    far = jnp.sum(parts[copies // 2 :, 0:padded, :].astype(F32), axis=0).astype(BF16)
    grads = (jnp.sum(parts[:, padded:rows, :].astype(F32), axis=0) * scale).astype(BF16)

    def write(n, carry):
        out[n, 0:padded, :] = near
        out[n, padded : 2 * padded, :] = far
        out[n, 2 * padded :, :] = grads
        return carry

    lax.fori_loop(0, copies, write, 0)


def share(parts, extra, scale):
    copies, rows, _ = parts.shape
    return vmem_call(
        lambda *refs: share_kernel(scale, *refs),
        jax.ShapeDtypeStruct((copies, 2 * rows - extra, LANES), BF16),
        (),
        pl.CostEstimate(flops=parts.size, bytes_accessed=6 * parts.size, transcendentals=0),
    )(parts)


def place(source, height, padded, which, bucket, buffer, sems):
    copies, count = (source.shape[0], sems.shape[0])
    step = 2 * copies // count
    sent = []
    for n in range(count):
        for m in range(n * step, (n + 1) * step):
            half, q = (m // copies, m % copies)
            value = source[q, half * padded : (half + 1) * padded, :].astype(F32)
            buffer[m * height : (m + 1) * height, :] = value[0:height]
        rows = pl.ds(n * step * height, step * height)
        at = (which * count + n) * step * height
        at = pl.ds(pl.multiple_of(at, 8), step * height)
        sent.append(pltpu.make_async_copy(buffer.at[rows], bucket.at[at], sems.at[n]))
        sent[-1].start()
    return sent


def start_kernel(height, padded, mine, bucket, buffer, sems):
    for copy in place(mine, height, padded, lax.axis_index("core"), bucket, buffer, sems):
        copy.wait()


def finish_kernel(
    sizes, height, padded, mine, other, partial,
    bucket, out_one, out_two,
    raw, one, two, out_sems, buffer, sems,
):
    c0, c1, c2 = sizes
    copies, rows, _ = mine.shape
    extra = rows - 2 * padded
    me = lax.axis_index("core")
    sent = place(other, height, padded, 1 - me, bucket, buffer, sems)

    for q in range(copies):
        for source, which in ((mine, me), (other, 1 - me)):
            at = pl.multiple_of((which * copies + q) * extra, 8)
            raw[pl.ds(at, extra), :] = source[q, 2 * padded : rows, :].astype(F32)
    block = 3 * c1
    first = -(-9 * c2 // LANES) * block
    for i in range(3):
        for j in range(3):
            column = ((2 - j) * 3 + 2 - i) * c2
            whole, lane = (column // LANES, column % LANES)
            two[(3 * i + j) * block : (3 * i + j + 1) * block, :] = raw[
                whole * block : (whole + 1) * block, lane : lane + c2
            ]
        at = pl.ds(3 * i * block, 3 * block)
        sent.append(pltpu.make_async_copy(two.at[at], out_two.at[at], out_sems.at[i]))
        sent[-1].start()
    for i in range(3):
        for j in range(3):
            row = first + (3 * j + i) * c0
            for k in range(3):
                to = (9 * i + 3 * j + k) * c0
                one[to : to + c0, :] = raw[row : row + c0, k * c1 : (k + 1) * c1]
        at = pl.ds(9 * i * c0, 9 * c0)
        sent.append(pltpu.make_async_copy(one.at[at], out_one.at[at], out_sems.at[3 + i]))
        sent[-1].start()
    for copy in sent:
        copy.wait()


def finish(mine, other, length, sizes):
    c0, c1, c2 = sizes
    copies, rows, _ = mine.shape
    height = length // LANES // (4 * copies)
    padded = ceil_to(height, 16)
    spec = pl.BlockSpec(memory_space=pltpu.VMEM)
    remote = pl.BlockSpec(memory_space=pltpu.HBM)
    whole = jax.ShapeDtypeStruct((length // LANES, LANES), F32)
    chunks = 4
    scratch = [
        pltpu.VMEM((2 * copies * height, LANES), F32),
        pltpu.SemaphoreType.DMA((chunks,)),
    ]
    params = pltpu.CompilerParams(vmem_limit_bytes=24 * 2**20)
    partial = pl.pallas_call(
        lambda *refs: start_kernel(height, padded, *refs),
        out_shape=whole,
        in_specs=[spec],
        out_specs=remote,
        scratch_shapes=scratch,
        compiler_params=params,
    )(mine)
    return pl.pallas_call(
        lambda *refs: finish_kernel(sizes, height, padded, *refs),
        out_shape=(
            whole,
            jax.ShapeDtypeStruct((27 * c0, c1), F32),
            jax.ShapeDtypeStruct((27 * c1, c2), F32),
        ),
        in_specs=[spec, spec, remote],
        out_specs=(remote, remote, remote),
        scratch_shapes=[
            pltpu.VMEM((2 * copies * (rows - 2 * padded), LANES), F32),
            pltpu.VMEM((27 * c0, c1), F32),
            pltpu.VMEM((27 * c1, c2), F32),
            pltpu.SemaphoreType.DMA((6,)),
        ]
        + scratch,
        input_output_aliases={2: 0},
        compiler_params=params,
    )(mine, other, partial)


def crossed(value):
    pairs = [(n, n + 1) for n in range(1, lax.axis_size(SPACE) - 1, 2)]
    return lax.ppermute(value, SPACE, pairs + [(m, n) for n, m in pairs])


def per_device(volume_in, hidden_act, out_cot, kernel_one, kernel_two, grad_bucket):
    c0, c1, c2 = (volume_in.shape[2], hidden_act.shape[2], out_cot.shape[2])
    devices, copies = (lax.axis_size(EVERY), lax.axis_size(SAME))
    length = grad_bucket.shape[1]
    bucket = grad_bucket.reshape(length // LANES, LANES)
    cot = pack(out_cot[0, 0], [], 256)
    cots = (swapped(cot), cot, crossed(cot))
    vol = pack(volume_in[0, 0], [cot], 16)
    vols = (swapped(vol), vol, crossed(vol))
    bucket, cot = lax.optimization_barrier((bucket, cot))
    core, half = (lax.axis_index("core"), bucket.shape[0] // 2)
    send = lax.dynamic_slice_in_dim(bucket, (1 - core) * half, half).astype(BF16)
    near = lax.dynamic_slice_in_dim(bucket, core * half, half)
    send, near = add(near, swapped(send))
    act, send, near = lax.optimization_barrier((hidden_act[0, 0], send, near))
    far = swapped(send, "x")

    used = -(-9 * c2 // LANES) * 3 * c1 + 9 * c0
    rows = ceil_to(used, 16 * devices)
    acts, w_two, w_one = prepare(act, kernel_two, kernel_one)
    pres, terms = first_part(cots, acts, w_two)
    send, keep = gradient_part(vols, pres, terms, rows, c1)
    own, inner, outer = input_part(pres, w_one)
    parts = combine(near, far, keep, swapped(send), copies)
    parts, inner, outer = lax.optimization_barrier((parts, inner, outer))
    parts = lax.all_to_all(parts, SAME, 0, 0)
    parts, inner, outer = lax.optimization_barrier((parts, swapped(inner), crossed(outer)))
    cells = volume_in.shape[3] * volume_in.shape[4] * devices
    shares = share(parts, rows // devices, 1.0 / math.sqrt(cells))

    mine = lax.all_to_all(shares, SAME, 0, 0)
    mine, own = lax.optimization_barrier((mine, own))
    grad_input = merge(own, inner, outer, volume_in.shape[2:])
    bucket_sum, total_one, total_two = finish(mine, swapped(mine), length, (c0, c1, c2))
    return (
        grad_input[None, None],
        total_one.reshape(3, 3, 3, c0, c1),
        total_two.reshape(3, 3, 3, c1, c2),
        bucket_sum.reshape(length),
    )


def solution(mesh):
    dp, space = (mesh.shape["dp"], mesh.shape["space"])
    split = Mesh(mesh.devices.reshape(dp // 2, 2, space // 2, 2), EVERY)
    volume = P(("z", "x"), SPACE, None, None, None)
    in_specs = (volume, volume, volume, P(), P(), P(EVERY, None))
    out_specs = (volume, P(), P(), P())
    return jax.shard_map(
        per_device, mesh=split, in_specs=in_specs, out_specs=out_specs, check_vma=False
    )
```

```python
import math

import jax
import jax.numpy as jnp
from jax import lax
from jax.experimental import pallas as pl
from jax.experimental.pallas import tpu as pltpu
from jax.sharding import Mesh, PartitionSpec as P

SPACE = ("y", "core")
SAME = ("x", "z", "y")
EVERY = ("z", "x", "y", "core")
GROUP = 8
LANES = 128
BF16 = jnp.bfloat16
F32 = jnp.float32


def ceil_to(value, step):
    return -(-value // step) * step


def slid(value, step):
    lane = lax.broadcasted_iota(jnp.int32, value.shape, 1)
    width = value.shape[1]
    keep = lane >= step if step > 0 else lane < width + step
    return jnp.where(keep, pltpu.roll(value, step % width, 1), 0.0)


def beside(window, rows, step, count):
    return jnp.concatenate([window[g * step : g * step + rows] for g in range(count)], axis=1)


def turned(src, flat, dst, offset, pitch, lead):
    chans, length, _ = src.shape

    def stage(c, carry):
        flat[pl.ds(pl.multiple_of(c * length, length), length), :] = src[c].astype(F32)
        return carry

    lax.fori_loop(0, chans, stage, 0, unroll=4)

    def gather(x, carry):
        rows = flat[pl.ds(x, chans, stride=length), :]
        at = pl.multiple_of((x + lead) * pitch + offset, 16)
        dst[pl.ds(at, chans), :] = rows.astype(BF16)
        return carry

    lax.fori_loop(0, length, gather, 0, unroll=4)


def pack_kernel(field, *refs):
    out, flat = refs[-2:]
    chans, length, width = field.shape
    zeros = jnp.zeros((chans, width), BF16)
    out[0:chans, :] = zeros
    out[(length + 1) * chans : (length + 2) * chans, :] = zeros
    turned(field, flat, out, 0, chans, 1)


def pack(field, after, weight):
    chans, length, width = field.shape
    spec = pl.BlockSpec(memory_space=pltpu.VMEM)
    return pl.pallas_call(
        pack_kernel,
        out_shape=jax.ShapeDtypeStruct(((length + 2) * chans, width), BF16),
        in_specs=[spec] + [pl.BlockSpec(memory_space=pl.ANY) for _ in after],
        out_specs=spec,
        scratch_shapes=[pltpu.VMEM((chans * length, width), F32)],
        compiler_params=pltpu.CompilerParams(vmem_limit_bytes=24 * 2**20),
        cost_estimate=pl.CostEstimate(
            flops=0, bytes_accessed=weight * field.size, transcendentals=0
        ),
    )(field, *after)


def in_steps(body, rows, count=8):
    step = rows // count

    def one(n, carry):
        body(n * step, step)
        return carry

    lax.fori_loop(0, count, one, 0)


def add_kernel(own, other, send, keep):
    rows = send.shape[0]
    mine = lax.axis_index("x") * rows
    theirs = rows - mine

    def total(at, step):
        at = pl.ds(pl.multiple_of(at, 16), step)
        return own[at, :] + other[at, :].astype(F32)

    def add(at, step):
        to = pl.ds(pl.multiple_of(at, 16), step)
        send[to, :] = total(theirs + at, step).astype(send.dtype)
        keep[to, :] = total(mine + at, step)

    in_steps(add, rows)


def add(own, other):
    rows = other.shape[0] // 2
    return vmem_call(
        add_kernel,
        (jax.ShapeDtypeStruct((rows, LANES), BF16), jax.ShapeDtypeStruct((rows, LANES), F32)),
        (),
        pl.CostEstimate(flops=0, bytes_accessed=8 * own.size, transcendentals=0),
    )(own, other)


def combine_kernel(keep, other, terms, more, out):
    parts, rows, _ = out.shape
    height, extra = (keep.shape[0] // parts, terms.shape[0] // parts)
    padded = rows - extra
    total = keep[...] + other[...].astype(F32)
    grads = terms[...] + more[...].astype(F32)
    for n in range(parts):
        value = total[n * height : (n + 1) * height]
        if padded > height:
            value = jnp.concatenate([value, jnp.zeros((padded - height, LANES), F32)], axis=0)
        out[n, 0:padded, :] = value.astype(out.dtype)
        out[n, padded:rows, :] = grads[n * extra : (n + 1) * extra].astype(out.dtype)


def combine(keep, other, terms, more, parts):
    rows = ceil_to(keep.shape[0] // parts, 16) + terms.shape[0] // parts
    return vmem_call(
        combine_kernel,
        jax.ShapeDtypeStruct((parts, rows, LANES), BF16),
        (),
        pl.CostEstimate(flops=0, bytes_accessed=8 * keep.size, transcendentals=0),
    )(keep, other, terms, more)


def split_to(total, mine, send, keep):
    half = total.shape[0] // 2
    keep[...] = total[pl.ds(pl.multiple_of(mine * half, 16), half), :]
    send[...] = total[pl.ds(pl.multiple_of((1 - mine) * half, 16), half), :].astype(send.dtype)


def swapped(value, axis="core"):
    return lax.ppermute(value, axis, [(0, 1), (1, 0)])


def plane_order():
    core = lax.axis_index("core")
    ahead = [core * n + (1 - core) * (2 - n) for n in range(3)]
    back = [core * (2 - n) + (1 - core) * n for n in range(3)]
    return (ahead, back)


def windows(packs, x, count):
    rows = [
        [p[pl.ds(pl.multiple_of((x + n) * count, 16), count), :] for p in packs]
        for n in range(GROUP + 2)
    ]
    return jnp.concatenate(
        [jnp.concatenate(sum(rows[g : g + 3], []), axis=0) for g in range(GROUP)], axis=1
    )


def ordered(acc, count, ahead):
    blocks = [pl.multiple_of((3 * j + n) * count, 16) for j in range(3) for n in ahead]
    return jnp.concatenate([acc[pl.ds(at, count), :] for at in blocks], axis=0)


def across_lanes(first, second):
    return lax.dot_general(
        first, second, (((1,), (1,)), ((), ())), preferred_element_type=F32
    )


def prepare_kernel(act, two, one, acts, w_two, w_one, flat):
    ahead, back = plane_order()
    turned(act, flat, acts, 0, act.shape[0], 0)
    w_two[...] = jnp.concatenate(
        [
            jnp.concatenate([two[back[n], 2 - j, 2 - k].astype(F32) for k in range(3)], axis=0)
            for j in range(3)
            for n in range(3)
        ],
        axis=1,
    ).astype(BF16)
    w_one[...] = jnp.concatenate(
        [
            jnp.concatenate([one[ahead[n], 2 - j, k].astype(F32) for n in range(3)], axis=0)
            for j in range(3)
            for k in range(3)
        ],
        axis=1,
    ).astype(BF16)


def prepare(act, kernel_two, kernel_one):
    c1, length, width = act.shape
    c0, c2 = (kernel_one.shape[3], kernel_two.shape[4])
    return vmem_call(
        prepare_kernel,
        (
            jax.ShapeDtypeStruct((length * c1, width), BF16),
            jax.ShapeDtypeStruct((3 * c1, 9 * c2), BF16),
            jax.ShapeDtypeStruct((3 * c0, 9 * c1), BF16),
        ),
        (pltpu.VMEM((c1 * length, width), F32),),
        pl.CostEstimate(flops=0, bytes_accessed=16 * act.size, transcendentals=0),
    )(act, kernel_two, kernel_one)


def first_kernel(pack_in, pack_0, pack_out, acts, w_two, pres, terms, acc):
    c1, c2 = (w_two.shape[0] // 3, w_two.shape[1] // 9)
    length = acts.shape[0] // c1
    packs = (pack_in, pack_0, pack_out)
    ahead, _ = plane_order()
    stacked = 3 * c1
    pres[0:stacked, :] = jnp.zeros((stacked, LANES), BF16)
    pres[(length + 1) * stacked : (length + 2) * stacked, :] = jnp.zeros((stacked, LANES), BF16)
    acc[...] = jnp.zeros_like(acc)

    def body(step, carry):
        x = step * GROUP
        right = windows(packs, x, c2)
        sums = jnp.dot(w_two[...], right, preferred_element_type=F32)
        columns = []
        for g in range(GROUP):
            part = sums[:, g * LANES : (g + 1) * LANES]
            grad = slid(part[0:c1], 1) + part[c1 : 2 * c1] + slid(part[2 * c1 : 3 * c1], -1)
            value = acts[pl.ds(pl.multiple_of((x + g) * c1, 16), c1), :].astype(F32)
            pre = (grad * jnp.where(value > 0, 1.0, 0.2)).astype(BF16).astype(F32)
            moved = jnp.concatenate([slid(pre, -1), pre, slid(pre, 1)], axis=0).astype(BF16)
            pres[pl.ds(pl.multiple_of((x + g + 1) * stacked, 16), stacked), :] = moved
            stack = jnp.concatenate([slid(value, 1), value, slid(value, -1)], axis=0)
            columns.append(stack.astype(BF16))
        acc[...] += across_lanes(right, jnp.concatenate(columns, axis=1))
        return carry

    lax.fori_loop(0, length // GROUP, body, 0, unroll=True)

    terms[...] = jnp.zeros_like(terms)
    total = ordered(acc, c2, ahead).T
    rows, width = total.shape
    for block in range(-(-width // LANES)):
        part = total[:, block * LANES : min(width, (block + 1) * LANES)]
        terms[block * rows : (block + 1) * rows, 0 : part.shape[1]] = part


def gradient_kernel(pack_in, pack_0, pack_out, pres, before, send, keep, acc, terms):
    c0, stacked = (acc.shape[0] // 9, acc.shape[1])
    packs = (pack_in, pack_0, pack_out)
    ahead, _ = plane_order()
    length = pres.shape[0] // stacked - 2
    acc[...] = jnp.zeros_like(acc)

    def body(step, carry):
        x = step * GROUP
        rows = [
            pres[pl.ds(pl.multiple_of((x + g + 1) * stacked, 16), stacked), :] for g in range(GROUP)
        ]
        acc[...] += across_lanes(windows(packs, x, c0), jnp.concatenate(rows, axis=1))
        return carry

    lax.fori_loop(0, length // GROUP, body, 0, unroll=True)

    used = before.shape[0]
    terms[0:used, :] = before[...]
    terms[used:, :] = jnp.zeros((terms.shape[0] - used, LANES), F32)
    total = ordered(acc, c0, ahead)
    terms[used : used + total.shape[0], 0 : total.shape[1]] = total
    split_to(terms, lax.axis_index("core"), send, keep)


def input_kernel(pres, w_one, own, inner, outer):
    c0, stacked = (w_one.shape[0] // 3, w_one.shape[1] // 3)
    length = pres.shape[0] // stacked - 2

    def body(step, carry):
        x = step * GROUP
        window = pres[pl.ds(pl.multiple_of(x * stacked, 16), (GROUP + 2) * stacked), :]
        moved = beside(window, 3 * stacked, stacked, GROUP)
        sums = jnp.dot(w_one[...], moved, preferred_element_type=F32)
        for g in range(GROUP):
            part = sums[:, g * LANES : (g + 1) * LANES]
            at = pl.ds(pl.multiple_of((x + g) * c0, 16), c0)
            for i, out in ((0, inner), (1, own), (2, outer)):
                out[at, :] = part[i * c0 : (i + 1) * c0].astype(out.dtype)
        return carry

    lax.fori_loop(0, length // GROUP, body, 0, unroll=True)


def vmem_call(body, out_shape, scratch=(), cost=None, limit=24 * 2**20):
    spec = pl.BlockSpec(memory_space=pltpu.VMEM)
    return pl.pallas_call(
        body,
        out_shape=out_shape,
        out_specs=jax.tree.map(lambda _: spec, out_shape),
        scratch_shapes=list(scratch),
        compiler_params=pltpu.CompilerParams(vmem_limit_bytes=limit),
        cost_estimate=cost,
    )


def first_part(packs, acts, w_two):
    c1, c2, width = (w_two.shape[0] // 3, w_two.shape[1] // 9, acts.shape[1])
    length = acts.shape[0] // c1
    return vmem_call(
        first_kernel,
        (
            jax.ShapeDtypeStruct(((length + 2) * 3 * c1, width), BF16),
            jax.ShapeDtypeStruct((-(-9 * c2 // LANES) * 3 * c1, LANES), F32),
        ),
        (pltpu.VMEM((9 * c2, 3 * c1), F32),),
        pl.CostEstimate(flops=10**9, bytes_accessed=20 * 2**20, transcendentals=0),
    )(*packs, acts, w_two)


def gradient_part(packs, pres, terms, rows, c1):
    width = pres.shape[1]
    c0 = packs[0].shape[0] // (pres.shape[0] // (3 * c1))
    return vmem_call(
        gradient_kernel,
        (
            jax.ShapeDtypeStruct((rows // 2, LANES), BF16),
            jax.ShapeDtypeStruct((rows // 2, LANES), F32),
        ),
        (pltpu.VMEM((9 * c0, 3 * c1), F32), pltpu.VMEM((rows, width), F32)),
        pl.CostEstimate(flops=10**9, bytes_accessed=5 * 2**20, transcendentals=0),
    )(*packs, pres, terms)


def input_part(pres, w_one):
    c0, stacked = (w_one.shape[0] // 3, w_one.shape[1] // 3)
    plane = ((pres.shape[0] // stacked - 2) * c0, pres.shape[1])
    return vmem_call(
        input_kernel,
        (
            jax.ShapeDtypeStruct(plane, F32),
            jax.ShapeDtypeStruct(plane, BF16),
            jax.ShapeDtypeStruct(plane, BF16),
        ),
        (),
        pl.CostEstimate(flops=10**9, bytes_accessed=5 * 2**20, transcendentals=0),
    )(pres, w_one)


def merge_kernel(own, first, second, out, flat):
    chans, length, _ = out.shape

    def add(step, carry):
        at = pl.ds(pl.multiple_of(step * 64, 64), 64)
        flat[at, :] = own[at, :] + first[at, :].astype(F32) + second[at, :].astype(F32)
        return carry

    lax.fori_loop(0, own.shape[0] // 64, add, 0, unroll=4)

    def gather(c, carry):
        out[c] = flat[pl.ds(c, length, stride=chans), :].astype(out.dtype)
        return carry

    lax.fori_loop(0, chans, gather, 0, unroll=4)


def merge(own, first, second, shape):
    return vmem_call(
        merge_kernel,
        jax.ShapeDtypeStruct(shape, BF16),
        (pltpu.VMEM(own.shape, F32),),
        pl.CostEstimate(flops=2 * own.size, bytes_accessed=8 * own.size, transcendentals=0),
    )(own, first, second)


def share_kernel(scale, parts, out):
    copies, rows, _ = parts.shape
    padded = out.shape[1] - rows
    near = jnp.sum(parts[0 : copies // 2, 0:padded, :].astype(F32), axis=0).astype(BF16)
    far = jnp.sum(parts[copies // 2 :, 0:padded, :].astype(F32), axis=0).astype(BF16)
    grads = (jnp.sum(parts[:, padded:rows, :].astype(F32), axis=0) * scale).astype(BF16)

    def write(n, carry):
        out[n, 0:padded, :] = near
        out[n, padded : 2 * padded, :] = far
        out[n, 2 * padded :, :] = grads
        return carry

    lax.fori_loop(0, copies, write, 0)


def share(parts, extra, scale):
    copies, rows, _ = parts.shape
    return vmem_call(
        lambda *refs: share_kernel(scale, *refs),
        jax.ShapeDtypeStruct((copies, 2 * rows - extra, LANES), BF16),
        (),
        pl.CostEstimate(flops=parts.size, bytes_accessed=6 * parts.size, transcendentals=0),
    )(parts)


def place(source, height, padded, which, bucket, buffer, sems):
    copies, count = (source.shape[0], sems.shape[0])
    step = 2 * copies // count
    sent = []
    for n in range(count):
        for m in range(n * step, (n + 1) * step):
            half, q = (m // copies, m % copies)
            value = source[q, half * padded : (half + 1) * padded, :].astype(F32)
            buffer[m * height : (m + 1) * height, :] = value[0:height]
        rows = pl.ds(n * step * height, step * height)
        at = (which * count + n) * step * height
        at = pl.ds(pl.multiple_of(at, 8), step * height)
        sent.append(pltpu.make_async_copy(buffer.at[rows], bucket.at[at], sems.at[n]))
        sent[-1].start()
    return sent


def start_kernel(height, padded, mine, bucket, buffer, sems):
    for copy in place(mine, height, padded, lax.axis_index("core"), bucket, buffer, sems):
        copy.wait()


def finish_kernel(
    sizes, height, padded, mine, other, partial,
    bucket, out_one, out_two,
    raw, one, two, out_sems, buffer, sems,
):
    c0, c1, c2 = sizes
    copies, rows, _ = mine.shape
    extra = rows - 2 * padded
    me = lax.axis_index("core")
    sent = place(other, height, padded, 1 - me, bucket, buffer, sems)

    for q in range(copies):
        for source, which in ((mine, me), (other, 1 - me)):
            at = pl.multiple_of((which * copies + q) * extra, 8)
            raw[pl.ds(at, extra), :] = source[q, 2 * padded : rows, :].astype(F32)
    block = 3 * c1
    first = -(-9 * c2 // LANES) * block
    for i in range(3):
        for j in range(3):
            column = ((2 - j) * 3 + 2 - i) * c2
            whole, lane = (column // LANES, column % LANES)
            two[(3 * i + j) * block : (3 * i + j + 1) * block, :] = raw[
                whole * block : (whole + 1) * block, lane : lane + c2
            ]
        at = pl.ds(3 * i * block, 3 * block)
        sent.append(pltpu.make_async_copy(two.at[at], out_two.at[at], out_sems.at[i]))
        sent[-1].start()
    for i in range(3):
        for j in range(3):
            row = first + (3 * j + i) * c0
            for k in range(3):
                to = (9 * i + 3 * j + k) * c0
                one[to : to + c0, :] = raw[row : row + c0, k * c1 : (k + 1) * c1]
        at = pl.ds(9 * i * c0, 9 * c0)
        sent.append(pltpu.make_async_copy(one.at[at], out_one.at[at], out_sems.at[3 + i]))
        sent[-1].start()
    for copy in sent:
        copy.wait()


def finish(mine, other, length, sizes):
    c0, c1, c2 = sizes
    copies, rows, _ = mine.shape
    height = length // LANES // (4 * copies)
    padded = ceil_to(height, 16)
    spec = pl.BlockSpec(memory_space=pltpu.VMEM)
    remote = pl.BlockSpec(memory_space=pltpu.HBM)
    whole = jax.ShapeDtypeStruct((length // LANES, LANES), F32)
    chunks = 4
    scratch = [
        pltpu.VMEM((2 * copies * height, LANES), F32),
        pltpu.SemaphoreType.DMA((chunks,)),
    ]
    params = pltpu.CompilerParams(vmem_limit_bytes=24 * 2**20)
    partial = pl.pallas_call(
        lambda *refs: start_kernel(height, padded, *refs),
        out_shape=whole,
        in_specs=[spec],
        out_specs=remote,
        scratch_shapes=scratch,
        compiler_params=params,
    )(mine)
    return pl.pallas_call(
        lambda *refs: finish_kernel(sizes, height, padded, *refs),
        out_shape=(
            whole,
            jax.ShapeDtypeStruct((27 * c0, c1), F32),
            jax.ShapeDtypeStruct((27 * c1, c2), F32),
        ),
        in_specs=[spec, spec, remote],
        out_specs=(remote, remote, remote),
        scratch_shapes=[
            pltpu.VMEM((2 * copies * (rows - 2 * padded), LANES), F32),
            pltpu.VMEM((27 * c0, c1), F32),
            pltpu.VMEM((27 * c1, c2), F32),
            pltpu.SemaphoreType.DMA((6,)),
        ]
        + scratch,
        input_output_aliases={2: 0},
        compiler_params=params,
    )(mine, other, partial)


def crossed(value):
    pairs = [(n, n + 1) for n in range(1, lax.axis_size(SPACE) - 1, 2)]
    return lax.ppermute(value, SPACE, pairs + [(m, n) for n, m in pairs])


def per_device(volume_in, hidden_act, out_cot, kernel_one, kernel_two, grad_bucket):
    c0, c1, c2 = (volume_in.shape[2], hidden_act.shape[2], out_cot.shape[2])
    devices, copies = (lax.axis_size(EVERY), lax.axis_size(SAME))
    length = grad_bucket.shape[1]
    bucket = grad_bucket.reshape(length // LANES, LANES)
    cot = pack(out_cot[0, 0], [], 256)
    bucket, cot = lax.optimization_barrier((bucket, cot))
    core, half = (lax.axis_index("core"), bucket.shape[0] // 2)
    send = lax.dynamic_slice_in_dim(bucket, (1 - core) * half, half).astype(BF16)
    near = lax.dynamic_slice_in_dim(bucket, core * half, half)
    cot, send, near = lax.optimization_barrier((cot, send, near))
    cots = (swapped(cot), cot, crossed(cot))
    vol = pack(volume_in[0, 0], [cot], 16)
    vols = (swapped(vol), vol, crossed(vol))
    send, near = add(near, swapped(send))
    act, send, near = lax.optimization_barrier((hidden_act[0, 0], send, near))
    far = swapped(send, "x")

    used = -(-9 * c2 // LANES) * 3 * c1 + 9 * c0
    rows = ceil_to(used, 16 * devices)
    acts, w_two, w_one = prepare(act, kernel_two, kernel_one)
    pres, terms = first_part(cots, acts, w_two)
    send, keep = gradient_part(vols, pres, terms, rows, c1)
    own, inner, outer = input_part(pres, w_one)
    parts = combine(near, far, keep, swapped(send), copies)
    parts, inner, outer = lax.optimization_barrier((parts, inner, outer))
    parts = lax.all_to_all(parts, SAME, 0, 0)
    parts, inner, outer = lax.optimization_barrier((parts, swapped(inner), crossed(outer)))
    cells = volume_in.shape[3] * volume_in.shape[4] * devices
    shares = share(parts, rows // devices, 1.0 / math.sqrt(cells))

    mine = lax.all_to_all(shares, SAME, 0, 0)
    mine, own = lax.optimization_barrier((mine, own))
    grad_input = merge(own, inner, outer, volume_in.shape[2:])
    bucket_sum, total_one, total_two = finish(mine, swapped(mine), length, (c0, c1, c2))
    return (
        grad_input[None, None],
        total_one.reshape(3, 3, 3, c0, c1),
        total_two.reshape(3, 3, 3, c1, c2),
        bucket_sum.reshape(length),
    )


def solution(mesh):
    dp, space = (mesh.shape["dp"], mesh.shape["space"])
    split = Mesh(mesh.devices.reshape(dp // 2, 2, space // 2, 2), EVERY)
    volume = P(("z", "x"), SPACE, None, None, None)
    in_specs = (volume, volume, volume, P(), P(), P(EVERY, None))
    out_specs = (volume, P(), P(), P())
    return jax.shard_map(
        per_device, mesh=split, in_specs=in_specs, out_specs=out_specs, check_vma=False
    )
```

```python
import math

import jax
import jax.numpy as jnp
from jax import lax
from jax.experimental import pallas as pl
from jax.experimental.pallas import tpu as pltpu
from jax.sharding import Mesh, PartitionSpec as P

SPACE = ("y", "core")
SAME = ("x", "z", "y")
EVERY = ("z", "x", "y", "core")
GROUP = 8
LANES = 128
BF16 = jnp.bfloat16
F32 = jnp.float32


def ceil_to(value, step):
    return -(-value // step) * step


def slid(value, step):
    lane = lax.broadcasted_iota(jnp.int32, value.shape, 1)
    width = value.shape[1]
    keep = lane >= step if step > 0 else lane < width + step
    return jnp.where(keep, pltpu.roll(value, step % width, 1), 0.0)


def beside(window, rows, step, count):
    return jnp.concatenate([window[g * step : g * step + rows] for g in range(count)], axis=1)


def turned(src, flat, dst, offset, pitch, lead):
    chans, length, _ = src.shape

    def stage(c, carry):
        flat[pl.ds(pl.multiple_of(c * length, length), length), :] = src[c].astype(F32)
        return carry

    lax.fori_loop(0, chans, stage, 0, unroll=4)

    def gather(x, carry):
        rows = flat[pl.ds(x, chans, stride=length), :]
        at = pl.multiple_of((x + lead) * pitch + offset, 16)
        dst[pl.ds(at, chans), :] = rows.astype(BF16)
        return carry

    lax.fori_loop(0, length, gather, 0, unroll=4)


def pack_kernel(field, *refs):
    out, flat = refs[-2:]
    chans, length, width = field.shape
    zeros = jnp.zeros((chans, width), BF16)
    out[0:chans, :] = zeros
    out[(length + 1) * chans : (length + 2) * chans, :] = zeros
    turned(field, flat, out, 0, chans, 1)


def pack(field, after, weight):
    chans, length, width = field.shape
    spec = pl.BlockSpec(memory_space=pltpu.VMEM)
    return pl.pallas_call(
        pack_kernel,
        out_shape=jax.ShapeDtypeStruct(((length + 2) * chans, width), BF16),
        in_specs=[spec] + [pl.BlockSpec(memory_space=pl.ANY) for _ in after],
        out_specs=spec,
        scratch_shapes=[pltpu.VMEM((chans * length, width), F32)],
        compiler_params=pltpu.CompilerParams(vmem_limit_bytes=24 * 2**20),
        cost_estimate=pl.CostEstimate(
            flops=0, bytes_accessed=weight * field.size, transcendentals=0
        ),
    )(field, *after)


def in_steps(body, rows, count=8):
    step = rows // count

    def one(n, carry):
        body(n * step, step)
        return carry

    lax.fori_loop(0, count, one, 0)


def add_kernel(own, other, send, keep):
    rows = send.shape[0]
    mine = lax.axis_index("x") * rows
    theirs = rows - mine

    def total(at, step):
        at = pl.ds(pl.multiple_of(at, 16), step)
        return own[at, :] + other[at, :].astype(F32)

    def add(at, step):
        to = pl.ds(pl.multiple_of(at, 16), step)
        send[to, :] = total(theirs + at, step).astype(send.dtype)
        keep[to, :] = total(mine + at, step)

    in_steps(add, rows)


def add(own, other):
    rows = other.shape[0] // 2
    return vmem_call(
        add_kernel,
        (jax.ShapeDtypeStruct((rows, LANES), BF16), jax.ShapeDtypeStruct((rows, LANES), F32)),
        (),
        pl.CostEstimate(flops=0, bytes_accessed=8 * own.size, transcendentals=0),
    )(own, other)


def combine_kernel(keep, other, terms, more, out):
    parts, rows, _ = out.shape
    height, extra = (keep.shape[0] // parts, terms.shape[0] // parts)
    padded = rows - extra
    total = keep[...] + other[...].astype(F32)
    grads = terms[...] + more[...].astype(F32)
    for n in range(parts):
        value = total[n * height : (n + 1) * height]
        if padded > height:
            value = jnp.concatenate([value, jnp.zeros((padded - height, LANES), F32)], axis=0)
        out[n, 0:padded, :] = value.astype(out.dtype)
        out[n, padded:rows, :] = grads[n * extra : (n + 1) * extra].astype(out.dtype)


def combine(keep, other, terms, more, parts):
    rows = ceil_to(keep.shape[0] // parts, 16) + terms.shape[0] // parts
    return vmem_call(
        combine_kernel,
        jax.ShapeDtypeStruct((parts, rows, LANES), BF16),
        (),
        pl.CostEstimate(flops=0, bytes_accessed=8 * keep.size, transcendentals=0),
    )(keep, other, terms, more)


def split_to(total, mine, send, keep):
    half = total.shape[0] // 2
    keep[...] = total[pl.ds(pl.multiple_of(mine * half, 16), half), :]
    send[...] = total[pl.ds(pl.multiple_of((1 - mine) * half, 16), half), :].astype(send.dtype)


def swapped(value, axis="core"):
    return lax.ppermute(value, axis, [(0, 1), (1, 0)])


def plane_order():
    core = lax.axis_index("core")
    ahead = [core * n + (1 - core) * (2 - n) for n in range(3)]
    back = [core * (2 - n) + (1 - core) * n for n in range(3)]
    return (ahead, back)


def windows(packs, x, count):
    rows = [
        [p[pl.ds(pl.multiple_of((x + n) * count, 16), count), :] for p in packs]
        for n in range(GROUP + 2)
    ]
    return jnp.concatenate(
        [jnp.concatenate(sum(rows[g : g + 3], []), axis=0) for g in range(GROUP)], axis=1
    )


def ordered(acc, count, ahead):
    blocks = [pl.multiple_of((3 * j + n) * count, 16) for j in range(3) for n in ahead]
    return jnp.concatenate([acc[pl.ds(at, count), :] for at in blocks], axis=0)


def across_lanes(first, second):
    return lax.dot_general(
        first, second, (((1,), (1,)), ((), ())), preferred_element_type=F32
    )


def prepare_kernel(act, two, one, acts, w_two, w_one, flat):
    ahead, back = plane_order()
    turned(act, flat, acts, 0, act.shape[0], 0)
    w_two[...] = jnp.concatenate(
        [
            jnp.concatenate([two[back[n], 2 - j, 2 - k].astype(F32) for k in range(3)], axis=0)
            for j in range(3)
            for n in range(3)
        ],
        axis=1,
    ).astype(BF16)
    w_one[...] = jnp.concatenate(
        [
            jnp.concatenate([one[ahead[n], 2 - j, k].astype(F32) for n in range(3)], axis=0)
            for j in range(3)
            for k in range(3)
        ],
        axis=1,
    ).astype(BF16)


def prepare(act, kernel_two, kernel_one):
    c1, length, width = act.shape
    c0, c2 = (kernel_one.shape[3], kernel_two.shape[4])
    return vmem_call(
        prepare_kernel,
        (
            jax.ShapeDtypeStruct((length * c1, width), BF16),
            jax.ShapeDtypeStruct((3 * c1, 9 * c2), BF16),
            jax.ShapeDtypeStruct((3 * c0, 9 * c1), BF16),
        ),
        (pltpu.VMEM((c1 * length, width), F32),),
        pl.CostEstimate(flops=0, bytes_accessed=16 * act.size, transcendentals=0),
    )(act, kernel_two, kernel_one)


def first_kernel(pack_in, pack_0, pack_out, acts, w_two, pres, terms, acc):
    c1, c2 = (w_two.shape[0] // 3, w_two.shape[1] // 9)
    length = acts.shape[0] // c1
    packs = (pack_in, pack_0, pack_out)
    ahead, _ = plane_order()
    stacked = 3 * c1
    pres[0:stacked, :] = jnp.zeros((stacked, LANES), BF16)
    pres[(length + 1) * stacked : (length + 2) * stacked, :] = jnp.zeros((stacked, LANES), BF16)
    acc[...] = jnp.zeros_like(acc)

    def body(step, carry):
        x = step * GROUP
        right = windows(packs, x, c2)
        sums = jnp.dot(w_two[...], right, preferred_element_type=F32)
        columns = []
        for g in range(GROUP):
            part = sums[:, g * LANES : (g + 1) * LANES]
            grad = slid(part[0:c1], 1) + part[c1 : 2 * c1] + slid(part[2 * c1 : 3 * c1], -1)
            value = acts[pl.ds(pl.multiple_of((x + g) * c1, 16), c1), :].astype(F32)
            pre = (grad * jnp.where(value > 0, 1.0, 0.2)).astype(BF16).astype(F32)
            moved = jnp.concatenate([slid(pre, -1), pre, slid(pre, 1)], axis=0).astype(BF16)
            pres[pl.ds(pl.multiple_of((x + g + 1) * stacked, 16), stacked), :] = moved
            stack = jnp.concatenate([slid(value, 1), value, slid(value, -1)], axis=0)
            columns.append(stack.astype(BF16))
        acc[...] += across_lanes(right, jnp.concatenate(columns, axis=1))
        return carry

    lax.fori_loop(0, length // GROUP, body, 0, unroll=True)

    terms[...] = jnp.zeros_like(terms)
    total = ordered(acc, c2, ahead).T
    rows, width = total.shape
    for block in range(-(-width // LANES)):
        part = total[:, block * LANES : min(width, (block + 1) * LANES)]
        terms[block * rows : (block + 1) * rows, 0 : part.shape[1]] = part


def gradient_kernel(pack_in, pack_0, pack_out, pres, before, send, keep, acc, terms):
    c0, stacked = (acc.shape[0] // 9, acc.shape[1])
    packs = (pack_in, pack_0, pack_out)
    ahead, _ = plane_order()
    length = pres.shape[0] // stacked - 2
    acc[...] = jnp.zeros_like(acc)

    def body(step, carry):
        x = step * GROUP
        rows = [
            pres[pl.ds(pl.multiple_of((x + g + 1) * stacked, 16), stacked), :] for g in range(GROUP)
        ]
        acc[...] += across_lanes(windows(packs, x, c0), jnp.concatenate(rows, axis=1))
        return carry

    lax.fori_loop(0, length // GROUP, body, 0, unroll=True)

    used = before.shape[0]
    terms[0:used, :] = before[...]
    terms[used:, :] = jnp.zeros((terms.shape[0] - used, LANES), F32)
    total = ordered(acc, c0, ahead)
    terms[used : used + total.shape[0], 0 : total.shape[1]] = total
    split_to(terms, lax.axis_index("core"), send, keep)


def input_kernel(pres, w_one, own, inner, outer):
    c0, stacked = (w_one.shape[0] // 3, w_one.shape[1] // 3)
    length = pres.shape[0] // stacked - 2

    def body(step, carry):
        x = step * GROUP
        window = pres[pl.ds(pl.multiple_of(x * stacked, 16), (GROUP + 2) * stacked), :]
        moved = beside(window, 3 * stacked, stacked, GROUP)
        sums = jnp.dot(w_one[...], moved, preferred_element_type=F32)
        for g in range(GROUP):
            part = sums[:, g * LANES : (g + 1) * LANES]
            at = pl.ds(pl.multiple_of((x + g) * c0, 16), c0)
            for i, out in ((0, inner), (1, own), (2, outer)):
                out[at, :] = part[i * c0 : (i + 1) * c0].astype(out.dtype)
        return carry

    lax.fori_loop(0, length // GROUP, body, 0, unroll=True)


def vmem_call(body, out_shape, scratch=(), cost=None, limit=24 * 2**20):
    spec = pl.BlockSpec(memory_space=pltpu.VMEM)
    return pl.pallas_call(
        body,
        out_shape=out_shape,
        out_specs=jax.tree.map(lambda _: spec, out_shape),
        scratch_shapes=list(scratch),
        compiler_params=pltpu.CompilerParams(vmem_limit_bytes=limit),
        cost_estimate=cost,
    )


def first_part(packs, acts, w_two):
    c1, c2, width = (w_two.shape[0] // 3, w_two.shape[1] // 9, acts.shape[1])
    length = acts.shape[0] // c1
    return vmem_call(
        first_kernel,
        (
            jax.ShapeDtypeStruct(((length + 2) * 3 * c1, width), BF16),
            jax.ShapeDtypeStruct((-(-9 * c2 // LANES) * 3 * c1, LANES), F32),
        ),
        (pltpu.VMEM((9 * c2, 3 * c1), F32),),
        pl.CostEstimate(flops=10**9, bytes_accessed=20 * 2**20, transcendentals=0),
    )(*packs, acts, w_two)


def gradient_part(packs, pres, terms, rows, c1):
    width = pres.shape[1]
    c0 = packs[0].shape[0] // (pres.shape[0] // (3 * c1))
    return vmem_call(
        gradient_kernel,
        (
            jax.ShapeDtypeStruct((rows // 2, LANES), BF16),
            jax.ShapeDtypeStruct((rows // 2, LANES), F32),
        ),
        (pltpu.VMEM((9 * c0, 3 * c1), F32), pltpu.VMEM((rows, width), F32)),
        pl.CostEstimate(flops=10**9, bytes_accessed=5 * 2**20, transcendentals=0),
    )(*packs, pres, terms)


def input_part(pres, w_one):
    c0, stacked = (w_one.shape[0] // 3, w_one.shape[1] // 3)
    plane = ((pres.shape[0] // stacked - 2) * c0, pres.shape[1])
    return vmem_call(
        input_kernel,
        (
            jax.ShapeDtypeStruct(plane, F32),
            jax.ShapeDtypeStruct(plane, BF16),
            jax.ShapeDtypeStruct(plane, BF16),
        ),
        (),
        pl.CostEstimate(flops=10**9, bytes_accessed=5 * 2**20, transcendentals=0),
    )(pres, w_one)


def merge_kernel(own, first, second, out, flat):
    chans, length, _ = out.shape

    def add(step, carry):
        at = pl.ds(pl.multiple_of(step * 64, 64), 64)
        flat[at, :] = own[at, :] + first[at, :].astype(F32) + second[at, :].astype(F32)
        return carry

    lax.fori_loop(0, own.shape[0] // 64, add, 0, unroll=4)

    def gather(c, carry):
        out[c] = flat[pl.ds(c, length, stride=chans), :].astype(out.dtype)
        return carry

    lax.fori_loop(0, chans, gather, 0, unroll=4)


def merge(own, first, second, shape):
    return vmem_call(
        merge_kernel,
        jax.ShapeDtypeStruct(shape, BF16),
        (pltpu.VMEM(own.shape, F32),),
        pl.CostEstimate(flops=2 * own.size, bytes_accessed=8 * own.size, transcendentals=0),
    )(own, first, second)


def share_kernel(scale, parts, out):
    copies, rows, _ = parts.shape
    padded = out.shape[1] - rows
    near = jnp.sum(parts[0 : copies // 2, 0:padded, :].astype(F32), axis=0).astype(BF16)
    far = jnp.sum(parts[copies // 2 :, 0:padded, :].astype(F32), axis=0).astype(BF16)
    grads = (jnp.sum(parts[:, padded:rows, :].astype(F32), axis=0) * scale).astype(BF16)

    def write(n, carry):
        out[n, 0:padded, :] = near
        out[n, padded : 2 * padded, :] = far
        out[n, 2 * padded :, :] = grads
        return carry

    lax.fori_loop(0, copies, write, 0)


def share(parts, extra, scale):
    copies, rows, _ = parts.shape
    return vmem_call(
        lambda *refs: share_kernel(scale, *refs),
        jax.ShapeDtypeStruct((copies, 2 * rows - extra, LANES), BF16),
        (),
        pl.CostEstimate(flops=parts.size, bytes_accessed=6 * parts.size, transcendentals=0),
    )(parts)


def place(source, height, padded, which, bucket, buffer, sems):
    copies, count = (source.shape[0], sems.shape[0])
    step = 2 * copies // count
    sent = []
    for n in range(count):
        for m in range(n * step, (n + 1) * step):
            half, q = (m // copies, m % copies)
            value = source[q, half * padded : (half + 1) * padded, :].astype(F32)
            buffer[m * height : (m + 1) * height, :] = value[0:height]
        rows = pl.ds(n * step * height, step * height)
        at = (which * count + n) * step * height
        at = pl.ds(pl.multiple_of(at, 8), step * height)
        sent.append(pltpu.make_async_copy(buffer.at[rows], bucket.at[at], sems.at[n]))
        sent[-1].start()
    return sent


def start_kernel(height, padded, mine, bucket, buffer, sems):
    for copy in place(mine, height, padded, lax.axis_index("core"), bucket, buffer, sems):
        copy.wait()


def finish_kernel(
    sizes, height, padded, mine, other, partial,
    bucket, out_one, out_two,
    raw, one, two, out_sems, buffer, sems,
):
    c0, c1, c2 = sizes
    copies, rows, _ = mine.shape
    extra = rows - 2 * padded
    me = lax.axis_index("core")
    sent = place(other, height, padded, 1 - me, bucket, buffer, sems)

    for q in range(copies):
        for source, which in ((mine, me), (other, 1 - me)):
            at = pl.multiple_of((which * copies + q) * extra, 8)
            raw[pl.ds(at, extra), :] = source[q, 2 * padded : rows, :].astype(F32)
    block = 3 * c1
    first = -(-9 * c2 // LANES) * block
    for i in range(3):
        for j in range(3):
            column = ((2 - j) * 3 + 2 - i) * c2
            whole, lane = (column // LANES, column % LANES)
            two[(3 * i + j) * block : (3 * i + j + 1) * block, :] = raw[
                whole * block : (whole + 1) * block, lane : lane + c2
            ]
        at = pl.ds(3 * i * block, 3 * block)
        sent.append(pltpu.make_async_copy(two.at[at], out_two.at[at], out_sems.at[i]))
        sent[-1].start()
    for i in range(3):
        for j in range(3):
            row = first + (3 * j + i) * c0
            for k in range(3):
                to = (9 * i + 3 * j + k) * c0
                one[to : to + c0, :] = raw[row : row + c0, k * c1 : (k + 1) * c1]
        at = pl.ds(9 * i * c0, 9 * c0)
        sent.append(pltpu.make_async_copy(one.at[at], out_one.at[at], out_sems.at[3 + i]))
        sent[-1].start()
    for copy in sent:
        copy.wait()


def finish(mine, other, length, sizes):
    c0, c1, c2 = sizes
    copies, rows, _ = mine.shape
    height = length // LANES // (4 * copies)
    padded = ceil_to(height, 16)
    spec = pl.BlockSpec(memory_space=pltpu.VMEM)
    remote = pl.BlockSpec(memory_space=pltpu.HBM)
    whole = jax.ShapeDtypeStruct((length // LANES, LANES), F32)
    chunks = 4
    scratch = [
        pltpu.VMEM((2 * copies * height, LANES), F32),
        pltpu.SemaphoreType.DMA((chunks,)),
    ]
    params = pltpu.CompilerParams(vmem_limit_bytes=24 * 2**20)
    partial = pl.pallas_call(
        lambda *refs: start_kernel(height, padded, *refs),
        out_shape=whole,
        in_specs=[spec],
        out_specs=remote,
        scratch_shapes=scratch,
        compiler_params=params,
    )(mine)
    return pl.pallas_call(
        lambda *refs: finish_kernel(sizes, height, padded, *refs),
        out_shape=(
            whole,
            jax.ShapeDtypeStruct((27 * c0, c1), F32),
            jax.ShapeDtypeStruct((27 * c1, c2), F32),
        ),
        in_specs=[spec, spec, remote],
        out_specs=(remote, remote, remote),
        scratch_shapes=[
            pltpu.VMEM((2 * copies * (rows - 2 * padded), LANES), F32),
            pltpu.VMEM((27 * c0, c1), F32),
            pltpu.VMEM((27 * c1, c2), F32),
            pltpu.SemaphoreType.DMA((6,)),
        ]
        + scratch,
        input_output_aliases={2: 0},
        compiler_params=params,
    )(mine, other, partial)


def crossed(value):
    pairs = [(n, n + 1) for n in range(1, lax.axis_size(SPACE) - 1, 2)]
    return lax.ppermute(value, SPACE, pairs + [(m, n) for n, m in pairs])


def per_device(volume_in, hidden_act, out_cot, kernel_one, kernel_two, grad_bucket):
    c0, c1, c2 = (volume_in.shape[2], hidden_act.shape[2], out_cot.shape[2])
    devices, copies = (lax.axis_size(EVERY), lax.axis_size(SAME))
    length = grad_bucket.shape[1]
    bucket = grad_bucket.reshape(length // LANES, LANES)
    cot = pack(out_cot[0, 0], [], 256)
    bucket, cot = lax.optimization_barrier((bucket, cot))
    core, half = (lax.axis_index("core"), bucket.shape[0] // 2)
    send = lax.dynamic_slice_in_dim(bucket, (1 - core) * half, half).astype(BF16)
    near = lax.dynamic_slice_in_dim(bucket, core * half, half)
    cot, send, near = lax.optimization_barrier((cot, send, near))
    cots = (swapped(cot), cot, crossed(cot))
    vol = pack(volume_in[0, 0], [cot], 16)
    vols = (swapped(vol), vol, crossed(vol))
    send, near = add(near, swapped(send))
    act, send, near = lax.optimization_barrier((hidden_act[0, 0], send, near))
    far = swapped(send, "x")

    used = -(-9 * c2 // LANES) * 3 * c1 + 9 * c0
    rows = ceil_to(used, 16 * devices)
    acts, w_two, w_one = prepare(act, kernel_two, kernel_one)
    pres, terms = first_part(cots, acts, w_two)
    send, keep = gradient_part(vols, pres, terms, rows, c1)
    own, inner, outer = input_part(pres, w_one)
    parts = combine(near, far, keep, swapped(send), copies)
    parts, inner, outer = lax.optimization_barrier((parts, inner, outer))
    parts = lax.all_to_all(parts, SAME, 0, 0)
    cells = volume_in.shape[3] * volume_in.shape[4] * devices
    shares = share(parts, rows // devices, 1.0 / math.sqrt(cells))

    shares, inner, outer = lax.optimization_barrier((shares, inner, outer))
    mine = lax.all_to_all(shares, SAME, 0, 0)
    inner, outer = (swapped(inner), crossed(outer))
    mine, own, inner, outer = lax.optimization_barrier((mine, own, inner, outer))
    grad_input = merge(own, inner, outer, volume_in.shape[2:])
    bucket_sum, total_one, total_two = finish(mine, swapped(mine), length, (c0, c1, c2))
    return (
        grad_input[None, None],
        total_one.reshape(3, 3, 3, c0, c1),
        total_two.reshape(3, 3, 3, c1, c2),
        bucket_sum.reshape(length),
    )


def solution(mesh):
    dp, space = (mesh.shape["dp"], mesh.shape["space"])
    split = Mesh(mesh.devices.reshape(dp // 2, 2, space // 2, 2), EVERY)
    volume = P(("z", "x"), SPACE, None, None, None)
    in_specs = (volume, volume, volume, P(), P(), P(EVERY, None))
    out_specs = (volume, P(), P(), P())
    return jax.shard_map(
        per_device, mesh=split, in_specs=in_specs, out_specs=out_specs, check_vma=False
    )
```

```python
import math

import jax
import jax.numpy as jnp
from jax import lax
from jax.experimental import pallas as pl
from jax.experimental.pallas import tpu as pltpu
from jax.sharding import Mesh, PartitionSpec as P

SPACE = ("y", "core")
SAME = ("x", "z", "y")
EVERY = ("z", "x", "y", "core")
GROUP = 8
LANES = 128
BF16 = jnp.bfloat16
F32 = jnp.float32


def ceil_to(value, step):
    return -(-value // step) * step


def slid(value, step):
    lane = lax.broadcasted_iota(jnp.int32, value.shape, 1)
    width = value.shape[1]
    keep = lane >= step if step > 0 else lane < width + step
    return jnp.where(keep, pltpu.roll(value, step % width, 1), 0.0)


def beside(window, rows, step, count):
    return jnp.concatenate([window[g * step : g * step + rows] for g in range(count)], axis=1)


def turned(src, flat, dst):
    chans, length, _ = src.shape

    def stage(c, carry):
        flat[pl.ds(pl.multiple_of(c * length, length), length), :] = src[c].astype(F32)
        return carry

    lax.fori_loop(0, chans, stage, 0, unroll=4)

    def gather(x, carry):
        rows = flat[pl.ds(x, chans, stride=length), :]
        dst[pl.ds(pl.multiple_of(x * chans, 16), chans), :] = rows.astype(BF16)
        return carry

    lax.fori_loop(0, length, gather, 0, unroll=4)


def pack_kernel(field, *refs):
    out, flat = refs[-2:]
    turned(field, flat, out)


def pack(field, after, weight):
    chans, length, width = field.shape
    spec = pl.BlockSpec(memory_space=pltpu.VMEM)
    return pl.pallas_call(
        pack_kernel,
        out_shape=jax.ShapeDtypeStruct((length * chans, width), BF16),
        in_specs=[spec] + [pl.BlockSpec(memory_space=pl.ANY) for _ in after],
        out_specs=spec,
        scratch_shapes=[pltpu.VMEM((chans * length, width), F32)],
        compiler_params=pltpu.CompilerParams(vmem_limit_bytes=24 * 2**20),
        cost_estimate=pl.CostEstimate(
            flops=0, bytes_accessed=weight * field.size, transcendentals=0
        ),
    )(field, *after)


def in_steps(body, rows, count=8):
    step = rows // count

    def one(n, carry):
        body(n * step, step)
        return carry

    lax.fori_loop(0, count, one, 0)


def add_kernel(own, other, send, keep):
    rows = send.shape[0]
    mine = lax.axis_index("x") * rows
    theirs = rows - mine

    def total(at, step):
        at = pl.ds(pl.multiple_of(at, 16), step)
        return own[at, :] + other[at, :].astype(F32)

    def add(at, step):
        to = pl.ds(pl.multiple_of(at, 16), step)
        send[to, :] = total(theirs + at, step).astype(send.dtype)
        keep[to, :] = total(mine + at, step)

    in_steps(add, rows)


def add(own, other):
    rows = other.shape[0] // 2
    return vmem_call(
        add_kernel,
        (jax.ShapeDtypeStruct((rows, LANES), BF16), jax.ShapeDtypeStruct((rows, LANES), F32)),
        (),
        pl.CostEstimate(flops=0, bytes_accessed=8 * own.size, transcendentals=0),
    )(own, other)


def combine_kernel(keep, other, terms, more, out):
    parts, rows, _ = out.shape
    height, extra = (keep.shape[0] // parts, terms.shape[0] // parts)
    padded = rows - extra
    total = keep[...] + other[...].astype(F32)
    grads = terms[...] + more[...].astype(F32)
    for n in range(parts):
        value = total[n * height : (n + 1) * height]
        if padded > height:
            value = jnp.concatenate([value, jnp.zeros((padded - height, LANES), F32)], axis=0)
        out[n, 0:padded, :] = value.astype(out.dtype)
        out[n, padded:rows, :] = grads[n * extra : (n + 1) * extra].astype(out.dtype)


def combine(keep, other, terms, more, parts):
    rows = ceil_to(keep.shape[0] // parts, 16) + terms.shape[0] // parts
    return vmem_call(
        combine_kernel,
        jax.ShapeDtypeStruct((parts, rows, LANES), BF16),
        (),
        pl.CostEstimate(flops=0, bytes_accessed=8 * keep.size, transcendentals=0),
    )(keep, other, terms, more)


def split_to(total, mine, send, keep):
    half = total.shape[0] // 2
    keep[...] = total[pl.ds(pl.multiple_of(mine * half, 16), half), :]
    send[...] = total[pl.ds(pl.multiple_of((1 - mine) * half, 16), half), :].astype(send.dtype)


def swapped(value, axis="core"):
    return lax.ppermute(value, axis, [(0, 1), (1, 0)])


def plane_order():
    core = lax.axis_index("core")
    ahead = [core * n + (1 - core) * (2 - n) for n in range(3)]
    back = [core * (2 - n) + (1 - core) * n for n in range(3)]
    return (ahead, back)


def windows(packs, x, count):
    length = packs[0].shape[0] // count

    def row(p, n):
        if 0 <= n < length:
            return p[n * count : (n + 1) * count, :]
        return jnp.zeros((count, LANES), BF16)

    rows = [[row(p, x + n - 1) for p in packs] for n in range(GROUP + 2)]
    return jnp.concatenate(
        [jnp.concatenate(sum(rows[g : g + 3], []), axis=0) for g in range(GROUP)], axis=1
    )


def ordered(acc, count, ahead):
    blocks = [pl.multiple_of((3 * j + n) * count, 16) for j in range(3) for n in ahead]
    return jnp.concatenate([acc[pl.ds(at, count), :] for at in blocks], axis=0)


def across_lanes(first, second):
    return lax.dot_general(
        first, second, (((1,), (1,)), ((), ())), preferred_element_type=F32
    )


def prepare_kernel(act, two, one, acts, w_two, w_one, flat):
    ahead, back = plane_order()
    turned(act, flat, acts)
    w_two[...] = jnp.concatenate(
        [
            jnp.concatenate([two[back[n], 2 - j, 2 - k].astype(F32) for k in range(3)], axis=0)
            for j in range(3)
            for n in range(3)
        ],
        axis=1,
    ).astype(BF16)
    w_one[...] = jnp.concatenate(
        [
            jnp.concatenate([one[ahead[n], 2 - j, k].astype(F32) for n in range(3)], axis=0)
            for j in range(3)
            for k in range(3)
        ],
        axis=1,
    ).astype(BF16)


def prepare(act, kernel_two, kernel_one):
    c1, length, width = act.shape
    c0, c2 = (kernel_one.shape[3], kernel_two.shape[4])
    return vmem_call(
        prepare_kernel,
        (
            jax.ShapeDtypeStruct((length * c1, width), BF16),
            jax.ShapeDtypeStruct((3 * c1, 9 * c2), BF16),
            jax.ShapeDtypeStruct((3 * c0, 9 * c1), BF16),
        ),
        (pltpu.VMEM((c1 * length, width), F32),),
        pl.CostEstimate(flops=0, bytes_accessed=16 * act.size, transcendentals=0),
    )(act, kernel_two, kernel_one)


def first_kernel(pack_in, pack_0, pack_out, acts, w_two, pres, terms, acc):
    c1, c2 = (w_two.shape[0] // 3, w_two.shape[1] // 9)
    length = acts.shape[0] // c1
    packs = (pack_in, pack_0, pack_out)
    ahead, _ = plane_order()
    stacked = 3 * c1
    pres[0:stacked, :] = jnp.zeros((stacked, LANES), BF16)
    pres[(length + 1) * stacked : (length + 2) * stacked, :] = jnp.zeros((stacked, LANES), BF16)
    acc[...] = jnp.zeros_like(acc)

    for x in range(0, length, GROUP):
        right = windows(packs, x, c2)
        sums = jnp.dot(w_two[...], right, preferred_element_type=F32)
        columns = []
        for g in range(GROUP):
            part = sums[:, g * LANES : (g + 1) * LANES]
            grad = slid(part[0:c1], 1) + part[c1 : 2 * c1] + slid(part[2 * c1 : 3 * c1], -1)
            value = acts[(x + g) * c1 : (x + g + 1) * c1, :].astype(F32)
            pre = (grad * jnp.where(value > 0, 1.0, 0.2)).astype(BF16).astype(F32)
            moved = jnp.concatenate([slid(pre, -1), pre, slid(pre, 1)], axis=0).astype(BF16)
            pres[(x + g + 1) * stacked : (x + g + 2) * stacked, :] = moved
            stack = jnp.concatenate([slid(value, 1), value, slid(value, -1)], axis=0)
            columns.append(stack.astype(BF16))
        acc[...] += across_lanes(right, jnp.concatenate(columns, axis=1))

    terms[...] = jnp.zeros_like(terms)
    total = ordered(acc, c2, ahead).T
    rows, width = total.shape
    for block in range(-(-width // LANES)):
        part = total[:, block * LANES : min(width, (block + 1) * LANES)]
        terms[block * rows : (block + 1) * rows, 0 : part.shape[1]] = part


def gradient_kernel(pack_in, pack_0, pack_out, pres, before, send, keep, acc, terms):
    c0, stacked = (acc.shape[0] // 9, acc.shape[1])
    packs = (pack_in, pack_0, pack_out)
    ahead, _ = plane_order()
    length = pres.shape[0] // stacked - 2
    acc[...] = jnp.zeros_like(acc)

    for x in range(0, length, GROUP):
        rows = [pres[(x + g + 1) * stacked : (x + g + 2) * stacked, :] for g in range(GROUP)]
        acc[...] += across_lanes(windows(packs, x, c0), jnp.concatenate(rows, axis=1))

    used = before.shape[0]
    terms[0:used, :] = before[...]
    terms[used:, :] = jnp.zeros((terms.shape[0] - used, LANES), F32)
    total = ordered(acc, c0, ahead)
    terms[used : used + total.shape[0], 0 : total.shape[1]] = total
    split_to(terms, lax.axis_index("core"), send, keep)


def input_kernel(pres, w_one, own, inner, outer):
    c0, stacked = (w_one.shape[0] // 3, w_one.shape[1] // 3)
    length = pres.shape[0] // stacked - 2

    for x in range(0, length, GROUP):
        window = pres[x * stacked : (x + GROUP + 2) * stacked, :]
        moved = beside(window, 3 * stacked, stacked, GROUP)
        sums = jnp.dot(w_one[...], moved, preferred_element_type=F32)
        for g in range(GROUP):
            part = sums[:, g * LANES : (g + 1) * LANES]
            at = pl.ds((x + g) * c0, c0)
            for i, out in ((0, inner), (1, own), (2, outer)):
                out[at, :] = part[i * c0 : (i + 1) * c0].astype(out.dtype)


def vmem_call(body, out_shape, scratch=(), cost=None, limit=24 * 2**20):
    spec = pl.BlockSpec(memory_space=pltpu.VMEM)
    return pl.pallas_call(
        body,
        out_shape=out_shape,
        out_specs=jax.tree.map(lambda _: spec, out_shape),
        scratch_shapes=list(scratch),
        compiler_params=pltpu.CompilerParams(vmem_limit_bytes=limit),
        cost_estimate=cost,
    )


def first_part(packs, acts, w_two):
    c1, c2, width = (w_two.shape[0] // 3, w_two.shape[1] // 9, acts.shape[1])
    length = acts.shape[0] // c1
    return vmem_call(
        first_kernel,
        (
            jax.ShapeDtypeStruct(((length + 2) * 3 * c1, width), BF16),
            jax.ShapeDtypeStruct((-(-9 * c2 // LANES) * 3 * c1, LANES), F32),
        ),
        (pltpu.VMEM((9 * c2, 3 * c1), F32),),
        pl.CostEstimate(flops=10**9, bytes_accessed=20 * 2**20, transcendentals=0),
    )(*packs, acts, w_two)


def gradient_part(packs, pres, terms, rows, c1):
    width = pres.shape[1]
    c0 = packs[0].shape[0] // (pres.shape[0] // (3 * c1) - 2)
    return vmem_call(
        gradient_kernel,
        (
            jax.ShapeDtypeStruct((rows // 2, LANES), BF16),
            jax.ShapeDtypeStruct((rows // 2, LANES), F32),
        ),
        (pltpu.VMEM((9 * c0, 3 * c1), F32), pltpu.VMEM((rows, width), F32)),
        pl.CostEstimate(flops=10**9, bytes_accessed=5 * 2**20, transcendentals=0),
    )(*packs, pres, terms)


def input_part(pres, w_one):
    c0, stacked = (w_one.shape[0] // 3, w_one.shape[1] // 3)
    plane = ((pres.shape[0] // stacked - 2) * c0, pres.shape[1])
    return vmem_call(
        input_kernel,
        (
            jax.ShapeDtypeStruct(plane, F32),
            jax.ShapeDtypeStruct(plane, BF16),
            jax.ShapeDtypeStruct(plane, BF16),
        ),
        (),
        pl.CostEstimate(flops=10**9, bytes_accessed=5 * 2**20, transcendentals=0),
    )(pres, w_one)


def merge_kernel(own, first, second, out, flat):
    chans, length, _ = out.shape

    def add(step, carry):
        at = pl.ds(pl.multiple_of(step * 64, 64), 64)
        flat[at, :] = own[at, :] + first[at, :].astype(F32) + second[at, :].astype(F32)
        return carry

    lax.fori_loop(0, own.shape[0] // 64, add, 0, unroll=4)

    def gather(c, carry):
        out[c] = flat[pl.ds(c, length, stride=chans), :].astype(out.dtype)
        return carry

    lax.fori_loop(0, chans, gather, 0, unroll=4)


def merge(own, first, second, shape):
    return vmem_call(
        merge_kernel,
        jax.ShapeDtypeStruct(shape, BF16),
        (pltpu.VMEM(own.shape, F32),),
        pl.CostEstimate(flops=2 * own.size, bytes_accessed=8 * own.size, transcendentals=0),
    )(own, first, second)


def share_kernel(scale, parts, out, buffer, sems):
    copies, rows, _ = parts.shape
    padded = out.shape[1] - rows
    far = copies // 2
    buffer[0:padded, :] = jnp.sum(parts[0:far, 0:padded, :].astype(F32), axis=0).astype(BF16)
    buffer[padded : 2 * padded, :] = jnp.sum(parts[far:, 0:padded, :].astype(F32), axis=0).astype(BF16)
    grads = jnp.sum(parts[:, padded:rows, :].astype(F32), axis=0) * scale
    buffer[2 * padded :, :] = grads.astype(BF16)
    sent = [pltpu.make_async_copy(buffer, out.at[n], sems.at[n]) for n in range(copies)]
    for copy in sent:
        copy.start()
    for copy in sent:
        copy.wait()


def share(parts, extra, scale):
    copies, rows, _ = parts.shape
    height = 2 * rows - extra
    return pl.pallas_call(
        lambda *refs: share_kernel(scale, *refs),
        out_shape=jax.ShapeDtypeStruct((copies, height, LANES), BF16),
        in_specs=[pl.BlockSpec(memory_space=pltpu.VMEM)],
        out_specs=pl.BlockSpec(memory_space=pl.ANY),
        scratch_shapes=[pltpu.VMEM((height, LANES), BF16), pltpu.SemaphoreType.DMA((copies,))],
        compiler_params=pltpu.CompilerParams(vmem_limit_bytes=24 * 2**20),
        cost_estimate=pl.CostEstimate(
            flops=parts.size, bytes_accessed=6 * parts.size, transcendentals=0
        ),
    )(parts)


def place(source, height, padded, which, bucket, buffer, sems):
    copies, count = (source.shape[0], sems.shape[0])
    step = 2 * copies // count
    sent = []
    for n in range(count):
        for m in range(n * step, (n + 1) * step):
            half, q = (m // copies, m % copies)
            value = source[q, half * padded : (half + 1) * padded, :].astype(F32)
            buffer[m * height : (m + 1) * height, :] = value[0:height]
        rows = pl.ds(n * step * height, step * height)
        at = (which * count + n) * step * height
        at = pl.ds(pl.multiple_of(at, 8), step * height)
        sent.append(pltpu.make_async_copy(buffer.at[rows], bucket.at[at], sems.at[n]))
        sent[-1].start()
    return sent


def start_kernel(height, padded, mine, bucket, buffer, sems):
    for copy in place(mine, height, padded, lax.axis_index("core"), bucket, buffer, sems):
        copy.wait()


def finish_kernel(
    sizes, height, padded, mine, other, partial,
    bucket, out_one, out_two,
    raw, one, two, out_sems, buffer, sems,
):
    c0, c1, c2 = sizes
    copies, rows, _ = mine.shape
    extra = rows - 2 * padded
    me = lax.axis_index("core")
    sent = place(other, height, padded, 1 - me, bucket, buffer, sems)

    for q in range(copies):
        for source, which in ((mine, me), (other, 1 - me)):
            at = pl.multiple_of((which * copies + q) * extra, 8)
            raw[pl.ds(at, extra), :] = source[q, 2 * padded : rows, :].astype(F32)
    block = 3 * c1
    first = -(-9 * c2 // LANES) * block
    for i in range(3):
        for j in range(3):
            column = ((2 - j) * 3 + 2 - i) * c2
            whole, lane = (column // LANES, column % LANES)
            two[(3 * i + j) * block : (3 * i + j + 1) * block, :] = raw[
                whole * block : (whole + 1) * block, lane : lane + c2
            ]
        at = pl.ds(3 * i * block, 3 * block)
        sent.append(pltpu.make_async_copy(two.at[at], out_two.at[at], out_sems.at[i]))
        sent[-1].start()
    for i in range(3):
        for j in range(3):
            row = first + (3 * j + i) * c0
            for k in range(3):
                to = (9 * i + 3 * j + k) * c0
                one[to : to + c0, :] = raw[row : row + c0, k * c1 : (k + 1) * c1]
        at = pl.ds(9 * i * c0, 9 * c0)
        sent.append(pltpu.make_async_copy(one.at[at], out_one.at[at], out_sems.at[3 + i]))
        sent[-1].start()
    for copy in sent:
        copy.wait()


def finish(mine, other, length, sizes):
    c0, c1, c2 = sizes
    copies, rows, _ = mine.shape
    height = length // LANES // (4 * copies)
    padded = ceil_to(height, 16)
    spec = pl.BlockSpec(memory_space=pltpu.VMEM)
    remote = pl.BlockSpec(memory_space=pltpu.HBM)
    whole = jax.ShapeDtypeStruct((length // LANES, LANES), F32)
    chunks = 4
    scratch = [
        pltpu.VMEM((2 * copies * height, LANES), F32),
        pltpu.SemaphoreType.DMA((chunks,)),
    ]
    params = pltpu.CompilerParams(vmem_limit_bytes=24 * 2**20)
    partial = pl.pallas_call(
        lambda *refs: start_kernel(height, padded, *refs),
        out_shape=whole,
        in_specs=[spec],
        out_specs=remote,
        scratch_shapes=scratch,
        compiler_params=params,
    )(mine)
    return pl.pallas_call(
        lambda *refs: finish_kernel(sizes, height, padded, *refs),
        out_shape=(
            whole,
            jax.ShapeDtypeStruct((27 * c0, c1), F32),
            jax.ShapeDtypeStruct((27 * c1, c2), F32),
        ),
        in_specs=[spec, spec, remote],
        out_specs=(remote, remote, remote),
        scratch_shapes=[
            pltpu.VMEM((2 * copies * (rows - 2 * padded), LANES), F32),
            pltpu.VMEM((27 * c0, c1), F32),
            pltpu.VMEM((27 * c1, c2), F32),
            pltpu.SemaphoreType.DMA((6,)),
        ]
        + scratch,
        input_output_aliases={2: 0},
        compiler_params=params,
    )(mine, other, partial)


def crossed(value):
    pairs = [(n, n + 1) for n in range(1, lax.axis_size(SPACE) - 1, 2)]
    return lax.ppermute(value, SPACE, pairs + [(m, n) for n, m in pairs])


def per_device(volume_in, hidden_act, out_cot, kernel_one, kernel_two, grad_bucket):
    c0, c1, c2 = (volume_in.shape[2], hidden_act.shape[2], out_cot.shape[2])
    devices, copies = (lax.axis_size(EVERY), lax.axis_size(SAME))
    length = grad_bucket.shape[1]
    bucket = grad_bucket.reshape(length // LANES, LANES)
    cot = pack(out_cot[0, 0], [], 256)
    bucket, cot = lax.optimization_barrier((bucket, cot))
    core, half = (lax.axis_index("core"), bucket.shape[0] // 2)
    send = lax.dynamic_slice_in_dim(bucket, (1 - core) * half, half).astype(BF16)
    near = lax.dynamic_slice_in_dim(bucket, core * half, half)
    cot, send, near = lax.optimization_barrier((cot, send, near))
    cots = (swapped(cot), cot, crossed(cot))
    vol = pack(volume_in[0, 0], [cot], 16)
    vols = (swapped(vol), vol, crossed(vol))
    send, near = add(near, swapped(send))
    act, send, near = lax.optimization_barrier((hidden_act[0, 0], send, near))
    far = swapped(send, "x")

    used = -(-9 * c2 // LANES) * 3 * c1 + 9 * c0
    rows = ceil_to(used, 16 * devices)
    acts, w_two, w_one = prepare(act, kernel_two, kernel_one)
    pres, terms = first_part(cots, acts, w_two)
    send, keep = gradient_part(vols, pres, terms, rows, c1)
    own, inner, outer = input_part(pres, w_one)
    parts = combine(near, far, keep, swapped(send), copies)
    parts, inner, outer = lax.optimization_barrier((parts, inner, outer))
    parts = lax.all_to_all(parts, SAME, 0, 0)
    cells = volume_in.shape[3] * volume_in.shape[4] * devices
    shares = share(parts, rows // devices, 1.0 / math.sqrt(cells))

    shares, inner, outer = lax.optimization_barrier((shares, inner, outer))
    mine = lax.all_to_all(shares, SAME, 0, 0)
    inner, outer = (swapped(inner), crossed(outer))
    grad_input = merge(own, inner, outer, volume_in.shape[2:])
    mine, grad_input = lax.optimization_barrier((mine, grad_input))
    bucket_sum, total_one, total_two = finish(mine, swapped(mine), length, (c0, c1, c2))
    return (
        grad_input[None, None],
        total_one.reshape(3, 3, 3, c0, c1),
        total_two.reshape(3, 3, 3, c1, c2),
        bucket_sum.reshape(length),
    )


def solution(mesh):
    dp, space = (mesh.shape["dp"], mesh.shape["space"])
    split = Mesh(mesh.devices.reshape(dp // 2, 2, space // 2, 2), EVERY)
    volume = P(("z", "x"), SPACE, None, None, None)
    in_specs = (volume, volume, volume, P(), P(), P(EVERY, None))
    out_specs = (volume, P(), P(), P())
    return jax.shard_map(
        per_device, mesh=split, in_specs=in_specs, out_specs=out_specs, check_vma=False
    )
```

```python
import math

import jax
import jax.numpy as jnp
from jax import lax
from jax.experimental import pallas as pl
from jax.experimental.pallas import tpu as pltpu
from jax.sharding import Mesh, PartitionSpec as P

SPACE = ("y", "core")
SAME = ("x", "z", "y")
EVERY = ("z", "x", "y", "core")
GROUP = 8
LANES = 128
BF16 = jnp.bfloat16
F32 = jnp.float32


def ceil_to(value, step):
    return -(-value // step) * step


def slid(value, step):
    lane = lax.broadcasted_iota(jnp.int32, value.shape, 1)
    width = value.shape[1]
    keep = lane >= step if step > 0 else lane < width + step
    return jnp.where(keep, pltpu.roll(value, step % width, 1), 0.0)


def beside(window, rows, step, count):
    return jnp.concatenate([window[g * step : g * step + rows] for g in range(count)], axis=1)


def turned(src, flat, dst):
    chans, length, _ = src.shape

    def stage(c, carry):
        flat[pl.ds(pl.multiple_of(c * length, length), length), :] = src[c].astype(F32)
        return carry

    lax.fori_loop(0, chans, stage, 0, unroll=4)

    def gather(x, carry):
        rows = flat[pl.ds(x, chans, stride=length), :]
        dst[pl.ds(pl.multiple_of(x * chans, 16), chans), :] = rows.astype(BF16)
        return carry

    lax.fori_loop(0, length, gather, 0, unroll=4)


def pack_kernel(field, *refs):
    out, flat = refs[-2:]
    turned(field, flat, out)


def pack(field, after, weight):
    chans, length, width = field.shape
    spec = pl.BlockSpec(memory_space=pltpu.VMEM)
    return pl.pallas_call(
        pack_kernel,
        out_shape=jax.ShapeDtypeStruct((length * chans, width), BF16),
        in_specs=[spec] + [pl.BlockSpec(memory_space=pl.ANY) for _ in after],
        out_specs=spec,
        scratch_shapes=[pltpu.VMEM((chans * length, width), F32)],
        compiler_params=pltpu.CompilerParams(vmem_limit_bytes=24 * 2**20),
        cost_estimate=pl.CostEstimate(
            flops=0, bytes_accessed=weight * field.size, transcendentals=0
        ),
    )(field, *after)


def in_steps(body, rows, count=8):
    step = rows // count

    def one(n, carry):
        body(n * step, step)
        return carry

    lax.fori_loop(0, count, one, 0)


def add_kernel(own, other, send, keep):
    rows = send.shape[0]
    mine = lax.axis_index("x") * rows
    theirs = rows - mine

    def total(at, step):
        at = pl.ds(pl.multiple_of(at, 16), step)
        return own[at, :] + other[at, :].astype(F32)

    def add(at, step):
        to = pl.ds(pl.multiple_of(at, 16), step)
        send[to, :] = total(theirs + at, step).astype(send.dtype)
        keep[to, :] = total(mine + at, step)

    in_steps(add, rows)


def add(own, other):
    rows = other.shape[0] // 2
    return vmem_call(
        add_kernel,
        (jax.ShapeDtypeStruct((rows, LANES), BF16), jax.ShapeDtypeStruct((rows, LANES), F32)),
        (),
        pl.CostEstimate(flops=0, bytes_accessed=8 * own.size, transcendentals=0),
    )(own, other)


def combine_kernel(keep, other, terms, more, out):
    parts, rows, _ = out.shape
    height, extra = (keep.shape[0] // parts, terms.shape[0] // parts)
    padded = rows - extra
    total = keep[...] + other[...].astype(F32)
    grads = terms[...] + more[...].astype(F32)
    for n in range(parts):
        value = total[n * height : (n + 1) * height]
        if padded > height:
            value = jnp.concatenate([value, jnp.zeros((padded - height, LANES), F32)], axis=0)
        out[n, 0:padded, :] = value.astype(out.dtype)
        out[n, padded:rows, :] = grads[n * extra : (n + 1) * extra].astype(out.dtype)


def combine(keep, other, terms, more, parts):
    rows = ceil_to(keep.shape[0] // parts, 16) + terms.shape[0] // parts
    return vmem_call(
        combine_kernel,
        jax.ShapeDtypeStruct((parts, rows, LANES), BF16),
        (),
        pl.CostEstimate(flops=0, bytes_accessed=8 * keep.size, transcendentals=0),
    )(keep, other, terms, more)


def split_to(total, mine, send, keep):
    half = total.shape[0] // 2
    keep[...] = total[pl.ds(pl.multiple_of(mine * half, 16), half), :]
    send[...] = total[pl.ds(pl.multiple_of((1 - mine) * half, 16), half), :].astype(send.dtype)


def swapped(value, axis="core"):
    return lax.ppermute(value, axis, [(0, 1), (1, 0)])


def plane_order():
    core = lax.axis_index("core")
    ahead = [core * n + (1 - core) * (2 - n) for n in range(3)]
    back = [core * (2 - n) + (1 - core) * n for n in range(3)]
    return (ahead, back)


def windows(packs, x, count):
    length = packs[0].shape[0] // count

    def row(p, n):
        if 0 <= n < length:
            return p[n * count : (n + 1) * count, :]
        return jnp.zeros((count, LANES), BF16)

    rows = [[row(p, x + n - 1) for p in packs] for n in range(GROUP + 2)]
    return jnp.concatenate(
        [jnp.concatenate(sum(rows[g : g + 3], []), axis=0) for g in range(GROUP)], axis=1
    )


def ordered(acc, count, ahead):
    blocks = [pl.multiple_of((3 * j + n) * count, 16) for j in range(3) for n in ahead]
    return jnp.concatenate([acc[pl.ds(at, count), :] for at in blocks], axis=0)


def across_lanes(first, second):
    return lax.dot_general(
        first, second, (((1,), (1,)), ((), ())), preferred_element_type=F32
    )


def prepare_kernel(act, two, one, acts, w_two, w_one, flat):
    ahead, back = plane_order()
    turned(act, flat, acts)
    w_two[...] = jnp.concatenate(
        [
            jnp.concatenate([two[back[n], 2 - j, 2 - k].astype(F32) for k in range(3)], axis=0)
            for j in range(3)
            for n in range(3)
        ],
        axis=1,
    ).astype(BF16)
    w_one[...] = jnp.concatenate(
        [
            jnp.concatenate([one[ahead[n], 2 - j, k].astype(F32) for n in range(3)], axis=0)
            for j in range(3)
            for k in range(3)
        ],
        axis=1,
    ).astype(BF16)


def prepare(act, kernel_two, kernel_one):
    c1, length, width = act.shape
    c0, c2 = (kernel_one.shape[3], kernel_two.shape[4])
    return vmem_call(
        prepare_kernel,
        (
            jax.ShapeDtypeStruct((length * c1, width), BF16),
            jax.ShapeDtypeStruct((3 * c1, 9 * c2), BF16),
            jax.ShapeDtypeStruct((3 * c0, 9 * c1), BF16),
        ),
        (pltpu.VMEM((c1 * length, width), F32),),
        pl.CostEstimate(flops=0, bytes_accessed=16 * act.size, transcendentals=0),
    )(act, kernel_two, kernel_one)


def first_kernel(pack_in, pack_0, pack_out, acts, w_two, pres, terms, acc):
    c1, c2 = (w_two.shape[0] // 3, w_two.shape[1] // 9)
    length = acts.shape[0] // c1
    packs = (pack_in, pack_0, pack_out)
    ahead, _ = plane_order()
    stacked = 3 * c1
    pres[0:stacked, :] = jnp.zeros((stacked, LANES), BF16)
    pres[(length + 1) * stacked : (length + 2) * stacked, :] = jnp.zeros((stacked, LANES), BF16)
    acc[...] = jnp.zeros_like(acc)

    for x in range(0, length, GROUP):
        right = windows(packs, x, c2)
        sums = jnp.dot(w_two[...], right, preferred_element_type=F32)
        columns = []
        for g in range(GROUP):
            part = sums[:, g * LANES : (g + 1) * LANES]
            grad = slid(part[0:c1], 1) + part[c1 : 2 * c1] + slid(part[2 * c1 : 3 * c1], -1)
            value = acts[(x + g) * c1 : (x + g + 1) * c1, :].astype(F32)
            pre = (grad * jnp.where(value > 0, 1.0, 0.2)).astype(BF16).astype(F32)
            moved = jnp.concatenate([slid(pre, -1), pre, slid(pre, 1)], axis=0).astype(BF16)
            pres[(x + g + 1) * stacked : (x + g + 2) * stacked, :] = moved
            stack = jnp.concatenate([slid(value, 1), value, slid(value, -1)], axis=0)
            columns.append(stack.astype(BF16))
        acc[...] += across_lanes(right, jnp.concatenate(columns, axis=1))

    terms[...] = jnp.zeros_like(terms)
    total = ordered(acc, c2, ahead).T
    rows, width = total.shape
    for block in range(-(-width // LANES)):
        part = total[:, block * LANES : min(width, (block + 1) * LANES)]
        terms[block * rows : (block + 1) * rows, 0 : part.shape[1]] = part


def gradient_kernel(pack_in, pack_0, pack_out, pres, before, send, keep, acc, terms):
    c0, stacked = (acc.shape[0] // 9, acc.shape[1])
    packs = (pack_in, pack_0, pack_out)
    ahead, _ = plane_order()
    length = pres.shape[0] // stacked - 2
    acc[...] = jnp.zeros_like(acc)

    for x in range(0, length, GROUP):
        rows = [pres[(x + g + 1) * stacked : (x + g + 2) * stacked, :] for g in range(GROUP)]
        acc[...] += across_lanes(windows(packs, x, c0), jnp.concatenate(rows, axis=1))

    used = before.shape[0]
    terms[0:used, :] = before[...]
    terms[used:, :] = jnp.zeros((terms.shape[0] - used, LANES), F32)
    total = ordered(acc, c0, ahead)
    terms[used : used + total.shape[0], 0 : total.shape[1]] = total
    split_to(terms, lax.axis_index("core"), send, keep)


def input_kernel(pres, w_one, own, inner, outer):
    c0, stacked = (w_one.shape[0] // 3, w_one.shape[1] // 3)
    length = pres.shape[0] // stacked - 2

    for x in range(0, length, GROUP):
        window = pres[x * stacked : (x + GROUP + 2) * stacked, :]
        moved = beside(window, 3 * stacked, stacked, GROUP)
        sums = jnp.dot(w_one[...], moved, preferred_element_type=F32)
        for g in range(GROUP):
            part = sums[:, g * LANES : (g + 1) * LANES]
            at = pl.ds((x + g) * c0, c0)
            for i, out in ((0, inner), (1, own), (2, outer)):
                out[at, :] = part[i * c0 : (i + 1) * c0].astype(out.dtype)


def vmem_call(body, out_shape, scratch=(), cost=None, limit=24 * 2**20):
    spec = pl.BlockSpec(memory_space=pltpu.VMEM)
    return pl.pallas_call(
        body,
        out_shape=out_shape,
        out_specs=jax.tree.map(lambda _: spec, out_shape),
        scratch_shapes=list(scratch),
        compiler_params=pltpu.CompilerParams(vmem_limit_bytes=limit),
        cost_estimate=cost,
    )


def first_part(packs, acts, w_two):
    c1, c2, width = (w_two.shape[0] // 3, w_two.shape[1] // 9, acts.shape[1])
    length = acts.shape[0] // c1
    return vmem_call(
        first_kernel,
        (
            jax.ShapeDtypeStruct(((length + 2) * 3 * c1, width), BF16),
            jax.ShapeDtypeStruct((-(-9 * c2 // LANES) * 3 * c1, LANES), F32),
        ),
        (pltpu.VMEM((9 * c2, 3 * c1), F32),),
        pl.CostEstimate(flops=10**9, bytes_accessed=20 * 2**20, transcendentals=0),
    )(*packs, acts, w_two)


def gradient_part(packs, pres, terms, rows, c1):
    width = pres.shape[1]
    c0 = packs[0].shape[0] // (pres.shape[0] // (3 * c1) - 2)
    return vmem_call(
        gradient_kernel,
        (
            jax.ShapeDtypeStruct((rows // 2, LANES), BF16),
            jax.ShapeDtypeStruct((rows // 2, LANES), F32),
        ),
        (pltpu.VMEM((9 * c0, 3 * c1), F32), pltpu.VMEM((rows, width), F32)),
        pl.CostEstimate(flops=10**9, bytes_accessed=5 * 2**20, transcendentals=0),
    )(*packs, pres, terms)


def input_part(pres, w_one):
    c0, stacked = (w_one.shape[0] // 3, w_one.shape[1] // 3)
    plane = ((pres.shape[0] // stacked - 2) * c0, pres.shape[1])
    return vmem_call(
        input_kernel,
        (
            jax.ShapeDtypeStruct(plane, F32),
            jax.ShapeDtypeStruct(plane, BF16),
            jax.ShapeDtypeStruct(plane, BF16),
        ),
        (),
        pl.CostEstimate(flops=10**9, bytes_accessed=5 * 2**20, transcendentals=0),
    )(pres, w_one)


def merge_kernel(own, first, second, out, flat):
    chans, length, _ = out.shape

    def add(step, carry):
        at = pl.ds(pl.multiple_of(step * 64, 64), 64)
        flat[at, :] = own[at, :] + first[at, :].astype(F32) + second[at, :].astype(F32)
        return carry

    lax.fori_loop(0, own.shape[0] // 64, add, 0, unroll=4)

    def gather(c, carry):
        out[c] = flat[pl.ds(c, length, stride=chans), :].astype(out.dtype)
        return carry

    lax.fori_loop(0, chans, gather, 0, unroll=4)


def merge(own, first, second, shape):
    return vmem_call(
        merge_kernel,
        jax.ShapeDtypeStruct(shape, BF16),
        (pltpu.VMEM(own.shape, F32),),
        pl.CostEstimate(flops=2 * own.size, bytes_accessed=8 * own.size, transcendentals=0),
    )(own, first, second)


def share_kernel(scale, parts, out, buffer, sems):
    copies, rows, _ = parts.shape
    padded = out.shape[1] - rows
    far = copies // 2
    buffer[0:padded, :] = jnp.sum(parts[0:far, 0:padded, :].astype(F32), axis=0).astype(BF16)
    buffer[padded : 2 * padded, :] = jnp.sum(parts[far:, 0:padded, :].astype(F32), axis=0).astype(BF16)
    grads = jnp.sum(parts[:, padded:rows, :].astype(F32), axis=0) * scale
    buffer[2 * padded :, :] = grads.astype(BF16)
    sent = [pltpu.make_async_copy(buffer, out.at[n], sems.at[n]) for n in range(copies)]
    for copy in sent:
        copy.start()
    for copy in sent:
        copy.wait()


def share(parts, extra, scale):
    copies, rows, _ = parts.shape
    height = 2 * rows - extra
    return pl.pallas_call(
        lambda *refs: share_kernel(scale, *refs),
        out_shape=jax.ShapeDtypeStruct((copies, height, LANES), BF16),
        in_specs=[pl.BlockSpec(memory_space=pltpu.VMEM)],
        out_specs=pl.BlockSpec(memory_space=pl.ANY),
        scratch_shapes=[pltpu.VMEM((height, LANES), BF16), pltpu.SemaphoreType.DMA((copies,))],
        compiler_params=pltpu.CompilerParams(vmem_limit_bytes=24 * 2**20),
        cost_estimate=pl.CostEstimate(
            flops=parts.size, bytes_accessed=6 * parts.size, transcendentals=0
        ),
    )(parts)


def place(source, height, padded, which, bucket, buffer, sems):
    copies, count = (source.shape[0], sems.shape[0])
    step = 2 * copies // count
    sent = []
    for n in range(count):
        for m in range(n * step, (n + 1) * step):
            half, q = (m // copies, m % copies)
            value = source[q, half * padded : (half + 1) * padded, :].astype(F32)
            buffer[m * height : (m + 1) * height, :] = value[0:height]
        rows = pl.ds(n * step * height, step * height)
        at = (which * count + n) * step * height
        at = pl.ds(pl.multiple_of(at, 8), step * height)
        sent.append(pltpu.make_async_copy(buffer.at[rows], bucket.at[at], sems.at[n]))
        sent[-1].start()
    return sent


def start_kernel(height, padded, mine, bucket, buffer, sems):
    for copy in place(mine, height, padded, lax.axis_index("core"), bucket, buffer, sems):
        copy.wait()


def finish_kernel(
    sizes, height, padded, mine, other, partial,
    bucket, out_one, out_two,
    raw, one, two, out_sems, buffer, sems,
):
    c0, c1, c2 = sizes
    copies, rows, _ = mine.shape
    extra = rows - 2 * padded
    me = lax.axis_index("core")
    sent = place(other, height, padded, 1 - me, bucket, buffer, sems)

    for q in range(copies):
        for source, which in ((mine, me), (other, 1 - me)):
            at = pl.multiple_of((which * copies + q) * extra, 8)
            raw[pl.ds(at, extra), :] = source[q, 2 * padded : rows, :].astype(F32)
    block = 3 * c1
    first = -(-9 * c2 // LANES) * block
    for i in range(3):
        for j in range(3):
            column = ((2 - j) * 3 + 2 - i) * c2
            whole, lane = (column // LANES, column % LANES)
            two[(3 * i + j) * block : (3 * i + j + 1) * block, :] = raw[
                whole * block : (whole + 1) * block, lane : lane + c2
            ]
        at = pl.ds(3 * i * block, 3 * block)
        sent.append(pltpu.make_async_copy(two.at[at], out_two.at[at], out_sems.at[i]))
        sent[-1].start()
    for i in range(3):
        for j in range(3):
            row = first + (3 * j + i) * c0
            for k in range(3):
                to = (9 * i + 3 * j + k) * c0
                one[to : to + c0, :] = raw[row : row + c0, k * c1 : (k + 1) * c1]
        at = pl.ds(9 * i * c0, 9 * c0)
        sent.append(pltpu.make_async_copy(one.at[at], out_one.at[at], out_sems.at[3 + i]))
        sent[-1].start()
    for copy in sent:
        copy.wait()


def finish(mine, other, length, sizes):
    c0, c1, c2 = sizes
    copies, rows, _ = mine.shape
    height = length // LANES // (4 * copies)
    padded = ceil_to(height, 16)
    spec = pl.BlockSpec(memory_space=pltpu.VMEM)
    remote = pl.BlockSpec(memory_space=pltpu.HBM)
    whole = jax.ShapeDtypeStruct((length // LANES, LANES), F32)
    chunks = 4
    scratch = [
        pltpu.VMEM((2 * copies * height, LANES), F32),
        pltpu.SemaphoreType.DMA((chunks,)),
    ]
    params = pltpu.CompilerParams(vmem_limit_bytes=24 * 2**20)
    partial = pl.pallas_call(
        lambda *refs: start_kernel(height, padded, *refs),
        out_shape=whole,
        in_specs=[spec],
        out_specs=remote,
        scratch_shapes=scratch,
        compiler_params=params,
    )(mine)
    return pl.pallas_call(
        lambda *refs: finish_kernel(sizes, height, padded, *refs),
        out_shape=(
            whole,
            jax.ShapeDtypeStruct((27 * c0, c1), F32),
            jax.ShapeDtypeStruct((27 * c1, c2), F32),
        ),
        in_specs=[spec, spec, remote],
        out_specs=(remote, remote, remote),
        scratch_shapes=[
            pltpu.VMEM((2 * copies * (rows - 2 * padded), LANES), F32),
            pltpu.VMEM((27 * c0, c1), F32),
            pltpu.VMEM((27 * c1, c2), F32),
            pltpu.SemaphoreType.DMA((6,)),
        ]
        + scratch,
        input_output_aliases={2: 0},
        compiler_params=params,
    )(mine, other, partial)


def crossed(value):
    pairs = [(n, n + 1) for n in range(1, lax.axis_size(SPACE) - 1, 2)]
    return lax.ppermute(value, SPACE, pairs + [(m, n) for n, m in pairs])


def per_device(volume_in, hidden_act, out_cot, kernel_one, kernel_two, grad_bucket):
    c0, c1, c2 = (volume_in.shape[2], hidden_act.shape[2], out_cot.shape[2])
    devices, copies = (lax.axis_size(EVERY), lax.axis_size(SAME))
    length = grad_bucket.shape[1]
    bucket = grad_bucket.reshape(length // LANES, LANES)
    cot = pack(out_cot[0, 0], [], 256)
    bucket, cot = lax.optimization_barrier((bucket, cot))
    core, half = (lax.axis_index("core"), bucket.shape[0] // 2)
    send = lax.dynamic_slice_in_dim(bucket, (1 - core) * half, half).astype(BF16)
    near = lax.dynamic_slice_in_dim(bucket, core * half, half)
    cot, send, near = lax.optimization_barrier((cot, send, near))
    cots = (swapped(cot), cot, crossed(cot))
    send, near = add(near, swapped(send))
    vol = pack(volume_in[0, 0], [send], 16)
    vols = (swapped(vol), vol, crossed(vol))
    act, send, near = lax.optimization_barrier((hidden_act[0, 0], send, near))
    far = swapped(send, "x")

    used = -(-9 * c2 // LANES) * 3 * c1 + 9 * c0
    rows = ceil_to(used, 16 * devices)
    acts, w_two, w_one = prepare(act, kernel_two, kernel_one)
    pres, terms = first_part(cots, acts, w_two)
    own, inner, outer = input_part(pres, w_one)
    terms, inner = lax.optimization_barrier((terms, inner))
    send, keep = gradient_part(vols, pres, terms, rows, c1)
    parts = combine(near, far, keep, swapped(send), copies)
    parts, inner, outer = lax.optimization_barrier((parts, inner, outer))
    parts = lax.all_to_all(parts, SAME, 0, 0)
    cells = volume_in.shape[3] * volume_in.shape[4] * devices
    shares = share(parts, rows // devices, 1.0 / math.sqrt(cells))

    shares, inner, outer = lax.optimization_barrier((shares, inner, outer))
    mine = lax.all_to_all(shares, SAME, 0, 0)
    inner, outer = (swapped(inner), crossed(outer))
    grad_input = merge(own, inner, outer, volume_in.shape[2:])
    mine, grad_input = lax.optimization_barrier((mine, grad_input))
    bucket_sum, total_one, total_two = finish(mine, swapped(mine), length, (c0, c1, c2))
    return (
        grad_input[None, None],
        total_one.reshape(3, 3, 3, c0, c1),
        total_two.reshape(3, 3, 3, c1, c2),
        bucket_sum.reshape(length),
    )


def solution(mesh):
    dp, space = (mesh.shape["dp"], mesh.shape["space"])
    split = Mesh(mesh.devices.reshape(dp // 2, 2, space // 2, 2), EVERY)
    volume = P(("z", "x"), SPACE, None, None, None)
    in_specs = (volume, volume, volume, P(), P(), P(EVERY, None))
    out_specs = (volume, P(), P(), P())
    return jax.shard_map(
        per_device, mesh=split, in_specs=in_specs, out_specs=out_specs, check_vma=False
    )
```

```python
import math

import jax
import jax.numpy as jnp
from jax import lax
from jax.experimental import pallas as pl
from jax.experimental.pallas import tpu as pltpu
from jax.sharding import Mesh, PartitionSpec as P

SPACE = ("y", "core")
SAME = ("x", "z", "y")
EVERY = ("z", "x", "y", "core")
GROUP = 8
LANES = 128
BF16 = jnp.bfloat16
F32 = jnp.float32


def ceil_to(value, step):
    return -(-value // step) * step


def slid(value, step):
    lane = lax.broadcasted_iota(jnp.int32, value.shape, 1)
    width = value.shape[1]
    keep = lane >= step if step > 0 else lane < width + step
    return jnp.where(keep, pltpu.roll(value, step % width, 1), 0.0)


def beside(window, rows, step, count):
    return jnp.concatenate([window[g * step : g * step + rows] for g in range(count)], axis=1)


def turned(src, flat, dst):
    chans, length, _ = src.shape

    def stage(c, carry):
        flat[pl.ds(pl.multiple_of(c * length, length), length), :] = src[c].astype(F32)
        return carry

    lax.fori_loop(0, chans, stage, 0, unroll=4)

    def gather(x, carry):
        rows = flat[pl.ds(x, chans, stride=length), :]
        dst[pl.ds(pl.multiple_of(x * chans, 16), chans), :] = rows.astype(BF16)
        return carry

    lax.fori_loop(0, length, gather, 0, unroll=4)


def pack_kernel(field, *refs):
    out, flat = refs[-2:]
    turned(field, flat, out)


def pack(field, after, weight):
    chans, length, width = field.shape
    spec = pl.BlockSpec(memory_space=pltpu.VMEM)
    return pl.pallas_call(
        pack_kernel,
        out_shape=jax.ShapeDtypeStruct((length * chans, width), BF16),
        in_specs=[spec] + [pl.BlockSpec(memory_space=pl.ANY) for _ in after],
        out_specs=spec,
        scratch_shapes=[pltpu.VMEM((chans * length, width), F32)],
        compiler_params=pltpu.CompilerParams(vmem_limit_bytes=24 * 2**20),
        cost_estimate=pl.CostEstimate(
            flops=0, bytes_accessed=weight * field.size, transcendentals=0
        ),
    )(field, *after)


def in_steps(body, rows, count=8):
    step = rows // count

    def one(n, carry):
        body(n * step, step)
        return carry

    lax.fori_loop(0, count, one, 0)


def add_kernel(own, other, send, keep):
    rows = send.shape[0]
    mine = lax.axis_index("x") * rows
    theirs = rows - mine

    def total(at, step):
        at = pl.ds(pl.multiple_of(at, 16), step)
        return own[at, :] + other[at, :].astype(F32)

    def add(at, step):
        to = pl.ds(pl.multiple_of(at, 16), step)
        send[to, :] = total(theirs + at, step).astype(send.dtype)
        keep[to, :] = total(mine + at, step)

    in_steps(add, rows)


def add(own, other):
    rows = other.shape[0] // 2
    return vmem_call(
        add_kernel,
        (jax.ShapeDtypeStruct((rows, LANES), BF16), jax.ShapeDtypeStruct((rows, LANES), F32)),
        (),
        pl.CostEstimate(flops=0, bytes_accessed=8 * own.size, transcendentals=0),
    )(own, other)


def combine_kernel(keep, other, terms, more, out):
    parts, rows, _ = out.shape
    height, extra = (keep.shape[0] // parts, terms.shape[0] // parts)
    padded = rows - extra
    total = keep[...] + other[...].astype(F32)
    grads = terms[...] + more[...].astype(F32)
    for n in range(parts):
        value = total[n * height : (n + 1) * height]
        if padded > height:
            value = jnp.concatenate([value, jnp.zeros((padded - height, LANES), F32)], axis=0)
        out[n, 0:padded, :] = value.astype(out.dtype)
        out[n, padded:rows, :] = grads[n * extra : (n + 1) * extra].astype(out.dtype)


def combine(keep, other, terms, more, parts):
    rows = ceil_to(keep.shape[0] // parts, 16) + terms.shape[0] // parts
    return vmem_call(
        combine_kernel,
        jax.ShapeDtypeStruct((parts, rows, LANES), BF16),
        (),
        pl.CostEstimate(flops=0, bytes_accessed=8 * keep.size, transcendentals=0),
    )(keep, other, terms, more)


def split_to(total, mine, send, keep):
    half = total.shape[0] // 2
    keep[...] = total[pl.ds(pl.multiple_of(mine * half, 16), half), :]
    send[...] = total[pl.ds(pl.multiple_of((1 - mine) * half, 16), half), :].astype(send.dtype)


def swapped(value, axis="core"):
    return lax.ppermute(value, axis, [(0, 1), (1, 0)])


def plane_order():
    core = lax.axis_index("core")
    ahead = [core * n + (1 - core) * (2 - n) for n in range(3)]
    back = [core * (2 - n) + (1 - core) * n for n in range(3)]
    return (ahead, back)


def windows(packs, x, count):
    length = packs[0].shape[0] // count

    def row(p, n):
        if 0 <= n < length:
            return p[n * count : (n + 1) * count, :]
        return jnp.zeros((count, LANES), BF16)

    rows = [[row(p, x + n - 1) for p in packs] for n in range(GROUP + 2)]
    return jnp.concatenate(
        [jnp.concatenate(sum(rows[g : g + 3], []), axis=0) for g in range(GROUP)], axis=1
    )


def ordered(acc, count, ahead):
    blocks = [pl.multiple_of((3 * j + n) * count, 16) for j in range(3) for n in ahead]
    return jnp.concatenate([acc[pl.ds(at, count), :] for at in blocks], axis=0)


def across_lanes(first, second):
    return lax.dot_general(
        first, second, (((1,), (1,)), ((), ())), preferred_element_type=F32
    )


def prepare_kernel(act, two, one, acts, w_two, w_one, flat):
    ahead, back = plane_order()
    turned(act, flat, acts)
    w_two[...] = jnp.concatenate(
        [
            jnp.concatenate([two[back[n], 2 - j, 2 - k].astype(F32) for k in range(3)], axis=0)
            for j in range(3)
            for n in range(3)
        ],
        axis=1,
    ).astype(BF16)
    w_one[...] = jnp.concatenate(
        [
            jnp.concatenate([one[ahead[n], 2 - j, k].astype(F32) for n in range(3)], axis=0)
            for j in range(3)
            for k in range(3)
        ],
        axis=1,
    ).astype(BF16)


def prepare(act, kernel_two, kernel_one):
    c1, length, width = act.shape
    c0, c2 = (kernel_one.shape[3], kernel_two.shape[4])
    return vmem_call(
        prepare_kernel,
        (
            jax.ShapeDtypeStruct((length * c1, width), BF16),
            jax.ShapeDtypeStruct((3 * c1, 9 * c2), BF16),
            jax.ShapeDtypeStruct((3 * c0, 9 * c1), BF16),
        ),
        (pltpu.VMEM((c1 * length, width), F32),),
        pl.CostEstimate(flops=0, bytes_accessed=16 * act.size, transcendentals=0),
    )(act, kernel_two, kernel_one)


def first_kernel(pack_in, pack_0, pack_out, acts, w_two, pres, terms, acc):
    c1, c2 = (w_two.shape[0] // 3, w_two.shape[1] // 9)
    length = acts.shape[0] // c1
    packs = (pack_in, pack_0, pack_out)
    ahead, _ = plane_order()
    stacked = 3 * c1
    pres[0:stacked, :] = jnp.zeros((stacked, LANES), BF16)
    pres[(length + 1) * stacked : (length + 2) * stacked, :] = jnp.zeros((stacked, LANES), BF16)
    acc[...] = jnp.zeros_like(acc)

    for x in range(0, length, GROUP):
        right = windows(packs, x, c2)
        sums = jnp.dot(w_two[...], right, preferred_element_type=F32)
        columns = []
        for g in range(GROUP):
            part = sums[:, g * LANES : (g + 1) * LANES]
            grad = slid(part[0:c1], 1) + part[c1 : 2 * c1] + slid(part[2 * c1 : 3 * c1], -1)
            value = acts[(x + g) * c1 : (x + g + 1) * c1, :].astype(F32)
            pre = (grad * jnp.where(value > 0, 1.0, 0.2)).astype(BF16).astype(F32)
            moved = jnp.concatenate([slid(pre, -1), pre, slid(pre, 1)], axis=0).astype(BF16)
            pres[(x + g + 1) * stacked : (x + g + 2) * stacked, :] = moved
            stack = jnp.concatenate([slid(value, 1), value, slid(value, -1)], axis=0)
            columns.append(stack.astype(BF16))
        acc[...] += across_lanes(right, jnp.concatenate(columns, axis=1))

    terms[...] = jnp.zeros_like(terms)
    total = ordered(acc, c2, ahead).T
    rows, width = total.shape
    for block in range(-(-width // LANES)):
        part = total[:, block * LANES : min(width, (block + 1) * LANES)]
        terms[block * rows : (block + 1) * rows, 0 : part.shape[1]] = part


def gradient_kernel(pack_in, pack_0, pack_out, pres, before, send, keep, acc, terms):
    c0, stacked = (acc.shape[0] // 9, acc.shape[1])
    packs = (pack_in, pack_0, pack_out)
    ahead, _ = plane_order()
    length = pres.shape[0] // stacked - 2
    acc[...] = jnp.zeros_like(acc)

    for x in range(0, length, GROUP):
        rows = [pres[(x + g + 1) * stacked : (x + g + 2) * stacked, :] for g in range(GROUP)]
        acc[...] += across_lanes(windows(packs, x, c0), jnp.concatenate(rows, axis=1))

    used = before.shape[0]
    terms[0:used, :] = before[...]
    terms[used:, :] = jnp.zeros((terms.shape[0] - used, LANES), F32)
    total = ordered(acc, c0, ahead)
    terms[used : used + total.shape[0], 0 : total.shape[1]] = total
    split_to(terms, lax.axis_index("core"), send, keep)


def input_kernel(pres, w_one, own, inner, outer):
    c0, stacked = (w_one.shape[0] // 3, w_one.shape[1] // 3)
    length = pres.shape[0] // stacked - 2

    for x in range(0, length, GROUP):
        window = pres[x * stacked : (x + GROUP + 2) * stacked, :]
        moved = beside(window, 3 * stacked, stacked, GROUP)
        sums = jnp.dot(w_one[...], moved, preferred_element_type=F32)
        for g in range(GROUP):
            part = sums[:, g * LANES : (g + 1) * LANES]
            at = pl.ds((x + g) * c0, c0)
            for i, out in ((0, inner), (1, own), (2, outer)):
                out[at, :] = part[i * c0 : (i + 1) * c0].astype(out.dtype)


def vmem_call(body, out_shape, scratch=(), cost=None, limit=24 * 2**20):
    spec = pl.BlockSpec(memory_space=pltpu.VMEM)
    return pl.pallas_call(
        body,
        out_shape=out_shape,
        out_specs=jax.tree.map(lambda _: spec, out_shape),
        scratch_shapes=list(scratch),
        compiler_params=pltpu.CompilerParams(vmem_limit_bytes=limit),
        cost_estimate=cost,
    )


def first_part(packs, acts, w_two):
    c1, c2, width = (w_two.shape[0] // 3, w_two.shape[1] // 9, acts.shape[1])
    length = acts.shape[0] // c1
    return vmem_call(
        first_kernel,
        (
            jax.ShapeDtypeStruct(((length + 2) * 3 * c1, width), BF16),
            jax.ShapeDtypeStruct((-(-9 * c2 // LANES) * 3 * c1, LANES), F32),
        ),
        (pltpu.VMEM((9 * c2, 3 * c1), F32),),
        pl.CostEstimate(flops=10**9, bytes_accessed=20 * 2**20, transcendentals=0),
    )(*packs, acts, w_two)


def gradient_part(packs, pres, terms, rows, c1):
    width = pres.shape[1]
    c0 = packs[0].shape[0] // (pres.shape[0] // (3 * c1) - 2)
    return vmem_call(
        gradient_kernel,
        (
            jax.ShapeDtypeStruct((rows // 2, LANES), BF16),
            jax.ShapeDtypeStruct((rows // 2, LANES), F32),
        ),
        (pltpu.VMEM((9 * c0, 3 * c1), F32), pltpu.VMEM((rows, width), F32)),
        pl.CostEstimate(flops=10**9, bytes_accessed=5 * 2**20, transcendentals=0),
    )(*packs, pres, terms)


def input_part(pres, w_one):
    c0, stacked = (w_one.shape[0] // 3, w_one.shape[1] // 3)
    plane = ((pres.shape[0] // stacked - 2) * c0, pres.shape[1])
    return vmem_call(
        input_kernel,
        (
            jax.ShapeDtypeStruct(plane, BF16),
            jax.ShapeDtypeStruct(plane, BF16),
            jax.ShapeDtypeStruct(plane, BF16),
        ),
        (),
        pl.CostEstimate(flops=10**9, bytes_accessed=5 * 2**20, transcendentals=0),
    )(pres, w_one)


def merge_kernel(own, first, second, out, flat):
    chans, length, _ = out.shape

    def add(step, carry):
        at = pl.ds(pl.multiple_of(step * 64, 64), 64)
        flat[at, :] = own[at, :].astype(F32) + first[at, :].astype(F32) + second[at, :].astype(F32)
        return carry

    lax.fori_loop(0, own.shape[0] // 64, add, 0, unroll=4)

    def gather(c, carry):
        out[c] = flat[pl.ds(c, length, stride=chans), :].astype(out.dtype)
        return carry

    lax.fori_loop(0, chans, gather, 0, unroll=4)


def merge(own, first, second, shape):
    return vmem_call(
        merge_kernel,
        jax.ShapeDtypeStruct(shape, BF16),
        (pltpu.VMEM(own.shape, F32),),
        pl.CostEstimate(flops=2 * own.size, bytes_accessed=8 * own.size, transcendentals=0),
    )(own, first, second)


def share_kernel(scale, parts, out, buffer, sems):
    copies, rows, _ = parts.shape
    padded = out.shape[1] - rows
    far = copies // 2
    buffer[0:padded, :] = jnp.sum(parts[0:far, 0:padded, :].astype(F32), axis=0).astype(BF16)
    buffer[padded : 2 * padded, :] = jnp.sum(parts[far:, 0:padded, :].astype(F32), axis=0).astype(BF16)
    grads = jnp.sum(parts[:, padded:rows, :].astype(F32), axis=0) * scale
    buffer[2 * padded :, :] = grads.astype(BF16)
    sent = [pltpu.make_async_copy(buffer, out.at[n], sems.at[n]) for n in range(copies)]
    for copy in sent:
        copy.start()
    for copy in sent:
        copy.wait()


def share(parts, extra, scale):
    copies, rows, _ = parts.shape
    height = 2 * rows - extra
    return pl.pallas_call(
        lambda *refs: share_kernel(scale, *refs),
        out_shape=jax.ShapeDtypeStruct((copies, height, LANES), BF16),
        in_specs=[pl.BlockSpec(memory_space=pltpu.VMEM)],
        out_specs=pl.BlockSpec(memory_space=pl.ANY),
        scratch_shapes=[pltpu.VMEM((height, LANES), BF16), pltpu.SemaphoreType.DMA((copies,))],
        compiler_params=pltpu.CompilerParams(vmem_limit_bytes=24 * 2**20),
        cost_estimate=pl.CostEstimate(
            flops=parts.size, bytes_accessed=6 * parts.size, transcendentals=0
        ),
    )(parts)


def place(source, height, padded, which, bucket, buffer, sems):
    copies, count = (source.shape[0], sems.shape[0])
    step = 2 * copies // count
    sent = []
    for n in range(count):
        for m in range(n * step, (n + 1) * step):
            half, q = (m // copies, m % copies)
            value = source[q, half * padded : (half + 1) * padded, :].astype(F32)
            buffer[m * height : (m + 1) * height, :] = value[0:height]
        rows = pl.ds(n * step * height, step * height)
        at = (which * count + n) * step * height
        at = pl.ds(pl.multiple_of(at, 8), step * height)
        sent.append(pltpu.make_async_copy(buffer.at[rows], bucket.at[at], sems.at[n]))
        sent[-1].start()
    return sent


def start_kernel(height, padded, mine, bucket, buffer, sems):
    for copy in place(mine, height, padded, lax.axis_index("core"), bucket, buffer, sems):
        copy.wait()


def finish_kernel(
    sizes, height, padded, mine, other, partial,
    bucket, out_one, out_two,
    raw, one, two, out_sems, buffer, sems,
):
    c0, c1, c2 = sizes
    copies, rows, _ = mine.shape
    extra = rows - 2 * padded
    me = lax.axis_index("core")
    sent = place(other, height, padded, 1 - me, bucket, buffer, sems)

    for q in range(copies):
        for source, which in ((mine, me), (other, 1 - me)):
            at = pl.multiple_of((which * copies + q) * extra, 8)
            raw[pl.ds(at, extra), :] = source[q, 2 * padded : rows, :].astype(F32)
    block = 3 * c1
    first = -(-9 * c2 // LANES) * block
    for i in range(3):
        for j in range(3):
            column = ((2 - j) * 3 + 2 - i) * c2
            whole, lane = (column // LANES, column % LANES)
            two[(3 * i + j) * block : (3 * i + j + 1) * block, :] = raw[
                whole * block : (whole + 1) * block, lane : lane + c2
            ]
        at = pl.ds(3 * i * block, 3 * block)
        sent.append(pltpu.make_async_copy(two.at[at], out_two.at[at], out_sems.at[i]))
        sent[-1].start()
    for i in range(3):
        for j in range(3):
            row = first + (3 * j + i) * c0
            for k in range(3):
                to = (9 * i + 3 * j + k) * c0
                one[to : to + c0, :] = raw[row : row + c0, k * c1 : (k + 1) * c1]
        at = pl.ds(9 * i * c0, 9 * c0)
        sent.append(pltpu.make_async_copy(one.at[at], out_one.at[at], out_sems.at[3 + i]))
        sent[-1].start()
    for copy in sent:
        copy.wait()


def finish(mine, other, length, sizes):
    c0, c1, c2 = sizes
    copies, rows, _ = mine.shape
    height = length // LANES // (4 * copies)
    padded = ceil_to(height, 16)
    spec = pl.BlockSpec(memory_space=pltpu.VMEM)
    remote = pl.BlockSpec(memory_space=pltpu.HBM)
    whole = jax.ShapeDtypeStruct((length // LANES, LANES), F32)
    chunks = 4
    scratch = [
        pltpu.VMEM((2 * copies * height, LANES), F32),
        pltpu.SemaphoreType.DMA((chunks,)),
    ]
    params = pltpu.CompilerParams(vmem_limit_bytes=24 * 2**20)
    partial = pl.pallas_call(
        lambda *refs: start_kernel(height, padded, *refs),
        out_shape=whole,
        in_specs=[spec],
        out_specs=remote,
        scratch_shapes=scratch,
        compiler_params=params,
    )(mine)
    return pl.pallas_call(
        lambda *refs: finish_kernel(sizes, height, padded, *refs),
        out_shape=(
            whole,
            jax.ShapeDtypeStruct((27 * c0, c1), F32),
            jax.ShapeDtypeStruct((27 * c1, c2), F32),
        ),
        in_specs=[spec, spec, remote],
        out_specs=(remote, remote, remote),
        scratch_shapes=[
            pltpu.VMEM((2 * copies * (rows - 2 * padded), LANES), F32),
            pltpu.VMEM((27 * c0, c1), F32),
            pltpu.VMEM((27 * c1, c2), F32),
            pltpu.SemaphoreType.DMA((6,)),
        ]
        + scratch,
        input_output_aliases={2: 0},
        compiler_params=params,
    )(mine, other, partial)


def crossed(value):
    pairs = [(n, n + 1) for n in range(1, lax.axis_size(SPACE) - 1, 2)]
    return lax.ppermute(value, SPACE, pairs + [(m, n) for n, m in pairs])


def per_device(volume_in, hidden_act, out_cot, kernel_one, kernel_two, grad_bucket):
    c0, c1, c2 = (volume_in.shape[2], hidden_act.shape[2], out_cot.shape[2])
    devices, copies = (lax.axis_size(EVERY), lax.axis_size(SAME))
    length = grad_bucket.shape[1]
    bucket = grad_bucket.reshape(length // LANES, LANES)
    cot = pack(out_cot[0, 0], [], 256)
    bucket, cot = lax.optimization_barrier((bucket, cot))
    core, half = (lax.axis_index("core"), bucket.shape[0] // 2)
    send = lax.dynamic_slice_in_dim(bucket, (1 - core) * half, half).astype(BF16)
    near = lax.dynamic_slice_in_dim(bucket, core * half, half)
    cot, send, near = lax.optimization_barrier((cot, send, near))
    cots = (swapped(cot), cot, crossed(cot))
    vol = pack(volume_in[0, 0], [cot], 16)
    vols = (swapped(vol), vol, crossed(vol))
    send, near = add(near, swapped(send))
    act, send, near = lax.optimization_barrier((hidden_act[0, 0], send, near))
    far = swapped(send, "x")

    used = -(-9 * c2 // LANES) * 3 * c1 + 9 * c0
    rows = ceil_to(used, 16 * devices)
    acts, w_two, w_one = prepare(act, kernel_two, kernel_one)
    pres, terms = first_part(cots, acts, w_two)
    send, keep = gradient_part(vols, pres, terms, rows, c1)
    own, inner, outer = input_part(pres, w_one)
    parts = combine(near, far, keep, swapped(send), copies)
    parts, inner, outer = lax.optimization_barrier((parts, inner, outer))
    parts = lax.all_to_all(parts, SAME, 0, 0)
    cells = volume_in.shape[3] * volume_in.shape[4] * devices
    shares = share(parts, rows // devices, 1.0 / math.sqrt(cells))

    shares, inner, outer = lax.optimization_barrier((shares, inner, outer))
    mine = lax.all_to_all(shares, SAME, 0, 0)
    inner, outer = (swapped(inner), crossed(outer))
    grad_input = merge(own, inner, outer, volume_in.shape[2:])
    mine, grad_input = lax.optimization_barrier((mine, grad_input))
    bucket_sum, total_one, total_two = finish(mine, swapped(mine), length, (c0, c1, c2))
    return (
        grad_input[None, None],
        total_one.reshape(3, 3, 3, c0, c1),
        total_two.reshape(3, 3, 3, c1, c2),
        bucket_sum.reshape(length),
    )


def solution(mesh):
    dp, space = (mesh.shape["dp"], mesh.shape["space"])
    split = Mesh(mesh.devices.reshape(dp // 2, 2, space // 2, 2), EVERY)
    volume = P(("z", "x"), SPACE, None, None, None)
    in_specs = (volume, volume, volume, P(), P(), P(EVERY, None))
    out_specs = (volume, P(), P(), P())
    return jax.shard_map(
        per_device, mesh=split, in_specs=in_specs, out_specs=out_specs, check_vma=False
    )
```

```python
import math

import jax
import jax.numpy as jnp
from jax import lax
from jax.experimental import pallas as pl
from jax.experimental.pallas import tpu as pltpu
from jax.sharding import Mesh, PartitionSpec as P

SPACE = ("y", "core")
SAME = ("x", "z", "y")
EVERY = ("z", "x", "y", "core")
GROUP = 8
LANES = 128
BF16 = jnp.bfloat16
F32 = jnp.float32


def ceil_to(value, step):
    return -(-value // step) * step


def slid(value, step):
    lane = lax.broadcasted_iota(jnp.int32, value.shape, 1)
    width = value.shape[1]
    keep = lane >= step if step > 0 else lane < width + step
    return jnp.where(keep, pltpu.roll(value, step % width, 1), 0.0)


def beside(window, rows, step, count):
    return jnp.concatenate([window[g * step : g * step + rows] for g in range(count)], axis=1)


def turned(src, flat, dst):
    chans, length, _ = src.shape

    def stage(c, carry):
        flat[pl.ds(pl.multiple_of(c * length, length), length), :] = src[c].astype(F32)
        return carry

    lax.fori_loop(0, chans, stage, 0, unroll=4)

    def gather(x, carry):
        rows = flat[pl.ds(x, chans, stride=length), :]
        dst[pl.ds(pl.multiple_of(x * chans, 16), chans), :] = rows.astype(BF16)
        return carry

    lax.fori_loop(0, length, gather, 0, unroll=4)


def pack_kernel(field, *refs):
    out, flat = refs[-2:]
    turned(field, flat, out)


def pack(field, after, weight):
    chans, length, width = field.shape
    spec = pl.BlockSpec(memory_space=pltpu.VMEM)
    return pl.pallas_call(
        pack_kernel,
        out_shape=jax.ShapeDtypeStruct((length * chans, width), BF16),
        in_specs=[spec] + [pl.BlockSpec(memory_space=pl.ANY) for _ in after],
        out_specs=spec,
        scratch_shapes=[pltpu.VMEM((chans * length, width), F32)],
        compiler_params=pltpu.CompilerParams(vmem_limit_bytes=24 * 2**20),
        cost_estimate=pl.CostEstimate(
            flops=0, bytes_accessed=weight * field.size, transcendentals=0
        ),
    )(field, *after)


def in_steps(body, rows, count=8):
    step = rows // count

    def one(n, carry):
        body(n * step, step)
        return carry

    lax.fori_loop(0, count, one, 0)


def add_kernel(own, other, send, keep):
    rows = send.shape[0]
    mine = lax.axis_index("x") * rows
    theirs = rows - mine

    def total(at, step):
        at = pl.ds(pl.multiple_of(at, 16), step)
        return own[at, :] + other[at, :].astype(F32)

    def add(at, step):
        to = pl.ds(pl.multiple_of(at, 16), step)
        send[to, :] = total(theirs + at, step).astype(send.dtype)
        keep[to, :] = total(mine + at, step)

    in_steps(add, rows)


def add(own, other):
    rows = other.shape[0] // 2
    return vmem_call(
        add_kernel,
        (jax.ShapeDtypeStruct((rows, LANES), BF16), jax.ShapeDtypeStruct((rows, LANES), F32)),
        (),
        pl.CostEstimate(flops=0, bytes_accessed=8 * own.size, transcendentals=0),
    )(own, other)


def combine_kernel(keep, other, terms, more, out):
    parts, rows, _ = out.shape
    height, extra = (keep.shape[0] // parts, terms.shape[0] // parts)
    padded = rows - extra
    total = keep[...] + other[...].astype(F32)
    grads = terms[...] + more[...].astype(F32)
    for n in range(parts):
        value = total[n * height : (n + 1) * height]
        if padded > height:
            value = jnp.concatenate([value, jnp.zeros((padded - height, LANES), F32)], axis=0)
        out[n, 0:padded, :] = value.astype(out.dtype)
        out[n, padded:rows, :] = grads[n * extra : (n + 1) * extra].astype(out.dtype)


def combine(keep, other, terms, more, parts):
    rows = ceil_to(keep.shape[0] // parts, 16) + terms.shape[0] // parts
    return vmem_call(
        combine_kernel,
        jax.ShapeDtypeStruct((parts, rows, LANES), BF16),
        (),
        pl.CostEstimate(flops=0, bytes_accessed=8 * keep.size, transcendentals=0),
    )(keep, other, terms, more)


def split_to(total, mine, send, keep):
    half = total.shape[0] // 2
    keep[...] = total[pl.ds(pl.multiple_of(mine * half, 16), half), :]
    send[...] = total[pl.ds(pl.multiple_of((1 - mine) * half, 16), half), :].astype(send.dtype)


def swapped(value, axis="core"):
    return lax.ppermute(value, axis, [(0, 1), (1, 0)])


def plane_order():
    core = lax.axis_index("core")
    ahead = [core * n + (1 - core) * (2 - n) for n in range(3)]
    back = [core * (2 - n) + (1 - core) * n for n in range(3)]
    return (ahead, back)


def windows(packs, x, count):
    length = packs[0].shape[0] // count

    def row(p, n):
        if 0 <= n < length:
            return p[n * count : (n + 1) * count, :]
        return jnp.zeros((count, LANES), BF16)

    rows = [[row(p, x + n - 1) for p in packs] for n in range(GROUP + 2)]
    return jnp.concatenate(
        [jnp.concatenate(sum(rows[g : g + 3], []), axis=0) for g in range(GROUP)], axis=1
    )


def ordered(acc, count, ahead):
    blocks = [pl.multiple_of((3 * j + n) * count, 16) for j in range(3) for n in ahead]
    return jnp.concatenate([acc[pl.ds(at, count), :] for at in blocks], axis=0)


def across_lanes(first, second):
    return lax.dot_general(
        first, second, (((1,), (1,)), ((), ())), preferred_element_type=F32
    )


def prepare_kernel(act, two, one, acts, w_two, w_one, flat):
    ahead, back = plane_order()
    turned(act, flat, acts)
    w_two[...] = jnp.concatenate(
        [
            jnp.concatenate([two[back[n], 2 - j, 2 - k].astype(F32) for k in range(3)], axis=0)
            for j in range(3)
            for n in range(3)
        ],
        axis=1,
    ).astype(BF16)
    w_one[...] = jnp.concatenate(
        [
            jnp.concatenate([one[ahead[n], 2 - j, k].astype(F32) for n in range(3)], axis=0)
            for j in range(3)
            for k in range(3)
        ],
        axis=1,
    ).astype(BF16)


def prepare(act, kernel_two, kernel_one):
    c1, length, width = act.shape
    c0, c2 = (kernel_one.shape[3], kernel_two.shape[4])
    return vmem_call(
        prepare_kernel,
        (
            jax.ShapeDtypeStruct((length * c1, width), BF16),
            jax.ShapeDtypeStruct((3 * c1, 9 * c2), BF16),
            jax.ShapeDtypeStruct((3 * c0, 9 * c1), BF16),
        ),
        (pltpu.VMEM((c1 * length, width), F32),),
        pl.CostEstimate(flops=0, bytes_accessed=16 * act.size, transcendentals=0),
    )(act, kernel_two, kernel_one)


def first_kernel(pack_in, pack_0, pack_out, acts, w_two, pres, terms, acc):
    c1, c2 = (w_two.shape[0] // 3, w_two.shape[1] // 9)
    length = acts.shape[0] // c1
    packs = (pack_in, pack_0, pack_out)
    ahead, _ = plane_order()
    stacked = 3 * c1
    pres[0:stacked, :] = jnp.zeros((stacked, LANES), BF16)
    pres[(length + 1) * stacked : (length + 2) * stacked, :] = jnp.zeros((stacked, LANES), BF16)
    acc[...] = jnp.zeros_like(acc)

    for x in range(0, length, GROUP):
        right = windows(packs, x, c2)
        sums = jnp.dot(w_two[...], right, preferred_element_type=F32)
        columns = []
        for g in range(GROUP):
            part = sums[:, g * LANES : (g + 1) * LANES]
            grad = slid(part[0:c1], 1) + part[c1 : 2 * c1] + slid(part[2 * c1 : 3 * c1], -1)
            value = acts[(x + g) * c1 : (x + g + 1) * c1, :].astype(F32)
            pre = (grad * jnp.where(value > 0, 1.0, 0.2)).astype(BF16).astype(F32)
            moved = jnp.concatenate([slid(pre, -1), pre, slid(pre, 1)], axis=0).astype(BF16)
            pres[(x + g + 1) * stacked : (x + g + 2) * stacked, :] = moved
            stack = jnp.concatenate([slid(value, 1), value, slid(value, -1)], axis=0)
            columns.append(stack.astype(BF16))
        acc[...] += across_lanes(right, jnp.concatenate(columns, axis=1))

    terms[...] = jnp.zeros_like(terms)
    total = ordered(acc, c2, ahead).T
    rows, width = total.shape
    for block in range(-(-width // LANES)):
        part = total[:, block * LANES : min(width, (block + 1) * LANES)]
        terms[block * rows : (block + 1) * rows, 0 : part.shape[1]] = part


def gradient_kernel(pack_in, pack_0, pack_out, pres, before, send, keep, acc, terms):
    c0, stacked = (acc.shape[0] // 9, acc.shape[1])
    packs = (pack_in, pack_0, pack_out)
    ahead, _ = plane_order()
    length = pres.shape[0] // stacked - 2
    acc[...] = jnp.zeros_like(acc)

    for x in range(0, length, GROUP):
        rows = [pres[(x + g + 1) * stacked : (x + g + 2) * stacked, :] for g in range(GROUP)]
        acc[...] += across_lanes(windows(packs, x, c0), jnp.concatenate(rows, axis=1))

    used = before.shape[0]
    terms[0:used, :] = before[...]
    terms[used:, :] = jnp.zeros((terms.shape[0] - used, LANES), F32)
    total = ordered(acc, c0, ahead)
    terms[used : used + total.shape[0], 0 : total.shape[1]] = total
    split_to(terms, lax.axis_index("core"), send, keep)


def input_kernel(pres, w_one, own, inner, outer):
    c0, stacked = (w_one.shape[0] // 3, w_one.shape[1] // 3)
    length = pres.shape[0] // stacked - 2

    for x in range(0, length, GROUP):
        window = pres[x * stacked : (x + GROUP + 2) * stacked, :]
        moved = beside(window, 3 * stacked, stacked, GROUP)
        sums = jnp.dot(w_one[...], moved, preferred_element_type=F32)
        for g in range(GROUP):
            part = sums[:, g * LANES : (g + 1) * LANES]
            at = pl.ds((x + g) * c0, c0)
            for i, out in ((0, inner), (1, own), (2, outer)):
                out[at, :] = part[i * c0 : (i + 1) * c0].astype(out.dtype)


def vmem_call(body, out_shape, scratch=(), cost=None, limit=24 * 2**20):
    spec = pl.BlockSpec(memory_space=pltpu.VMEM)
    return pl.pallas_call(
        body,
        out_shape=out_shape,
        out_specs=jax.tree.map(lambda _: spec, out_shape),
        scratch_shapes=list(scratch),
        compiler_params=pltpu.CompilerParams(vmem_limit_bytes=limit),
        cost_estimate=cost,
    )


def first_part(packs, acts, w_two):
    c1, c2, width = (w_two.shape[0] // 3, w_two.shape[1] // 9, acts.shape[1])
    length = acts.shape[0] // c1
    return vmem_call(
        first_kernel,
        (
            jax.ShapeDtypeStruct(((length + 2) * 3 * c1, width), BF16),
            jax.ShapeDtypeStruct((-(-9 * c2 // LANES) * 3 * c1, LANES), F32),
        ),
        (pltpu.VMEM((9 * c2, 3 * c1), F32),),
        pl.CostEstimate(flops=10**9, bytes_accessed=20 * 2**20, transcendentals=0),
    )(*packs, acts, w_two)


def gradient_part(packs, pres, terms, rows, c1):
    width = pres.shape[1]
    c0 = packs[0].shape[0] // (pres.shape[0] // (3 * c1) - 2)
    return vmem_call(
        gradient_kernel,
        (
            jax.ShapeDtypeStruct((rows // 2, LANES), BF16),
            jax.ShapeDtypeStruct((rows // 2, LANES), F32),
        ),
        (pltpu.VMEM((9 * c0, 3 * c1), F32), pltpu.VMEM((rows, width), F32)),
        pl.CostEstimate(flops=10**9, bytes_accessed=5 * 2**20, transcendentals=0),
    )(*packs, pres, terms)


def input_part(pres, w_one):
    c0, stacked = (w_one.shape[0] // 3, w_one.shape[1] // 3)
    plane = ((pres.shape[0] // stacked - 2) * c0, pres.shape[1])
    return vmem_call(
        input_kernel,
        (
            jax.ShapeDtypeStruct(plane, BF16),
            jax.ShapeDtypeStruct(plane, BF16),
            jax.ShapeDtypeStruct(plane, BF16),
        ),
        (),
        pl.CostEstimate(flops=10**9, bytes_accessed=5 * 2**20, transcendentals=0),
    )(pres, w_one)


def merge_kernel(own, first, second, out, flat):
    chans, length, _ = out.shape

    def add(step, carry):
        at = pl.ds(pl.multiple_of(step * 64, 64), 64)
        flat[at, :] = own[at, :].astype(F32) + first[at, :].astype(F32) + second[at, :].astype(F32)
        return carry

    lax.fori_loop(0, own.shape[0] // 64, add, 0, unroll=4)

    def gather(c, carry):
        out[c] = flat[pl.ds(c, length, stride=chans), :].astype(out.dtype)
        return carry

    lax.fori_loop(0, chans, gather, 0, unroll=4)


def merge(own, first, second, shape):
    return vmem_call(
        merge_kernel,
        jax.ShapeDtypeStruct(shape, BF16),
        (pltpu.VMEM(own.shape, F32),),
        pl.CostEstimate(flops=2 * own.size, bytes_accessed=8 * own.size, transcendentals=0),
    )(own, first, second)


def share_kernel(scale, parts, out, buffer, sems):
    copies, rows, _ = parts.shape
    padded = out.shape[1] - rows
    far = copies // 2
    buffer[0:padded, :] = jnp.sum(parts[0:far, 0:padded, :].astype(F32), axis=0).astype(BF16)
    buffer[padded : 2 * padded, :] = jnp.sum(parts[far:, 0:padded, :].astype(F32), axis=0).astype(BF16)
    grads = jnp.sum(parts[:, padded:rows, :].astype(F32), axis=0) * scale
    buffer[2 * padded :, :] = grads.astype(BF16)
    sent = [pltpu.make_async_copy(buffer, out.at[n], sems.at[n]) for n in range(copies)]
    for copy in sent:
        copy.start()
    for copy in sent:
        copy.wait()


def share(parts, extra, scale):
    copies, rows, _ = parts.shape
    height = 2 * rows - extra
    return pl.pallas_call(
        lambda *refs: share_kernel(scale, *refs),
        out_shape=jax.ShapeDtypeStruct((copies, height, LANES), BF16),
        in_specs=[pl.BlockSpec(memory_space=pltpu.VMEM)],
        out_specs=pl.BlockSpec(memory_space=pl.ANY),
        scratch_shapes=[pltpu.VMEM((height, LANES), BF16), pltpu.SemaphoreType.DMA((copies,))],
        compiler_params=pltpu.CompilerParams(vmem_limit_bytes=24 * 2**20),
        cost_estimate=pl.CostEstimate(
            flops=parts.size, bytes_accessed=6 * parts.size, transcendentals=0
        ),
    )(parts)


def place(source, height, padded, which, bucket, buffer, sems):
    copies, count = (source.shape[0], sems.shape[0])
    step = 2 * copies // count
    sent = []
    for n in range(count):
        for m in range(n * step, (n + 1) * step):
            half, q = (m // copies, m % copies)
            value = source[q, half * padded : (half + 1) * padded, :].astype(F32)
            buffer[m * height : (m + 1) * height, :] = value[0:height]
        rows = pl.ds(n * step * height, step * height)
        at = (which * count + n) * step * height
        at = pl.ds(pl.multiple_of(at, 8), step * height)
        sent.append(pltpu.make_async_copy(buffer.at[rows], bucket.at[at], sems.at[n]))
        sent[-1].start()
    return sent


def start_kernel(height, padded, mine, bucket, buffer, sems):
    for copy in place(mine, height, padded, lax.axis_index("core"), bucket, buffer, sems):
        copy.wait()


def finish_kernel(
    sizes, height, padded, mine, other, partial,
    bucket, out_one, out_two,
    raw, one, two, out_sems, buffer, sems,
):
    c0, c1, c2 = sizes
    copies, rows, _ = mine.shape
    extra = rows - 2 * padded
    me = lax.axis_index("core")
    sent = place(other, height, padded, 1 - me, bucket, buffer, sems)

    for q in range(copies):
        for source, which in ((mine, me), (other, 1 - me)):
            at = pl.multiple_of((which * copies + q) * extra, 8)
            raw[pl.ds(at, extra), :] = source[q, 2 * padded : rows, :].astype(F32)
    block = 3 * c1
    first = -(-9 * c2 // LANES) * block
    for i in range(3):
        for j in range(3):
            column = ((2 - j) * 3 + 2 - i) * c2
            whole, lane = (column // LANES, column % LANES)
            two[(3 * i + j) * block : (3 * i + j + 1) * block, :] = raw[
                whole * block : (whole + 1) * block, lane : lane + c2
            ]
        at = pl.ds(3 * i * block, 3 * block)
        sent.append(pltpu.make_async_copy(two.at[at], out_two.at[at], out_sems.at[i]))
        sent[-1].start()
    for i in range(3):
        for j in range(3):
            row = first + (3 * j + i) * c0
            for k in range(3):
                to = (9 * i + 3 * j + k) * c0
                one[to : to + c0, :] = raw[row : row + c0, k * c1 : (k + 1) * c1]
        at = pl.ds(9 * i * c0, 9 * c0)
        sent.append(pltpu.make_async_copy(one.at[at], out_one.at[at], out_sems.at[3 + i]))
        sent[-1].start()
    for copy in sent:
        copy.wait()


def finish(mine, other, length, sizes):
    c0, c1, c2 = sizes
    copies, rows, _ = mine.shape
    height = length // LANES // (4 * copies)
    padded = ceil_to(height, 16)
    spec = pl.BlockSpec(memory_space=pltpu.VMEM)
    remote = pl.BlockSpec(memory_space=pltpu.HBM)
    whole = jax.ShapeDtypeStruct((length // LANES, LANES), F32)
    chunks = 4
    scratch = [
        pltpu.VMEM((2 * copies * height, LANES), F32),
        pltpu.SemaphoreType.DMA((chunks,)),
    ]
    params = pltpu.CompilerParams(vmem_limit_bytes=24 * 2**20)
    partial = pl.pallas_call(
        lambda *refs: start_kernel(height, padded, *refs),
        out_shape=whole,
        in_specs=[spec],
        out_specs=remote,
        scratch_shapes=scratch,
        compiler_params=params,
    )(mine)
    return pl.pallas_call(
        lambda *refs: finish_kernel(sizes, height, padded, *refs),
        out_shape=(
            whole,
            jax.ShapeDtypeStruct((27 * c0, c1), F32),
            jax.ShapeDtypeStruct((27 * c1, c2), F32),
        ),
        in_specs=[spec, spec, remote],
        out_specs=(remote, remote, remote),
        scratch_shapes=[
            pltpu.VMEM((2 * copies * (rows - 2 * padded), LANES), F32),
            pltpu.VMEM((27 * c0, c1), F32),
            pltpu.VMEM((27 * c1, c2), F32),
            pltpu.SemaphoreType.DMA((6,)),
        ]
        + scratch,
        input_output_aliases={2: 0},
        compiler_params=params,
    )(mine, other, partial)


def crossed(value):
    pairs = [(n, n + 1) for n in range(1, lax.axis_size(SPACE) - 1, 2)]
    return lax.ppermute(value, SPACE, pairs + [(m, n) for n, m in pairs])


def per_device(volume_in, hidden_act, out_cot, kernel_one, kernel_two, grad_bucket):
    c0, c1, c2 = (volume_in.shape[2], hidden_act.shape[2], out_cot.shape[2])
    devices, copies = (lax.axis_size(EVERY), lax.axis_size(SAME))
    length = grad_bucket.shape[1]
    bucket = grad_bucket.reshape(length // LANES, LANES)
    cot = pack(out_cot[0, 0], [], 256)
    bucket, cot = lax.optimization_barrier((bucket, cot))
    core, half = (lax.axis_index("core"), bucket.shape[0] // 2)
    send = lax.dynamic_slice_in_dim(bucket, (1 - core) * half, half).astype(BF16)
    near = lax.dynamic_slice_in_dim(bucket, core * half, half)
    cot, send, near = lax.optimization_barrier((cot, send, near))
    cots = (swapped(cot), cot, pack(crossed(out_cot[0, 0]), [], 16))
    vol = pack(volume_in[0, 0], [cot], 16)
    vols = (swapped(vol), vol, crossed(vol))
    send, near = add(near, swapped(send))
    act, send, near = lax.optimization_barrier((hidden_act[0, 0], send, near))
    far = swapped(send, "x")

    used = -(-9 * c2 // LANES) * 3 * c1 + 9 * c0
    rows = ceil_to(used, 16 * devices)
    acts, w_two, w_one = prepare(act, kernel_two, kernel_one)
    pres, terms = first_part(cots, acts, w_two)
    send, keep = gradient_part(vols, pres, terms, rows, c1)
    own, inner, outer = input_part(pres, w_one)
    parts = combine(near, far, keep, swapped(send), copies)
    parts, inner, outer = lax.optimization_barrier((parts, inner, outer))
    parts = lax.all_to_all(parts, SAME, 0, 0)
    cells = volume_in.shape[3] * volume_in.shape[4] * devices
    shares = share(parts, rows // devices, 1.0 / math.sqrt(cells))

    shares, inner, outer = lax.optimization_barrier((shares, inner, outer))
    mine = lax.all_to_all(shares, SAME, 0, 0)
    inner, outer = (swapped(inner), crossed(outer))
    grad_input = merge(own, inner, outer, volume_in.shape[2:])
    mine, grad_input = lax.optimization_barrier((mine, grad_input))
    bucket_sum, total_one, total_two = finish(mine, swapped(mine), length, (c0, c1, c2))
    return (
        grad_input[None, None],
        total_one.reshape(3, 3, 3, c0, c1),
        total_two.reshape(3, 3, 3, c1, c2),
        bucket_sum.reshape(length),
    )


def solution(mesh):
    dp, space = (mesh.shape["dp"], mesh.shape["space"])
    split = Mesh(mesh.devices.reshape(dp // 2, 2, space // 2, 2), EVERY)
    volume = P(("z", "x"), SPACE, None, None, None)
    in_specs = (volume, volume, volume, P(), P(), P(EVERY, None))
    out_specs = (volume, P(), P(), P())
    return jax.shard_map(
        per_device, mesh=split, in_specs=in_specs, out_specs=out_specs, check_vma=False
    )
```

```python
import math

import jax
import jax.numpy as jnp
from jax import lax
from jax.experimental import pallas as pl
from jax.experimental.pallas import tpu as pltpu
from jax.sharding import Mesh, PartitionSpec as P

SPACE = ("y", "core")
SAME = ("x", "z", "y")
EVERY = ("z", "x", "y", "core")
GROUP = 16
LANES = 128
BF16 = jnp.bfloat16
F32 = jnp.float32


def ceil_to(value, step):
    return -(-value // step) * step


def slid(value, step):
    lane = lax.broadcasted_iota(jnp.int32, value.shape, 1)
    width = value.shape[1]
    keep = lane >= step if step > 0 else lane < width + step
    return jnp.where(keep, pltpu.roll(value, step % width, 1), 0.0)


def beside(window, rows, step, count):
    return jnp.concatenate([window[g * step : g * step + rows] for g in range(count)], axis=1)


def turned(src, flat, dst):
    chans, length, _ = src.shape

    def stage(c, carry):
        flat[pl.ds(pl.multiple_of(c * length, length), length), :] = src[c].astype(F32)
        return carry

    lax.fori_loop(0, chans, stage, 0, unroll=8)

    def gather(x, carry):
        rows = flat[pl.ds(x, chans, stride=length), :]
        dst[pl.ds(pl.multiple_of(x * chans, 16), chans), :] = rows.astype(BF16)
        return carry

    lax.fori_loop(0, length, gather, 0, unroll=8)


def pack_kernel(field, *refs):
    out, flat = refs[-2:]
    turned(field, flat, out)


def pack(field, after, weight):
    chans, length, width = field.shape
    spec = pl.BlockSpec(memory_space=pltpu.VMEM)
    return pl.pallas_call(
        pack_kernel,
        out_shape=jax.ShapeDtypeStruct((length * chans, width), BF16),
        in_specs=[spec] + [pl.BlockSpec(memory_space=pl.ANY) for _ in after],
        out_specs=spec,
        scratch_shapes=[pltpu.VMEM((chans * length, width), F32)],
        compiler_params=pltpu.CompilerParams(vmem_limit_bytes=24 * 2**20),
        cost_estimate=pl.CostEstimate(
            flops=0, bytes_accessed=weight * field.size, transcendentals=0
        ),
    )(field, *after)


def in_steps(body, rows, count=8):
    step = rows // count

    def one(n, carry):
        body(n * step, step)
        return carry

    lax.fori_loop(0, count, one, 0)


def add_kernel(own, other, send, keep):
    rows = send.shape[0]
    mine = lax.axis_index("x") * rows
    theirs = rows - mine

    def total(at, step):
        at = pl.ds(pl.multiple_of(at, 16), step)
        return own[at, :] + other[at, :].astype(F32)

    def add(at, step):
        to = pl.ds(pl.multiple_of(at, 16), step)
        send[to, :] = total(theirs + at, step).astype(send.dtype)
        keep[to, :] = total(mine + at, step)

    in_steps(add, rows)


def add(own, other):
    rows = other.shape[0] // 2
    return vmem_call(
        add_kernel,
        (jax.ShapeDtypeStruct((rows, LANES), BF16), jax.ShapeDtypeStruct((rows, LANES), F32)),
        (),
        pl.CostEstimate(flops=0, bytes_accessed=8 * own.size, transcendentals=0),
    )(own, other)


def combine_kernel(keep, other, terms, more, out):
    parts, rows, _ = out.shape
    height, extra = (keep.shape[0] // parts, terms.shape[0] // parts)
    padded = rows - extra
    total = keep[...] + other[...].astype(F32)
    grads = terms[...] + more[...].astype(F32)
    for n in range(parts):
        value = total[n * height : (n + 1) * height]
        if padded > height:
            value = jnp.concatenate([value, jnp.zeros((padded - height, LANES), F32)], axis=0)
        out[n, 0:padded, :] = value.astype(out.dtype)
        out[n, padded:rows, :] = grads[n * extra : (n + 1) * extra].astype(out.dtype)


def combine(keep, other, terms, more, parts):
    rows = ceil_to(keep.shape[0] // parts, 16) + terms.shape[0] // parts
    return vmem_call(
        combine_kernel,
        jax.ShapeDtypeStruct((parts, rows, LANES), BF16),
        (),
        pl.CostEstimate(flops=0, bytes_accessed=8 * keep.size, transcendentals=0),
    )(keep, other, terms, more)


def split_to(total, mine, send, keep):
    half = total.shape[0] // 2
    keep[...] = total[pl.ds(pl.multiple_of(mine * half, 16), half), :]
    send[...] = total[pl.ds(pl.multiple_of((1 - mine) * half, 16), half), :].astype(send.dtype)


def swapped(value, axis="core"):
    return lax.ppermute(value, axis, [(0, 1), (1, 0)])


def plane_order():
    core = lax.axis_index("core")
    ahead = [core * n + (1 - core) * (2 - n) for n in range(3)]
    back = [core * (2 - n) + (1 - core) * n for n in range(3)]
    return (ahead, back)


def windows(packs, x, count):
    length = packs[0].shape[0] // count

    def row(p, n):
        if 0 <= n < length:
            return p[n * count : (n + 1) * count, :]
        return jnp.zeros((count, LANES), BF16)

    rows = [[row(p, x + n - 1) for p in packs] for n in range(GROUP + 2)]
    return jnp.concatenate(
        [jnp.concatenate(sum(rows[g : g + 3], []), axis=0) for g in range(GROUP)], axis=1
    )


def ordered(acc, count, ahead):
    blocks = [pl.multiple_of((3 * j + n) * count, 16) for j in range(3) for n in ahead]
    return jnp.concatenate([acc[pl.ds(at, count), :] for at in blocks], axis=0)


def across_lanes(first, second):
    return lax.dot_general(
        first, second, (((1,), (1,)), ((), ())), preferred_element_type=F32
    )


def prepare_kernel(act, two, one, acts, w_two, w_one, flat):
    ahead, back = plane_order()
    turned(act, flat, acts)
    w_two[...] = jnp.concatenate(
        [
            jnp.concatenate([two[back[n], 2 - j, 2 - k].astype(F32) for k in range(3)], axis=0)
            for j in range(3)
            for n in range(3)
        ],
        axis=1,
    ).astype(BF16)
    w_one[...] = jnp.concatenate(
        [
            jnp.concatenate([one[ahead[n], 2 - j, k].astype(F32) for n in range(3)], axis=0)
            for j in range(3)
            for k in range(3)
        ],
        axis=1,
    ).astype(BF16)


def prepare(act, kernel_two, kernel_one):
    c1, length, width = act.shape
    c0, c2 = (kernel_one.shape[3], kernel_two.shape[4])
    return vmem_call(
        prepare_kernel,
        (
            jax.ShapeDtypeStruct((length * c1, width), BF16),
            jax.ShapeDtypeStruct((3 * c1, 9 * c2), BF16),
            jax.ShapeDtypeStruct((3 * c0, 9 * c1), BF16),
        ),
        (pltpu.VMEM((c1 * length, width), F32),),
        pl.CostEstimate(flops=0, bytes_accessed=16 * act.size, transcendentals=0),
    )(act, kernel_two, kernel_one)


def first_kernel(pack_in, pack_0, pack_out, acts, w_two, pres, terms, acc):
    c1, c2 = (w_two.shape[0] // 3, w_two.shape[1] // 9)
    length = acts.shape[0] // c1
    packs = (pack_in, pack_0, pack_out)
    ahead, _ = plane_order()
    stacked = 3 * c1
    pres[0:stacked, :] = jnp.zeros((stacked, LANES), BF16)
    pres[(length + 1) * stacked : (length + 2) * stacked, :] = jnp.zeros((stacked, LANES), BF16)
    acc[...] = jnp.zeros_like(acc)

    for x in range(0, length, GROUP):
        right = windows(packs, x, c2)
        sums = jnp.dot(w_two[...], right, preferred_element_type=F32)
        columns = []
        for g in range(GROUP):
            part = sums[:, g * LANES : (g + 1) * LANES]
            grad = slid(part[0:c1], 1) + part[c1 : 2 * c1] + slid(part[2 * c1 : 3 * c1], -1)
            value = acts[(x + g) * c1 : (x + g + 1) * c1, :].astype(F32)
            pre = (grad * jnp.where(value > 0, 1.0, 0.2)).astype(BF16).astype(F32)
            moved = jnp.concatenate([slid(pre, -1), pre, slid(pre, 1)], axis=0).astype(BF16)
            pres[(x + g + 1) * stacked : (x + g + 2) * stacked, :] = moved
            stack = jnp.concatenate([slid(value, 1), value, slid(value, -1)], axis=0)
            columns.append(stack.astype(BF16))
        acc[...] += across_lanes(right, jnp.concatenate(columns, axis=1))

    terms[...] = jnp.zeros_like(terms)
    total = ordered(acc, c2, ahead).T
    rows, width = total.shape
    for block in range(-(-width // LANES)):
        part = total[:, block * LANES : min(width, (block + 1) * LANES)]
        terms[block * rows : (block + 1) * rows, 0 : part.shape[1]] = part


def gradient_kernel(pack_in, pack_0, pack_out, pres, before, send, keep, acc, terms):
    c0, stacked = (acc.shape[0] // 9, acc.shape[1])
    packs = (pack_in, pack_0, pack_out)
    ahead, _ = plane_order()
    length = pres.shape[0] // stacked - 2
    acc[...] = jnp.zeros_like(acc)

    for x in range(0, length, GROUP):
        rows = [pres[(x + g + 1) * stacked : (x + g + 2) * stacked, :] for g in range(GROUP)]
        acc[...] += across_lanes(windows(packs, x, c0), jnp.concatenate(rows, axis=1))

    used = before.shape[0]
    terms[0:used, :] = before[...]
    terms[used:, :] = jnp.zeros((terms.shape[0] - used, LANES), F32)
    total = ordered(acc, c0, ahead)
    terms[used : used + total.shape[0], 0 : total.shape[1]] = total
    split_to(terms, lax.axis_index("core"), send, keep)


def input_kernel(pres, w_one, own, inner, outer):
    c0, stacked = (w_one.shape[0] // 3, w_one.shape[1] // 3)
    length = pres.shape[0] // stacked - 2

    for x in range(0, length, GROUP):
        window = pres[x * stacked : (x + GROUP + 2) * stacked, :]
        moved = beside(window, 3 * stacked, stacked, GROUP)
        sums = jnp.dot(w_one[...], moved, preferred_element_type=F32)
        for g in range(GROUP):
            part = sums[:, g * LANES : (g + 1) * LANES]
            at = pl.ds((x + g) * c0, c0)
            for i, out in ((0, inner), (1, own), (2, outer)):
                out[at, :] = part[i * c0 : (i + 1) * c0].astype(out.dtype)


def vmem_call(body, out_shape, scratch=(), cost=None, limit=24 * 2**20):
    spec = pl.BlockSpec(memory_space=pltpu.VMEM)
    return pl.pallas_call(
        body,
        out_shape=out_shape,
        out_specs=jax.tree.map(lambda _: spec, out_shape),
        scratch_shapes=list(scratch),
        compiler_params=pltpu.CompilerParams(vmem_limit_bytes=limit),
        cost_estimate=cost,
    )


def first_part(packs, acts, w_two):
    c1, c2, width = (w_two.shape[0] // 3, w_two.shape[1] // 9, acts.shape[1])
    length = acts.shape[0] // c1
    return vmem_call(
        first_kernel,
        (
            jax.ShapeDtypeStruct(((length + 2) * 3 * c1, width), BF16),
            jax.ShapeDtypeStruct((-(-9 * c2 // LANES) * 3 * c1, LANES), F32),
        ),
        (pltpu.VMEM((9 * c2, 3 * c1), F32),),
        pl.CostEstimate(flops=10**9, bytes_accessed=20 * 2**20, transcendentals=0),
    )(*packs, acts, w_two)


def gradient_part(packs, pres, terms, rows, c1):
    width = pres.shape[1]
    c0 = packs[0].shape[0] // (pres.shape[0] // (3 * c1) - 2)
    return vmem_call(
        gradient_kernel,
        (
            jax.ShapeDtypeStruct((rows // 2, LANES), BF16),
            jax.ShapeDtypeStruct((rows // 2, LANES), F32),
        ),
        (pltpu.VMEM((9 * c0, 3 * c1), F32), pltpu.VMEM((rows, width), F32)),
        pl.CostEstimate(flops=10**9, bytes_accessed=5 * 2**20, transcendentals=0),
    )(*packs, pres, terms)


def input_part(pres, w_one):
    c0, stacked = (w_one.shape[0] // 3, w_one.shape[1] // 3)
    plane = ((pres.shape[0] // stacked - 2) * c0, pres.shape[1])
    return vmem_call(
        input_kernel,
        (
            jax.ShapeDtypeStruct(plane, BF16),
            jax.ShapeDtypeStruct(plane, BF16),
            jax.ShapeDtypeStruct(plane, BF16),
        ),
        (),
        pl.CostEstimate(flops=10**9, bytes_accessed=5 * 2**20, transcendentals=0),
    )(pres, w_one)


def merge_kernel(own, first, second, out, flat):
    chans, length, _ = out.shape

    def add(step, carry):
        at = pl.ds(pl.multiple_of(step * 64, 64), 64)
        flat[at, :] = own[at, :].astype(F32) + first[at, :].astype(F32) + second[at, :].astype(F32)
        return carry

    lax.fori_loop(0, own.shape[0] // 64, add, 0, unroll=8)

    def gather(c, carry):
        out[c] = flat[pl.ds(c, length, stride=chans), :].astype(out.dtype)
        return carry

    lax.fori_loop(0, chans, gather, 0, unroll=8)


def merge(own, first, second, shape):
    return vmem_call(
        merge_kernel,
        jax.ShapeDtypeStruct(shape, BF16),
        (pltpu.VMEM(own.shape, F32),),
        pl.CostEstimate(flops=2 * own.size, bytes_accessed=8 * own.size, transcendentals=0),
    )(own, first, second)


def share_kernel(scale, parts, out, buffer, sems):
    copies, rows, _ = parts.shape
    padded = out.shape[1] - rows
    far = copies // 2
    buffer[0:padded, :] = jnp.sum(parts[0:far, 0:padded, :].astype(F32), axis=0).astype(BF16)
    buffer[padded : 2 * padded, :] = jnp.sum(parts[far:, 0:padded, :].astype(F32), axis=0).astype(BF16)
    grads = jnp.sum(parts[:, padded:rows, :].astype(F32), axis=0) * scale
    buffer[2 * padded :, :] = grads.astype(BF16)
    sent = [pltpu.make_async_copy(buffer, out.at[n], sems.at[n]) for n in range(copies)]
    for copy in sent:
        copy.start()
    for copy in sent:
        copy.wait()


def share(parts, extra, scale):
    copies, rows, _ = parts.shape
    height = 2 * rows - extra
    return pl.pallas_call(
        lambda *refs: share_kernel(scale, *refs),
        out_shape=jax.ShapeDtypeStruct((copies, height, LANES), BF16),
        in_specs=[pl.BlockSpec(memory_space=pltpu.VMEM)],
        out_specs=pl.BlockSpec(memory_space=pl.ANY),
        scratch_shapes=[pltpu.VMEM((height, LANES), BF16), pltpu.SemaphoreType.DMA((copies,))],
        compiler_params=pltpu.CompilerParams(vmem_limit_bytes=24 * 2**20),
        cost_estimate=pl.CostEstimate(
            flops=parts.size, bytes_accessed=6 * parts.size, transcendentals=0
        ),
    )(parts)


def place(source, height, padded, which, bucket, buffer, sems):
    copies, count = (source.shape[0], sems.shape[0])
    step = 2 * copies // count
    sent = []
    for n in range(count):
        for m in range(n * step, (n + 1) * step):
            half, q = (m // copies, m % copies)
            value = source[q, half * padded : (half + 1) * padded, :].astype(F32)
            buffer[m * height : (m + 1) * height, :] = value[0:height]
        rows = pl.ds(n * step * height, step * height)
        at = (which * count + n) * step * height
        at = pl.ds(pl.multiple_of(at, 8), step * height)
        sent.append(pltpu.make_async_copy(buffer.at[rows], bucket.at[at], sems.at[n]))
        sent[-1].start()
    return sent


def start_kernel(height, padded, mine, bucket, buffer, sems):
    for copy in place(mine, height, padded, lax.axis_index("core"), bucket, buffer, sems):
        copy.wait()


def finish_kernel(
    sizes, height, padded, mine, other, partial,
    bucket, out_one, out_two,
    raw, one, two, out_sems, buffer, sems,
):
    c0, c1, c2 = sizes
    copies, rows, _ = mine.shape
    extra = rows - 2 * padded
    me = lax.axis_index("core")
    sent = place(other, height, padded, 1 - me, bucket, buffer, sems)

    for q in range(copies):
        for source, which in ((mine, me), (other, 1 - me)):
            at = pl.multiple_of((which * copies + q) * extra, 8)
            raw[pl.ds(at, extra), :] = source[q, 2 * padded : rows, :].astype(F32)
    block = 3 * c1
    first = -(-9 * c2 // LANES) * block
    for i in range(3):
        for j in range(3):
            column = ((2 - j) * 3 + 2 - i) * c2
            whole, lane = (column // LANES, column % LANES)
            two[(3 * i + j) * block : (3 * i + j + 1) * block, :] = raw[
                whole * block : (whole + 1) * block, lane : lane + c2
            ]
        at = pl.ds(3 * i * block, 3 * block)
        sent.append(pltpu.make_async_copy(two.at[at], out_two.at[at], out_sems.at[i]))
        sent[-1].start()
    for i in range(3):
        for j in range(3):
            row = first + (3 * j + i) * c0
            for k in range(3):
                to = (9 * i + 3 * j + k) * c0
                one[to : to + c0, :] = raw[row : row + c0, k * c1 : (k + 1) * c1]
        at = pl.ds(9 * i * c0, 9 * c0)
        sent.append(pltpu.make_async_copy(one.at[at], out_one.at[at], out_sems.at[3 + i]))
        sent[-1].start()
    for copy in sent:
        copy.wait()


def finish(mine, other, length, sizes):
    c0, c1, c2 = sizes
    copies, rows, _ = mine.shape
    height = length // LANES // (4 * copies)
    padded = ceil_to(height, 16)
    spec = pl.BlockSpec(memory_space=pltpu.VMEM)
    remote = pl.BlockSpec(memory_space=pltpu.HBM)
    whole = jax.ShapeDtypeStruct((length // LANES, LANES), F32)
    chunks = 4
    scratch = [
        pltpu.VMEM((2 * copies * height, LANES), F32),
        pltpu.SemaphoreType.DMA((chunks,)),
    ]
    params = pltpu.CompilerParams(vmem_limit_bytes=24 * 2**20)
    partial = pl.pallas_call(
        lambda *refs: start_kernel(height, padded, *refs),
        out_shape=whole,
        in_specs=[spec],
        out_specs=remote,
        scratch_shapes=scratch,
        compiler_params=params,
    )(mine)
    return pl.pallas_call(
        lambda *refs: finish_kernel(sizes, height, padded, *refs),
        out_shape=(
            whole,
            jax.ShapeDtypeStruct((27 * c0, c1), F32),
            jax.ShapeDtypeStruct((27 * c1, c2), F32),
        ),
        in_specs=[spec, spec, remote],
        out_specs=(remote, remote, remote),
        scratch_shapes=[
            pltpu.VMEM((2 * copies * (rows - 2 * padded), LANES), F32),
            pltpu.VMEM((27 * c0, c1), F32),
            pltpu.VMEM((27 * c1, c2), F32),
            pltpu.SemaphoreType.DMA((6,)),
        ]
        + scratch,
        input_output_aliases={2: 0},
        compiler_params=params,
    )(mine, other, partial)


def crossed(value):
    pairs = [(n, n + 1) for n in range(1, lax.axis_size(SPACE) - 1, 2)]
    return lax.ppermute(value, SPACE, pairs + [(m, n) for n, m in pairs])


def per_device(volume_in, hidden_act, out_cot, kernel_one, kernel_two, grad_bucket):
    c0, c1, c2 = (volume_in.shape[2], hidden_act.shape[2], out_cot.shape[2])
    devices, copies = (lax.axis_size(EVERY), lax.axis_size(SAME))
    length = grad_bucket.shape[1]
    bucket = grad_bucket.reshape(length // LANES, LANES)
    cot = pack(out_cot[0, 0], [], 256)
    bucket, cot = lax.optimization_barrier((bucket, cot))
    core, half = (lax.axis_index("core"), bucket.shape[0] // 2)
    send = lax.dynamic_slice_in_dim(bucket, (1 - core) * half, half).astype(BF16)
    near = lax.dynamic_slice_in_dim(bucket, core * half, half)
    cot, send, near = lax.optimization_barrier((cot, send, near))
    cots = (swapped(cot), cot, crossed(cot))
    vol = pack(volume_in[0, 0], [cot], 16)
    vols = (swapped(vol), vol, crossed(vol))
    send, near = add(near, swapped(send))
    act, send, near = lax.optimization_barrier((hidden_act[0, 0], send, near))
    far = swapped(send, "x")

    used = -(-9 * c2 // LANES) * 3 * c1 + 9 * c0
    rows = ceil_to(used, 16 * devices)
    acts, w_two, w_one = prepare(act, kernel_two, kernel_one)
    pres, terms = first_part(cots, acts, w_two)
    send, keep = gradient_part(vols, pres, terms, rows, c1)
    own, inner, outer = input_part(pres, w_one)
    parts = combine(near, far, keep, swapped(send), copies)
    parts, inner, outer = lax.optimization_barrier((parts, inner, outer))
    parts = lax.all_to_all(parts, SAME, 0, 0)
    cells = volume_in.shape[3] * volume_in.shape[4] * devices
    shares = share(parts, rows // devices, 1.0 / math.sqrt(cells))

    shares, inner, outer = lax.optimization_barrier((shares, inner, outer))
    mine = lax.all_to_all(shares, SAME, 0, 0)
    inner, outer = (swapped(inner), crossed(outer))
    grad_input = merge(own, inner, outer, volume_in.shape[2:])
    mine, grad_input = lax.optimization_barrier((mine, grad_input))
    bucket_sum, total_one, total_two = finish(mine, swapped(mine), length, (c0, c1, c2))
    return (
        grad_input[None, None],
        total_one.reshape(3, 3, 3, c0, c1),
        total_two.reshape(3, 3, 3, c1, c2),
        bucket_sum.reshape(length),
    )


def solution(mesh):
    dp, space = (mesh.shape["dp"], mesh.shape["space"])
    split = Mesh(mesh.devices.reshape(dp // 2, 2, space // 2, 2), EVERY)
    volume = P(("z", "x"), SPACE, None, None, None)
    in_specs = (volume, volume, volume, P(), P(), P(EVERY, None))
    out_specs = (volume, P(), P(), P())
    return jax.shard_map(
        per_device, mesh=split, in_specs=in_specs, out_specs=out_specs, check_vma=False
    )
```

```python
import math

import jax
import jax.numpy as jnp
from jax import lax
from jax.experimental import pallas as pl
from jax.experimental.pallas import tpu as pltpu
from jax.sharding import Mesh, PartitionSpec as P

SPACE = ("y", "core")
SAME = ("x", "y", "z")
EVERY = ("z", "x", "y", "core")
GROUP = 8
LANES = 128
BF16 = jnp.bfloat16
F32 = jnp.float32


def ceil_to(value, step):
    return -(-value // step) * step


def slid(value, step):
    lane = lax.broadcasted_iota(jnp.int32, value.shape, 1)
    width = value.shape[1]
    keep = lane >= step if step > 0 else lane < width + step
    return jnp.where(keep, pltpu.roll(value, step % width, 1), 0.0)


def beside(window, rows, step, count):
    return jnp.concatenate([window[g * step : g * step + rows] for g in range(count)], axis=1)


def turned(src, flat, dst):
    chans, length, _ = src.shape

    def stage(c, carry):
        flat[pl.ds(pl.multiple_of(c * length, length), length), :] = src[c].astype(F32)
        return carry

    lax.fori_loop(0, chans, stage, 0, unroll=4)

    def gather(x, carry):
        rows = flat[pl.ds(x, chans, stride=length), :]
        dst[pl.ds(pl.multiple_of(x * chans, 16), chans), :] = rows.astype(BF16)
        return carry

    lax.fori_loop(0, length, gather, 0, unroll=4)


def pack_kernel(field, *refs):
    out, flat = refs[-2:]
    turned(field, flat, out)


def pack(field, after, weight):
    chans, length, width = field.shape
    spec = pl.BlockSpec(memory_space=pltpu.VMEM)
    return pl.pallas_call(
        pack_kernel,
        out_shape=jax.ShapeDtypeStruct((length * chans, width), BF16),
        in_specs=[spec] + [pl.BlockSpec(memory_space=pl.ANY) for _ in after],
        out_specs=spec,
        scratch_shapes=[pltpu.VMEM((chans * length, width), F32)],
        compiler_params=pltpu.CompilerParams(vmem_limit_bytes=24 * 2**20),
        cost_estimate=pl.CostEstimate(
            flops=0, bytes_accessed=weight * field.size, transcendentals=0
        ),
    )(field, *after)


def in_steps(body, rows, count=8):
    step = rows // count

    def one(n, carry):
        body(n * step, step)
        return carry

    lax.fori_loop(0, count, one, 0)


def add_kernel(own, other, send, keep):
    rows = send.shape[0]
    mine = lax.axis_index("x") * rows
    theirs = rows - mine

    def total(at, step):
        at = pl.ds(pl.multiple_of(at, 16), step)
        return own[at, :] + other[at, :].astype(F32)

    def add(at, step):
        to = pl.ds(pl.multiple_of(at, 16), step)
        send[to, :] = total(theirs + at, step).astype(send.dtype)
        keep[to, :] = total(mine + at, step)

    in_steps(add, rows)


def add(own, other):
    rows = other.shape[0] // 2
    return vmem_call(
        add_kernel,
        (jax.ShapeDtypeStruct((rows, LANES), BF16), jax.ShapeDtypeStruct((rows, LANES), F32)),
        (),
        pl.CostEstimate(flops=0, bytes_accessed=8 * own.size, transcendentals=0),
    )(own, other)


def combine_kernel(keep, other, terms, more, out):
    parts, rows, _ = out.shape
    height, extra = (keep.shape[0] // parts, terms.shape[0] // parts)
    padded = rows - extra
    total = keep[...] + other[...].astype(F32)
    grads = terms[...] + more[...].astype(F32)
    for n in range(parts):
        value = total[n * height : (n + 1) * height]
        if padded > height:
            value = jnp.concatenate([value, jnp.zeros((padded - height, LANES), F32)], axis=0)
        out[n, 0:padded, :] = value.astype(out.dtype)
        out[n, padded:rows, :] = grads[n * extra : (n + 1) * extra].astype(out.dtype)


def combine(keep, other, terms, more, parts):
    rows = ceil_to(keep.shape[0] // parts, 16) + terms.shape[0] // parts
    return vmem_call(
        combine_kernel,
        jax.ShapeDtypeStruct((parts, rows, LANES), BF16),
        (),
        pl.CostEstimate(flops=0, bytes_accessed=8 * keep.size, transcendentals=0),
    )(keep, other, terms, more)


def split_to(total, mine, send, keep):
    half = total.shape[0] // 2
    keep[...] = total[pl.ds(pl.multiple_of(mine * half, 16), half), :]
    send[...] = total[pl.ds(pl.multiple_of((1 - mine) * half, 16), half), :].astype(send.dtype)


def swapped(value, axis="core"):
    return lax.ppermute(value, axis, [(0, 1), (1, 0)])


def plane_order():
    core = lax.axis_index("core")
    ahead = [core * n + (1 - core) * (2 - n) for n in range(3)]
    back = [core * (2 - n) + (1 - core) * n for n in range(3)]
    return (ahead, back)


def windows(packs, x, count):
    length = packs[0].shape[0] // count

    def row(p, n):
        if 0 <= n < length:
            return p[n * count : (n + 1) * count, :]
        return jnp.zeros((count, LANES), BF16)

    rows = [[row(p, x + n - 1) for p in packs] for n in range(GROUP + 2)]
    return jnp.concatenate(
        [jnp.concatenate(sum(rows[g : g + 3], []), axis=0) for g in range(GROUP)], axis=1
    )


def ordered(acc, count, ahead):
    blocks = [pl.multiple_of((3 * j + n) * count, 16) for j in range(3) for n in ahead]
    return jnp.concatenate([acc[pl.ds(at, count), :] for at in blocks], axis=0)


def across_lanes(first, second):
    return lax.dot_general(
        first, second, (((1,), (1,)), ((), ())), preferred_element_type=F32
    )


def prepare_kernel(act, two, one, acts, w_two, w_one, flat):
    ahead, back = plane_order()
    turned(act, flat, acts)
    w_two[...] = jnp.concatenate(
        [
            jnp.concatenate([two[back[n], 2 - j, 2 - k].astype(F32) for k in range(3)], axis=0)
            for j in range(3)
            for n in range(3)
        ],
        axis=1,
    ).astype(BF16)
    w_one[...] = jnp.concatenate(
        [
            jnp.concatenate([one[ahead[n], 2 - j, k].astype(F32) for n in range(3)], axis=0)
            for j in range(3)
            for k in range(3)
        ],
        axis=1,
    ).astype(BF16)


def prepare(act, kernel_two, kernel_one):
    c1, length, width = act.shape
    c0, c2 = (kernel_one.shape[3], kernel_two.shape[4])
    return vmem_call(
        prepare_kernel,
        (
            jax.ShapeDtypeStruct((length * c1, width), BF16),
            jax.ShapeDtypeStruct((3 * c1, 9 * c2), BF16),
            jax.ShapeDtypeStruct((3 * c0, 9 * c1), BF16),
        ),
        (pltpu.VMEM((c1 * length, width), F32),),
        pl.CostEstimate(flops=0, bytes_accessed=16 * act.size, transcendentals=0),
    )(act, kernel_two, kernel_one)


def first_kernel(pack_in, pack_0, pack_out, acts, w_two, pres, terms, acc):
    c1, c2 = (w_two.shape[0] // 3, w_two.shape[1] // 9)
    length = acts.shape[0] // c1
    packs = (pack_in, pack_0, pack_out)
    ahead, _ = plane_order()
    stacked = 3 * c1
    pres[0:stacked, :] = jnp.zeros((stacked, LANES), BF16)
    pres[(length + 1) * stacked : (length + 2) * stacked, :] = jnp.zeros((stacked, LANES), BF16)
    acc[...] = jnp.zeros_like(acc)

    for x in range(0, length, GROUP):
        right = windows(packs, x, c2)
        sums = jnp.dot(w_two[...], right, preferred_element_type=F32)
        columns = []
        for g in range(GROUP):
            part = sums[:, g * LANES : (g + 1) * LANES]
            grad = slid(part[0:c1], 1) + part[c1 : 2 * c1] + slid(part[2 * c1 : 3 * c1], -1)
            value = acts[(x + g) * c1 : (x + g + 1) * c1, :].astype(F32)
            pre = (grad * jnp.where(value > 0, 1.0, 0.2)).astype(BF16).astype(F32)
            moved = jnp.concatenate([slid(pre, -1), pre, slid(pre, 1)], axis=0).astype(BF16)
            pres[(x + g + 1) * stacked : (x + g + 2) * stacked, :] = moved
            stack = jnp.concatenate([slid(value, 1), value, slid(value, -1)], axis=0)
            columns.append(stack.astype(BF16))
        acc[...] += across_lanes(right, jnp.concatenate(columns, axis=1))

    terms[...] = jnp.zeros_like(terms)
    total = ordered(acc, c2, ahead).T
    rows, width = total.shape
    for block in range(-(-width // LANES)):
        part = total[:, block * LANES : min(width, (block + 1) * LANES)]
        terms[block * rows : (block + 1) * rows, 0 : part.shape[1]] = part


def gradient_kernel(pack_in, pack_0, pack_out, pres, before, send, keep, acc, terms):
    c0, stacked = (acc.shape[0] // 9, acc.shape[1])
    packs = (pack_in, pack_0, pack_out)
    ahead, _ = plane_order()
    length = pres.shape[0] // stacked - 2
    acc[...] = jnp.zeros_like(acc)

    for x in range(0, length, GROUP):
        rows = [pres[(x + g + 1) * stacked : (x + g + 2) * stacked, :] for g in range(GROUP)]
        acc[...] += across_lanes(windows(packs, x, c0), jnp.concatenate(rows, axis=1))

    used = before.shape[0]
    terms[0:used, :] = before[...]
    terms[used:, :] = jnp.zeros((terms.shape[0] - used, LANES), F32)
    total = ordered(acc, c0, ahead)
    terms[used : used + total.shape[0], 0 : total.shape[1]] = total
    split_to(terms, lax.axis_index("core"), send, keep)


def input_kernel(pres, w_one, own, inner, outer):
    c0, stacked = (w_one.shape[0] // 3, w_one.shape[1] // 3)
    length = pres.shape[0] // stacked - 2

    for x in range(0, length, GROUP):
        window = pres[x * stacked : (x + GROUP + 2) * stacked, :]
        moved = beside(window, 3 * stacked, stacked, GROUP)
        sums = jnp.dot(w_one[...], moved, preferred_element_type=F32)
        for g in range(GROUP):
            part = sums[:, g * LANES : (g + 1) * LANES]
            at = pl.ds((x + g) * c0, c0)
            for i, out in ((0, inner), (1, own), (2, outer)):
                out[at, :] = part[i * c0 : (i + 1) * c0].astype(out.dtype)


def vmem_call(body, out_shape, scratch=(), cost=None, limit=24 * 2**20):
    spec = pl.BlockSpec(memory_space=pltpu.VMEM)
    return pl.pallas_call(
        body,
        out_shape=out_shape,
        out_specs=jax.tree.map(lambda _: spec, out_shape),
        scratch_shapes=list(scratch),
        compiler_params=pltpu.CompilerParams(vmem_limit_bytes=limit),
        cost_estimate=cost,
    )


def first_part(packs, acts, w_two):
    c1, c2, width = (w_two.shape[0] // 3, w_two.shape[1] // 9, acts.shape[1])
    length = acts.shape[0] // c1
    return vmem_call(
        first_kernel,
        (
            jax.ShapeDtypeStruct(((length + 2) * 3 * c1, width), BF16),
            jax.ShapeDtypeStruct((-(-9 * c2 // LANES) * 3 * c1, LANES), F32),
        ),
        (pltpu.VMEM((9 * c2, 3 * c1), F32),),
        pl.CostEstimate(flops=10**9, bytes_accessed=20 * 2**20, transcendentals=0),
    )(*packs, acts, w_two)


def gradient_part(packs, pres, terms, rows, c1):
    width = pres.shape[1]
    c0 = packs[0].shape[0] // (pres.shape[0] // (3 * c1) - 2)
    return vmem_call(
        gradient_kernel,
        (
            jax.ShapeDtypeStruct((rows // 2, LANES), BF16),
            jax.ShapeDtypeStruct((rows // 2, LANES), F32),
        ),
        (pltpu.VMEM((9 * c0, 3 * c1), F32), pltpu.VMEM((rows, width), F32)),
        pl.CostEstimate(flops=10**9, bytes_accessed=5 * 2**20, transcendentals=0),
    )(*packs, pres, terms)


def input_part(pres, w_one):
    c0, stacked = (w_one.shape[0] // 3, w_one.shape[1] // 3)
    plane = ((pres.shape[0] // stacked - 2) * c0, pres.shape[1])
    return vmem_call(
        input_kernel,
        (
            jax.ShapeDtypeStruct(plane, BF16),
            jax.ShapeDtypeStruct(plane, BF16),
            jax.ShapeDtypeStruct(plane, BF16),
        ),
        (),
        pl.CostEstimate(flops=10**9, bytes_accessed=5 * 2**20, transcendentals=0),
    )(pres, w_one)


def merge_kernel(own, first, second, out, flat):
    chans, length, _ = out.shape

    def add(step, carry):
        at = pl.ds(pl.multiple_of(step * 64, 64), 64)
        flat[at, :] = own[at, :].astype(F32) + first[at, :].astype(F32) + second[at, :].astype(F32)
        return carry

    lax.fori_loop(0, own.shape[0] // 64, add, 0, unroll=4)

    def gather(c, carry):
        out[c] = flat[pl.ds(c, length, stride=chans), :].astype(out.dtype)
        return carry

    lax.fori_loop(0, chans, gather, 0, unroll=4)


def merge(own, first, second, shape):
    return vmem_call(
        merge_kernel,
        jax.ShapeDtypeStruct(shape, BF16),
        (pltpu.VMEM(own.shape, F32),),
        pl.CostEstimate(flops=2 * own.size, bytes_accessed=8 * own.size, transcendentals=0),
    )(own, first, second)


def share_kernel(scale, parts, out, buffer, sems):
    copies, rows, _ = parts.shape
    padded = out.shape[1] - rows
    far = copies // 2
    buffer[0:padded, :] = jnp.sum(parts[0:far, 0:padded, :].astype(F32), axis=0).astype(BF16)
    buffer[padded : 2 * padded, :] = jnp.sum(parts[far:, 0:padded, :].astype(F32), axis=0).astype(BF16)
    grads = jnp.sum(parts[:, padded:rows, :].astype(F32), axis=0) * scale
    buffer[2 * padded :, :] = grads.astype(BF16)
    sent = [pltpu.make_async_copy(buffer, out.at[n], sems.at[n]) for n in range(copies)]
    for copy in sent:
        copy.start()
    for copy in sent:
        copy.wait()


def share(parts, extra, scale):
    copies, rows, _ = parts.shape
    height = 2 * rows - extra
    return pl.pallas_call(
        lambda *refs: share_kernel(scale, *refs),
        out_shape=jax.ShapeDtypeStruct((copies, height, LANES), BF16),
        in_specs=[pl.BlockSpec(memory_space=pltpu.VMEM)],
        out_specs=pl.BlockSpec(memory_space=pl.ANY),
        scratch_shapes=[pltpu.VMEM((height, LANES), BF16), pltpu.SemaphoreType.DMA((copies,))],
        compiler_params=pltpu.CompilerParams(vmem_limit_bytes=24 * 2**20),
        cost_estimate=pl.CostEstimate(
            flops=parts.size, bytes_accessed=6 * parts.size, transcendentals=0
        ),
    )(parts)


def place(source, height, padded, which, bucket, buffer, sems):
    copies, count = (source.shape[0], sems.shape[0])
    step = 2 * copies // count
    sent = []
    for n in range(count):
        for m in range(n * step, (n + 1) * step):
            half, q = (m // copies, m % copies)
            value = source[q, half * padded : (half + 1) * padded, :].astype(F32)
            buffer[m * height : (m + 1) * height, :] = value[0:height]
        rows = pl.ds(n * step * height, step * height)
        at = (which * count + n) * step * height
        at = pl.ds(pl.multiple_of(at, 8), step * height)
        sent.append(pltpu.make_async_copy(buffer.at[rows], bucket.at[at], sems.at[n]))
        sent[-1].start()
    return sent


def start_kernel(height, padded, mine, bucket, buffer, sems):
    for copy in place(mine, height, padded, lax.axis_index("core"), bucket, buffer, sems):
        copy.wait()


def finish_kernel(
    sizes, height, padded, mine, other, partial,
    bucket, out_one, out_two,
    raw, one, two, out_sems, buffer, sems,
):
    c0, c1, c2 = sizes
    copies, rows, _ = mine.shape
    extra = rows - 2 * padded
    me = lax.axis_index("core")
    sent = place(other, height, padded, 1 - me, bucket, buffer, sems)

    for q in range(copies):
        for source, which in ((mine, me), (other, 1 - me)):
            at = pl.multiple_of((which * copies + q) * extra, 8)
            raw[pl.ds(at, extra), :] = source[q, 2 * padded : rows, :].astype(F32)
    block = 3 * c1
    first = -(-9 * c2 // LANES) * block
    for i in range(3):
        for j in range(3):
            column = ((2 - j) * 3 + 2 - i) * c2
            whole, lane = (column // LANES, column % LANES)
            two[(3 * i + j) * block : (3 * i + j + 1) * block, :] = raw[
                whole * block : (whole + 1) * block, lane : lane + c2
            ]
        at = pl.ds(3 * i * block, 3 * block)
        sent.append(pltpu.make_async_copy(two.at[at], out_two.at[at], out_sems.at[i]))
        sent[-1].start()
    for i in range(3):
        for j in range(3):
            row = first + (3 * j + i) * c0
            for k in range(3):
                to = (9 * i + 3 * j + k) * c0
                one[to : to + c0, :] = raw[row : row + c0, k * c1 : (k + 1) * c1]
        at = pl.ds(9 * i * c0, 9 * c0)
        sent.append(pltpu.make_async_copy(one.at[at], out_one.at[at], out_sems.at[3 + i]))
        sent[-1].start()
    for copy in sent:
        copy.wait()


def finish(mine, other, length, sizes):
    c0, c1, c2 = sizes
    copies, rows, _ = mine.shape
    height = length // LANES // (4 * copies)
    padded = ceil_to(height, 16)
    spec = pl.BlockSpec(memory_space=pltpu.VMEM)
    remote = pl.BlockSpec(memory_space=pltpu.HBM)
    whole = jax.ShapeDtypeStruct((length // LANES, LANES), F32)
    chunks = 4
    scratch = [
        pltpu.VMEM((2 * copies * height, LANES), F32),
        pltpu.SemaphoreType.DMA((chunks,)),
    ]
    params = pltpu.CompilerParams(vmem_limit_bytes=24 * 2**20)
    partial = pl.pallas_call(
        lambda *refs: start_kernel(height, padded, *refs),
        out_shape=whole,
        in_specs=[spec],
        out_specs=remote,
        scratch_shapes=scratch,
        compiler_params=params,
    )(mine)
    return pl.pallas_call(
        lambda *refs: finish_kernel(sizes, height, padded, *refs),
        out_shape=(
            whole,
            jax.ShapeDtypeStruct((27 * c0, c1), F32),
            jax.ShapeDtypeStruct((27 * c1, c2), F32),
        ),
        in_specs=[spec, spec, remote],
        out_specs=(remote, remote, remote),
        scratch_shapes=[
            pltpu.VMEM((2 * copies * (rows - 2 * padded), LANES), F32),
            pltpu.VMEM((27 * c0, c1), F32),
            pltpu.VMEM((27 * c1, c2), F32),
            pltpu.SemaphoreType.DMA((6,)),
        ]
        + scratch,
        input_output_aliases={2: 0},
        compiler_params=params,
    )(mine, other, partial)


def crossed(value):
    pairs = [(n, n + 1) for n in range(1, lax.axis_size(SPACE) - 1, 2)]
    return lax.ppermute(value, SPACE, pairs + [(m, n) for n, m in pairs])


def per_device(volume_in, hidden_act, out_cot, kernel_one, kernel_two, grad_bucket):
    c0, c1, c2 = (volume_in.shape[2], hidden_act.shape[2], out_cot.shape[2])
    devices, copies = (lax.axis_size(EVERY), lax.axis_size(SAME))
    length = grad_bucket.shape[1]
    bucket = grad_bucket.reshape(length // LANES, LANES)
    cot = pack(out_cot[0, 0], [], 256)
    bucket, cot = lax.optimization_barrier((bucket, cot))
    core, half = (lax.axis_index("core"), bucket.shape[0] // 2)
    send = lax.dynamic_slice_in_dim(bucket, (1 - core) * half, half).astype(BF16)
    near = lax.dynamic_slice_in_dim(bucket, core * half, half)
    cot, send, near = lax.optimization_barrier((cot, send, near))
    cots = (swapped(cot), cot, crossed(cot))
    vol = pack(volume_in[0, 0], [cot], 16)
    vols = (swapped(vol), vol, crossed(vol))
    send, near = add(near, swapped(send))
    act, send, near = lax.optimization_barrier((hidden_act[0, 0], send, near))
    far = swapped(send, "x")

    used = -(-9 * c2 // LANES) * 3 * c1 + 9 * c0
    rows = ceil_to(used, 16 * devices)
    acts, w_two, w_one = prepare(act, kernel_two, kernel_one)
    pres, terms = first_part(cots, acts, w_two)
    send, keep = gradient_part(vols, pres, terms, rows, c1)
    own, inner, outer = input_part(pres, w_one)
    parts = combine(near, far, keep, swapped(send), copies)
    parts, inner, outer = lax.optimization_barrier((parts, inner, outer))
    parts = lax.all_to_all(parts, SAME, 0, 0)
    cells = volume_in.shape[3] * volume_in.shape[4] * devices
    shares = share(parts, rows // devices, 1.0 / math.sqrt(cells))

    shares, inner, outer = lax.optimization_barrier((shares, inner, outer))
    mine = lax.all_to_all(shares, SAME, 0, 0)
    inner, outer = (swapped(inner), crossed(outer))
    grad_input = merge(own, inner, outer, volume_in.shape[2:])
    mine, grad_input = lax.optimization_barrier((mine, grad_input))
    bucket_sum, total_one, total_two = finish(mine, swapped(mine), length, (c0, c1, c2))
    return (
        grad_input[None, None],
        total_one.reshape(3, 3, 3, c0, c1),
        total_two.reshape(3, 3, 3, c1, c2),
        bucket_sum.reshape(length),
    )


def solution(mesh):
    dp, space = (mesh.shape["dp"], mesh.shape["space"])
    split = Mesh(mesh.devices.reshape(dp // 2, 2, space // 2, 2), EVERY)
    volume = P(("z", "x"), SPACE, None, None, None)
    in_specs = (volume, volume, volume, P(), P(), P(EVERY, None))
    out_specs = (volume, P(), P(), P())
    return jax.shard_map(
        per_device, mesh=split, in_specs=in_specs, out_specs=out_specs, check_vma=False
    )
```

```python
import math

import jax
import jax.numpy as jnp
from jax import lax
from jax.experimental import pallas as pl
from jax.experimental.pallas import tpu as pltpu
from jax.sharding import Mesh, PartitionSpec as P

SPACE = ("y", "core")
SAME = ("x", "z", "y")
GATHER = ("z", "x", "y")
EVERY = ("z", "x", "y", "core")
GROUP = 8
LANES = 128
BF16 = jnp.bfloat16
F32 = jnp.float32


def ceil_to(value, step):
    return -(-value // step) * step


def slid(value, step):
    lane = lax.broadcasted_iota(jnp.int32, value.shape, 1)
    width = value.shape[1]
    keep = lane >= step if step > 0 else lane < width + step
    return jnp.where(keep, pltpu.roll(value, step % width, 1), 0.0)


def beside(window, rows, step, count):
    return jnp.concatenate([window[g * step : g * step + rows] for g in range(count)], axis=1)


def turned(src, flat, dst):
    chans, length, _ = src.shape

    def stage(c, carry):
        flat[pl.ds(pl.multiple_of(c * length, length), length), :] = src[c].astype(F32)
        return carry

    lax.fori_loop(0, chans, stage, 0, unroll=4)

    def gather(x, carry):
        rows = flat[pl.ds(x, chans, stride=length), :]
        dst[pl.ds(pl.multiple_of(x * chans, 16), chans), :] = rows.astype(BF16)
        return carry

    lax.fori_loop(0, length, gather, 0, unroll=4)


def pack_kernel(field, *refs):
    out, flat = refs[-2:]
    turned(field, flat, out)


def pack(field, after, weight):
    chans, length, width = field.shape
    spec = pl.BlockSpec(memory_space=pltpu.VMEM)
    return pl.pallas_call(
        pack_kernel,
        out_shape=jax.ShapeDtypeStruct((length * chans, width), BF16),
        in_specs=[spec] + [pl.BlockSpec(memory_space=pl.ANY) for _ in after],
        out_specs=spec,
        scratch_shapes=[pltpu.VMEM((chans * length, width), F32)],
        compiler_params=pltpu.CompilerParams(vmem_limit_bytes=24 * 2**20),
        cost_estimate=pl.CostEstimate(
            flops=0, bytes_accessed=weight * field.size, transcendentals=0
        ),
    )(field, *after)


def in_steps(body, rows, count=8):
    step = rows // count

    def one(n, carry):
        body(n * step, step)
        return carry

    lax.fori_loop(0, count, one, 0)


def add_kernel(own, other, send, keep):
    rows = send.shape[0]
    mine = lax.axis_index("x") * rows
    theirs = rows - mine

    def total(at, step):
        at = pl.ds(pl.multiple_of(at, 16), step)
        return own[at, :] + other[at, :].astype(F32)

    def add(at, step):
        to = pl.ds(pl.multiple_of(at, 16), step)
        send[to, :] = total(theirs + at, step).astype(send.dtype)
        keep[to, :] = total(mine + at, step)

    in_steps(add, rows)


def add(own, other):
    rows = other.shape[0] // 2
    return vmem_call(
        add_kernel,
        (jax.ShapeDtypeStruct((rows, LANES), BF16), jax.ShapeDtypeStruct((rows, LANES), F32)),
        (),
        pl.CostEstimate(flops=0, bytes_accessed=8 * own.size, transcendentals=0),
    )(own, other)


def combine_kernel(keep, other, terms, more, out):
    parts, rows, _ = out.shape
    height, extra = (keep.shape[0] // parts, terms.shape[0] // parts)
    padded = rows - extra
    total = keep[...] + other[...].astype(F32)
    grads = terms[...] + more[...].astype(F32)
    for n in range(parts):
        value = total[n * height : (n + 1) * height]
        if padded > height:
            value = jnp.concatenate([value, jnp.zeros((padded - height, LANES), F32)], axis=0)
        out[n, 0:padded, :] = value.astype(out.dtype)
        out[n, padded:rows, :] = grads[n * extra : (n + 1) * extra].astype(out.dtype)


def combine(keep, other, terms, more, parts):
    rows = ceil_to(keep.shape[0] // parts, 16) + terms.shape[0] // parts
    return vmem_call(
        combine_kernel,
        jax.ShapeDtypeStruct((parts, rows, LANES), BF16),
        (),
        pl.CostEstimate(flops=0, bytes_accessed=8 * keep.size, transcendentals=0),
    )(keep, other, terms, more)


def split_to(total, mine, send, keep):
    half = total.shape[0] // 2
    keep[...] = total[pl.ds(pl.multiple_of(mine * half, 16), half), :]
    send[...] = total[pl.ds(pl.multiple_of((1 - mine) * half, 16), half), :].astype(send.dtype)


def swapped(value, axis="core"):
    return lax.ppermute(value, axis, [(0, 1), (1, 0)])


def plane_order():
    core = lax.axis_index("core")
    ahead = [core * n + (1 - core) * (2 - n) for n in range(3)]
    back = [core * (2 - n) + (1 - core) * n for n in range(3)]
    return (ahead, back)


def windows(packs, x, count):
    length = packs[0].shape[0] // count

    def row(p, n):
        if 0 <= n < length:
            return p[n * count : (n + 1) * count, :]
        return jnp.zeros((count, LANES), BF16)

    rows = [[row(p, x + n - 1) for p in packs] for n in range(GROUP + 2)]
    return jnp.concatenate(
        [jnp.concatenate(sum(rows[g : g + 3], []), axis=0) for g in range(GROUP)], axis=1
    )


def ordered(acc, count, ahead):
    blocks = [pl.multiple_of((3 * j + n) * count, 16) for j in range(3) for n in ahead]
    return jnp.concatenate([acc[pl.ds(at, count), :] for at in blocks], axis=0)


def across_lanes(first, second):
    return lax.dot_general(
        first, second, (((1,), (1,)), ((), ())), preferred_element_type=F32
    )


def prepare_kernel(act, two, one, acts, w_two, w_one, flat):
    ahead, back = plane_order()
    turned(act, flat, acts)
    w_two[...] = jnp.concatenate(
        [
            jnp.concatenate([two[back[n], 2 - j, 2 - k].astype(F32) for k in range(3)], axis=0)
            for j in range(3)
            for n in range(3)
        ],
        axis=1,
    ).astype(BF16)
    w_one[...] = jnp.concatenate(
        [
            jnp.concatenate([one[ahead[n], 2 - j, k].astype(F32) for n in range(3)], axis=0)
            for j in range(3)
            for k in range(3)
        ],
        axis=1,
    ).astype(BF16)


def prepare(act, kernel_two, kernel_one):
    c1, length, width = act.shape
    c0, c2 = (kernel_one.shape[3], kernel_two.shape[4])
    return vmem_call(
        prepare_kernel,
        (
            jax.ShapeDtypeStruct((length * c1, width), BF16),
            jax.ShapeDtypeStruct((3 * c1, 9 * c2), BF16),
            jax.ShapeDtypeStruct((3 * c0, 9 * c1), BF16),
        ),
        (pltpu.VMEM((c1 * length, width), F32),),
        pl.CostEstimate(flops=0, bytes_accessed=16 * act.size, transcendentals=0),
    )(act, kernel_two, kernel_one)


def first_kernel(pack_in, pack_0, pack_out, acts, w_two, pres, terms, acc):
    c1, c2 = (w_two.shape[0] // 3, w_two.shape[1] // 9)
    length = acts.shape[0] // c1
    packs = (pack_in, pack_0, pack_out)
    ahead, _ = plane_order()
    stacked = 3 * c1
    pres[0:stacked, :] = jnp.zeros((stacked, LANES), BF16)
    pres[(length + 1) * stacked : (length + 2) * stacked, :] = jnp.zeros((stacked, LANES), BF16)
    acc[...] = jnp.zeros_like(acc)

    for x in range(0, length, GROUP):
        right = windows(packs, x, c2)
        sums = jnp.dot(w_two[...], right, preferred_element_type=F32)
        columns = []
        for g in range(GROUP):
            part = sums[:, g * LANES : (g + 1) * LANES]
            grad = slid(part[0:c1], 1) + part[c1 : 2 * c1] + slid(part[2 * c1 : 3 * c1], -1)
            value = acts[(x + g) * c1 : (x + g + 1) * c1, :].astype(F32)
            pre = (grad * jnp.where(value > 0, 1.0, 0.2)).astype(BF16).astype(F32)
            moved = jnp.concatenate([slid(pre, -1), pre, slid(pre, 1)], axis=0).astype(BF16)
            pres[(x + g + 1) * stacked : (x + g + 2) * stacked, :] = moved
            stack = jnp.concatenate([slid(value, 1), value, slid(value, -1)], axis=0)
            columns.append(stack.astype(BF16))
        acc[...] += across_lanes(right, jnp.concatenate(columns, axis=1))

    terms[...] = jnp.zeros_like(terms)
    total = ordered(acc, c2, ahead).T
    rows, width = total.shape
    for block in range(-(-width // LANES)):
        part = total[:, block * LANES : min(width, (block + 1) * LANES)]
        terms[block * rows : (block + 1) * rows, 0 : part.shape[1]] = part


def gradient_kernel(pack_in, pack_0, pack_out, pres, before, send, keep, acc, terms):
    c0, stacked = (acc.shape[0] // 9, acc.shape[1])
    packs = (pack_in, pack_0, pack_out)
    ahead, _ = plane_order()
    length = pres.shape[0] // stacked - 2
    acc[...] = jnp.zeros_like(acc)

    for x in range(0, length, GROUP):
        rows = [pres[(x + g + 1) * stacked : (x + g + 2) * stacked, :] for g in range(GROUP)]
        acc[...] += across_lanes(windows(packs, x, c0), jnp.concatenate(rows, axis=1))

    used = before.shape[0]
    terms[0:used, :] = before[...]
    terms[used:, :] = jnp.zeros((terms.shape[0] - used, LANES), F32)
    total = ordered(acc, c0, ahead)
    terms[used : used + total.shape[0], 0 : total.shape[1]] = total
    split_to(terms, lax.axis_index("core"), send, keep)


def input_kernel(pres, w_one, own, inner, outer):
    c0, stacked = (w_one.shape[0] // 3, w_one.shape[1] // 3)
    length = pres.shape[0] // stacked - 2

    for x in range(0, length, GROUP):
        window = pres[x * stacked : (x + GROUP + 2) * stacked, :]
        moved = beside(window, 3 * stacked, stacked, GROUP)
        sums = jnp.dot(w_one[...], moved, preferred_element_type=F32)
        for g in range(GROUP):
            part = sums[:, g * LANES : (g + 1) * LANES]
            at = pl.ds((x + g) * c0, c0)
            for i, out in ((0, inner), (1, own), (2, outer)):
                out[at, :] = part[i * c0 : (i + 1) * c0].astype(out.dtype)


def vmem_call(body, out_shape, scratch=(), cost=None, limit=24 * 2**20):
    spec = pl.BlockSpec(memory_space=pltpu.VMEM)
    return pl.pallas_call(
        body,
        out_shape=out_shape,
        out_specs=jax.tree.map(lambda _: spec, out_shape),
        scratch_shapes=list(scratch),
        compiler_params=pltpu.CompilerParams(vmem_limit_bytes=limit),
        cost_estimate=cost,
    )


def first_part(packs, acts, w_two):
    c1, c2, width = (w_two.shape[0] // 3, w_two.shape[1] // 9, acts.shape[1])
    length = acts.shape[0] // c1
    return vmem_call(
        first_kernel,
        (
            jax.ShapeDtypeStruct(((length + 2) * 3 * c1, width), BF16),
            jax.ShapeDtypeStruct((-(-9 * c2 // LANES) * 3 * c1, LANES), F32),
        ),
        (pltpu.VMEM((9 * c2, 3 * c1), F32),),
        pl.CostEstimate(flops=10**9, bytes_accessed=20 * 2**20, transcendentals=0),
    )(*packs, acts, w_two)


def gradient_part(packs, pres, terms, rows, c1):
    width = pres.shape[1]
    c0 = packs[0].shape[0] // (pres.shape[0] // (3 * c1) - 2)
    return vmem_call(
        gradient_kernel,
        (
            jax.ShapeDtypeStruct((rows // 2, LANES), BF16),
            jax.ShapeDtypeStruct((rows // 2, LANES), F32),
        ),
        (pltpu.VMEM((9 * c0, 3 * c1), F32), pltpu.VMEM((rows, width), F32)),
        pl.CostEstimate(flops=10**9, bytes_accessed=5 * 2**20, transcendentals=0),
    )(*packs, pres, terms)


def input_part(pres, w_one):
    c0, stacked = (w_one.shape[0] // 3, w_one.shape[1] // 3)
    plane = ((pres.shape[0] // stacked - 2) * c0, pres.shape[1])
    return vmem_call(
        input_kernel,
        (
            jax.ShapeDtypeStruct(plane, BF16),
            jax.ShapeDtypeStruct(plane, BF16),
            jax.ShapeDtypeStruct(plane, BF16),
        ),
        (),
        pl.CostEstimate(flops=10**9, bytes_accessed=5 * 2**20, transcendentals=0),
    )(pres, w_one)


def merge_kernel(own, first, second, out, flat):
    chans, length, _ = out.shape

    def add(step, carry):
        at = pl.ds(pl.multiple_of(step * 64, 64), 64)
        flat[at, :] = own[at, :].astype(F32) + first[at, :].astype(F32) + second[at, :].astype(F32)
        return carry

    lax.fori_loop(0, own.shape[0] // 64, add, 0, unroll=4)

    def gather(c, carry):
        out[c] = flat[pl.ds(c, length, stride=chans), :].astype(out.dtype)
        return carry

    lax.fori_loop(0, chans, gather, 0, unroll=4)


def merge(own, first, second, shape):
    return vmem_call(
        merge_kernel,
        jax.ShapeDtypeStruct(shape, BF16),
        (pltpu.VMEM(own.shape, F32),),
        pl.CostEstimate(flops=2 * own.size, bytes_accessed=8 * own.size, transcendentals=0),
    )(own, first, second)


def share_kernel(scale, parts, out, buffer, sems):
    copies, rows, _ = parts.shape
    padded = out.shape[1] - rows
    far = copies // 2
    buffer[0:padded, :] = jnp.sum(parts[0:far, 0:padded, :].astype(F32), axis=0).astype(BF16)
    buffer[padded : 2 * padded, :] = jnp.sum(parts[far:, 0:padded, :].astype(F32), axis=0).astype(BF16)
    grads = jnp.sum(parts[:, padded:rows, :].astype(F32), axis=0) * scale
    buffer[2 * padded :, :] = grads.astype(BF16)
    sent = [pltpu.make_async_copy(buffer, out.at[n], sems.at[n]) for n in range(copies)]
    for copy in sent:
        copy.start()
    for copy in sent:
        copy.wait()


def share(parts, extra, scale):
    copies, rows, _ = parts.shape
    height = 2 * rows - extra
    return pl.pallas_call(
        lambda *refs: share_kernel(scale, *refs),
        out_shape=jax.ShapeDtypeStruct((copies, height, LANES), BF16),
        in_specs=[pl.BlockSpec(memory_space=pltpu.VMEM)],
        out_specs=pl.BlockSpec(memory_space=pl.ANY),
        scratch_shapes=[pltpu.VMEM((height, LANES), BF16), pltpu.SemaphoreType.DMA((copies,))],
        compiler_params=pltpu.CompilerParams(vmem_limit_bytes=24 * 2**20),
        cost_estimate=pl.CostEstimate(
            flops=parts.size, bytes_accessed=6 * parts.size, transcendentals=0
        ),
    )(parts)


def place(source, height, padded, order, which, bucket, buffer, sems):
    copies, count = (source.shape[0], sems.shape[0])
    step = 2 * copies // count
    sent = []
    for n in range(count):
        for m in range(n * step, (n + 1) * step):
            half, q = (m // copies, m % copies)
            value = source[order[q], half * padded : (half + 1) * padded, :].astype(F32)
            buffer[m * height : (m + 1) * height, :] = value[0:height]
        rows = pl.ds(n * step * height, step * height)
        at = (which * count + n) * step * height
        at = pl.ds(pl.multiple_of(at, 8), step * height)
        sent.append(pltpu.make_async_copy(buffer.at[rows], bucket.at[at], sems.at[n]))
        sent[-1].start()
    return sent


def start_kernel(height, padded, order, mine, bucket, buffer, sems):
    for copy in place(mine, height, padded, order, lax.axis_index("core"), bucket, buffer, sems):
        copy.wait()


def finish_kernel(
    sizes, height, padded, order, mine, other, partial,
    bucket, out_one, out_two,
    raw, one, two, out_sems, buffer, sems,
):
    c0, c1, c2 = sizes
    copies, rows, _ = mine.shape
    extra = rows - 2 * padded
    me = lax.axis_index("core")
    sent = place(other, height, padded, order, 1 - me, bucket, buffer, sems)

    for q in range(copies):
        for source, which in ((mine, me), (other, 1 - me)):
            at = pl.multiple_of((which * copies + q) * extra, 8)
            raw[pl.ds(at, extra), :] = source[order[q], 2 * padded : rows, :].astype(F32)
    block = 3 * c1
    first = -(-9 * c2 // LANES) * block
    for i in range(3):
        for j in range(3):
            column = ((2 - j) * 3 + 2 - i) * c2
            whole, lane = (column // LANES, column % LANES)
            two[(3 * i + j) * block : (3 * i + j + 1) * block, :] = raw[
                whole * block : (whole + 1) * block, lane : lane + c2
            ]
        at = pl.ds(3 * i * block, 3 * block)
        sent.append(pltpu.make_async_copy(two.at[at], out_two.at[at], out_sems.at[i]))
        sent[-1].start()
    for i in range(3):
        for j in range(3):
            row = first + (3 * j + i) * c0
            for k in range(3):
                to = (9 * i + 3 * j + k) * c0
                one[to : to + c0, :] = raw[row : row + c0, k * c1 : (k + 1) * c1]
        at = pl.ds(9 * i * c0, 9 * c0)
        sent.append(pltpu.make_async_copy(one.at[at], out_one.at[at], out_sems.at[3 + i]))
        sent[-1].start()
    for copy in sent:
        copy.wait()


def finish(mine, other, length, sizes):
    c0, c1, c2 = sizes
    copies, rows, _ = mine.shape
    height = length // LANES // (4 * copies)
    padded = ceil_to(height, 16)
    nx, nz, ny = [lax.axis_size(axis) for axis in SAME]
    order = [(z * nx + x) * ny + y for x in range(nx) for z in range(nz) for y in range(ny)]
    spec = pl.BlockSpec(memory_space=pltpu.VMEM)
    remote = pl.BlockSpec(memory_space=pltpu.HBM)
    whole = jax.ShapeDtypeStruct((length // LANES, LANES), F32)
    chunks = 4
    scratch = [
        pltpu.VMEM((2 * copies * height, LANES), F32),
        pltpu.SemaphoreType.DMA((chunks,)),
    ]
    params = pltpu.CompilerParams(vmem_limit_bytes=24 * 2**20)
    partial = pl.pallas_call(
        lambda *refs: start_kernel(height, padded, order, *refs),
        out_shape=whole,
        in_specs=[spec],
        out_specs=remote,
        scratch_shapes=scratch,
        compiler_params=params,
    )(mine)
    return pl.pallas_call(
        lambda *refs: finish_kernel(sizes, height, padded, order, *refs),
        out_shape=(
            whole,
            jax.ShapeDtypeStruct((27 * c0, c1), F32),
            jax.ShapeDtypeStruct((27 * c1, c2), F32),
        ),
        in_specs=[spec, spec, remote],
        out_specs=(remote, remote, remote),
        scratch_shapes=[
            pltpu.VMEM((2 * copies * (rows - 2 * padded), LANES), F32),
            pltpu.VMEM((27 * c0, c1), F32),
            pltpu.VMEM((27 * c1, c2), F32),
            pltpu.SemaphoreType.DMA((6,)),
        ]
        + scratch,
        input_output_aliases={2: 0},
        compiler_params=params,
    )(mine, other, partial)


def crossed(value):
    pairs = [(n, n + 1) for n in range(1, lax.axis_size(SPACE) - 1, 2)]
    return lax.ppermute(value, SPACE, pairs + [(m, n) for n, m in pairs])


def per_device(volume_in, hidden_act, out_cot, kernel_one, kernel_two, grad_bucket):
    c0, c1, c2 = (volume_in.shape[2], hidden_act.shape[2], out_cot.shape[2])
    devices, copies = (lax.axis_size(EVERY), lax.axis_size(SAME))
    length = grad_bucket.shape[1]
    bucket = grad_bucket.reshape(length // LANES, LANES)
    cot = pack(out_cot[0, 0], [], 256)
    bucket, cot = lax.optimization_barrier((bucket, cot))
    core, half = (lax.axis_index("core"), bucket.shape[0] // 2)
    send = lax.dynamic_slice_in_dim(bucket, (1 - core) * half, half).astype(BF16)
    near = lax.dynamic_slice_in_dim(bucket, core * half, half)
    cot, send, near = lax.optimization_barrier((cot, send, near))
    cots = (swapped(cot), cot, crossed(cot))
    vol = pack(volume_in[0, 0], [cot], 16)
    vols = (swapped(vol), vol, crossed(vol))
    send, near = add(near, swapped(send))
    act, send, near = lax.optimization_barrier((hidden_act[0, 0], send, near))
    far = swapped(send, "x")

    used = -(-9 * c2 // LANES) * 3 * c1 + 9 * c0
    rows = ceil_to(used, 16 * devices)
    acts, w_two, w_one = prepare(act, kernel_two, kernel_one)
    pres, terms = first_part(cots, acts, w_two)
    send, keep = gradient_part(vols, pres, terms, rows, c1)
    own, inner, outer = input_part(pres, w_one)
    parts = combine(near, far, keep, swapped(send), copies)
    parts, inner, outer = lax.optimization_barrier((parts, inner, outer))
    parts = lax.all_to_all(parts, SAME, 0, 0)
    cells = volume_in.shape[3] * volume_in.shape[4] * devices
    shares = share(parts, rows // devices, 1.0 / math.sqrt(cells))

    shares, inner, outer = lax.optimization_barrier((shares, inner, outer))
    mine = lax.all_to_all(shares, GATHER, 0, 0)
    inner, outer = (swapped(inner), crossed(outer))
    grad_input = merge(own, inner, outer, volume_in.shape[2:])
    mine, grad_input = lax.optimization_barrier((mine, grad_input))
    bucket_sum, total_one, total_two = finish(mine, swapped(mine), length, (c0, c1, c2))
    return (
        grad_input[None, None],
        total_one.reshape(3, 3, 3, c0, c1),
        total_two.reshape(3, 3, 3, c1, c2),
        bucket_sum.reshape(length),
    )


def solution(mesh):
    dp, space = (mesh.shape["dp"], mesh.shape["space"])
    split = Mesh(mesh.devices.reshape(dp // 2, 2, space // 2, 2), EVERY)
    volume = P(("z", "x"), SPACE, None, None, None)
    in_specs = (volume, volume, volume, P(), P(), P(EVERY, None))
    out_specs = (volume, P(), P(), P())
    return jax.shard_map(
        per_device, mesh=split, in_specs=in_specs, out_specs=out_specs, check_vma=False
    )
```
